32 devices in a mesh: groups: 2 (over x), tensor: 16 (over z, y, core).
Axes of the slice: x: 2, y: 2, z: 4, core: 2. Of those that a mesh axis runs over, the one named last changes fastest.
Arguments:
- activations: bfloat16 [512, 8192], P(('groups', 'tensor')), parts along dimension 0, may hold values from -6 to 6
- dhidden: bfloat16 [512, 28672], P('groups', 'tensor'), parts along dimension 0, may hold values from -6 to 6
- frozen: bfloat16 [2, 8192, 28672], P(None, None, 'tensor'), may hold values from -0.0625 to 0.0625
- adapter_down_factors: bfloat16 [24, 8192, 128], P(None, 'tensor'), may hold values from -0.0625 to 0.0625
- adapter_up_factors: bfloat16 [24, 128, 28672], P(None, None, 'tensor'), may hold values from -0.75 to 0.75
- segment_adapter_index: int32 [2, 8], P('groups'), parts along dimension 0, may hold values from 0 to 23
- segment_row_counts: int32 [2, 8], P('groups'), parts along dimension 0, may hold values from 1 to 96, 256 in all within a row
- ranks: int32 [24], replicated, may hold values from 16 to 64, as said below
Outputs:
- dinput: bfloat16 [512, 8192], P(('groups', 'tensor')), parts along dimension 0
- grad_a: float32 [48, 8192, 128], P('groups', 'tensor'), parts along dimension 0
- grad_b: float32 [48, 128, 28672], P('groups', None, 'tensor'), parts along dimension 0
The draws below stay inside these ranges and needn't reach their ends.
There are 2 independent parts, one for each index of `groups`. The reference program is written for one: setup_inputs(seed, part) draws one part's arguments, and reference() takes and returns one part's arrays. A program takes and returns all parts, laid end to end along the dimension named above; an argument that names none is the same for every part. Nothing has to cross between parts.
Inputs may be any that keep to these rules, and one draw needn't show every extreme that they name: `ranks`: at least one adapter has rank 64. `segment_row_counts`: each micro-batch's rows sum to 256; in each micro-batch one segment has exactly 96 rows.
All inputs are finite; a program needn't handle non-finite values.
Results may differ from the reference program's by a relative error of at most 0.0053.
Values may be sent and summed in bfloat16 or wider, within the bound.
No kernel may reach another device: no remote copies, remote signals or barrier semaphores. Data moves between devices by JAX's collectives and lax.ppermute only.
A program may use at most 256 MiB of HBM per device.

```python
import math
import jax
import jax.numpy as jnp
import numpy as np
from jax import lax

MODEL_WIDTH = 8192
HIDDEN_UNITS = 28672
ADAPTER_COUNT = 24
MAX_RANK = 64
MB_TOK = 256
SEGS = 8
MB = 1
SEG_MOST = 96
TOKENS = 256


def draw_ranks(key, part):
    key = jax.random.fold_in(key, 7)
    first, second = jax.random.split(key)
    drawn = jax.random.randint(first, (ADAPTER_COUNT,), 16, MAX_RANK + 1, dtype=jnp.int32)
    widest = jax.random.randint(second, (), 0, ADAPTER_COUNT, dtype=jnp.int32)
    return jnp.where(jnp.arange(ADAPTER_COUNT, dtype=jnp.int32) == widest, MAX_RANK, drawn).astype(jnp.int32)


def touch_ends(entries, key, least, largest):
    place = [jax.random.randint(jax.random.fold_in(key, axis), (), 0, length) for axis, length in enumerate(entries.shape)]
    main_axis = entries.shape.index(max(entries.shape))
    next_to = place[:main_axis] + [(place[main_axis] + 1) % entries.shape[main_axis]] + place[main_axis + 1:]
    return entries.at[tuple(place)].set(least).at[tuple(next_to)].set(largest)


def strengthened(result, own_key, source, target, parts, factor):
    def block_of(axis_at):
        return (jnp.arange(result.shape[axis_at]) // (result.shape[axis_at] // parts)).reshape((-1,) + (1,) * (result.ndim - 1 - axis_at))

    near = jax.random.permutation(own_key, parts)[block_of(target)]
    second = (block_of(target) + parts // 2) % parts
    return jnp.where((block_of(source) == near) | (block_of(source) == second), factor * result, result)


def block_scale(stream_key, dims, cuts, least, top_value):
    gain = 1.0
    for position, parts in cuts:
        steps = jax.random.uniform(jax.random.fold_in(jax.random.fold_in(stream_key, 6), position), (parts,), jnp.float32, least / len(cuts), top_value / len(cuts))
        gain = gain * jnp.repeat(jnp.exp(steps), dims[position] // parts).reshape((-1,) + (1,) * (len(dims) - 1 - position))
    return gain


def profile(number_of, total, reach, skew):
    weights = [(1 << 20) // math.isqrt(grade ** skew) + 1 for grade in range(2, number_of + 1)]
    surplus, holding = total - reach - (number_of - 1), [1] * (number_of - 1)
    while surplus > 0:
        free = [i for i in range(number_of - 1) if holding[i] < reach]
        mass, remaining = sum([weights[i] for i in free]), surplus
        for i in free:
            addition = min(reach - holding[i], max(1, remaining * weights[i] // mass), surplus)
            holding[i] = holding[i] + addition
            surplus = surplus - addition
    return np.array([reach] + holding)


def ragged(key, count, total, bound, skew):
    if count == 2:
        one = jax.random.randint(key, (), max(1, total - bound), min(bound, total - 1) + 1)
        return jnp.stack([one, total - one])
    lengths = jnp.asarray(profile(count, total, bound, skew), jnp.int32)
    couples = (count - 1) // 2
    donor, taker = lengths[1:1 + 2 * couples:2], lengths[2:2 + 2 * couples:2]
    room = jnp.minimum(donor - 1, bound - taker)
    shifted = jax.random.randint(jax.random.fold_in(key, 1), (couples,), 0, 1 << 20) % (room + 1)
    lengths = lengths.at[1:1 + 2 * couples:2].set(donor - shifted).at[2:2 + 2 * couples:2].set(taker + shifted)
    return lengths[jax.random.permutation(jax.random.fold_in(key, 2), count)]


def normal_values(key, dims, spread, reach, shards=(), kind=jnp.bfloat16):
    entries = spread * jax.random.normal(key, dims, jnp.float32)
    if shards:
        entries = entries * block_scale(key, dims, shards, -0.22, 0.18)
    return jnp.clip(entries, -reach, reach).astype(kind)


def noise_with(key, shape, scale, bound, pieces, heavy, held_as=jnp.bfloat16):
    values = scale * jax.random.normal(key, shape, jnp.float32)
    if pieces:
        values = values * block_scale(key, shape, pieces, -0.22, 0.18)
    return jnp.clip(strengthened(values, jax.random.fold_in(key, 3), *heavy), -bound, bound).astype(held_as)


def setup_inputs(seed: int = 0, part: int = 0) -> dict:
    arg_keys = jax.random.split(jax.random.key(seed), 9)
    own_keys = jax.random.split(jax.random.fold_in(arg_keys[8], part), 9)
    return {
        "activations": normal_values(own_keys[0], (TOKENS, MODEL_WIDTH), 1.0, 6.0, ((0, 16),)),
        "dhidden": noise_with(own_keys[1], (TOKENS, HIDDEN_UNITS), 1.0, 6.0, ((1, 16),), (1, 0, 16, 2.0)),
        "frozen": normal_values(arg_keys[2], (2, MODEL_WIDTH, HIDDEN_UNITS), MODEL_WIDTH ** -0.5, 0.0625, ((2, 16),)),
        "adapter_down_factors": normal_values(arg_keys[3], (ADAPTER_COUNT, MODEL_WIDTH, 2 * MAX_RANK), MODEL_WIDTH ** -0.5, 0.0625, ((1, 16),)),
        "adapter_up_factors": normal_values(arg_keys[4], (ADAPTER_COUNT, 2 * MAX_RANK, HIDDEN_UNITS), MAX_RANK ** -0.5, 0.75, ((2, 16),)),
        "segment_adapter_index": touch_ends(jax.random.randint(own_keys[5], (MB, SEGS), 0, ADAPTER_COUNT), jax.random.fold_in(own_keys[5], 1), 0, ADAPTER_COUNT - 1).astype(jnp.int32),
        "segment_row_counts": jax.vmap(lambda own: ragged(own, SEGS, MB_TOK, SEG_MOST, 2))(jax.random.split(own_keys[6], MB)).reshape((MB, SEGS)).astype(jnp.int32),
        "ranks": draw_ranks(jax.random.fold_in(arg_keys[8], 71), part),
    }


def token_onehot(segment_adapter_index, segment_row_counts, adapter_list):
    ends = jnp.cumsum(segment_row_counts, axis=1).astype(jnp.int32)
    segments = segment_row_counts.shape[1]
    places = jnp.arange(MB_TOK, dtype=jnp.int32)
    segment_of = jnp.sum((places[None, :, None] >= ends[:, None, :]).astype(jnp.int32), axis=2)
    match = segment_of[:, :, None] == jnp.arange(segments, dtype=jnp.int32)[None, None, :]
    adapter = jnp.sum(jnp.where(match, segment_adapter_index[:, None, :], 0), axis=2).reshape(-1)
    return (adapter[:, None] == jnp.arange(adapter_list, dtype=jnp.int32)[None, :]).astype(jnp.float32)


def adapter_factor(ranks, largest_rank):
    scale = 16.0 / ranks.astype(jnp.float32)
    column = jnp.arange(2 * largest_rank, dtype=jnp.int32) % largest_rank
    live = (column[None, :] < ranks[:, None]).astype(jnp.float32)
    return live * scale[:, None]


def contract_first(left, right):
    return lax.dot_general(left, right, (((0,), (0,)), ((), ())), preferred_element_type=jnp.float32)


def contract_last(left, right):
    return lax.dot_general(left, right, (((1,), (1,)), ((), ())), preferred_element_type=jnp.float32)


def reference(activations, dhidden, frozen, adapter_down_factors, adapter_up_factors, segment_adapter_index, segment_row_counts, ranks):
    adapter_list, feature_width, gate_and_up = adapter_down_factors.shape
    largest_rank = gate_and_up // 2
    tokens = activations.shape[0]
    onehot = token_onehot(segment_adapter_index, segment_row_counts, adapter_list)
    tok_factor = jnp.dot(onehot, adapter_factor(ranks, largest_rank), precision=lax.Precision.HIGHEST)
    down_factors_joined = adapter_down_factors.transpose(1, 0, 2).reshape(feature_width, adapter_list * gate_and_up)
    project = jnp.dot(activations, down_factors_joined, preferred_element_type=jnp.float32).reshape(tokens, adapter_list, gate_and_up)
    low_in = jnp.einsum('ta,tar->tr', onehot, project, precision=lax.Precision.HIGHEST)
    low_in_b = (low_in * tok_factor).astype(jnp.bfloat16)
    spread_in = (onehot[:, :, None] * low_in_b.astype(jnp.float32)[:, None, :]).astype(jnp.bfloat16)
    gate_rows = spread_in[:, :, :largest_rank].reshape(tokens, adapter_list * largest_rank)
    up_rows = spread_in[:, :, largest_rank:].reshape(tokens, adapter_list * largest_rank)
    gate_up_factor = adapter_up_factors[:, :largest_rank, :].reshape(adapter_list * largest_rank, -1)
    up_branch_factor = adapter_up_factors[:, largest_rank:, :].reshape(adapter_list * largest_rank, -1)
    gate = jnp.dot(activations, frozen[0], preferred_element_type=jnp.float32) + jnp.dot(gate_rows, gate_up_factor, preferred_element_type=jnp.float32)
    up = jnp.dot(activations, frozen[1], preferred_element_type=jnp.float32) + jnp.dot(up_rows, up_branch_factor, preferred_element_type=jnp.float32)
    sigma = jax.nn.sigmoid(gate)
    grad_f = dhidden.astype(jnp.float32)
    dgate = (grad_f * up * sigma * (1.0 + gate * (1.0 - sigma))).astype(jnp.bfloat16)
    dup = (grad_f * gate * sigma).astype(jnp.bfloat16)
    back_gate = contract_last(dgate, gate_up_factor).reshape(tokens, adapter_list, largest_rank)
    back_up = contract_last(dup, up_branch_factor).reshape(tokens, adapter_list, largest_rank)
    back = jnp.concatenate([back_gate, back_up], axis=2)
    low_out_f = jnp.einsum('ta,tar->tr', onehot, back, precision=lax.Precision.HIGHEST)
    low_out = (low_out_f * tok_factor).astype(jnp.bfloat16)
    grad_b = jnp.concatenate([contract_first(gate_rows, dgate).reshape(adapter_list, largest_rank, -1), contract_first(up_rows, dup).reshape(adapter_list, largest_rank, -1)], axis=1)
    spread_out = (onehot[:, :, None] * low_out.astype(jnp.float32)[:, None, :]).astype(jnp.bfloat16).reshape(tokens, adapter_list * gate_and_up)
    grad_a = contract_first(activations, spread_out).reshape(feature_width, adapter_list, gate_and_up).transpose(1, 0, 2)
    down_factor_gradient = adapter_down_factors.transpose(0, 2, 1).reshape(adapter_list * gate_and_up, feature_width)
    total = contract_last(dgate, frozen[0]) + contract_last(dup, frozen[1]) + jnp.dot(spread_out, down_factor_gradient, preferred_element_type=jnp.float32)
    return total.astype(jnp.bfloat16), grad_a, grad_b
```

```python
import jax
import jax.numpy as jnp
from jax import lax
from jax.sharding import PartitionSpec as P

CHUNKS = 4


def contract_first(left, right):
    return lax.dot_general(
        left, right, (((0,), (0,)), ((), ())), preferred_element_type=jnp.float32
    )


def contract_last(left, right):
    return lax.dot_general(
        left, right, (((1,), (1,)), ((), ())), preferred_element_type=jnp.float32
    )


class Torus:
    def __init__(self, size):
        core = 2 if size % 2 == 0 else 1
        chips = size // core
        inner = 1
        while inner * 2 * inner * 2 <= chips and chips % (inner * 2) == 0:
            inner *= 2
        self.size = size
        self.dims = (chips // inner, inner, core)
        self.strides = (inner * core, core, 1)

    def place(self, index):
        return [index // s % n for s, n in zip(self.strides, self.dims)]

    def shifted(self, index, dim, by):
        at = index // self.strides[dim] % self.dims[dim]
        return index + ((at + by) % self.dims[dim] - at) * self.strides[dim]

    def move(self, x, dim, by):
        pairs = [(i, self.shifted(i, dim, by)) for i in range(self.size)]
        return lax.ppermute(x, "tensor", pairs)

    def gather(self, x):
        for dim in range(3):
            parts = [x] + [self.move(x, dim, -k) for k in range(1, self.dims[dim])]
            x = jnp.stack(parts)
        return x

    def scatter_sum(self, x, kind):
        for dim in (2, 1, 0):
            total = x[0].astype(jnp.float32)
            for k in range(1, self.dims[dim]):
                total = total + self.move(x[k].astype(kind), dim, k).astype(jnp.float32)
            x = total
        return x

    def slot_devices(self, index):
        outer, inner, core = self.place(index)
        a, b, c = self.dims
        cs = lax.broadcasted_iota(jnp.int32, (c, b, a), 0)
        bs = lax.broadcasted_iota(jnp.int32, (c, b, a), 1)
        zs = lax.broadcasted_iota(jnp.int32, (c, b, a), 2)
        return (((outer + zs) % a * b + (inner + bs) % b) * c + (core + cs) % c).reshape(-1)


def local(
    activations,
    dhidden,
    frozen,
    adapter_down_factors,
    adapter_up_factors,
    segment_adapter_index,
    segment_row_counts,
    ranks,
):
    adapter_list, shard_width, gate_and_up = adapter_down_factors.shape
    rank = gate_and_up // 2
    hidden = frozen.shape[2]
    width = frozen.shape[1]
    rows = activations.shape[0]
    torus = Torus(width // shard_width)
    tokens = rows * torus.size
    index = lax.axis_index("tensor")
    slots = torus.slot_devices(index)
    token = (slots[:, None] * rows + jnp.arange(rows, dtype=jnp.int32)[None, :]).reshape(-1)

    ends = jnp.cumsum(segment_row_counts[0])
    seg_adapter = segment_adapter_index[0]

    def adapter_of(place):
        segment = jnp.sum((place[:, None] >= ends[None, :]).astype(jnp.int32), axis=1)
        match = segment[:, None] == jnp.arange(ends.shape[0], dtype=jnp.int32)[None, :]
        return match, jnp.sum(jnp.where(match, seg_adapter[None, :], 0), axis=1)

    column = jnp.arange(gate_and_up, dtype=jnp.int32) % rank

    def factor_of(adapter):
        hit = adapter[:, None] == jnp.arange(adapter_list, dtype=jnp.int32)[None, :]
        mine = jnp.sum(jnp.where(hit, ranks[None, :], 0), axis=1)
        return jnp.where(column[None, :] < mine[:, None], 16.0 / mine.astype(jnp.float32)[:, None], 0.0)

    seg_hot, adapter = adapter_of(token)
    hot = adapter[:, None] == jnp.arange(adapter_list, dtype=jnp.int32)[None, :]
    mine = index * rows + jnp.arange(rows, dtype=jnp.int32)
    factor = factor_of(adapter_of(mine)[1])

    order = (token[:, None] == jnp.arange(tokens, dtype=jnp.int32)[None, :]).astype(jnp.bfloat16)
    grad_f = jnp.dot(order, dhidden, preferred_element_type=jnp.float32)
    down = jnp.take(adapter_down_factors, seg_adapter, axis=0)
    up_f = jnp.take(adapter_up_factors, seg_adapter, axis=0)
    segments = seg_adapter.shape[0]

    step = width // CHUNKS
    pieces = [
        torus.gather(activations[:, q * step : (q + 1) * step]).reshape(tokens, step)
        for q in range(CHUNKS)
    ]
    gate = up = None
    columns = None
    for q, x in enumerate(pieces):
        g = jnp.dot(x, frozen[0, q * step : (q + 1) * step], preferred_element_type=jnp.float32)
        u = jnp.dot(x, frozen[1, q * step : (q + 1) * step], preferred_element_type=jnp.float32)
        gate = g if gate is None else gate + g
        up = u if up is None else up + u
        first = index * shard_width - q * step
        cut = lax.dynamic_slice_in_dim(x, jnp.clip(first, 0, step - shard_width), shard_width, 1)
        inside = (first >= 0) & (first < step)
        columns = cut if columns is None else jnp.where(inside, cut, columns)

    project = lax.dot_general(
        columns, down, (((1,), (1,)), ((), ())), preferred_element_type=jnp.float32
    )
    partial_in = jnp.sum(jnp.where(seg_hot[:, :, None], project, 0.0), axis=1)
    c, b, a = torus.dims[::-1]
    shape = (c, b, a, rows, gate_and_up)
    low_in = torus.scatter_sum(partial_in.reshape(shape), jnp.float32)
    low_in_b = torus.gather((low_in * factor).astype(jnp.bfloat16)).reshape(tokens, gate_and_up)

    def spread(flags, values):
        return jnp.where(flags[:, :, None], values[:, None, :], jnp.bfloat16(0))

    seg_in = spread(seg_hot, low_in_b)
    gate = gate + lax.dot_general(
        seg_in[:, :, :rank], up_f[:, :rank], (((1, 2), (0, 1)), ((), ())),
        preferred_element_type=jnp.float32,
    )
    up = up + lax.dot_general(
        seg_in[:, :, rank:], up_f[:, rank:], (((1, 2), (0, 1)), ((), ())),
        preferred_element_type=jnp.float32,
    )
    sigma = jax.nn.sigmoid(gate)
    dgate = (grad_f * up * sigma * (1.0 + gate * (1.0 - sigma))).astype(jnp.bfloat16)
    dup = (grad_f * gate * sigma).astype(jnp.bfloat16)

    back = jnp.concatenate(
        [
            lax.dot_general(dgate, up_f[:, :rank], (((1,), (2,)), ((), ())), preferred_element_type=jnp.float32),
            lax.dot_general(dup, up_f[:, rank:], (((1,), (2,)), ((), ())), preferred_element_type=jnp.float32),
        ],
        axis=2,
    )
    partial_out = jnp.sum(jnp.where(seg_hot[:, :, None], back, 0.0), axis=1)
    low_out_f = torus.scatter_sum(partial_out.reshape(shape), jnp.float32)
    low_out = torus.gather((low_out_f * factor).astype(jnp.bfloat16)).reshape(tokens, gate_and_up)

    side = lax.dot_general(
        spread(seg_hot, low_out), down, (((1, 2), (0, 2)), ((), ())),
        preferred_element_type=jnp.float32,
    )
    blocks = []
    for q in range(CHUNKS):
        at = slice(q * step, (q + 1) * step)
        term = contract_last(dgate, frozen[0, at]) + contract_last(dup, frozen[1, at])
        first = index * shard_width - q * step
        where = jnp.clip(first, 0, step - shard_width)
        inside = (first >= 0) & (first < step)
        cut = lax.dynamic_slice_in_dim(term, where, shard_width, 1)
        term = lax.dynamic_update_slice_in_dim(
            term, cut + jnp.where(inside, side, 0.0), where, 1
        )
        term = term.astype(jnp.bfloat16).reshape(c, b, a, rows, step)
        blocks.append(torus.scatter_sum(term, jnp.bfloat16).astype(jnp.bfloat16))
    dinput = jnp.concatenate(blocks, axis=1)

    all_in = spread(hot, low_in_b)
    grad_b = jnp.concatenate(
        [
            contract_first(all_in[:, :, :rank].reshape(tokens, -1), dgate).reshape(adapter_list, rank, hidden),
            contract_first(all_in[:, :, rank:].reshape(tokens, -1), dup).reshape(adapter_list, rank, hidden),
        ],
        axis=1,
    )
    all_out = spread(hot, low_out).reshape(tokens, -1)
    grad_a = (
        contract_first(columns, all_out)
        .reshape(shard_width, adapter_list, gate_and_up)
        .transpose(1, 0, 2)
    )
    return (dinput, grad_a, grad_b)


def solution(mesh):
    placed = (
        P(("groups", "tensor"), None),
        P("groups", "tensor"),
        P(None, None, "tensor"),
        P(None, "tensor", None),
        P(None, None, "tensor"),
        P("groups", None),
        P("groups", None),
        P(),
    )
    return jax.shard_map(
        local,
        mesh=mesh,
        in_specs=placed,
        out_specs=(
            P(("groups", "tensor"), None),
            P("groups", "tensor", None),
            P("groups", None, "tensor"),
        ),
        check_vma=False,
    )
```

```python
import functools

import jax
import jax.numpy as jnp
from jax import lax
from jax.experimental import pallas as pl
from jax.experimental.pallas import tpu as pltpu
from jax.sharding import PartitionSpec as P

CHUNKS = 4
MIB = 1024 * 1024
BF16 = jnp.bfloat16
F32 = jnp.float32


def dot(left, right, dims=((1,), (0,))):
    return lax.dot_general(left, right, (dims, ((), ())), preferred_element_type=F32)


def params(mib):
    return pltpu.CompilerParams(vmem_limit_bytes=mib * MIB)


def cost(flops, moved):
    return pl.CostEstimate(flops=int(flops), bytes_accessed=int(moved), transcendentals=0)


def tile_of(size, most):
    return most if size % most == 0 else size


class Torus:
    def __init__(self, size):
        core = 2 if size % 2 == 0 else 1
        chips = size // core
        inner = 1
        while inner * 2 * inner * 2 <= chips and chips % (inner * 2) == 0:
            inner *= 2
        self.size = size
        self.dims = (chips // inner, inner, core)
        self.strides = (inner * core, core, 1)

    def place(self, index):
        return [index // s % n for s, n in zip(self.strides, self.dims)]

    def shifted(self, index, dim, by):
        at = index // self.strides[dim] % self.dims[dim]
        return index + ((at + by) % self.dims[dim] - at) * self.strides[dim]

    def move(self, x, dim, by):
        pairs = [(i, self.shifted(i, dim, by)) for i in range(self.size)]
        return lax.ppermute(x, "tensor", pairs)

    def gather(self, x, dim):
        return jnp.stack([x] + [self.move(x, dim, -k) for k in range(1, self.dims[dim])])

    def scatter_sum(self, x, dim):
        total = x[0].astype(F32)
        for k in range(1, self.dims[dim]):
            total = total + self.move(x[k], dim, k).astype(F32)
        return total

    def slot_devices(self, index):
        outer, inner, core = self.place(index)
        a, b, c = self.dims
        cs = lax.broadcasted_iota(jnp.int32, (c, b, a), 0)
        bs = lax.broadcasted_iota(jnp.int32, (c, b, a), 1)
        zs = lax.broadcasted_iota(jnp.int32, (c, b, a), 2)
        return (((outer + zs) % a * b + (inner + bs) % b) * c + (core + cs) % c).reshape(-1)

    def slots_of(self, index):
        outer, inner, core = self.place(index)
        a, b, c = self.dims
        zs = lax.broadcasted_iota(jnp.int32, (a, b, c), 0)
        bs = lax.broadcasted_iota(jnp.int32, (a, b, c), 1)
        cs = lax.broadcasted_iota(jnp.int32, (a, b, c), 2)
        return (((cs - core) % c * b + (bs - inner) % b) * a + (zs - outer) % a).reshape(-1)


def forward_kernel(has_start, tile, near, far, w, *rest):
    out = rest[-1]
    x = jnp.concatenate([near[...], far[...]], axis=0)
    first = pl.program_id(0) == 0
    for i in range(2):
        for n in range(0, out.shape[2], tile):
            at = (i, slice(None), slice(n, n + tile))
            part = dot(x, w[i, :, n : n + tile])
            if has_start:
                before = jnp.where(first, rest[0][at], out[at])
            else:
                before = jnp.where(first, 0.0, out[at])
            out[at] = before + part


def forward_chunk(near, far, frozen, start, q):
    half, step = near.shape
    hidden = frozen.shape[2]
    depth = tile_of(step, 512)
    base = q * (step // depth)
    whole = pl.BlockSpec((2, 2 * half, hidden), lambda k: (0, 0, 0))
    operands = [near, far, frozen]
    specs = [
        pl.BlockSpec((half, depth), lambda k: (0, k)),
        pl.BlockSpec((half, depth), lambda k: (0, k)),
        pl.BlockSpec((2, depth, hidden), lambda k: (0, base + k, 0)),
    ]
    if start is not None:
        operands.append(start)
        specs.append(whole)
    return pl.pallas_call(
        functools.partial(forward_kernel, start is not None, tile_of(hidden, 256)),
        grid=(step // depth,),
        in_specs=specs,
        out_specs=whole,
        out_shape=jax.ShapeDtypeStruct((2, 2 * half, hidden), F32),
        compiler_params=params(32),
        cost_estimate=cost(8 * half * step * hidden, 4 * step * hidden),
    )(*operands)


def low_in_kernel(segments, rows, adapters, slots, columns, seg, *rest):
    out = rest[-1]
    total = jnp.zeros((columns.shape[0], out.shape[1]), F32)
    for s in range(segments):
        part = dot(columns[...], rest[s][0])
        total = total + jnp.where(seg[...] == s, part, 0.0)
    put_rows(out, total, slots, rows)


def put_rows(out, total, slots, rows):
    if rows % 8:
        out[...] = total
        return
    for s in range(total.shape[0] // rows):
        out[pl.ds(pl.multiple_of(slots[s] * rows, rows), rows), :] = total[s * rows : (s + 1) * rows]


def of_segment(shape, s):
    return pl.BlockSpec((1,) + shape[1:], lambda *a: (a[-2][s], 0, 0))


def low_in_partial(columns, seg, down, adapters, slots, rows):
    segments = adapters.shape[0]
    tokens = columns.shape[0]
    full = lambda shape: pl.BlockSpec(shape, lambda *a: (0,) * len(shape))
    return pl.pallas_call(
        functools.partial(low_in_kernel, segments, rows),
        grid_spec=pltpu.PrefetchScalarGridSpec(
            num_scalar_prefetch=2,
            grid=(1,),
            in_specs=[full(columns.shape), full(seg.shape)]
            + [of_segment(down.shape, s) for s in range(segments)],
            out_specs=full((tokens, down.shape[2])),
        ),
        out_shape=jax.ShapeDtypeStruct((tokens, down.shape[2]), F32),
        compiler_params=params(16),
        cost_estimate=cost(2 * tokens * down[0].size * segments, 2 * down[0].size * segments),
    )(adapters, slots, columns, seg, *([down] * segments))


def middle_kernel(segments, rows, adapters, slots, base, dhidden, order, low, seg, *rest):
    factors = rest[:segments]
    dgate, dup, out, left, back = rest[segments:]
    rank = low.shape[1] // 2
    tokens = order.shape[0]
    n = pl.program_id(0)
    lane = lax.broadcasted_iota(jnp.int32, (tokens, segments * rank), 1) // rank
    mask = lane == seg[...]

    @pl.when(n == 0)
    def _():
        mine = dot(order[...], low[...])
        for i in range(2):
            wide = jnp.concatenate([mine[:, i * rank : (i + 1) * rank]] * segments, axis=1)
            left[i] = jnp.where(mask, wide, 0.0).astype(BF16)
        back[...] = jnp.zeros_like(back)

    up_g = jnp.concatenate([f[0, :rank] for f in factors], axis=0)
    up_u = jnp.concatenate([f[0, rank:] for f in factors], axis=0)
    gate = base[0] + dot(left[0], up_g)
    up = base[1] + dot(left[1], up_u)
    grad = dot(order[...], dhidden[...])
    sigma = 1.0 / (1.0 + jnp.exp(-gate))
    g = (grad * up * sigma * (1.0 + gate * (1.0 - sigma))).astype(BF16)
    u = (grad * gate * sigma).astype(BF16)
    dgate[...] = g
    dup[...] = u
    back[0] += dot(g, up_g, ((1,), (1,)))
    back[1] += dot(u, up_u, ((1,), (1,)))

    @pl.when(n == pl.num_programs(0) - 1)
    def _():
        parts = []
        for i in range(2):
            kept = jnp.where(mask, back[i], 0.0)
            parts.append(sum(kept[:, s * rank : (s + 1) * rank] for s in range(segments)))
        put_rows(out, jnp.concatenate(parts, axis=1), slots, rows)


def middle(base, dhidden, order, low, seg, up, adapters, slots, rows):
    segments = adapters.shape[0]
    tokens, hidden = dhidden.shape
    wide = up.shape[1]
    tile = tile_of(hidden, 256)
    full = lambda shape: pl.BlockSpec(shape, lambda *a: (0,) * len(shape))
    across = lambda lead: pl.BlockSpec(lead + (tokens, tile), lambda n, *a: (0,) * len(lead) + (0, n))

    def factor(s):
        return pl.BlockSpec((1, wide, tile), lambda n, adapters, slots: (adapters[s], 0, n))

    return pl.pallas_call(
        functools.partial(middle_kernel, segments, rows),
        grid_spec=pltpu.PrefetchScalarGridSpec(
            num_scalar_prefetch=2,
            grid=(hidden // tile,),
            in_specs=[across((2,)), across(()), full(order.shape), full(low.shape), full(seg.shape)]
            + [factor(s) for s in range(segments)],
            out_specs=[across(()), across(()), full((tokens, wide))],
            scratch_shapes=[
                pltpu.VMEM((2, tokens, segments * wide // 2), BF16),
                pltpu.VMEM((2, tokens, segments * wide // 2), F32),
            ],
        ),
        out_shape=[
            jax.ShapeDtypeStruct((tokens, hidden), BF16),
            jax.ShapeDtypeStruct((tokens, hidden), BF16),
            jax.ShapeDtypeStruct((tokens, wide), F32),
        ],
        compiler_params=params(32),
        cost_estimate=cost(
            4 * tokens * hidden * segments * wide, hidden * (tokens * 14 + segments * wide * 2)
        ),
    )(adapters, slots, base, dhidden, order, low, seg, *([up] * segments))


def grad_b_kernel(dgate, dup, order, low, adapter, out, left):
    adapters, wide, tile = out.shape
    rank = wide // 2

    @pl.when(pl.program_id(0) == 0)
    def _():
        turned = dot(order[...], low[...]).T
        for a in range(adapters):
            kept = jnp.where(adapter[...] == a, turned, 0.0).astype(BF16)
            left[0, a * rank : (a + 1) * rank] = kept[:rank]
            left[1, a * rank : (a + 1) * rank] = kept[rank:]

    for i, grad in enumerate((dgate, dup)):
        part = dot(left[i], grad[...])
        out[:, i * rank : (i + 1) * rank, :] = part.reshape(adapters, rank, tile)


def grad_b_of(dgate, dup, order, low, adapter_row, adapters):
    tokens, hidden = dgate.shape
    wide = low.shape[1]
    tile = tile_of(hidden, 256)
    full = lambda shape: pl.BlockSpec(shape, lambda n: (0,) * len(shape))
    across = pl.BlockSpec((tokens, tile), lambda n: (0, n))
    return pl.pallas_call(
        grad_b_kernel,
        grid=(hidden // tile,),
        in_specs=[across, across, full(order.shape), full(low.shape), full(adapter_row.shape)],
        out_specs=pl.BlockSpec((adapters, wide, tile), lambda n: (0, 0, n)),
        out_shape=jax.ShapeDtypeStruct((adapters, wide, hidden), F32),
        scratch_shapes=[pltpu.VMEM((2, adapters * wide // 2, tokens), BF16)],
        compiler_params=params(32),
        cost_estimate=cost(2 * tokens * hidden * adapters * wide, 4 * hidden * adapters * wide),
    )(dgate, dup, order, low, adapter_row)


def grad_a_kernel(per, columns, order, low, adapter, out, turned, mine):
    @pl.when(pl.program_id(0) == 0)
    def _():
        turned[...] = columns[...].astype(F32).T.astype(BF16)
        mine[...] = dot(order[...], low[...])

    for j in range(per):
        a = pl.program_id(0) * per + j
        kept = jnp.where(adapter[...] == a, mine[...], 0.0).astype(BF16)
        out[j] = dot(turned[...], kept)


def grad_a_of(columns, order, low, adapter, adapters):
    tokens, shard = columns.shape
    wide = low.shape[1]
    per = 4 if adapters % 4 == 0 else 1
    full = lambda shape: pl.BlockSpec(shape, lambda n: (0,) * len(shape))
    return pl.pallas_call(
        functools.partial(grad_a_kernel, per),
        grid=(adapters // per,),
        in_specs=[full(columns.shape), full(order.shape), full(low.shape), full(adapter.shape)],
        out_specs=pl.BlockSpec((per, shard, wide), lambda n: (n, 0, 0)),
        out_shape=jax.ShapeDtypeStruct((adapters, shard, wide), F32),
        scratch_shapes=[pltpu.VMEM((shard, tokens), BF16), pltpu.VMEM((tokens, wide), F32)],
        compiler_params=params(16),
        cost_estimate=cost(2 * tokens * shard * adapters * wide, 4 * shard * adapters * wide),
    )(columns, order, low, adapter)


def side_kernel(segments, adapters, slots, order, low, seg, *rest):
    out = rest[-1]
    turned = dot(order[...], low[...]).T
    total = jnp.zeros(out.shape, F32)
    for s in range(segments):
        kept = jnp.where(seg[...] == s, turned, 0.0).astype(BF16)
        total = total + dot(rest[s][0], kept)
    out[...] = total


def side_of(order, low, seg_row, down, adapters, slots):
    segments = adapters.shape[0]
    tokens = order.shape[0]
    shard = down.shape[1]
    full = lambda shape: pl.BlockSpec(shape, lambda *a: (0,) * len(shape))
    return pl.pallas_call(
        functools.partial(side_kernel, segments),
        grid_spec=pltpu.PrefetchScalarGridSpec(
            num_scalar_prefetch=2,
            grid=(1,),
            in_specs=[full(order.shape), full(low.shape), full(seg_row.shape)]
            + [of_segment(down.shape, s) for s in range(segments)],
            out_specs=full((shard, tokens)),
        ),
        out_shape=jax.ShapeDtypeStruct((shard, tokens), F32),
        compiler_params=params(16),
        cost_estimate=cost(2 * tokens * down[0].size * segments, 2 * down[0].size * segments),
    )(adapters, slots, order, low, seg_row, *([down] * segments))


def backward_kernel(base, at, w, dgate, dup, side, out, total):
    block, tokens = total.shape
    shard = side.shape[0]
    total[...] = dot(w[0], dgate[...], ((1,), (1,))) + dot(w[1], dup[...], ((1,), (1,)))
    first = at[0] * shard

    @pl.when(first // block == base + pl.program_id(0))
    def _():
        here = pl.ds(pl.multiple_of(first % block, shard), shard)
        total[here, :] += side[...]

    out[...] = total[...].T.astype(BF16)


def backward_chunk(frozen, dgate, dup, side, at, q, step):
    tokens, hidden = dgate.shape
    block = tile_of(step, 512)
    base = q * (step // block)
    full = lambda shape: pl.BlockSpec(shape, lambda *a: (0,) * len(shape))
    return pl.pallas_call(
        functools.partial(backward_kernel, base),
        grid_spec=pltpu.PrefetchScalarGridSpec(
            num_scalar_prefetch=1,
            grid=(step // block,),
            in_specs=[
                pl.BlockSpec((2, block, hidden), lambda k, at: (0, base + k, 0)),
                full(dgate.shape),
                full(dup.shape),
                full(side.shape),
            ],
            out_specs=pl.BlockSpec((tokens, block), lambda k, at: (0, k)),
            scratch_shapes=[pltpu.VMEM((block, tokens), F32)],
        ),
        out_shape=jax.ShapeDtypeStruct((tokens, step), BF16),
        compiler_params=params(32),
        cost_estimate=cost(4 * tokens * step * hidden, 4 * step * hidden),
    )(at, frozen, dgate, dup, side)


def local(
    activations,
    dhidden,
    frozen,
    adapter_down_factors,
    adapter_up_factors,
    segment_adapter_index,
    segment_row_counts,
    ranks,
):
    adapter_list, shard_width, gate_and_up = adapter_down_factors.shape
    rank = gate_and_up // 2
    width = frozen.shape[1]
    rows = activations.shape[0]
    torus = Torus(width // shard_width)
    tokens = rows * torus.size
    a, b, c = torus.dims
    index = lax.axis_index("tensor")
    slots = torus.slot_devices(index)
    token = (slots[:, None] * rows + jnp.arange(rows, dtype=jnp.int32)[None, :]).reshape(-1)

    ends = jnp.cumsum(segment_row_counts[0])
    seg_adapter = segment_adapter_index[0]
    count = ends.shape[0]

    def segment_of(place):
        return jnp.sum((place[:, None] >= ends[None, :]).astype(jnp.int32), axis=1)

    def adapter_of(segment):
        match = segment[:, None] == jnp.arange(count, dtype=jnp.int32)[None, :]
        return jnp.sum(jnp.where(match, seg_adapter[None, :], 0), axis=1)

    column = jnp.arange(gate_and_up, dtype=jnp.int32) % rank
    mine = index * rows + jnp.arange(rows, dtype=jnp.int32)
    my_adapter = adapter_of(segment_of(mine))
    hit = my_adapter[:, None] == jnp.arange(adapter_list, dtype=jnp.int32)[None, :]
    my_rank = jnp.sum(jnp.where(hit, ranks[None, :], 0), axis=1)[:, None]
    factor = jnp.where(column[None, :] < my_rank, 16.0 / my_rank.astype(F32), 0.0)

    segment = segment_of(token)
    adapter = adapter_of(segment)
    order = (token[:, None] == jnp.arange(tokens, dtype=jnp.int32)[None, :]).astype(BF16)

    def whole_sum(partial):
        if rows % 8:
            partial = jnp.take(
                partial.reshape(torus.size, rows, -1), torus.slots_of(index), axis=0
            )
        parts = lax.all_to_all(partial.reshape(torus.size, rows, gate_and_up), "tensor", 0, 0)
        low = (jnp.sum(parts, axis=0) * factor).astype(BF16)
        spread = jnp.broadcast_to(low[None], (torus.size, rows, gate_and_up))
        return lax.all_to_all(spread, "tensor", 0, 0).reshape(tokens, gate_and_up)

    step = width // CHUNKS
    pieces = []
    columns = None
    for q in range(CHUNKS):
        x = torus.gather(activations[:, q * step : (q + 1) * step], 0)
        x = torus.gather(x, 1).reshape(tokens // c, step)
        y = torus.move(x, 2, -1)
        pieces.append((x, y))
        first = index * shard_width - q * step
        at = jnp.clip(first, 0, step - shard_width)
        cut = jnp.concatenate(
            [lax.dynamic_slice_in_dim(v, at, shard_width, 1) for v in (x, y)], axis=0
        )
        inside = (first >= 0) & (first < step)
        columns = cut if columns is None else jnp.where(inside, cut, columns)

    base = None
    for q, (x, y) in enumerate(pieces):
        base = forward_chunk(x, y, frozen, base, q)

    partial_in = low_in_partial(
        columns, segment[:, None], adapter_down_factors, seg_adapter, slots, rows
    )
    low_in = whole_sum(partial_in)
    dgate, dup, partial_out = middle(
        base, dhidden, order, low_in, segment[:, None], adapter_up_factors, seg_adapter, slots, rows
    )
    low_out = whole_sum(partial_out)
    grad_b = grad_b_of(dgate, dup, order, low_in, adapter[None, :], adapter_list)
    side = side_of(order, low_out, segment[None, :], adapter_down_factors, seg_adapter, slots)
    blocks = []
    for q in range(CHUNKS):
        term = backward_chunk(frozen, dgate, dup, side, index[None], q, step)
        term = term.reshape(c, b, a, rows, step)
        term = torus.scatter_sum(term, 2).astype(BF16)
        term = torus.scatter_sum(term, 1).astype(BF16)
        blocks.append(torus.scatter_sum(term, 0).astype(BF16))
    dinput = jnp.concatenate(blocks, axis=1)
    grad_a = grad_a_of(columns, order, low_out, adapter[:, None], adapter_list)
    return (dinput, grad_a, grad_b)


def solution(mesh):
    placed = (
        P(("groups", "tensor"), None),
        P("groups", "tensor"),
        P(None, None, "tensor"),
        P(None, "tensor", None),
        P(None, None, "tensor"),
        P("groups", None),
        P("groups", None),
        P(),
    )
    return jax.shard_map(
        local,
        mesh=mesh,
        in_specs=placed,
        out_specs=(
            P(("groups", "tensor"), None),
            P("groups", "tensor", None),
            P("groups", None, "tensor"),
        ),
        check_vma=False,
    )
```

```python
import functools

import jax
import jax.numpy as jnp
from jax import lax
from jax.experimental import pallas as pl
from jax.experimental.pallas import tpu as pltpu
from jax.sharding import PartitionSpec as P

GATHER_CHUNKS = 2
SUM_SHARES = (3, 3, 2)
MIB = 1024 * 1024
BF16 = jnp.bfloat16
F32 = jnp.float32


def dot(left, right, dims=((1,), (0,))):
    return lax.dot_general(left, right, (dims, ((), ())), preferred_element_type=F32)


def params(mib):
    return pltpu.CompilerParams(vmem_limit_bytes=mib * MIB)


def cost(flops, moved):
    return pl.CostEstimate(flops=int(flops), bytes_accessed=int(moved), transcendentals=0)


def tile_of(size, most):
    return most if size % most == 0 else size


def parts_of(count, parts):
    parts = min(parts, count)
    ends = [count * k // parts for k in range(parts + 1)]
    return list(zip(ends[:-1], ends[1:]))


def after(x, other):
    return lax.optimization_barrier((x, other))[0]


class Torus:
    def __init__(self, size):
        core = 2 if size % 2 == 0 else 1
        chips = size // core
        inner = 1
        while inner * 2 * inner * 2 <= chips and chips % (inner * 2) == 0:
            inner *= 2
        self.size = size
        self.dims = (chips // inner, inner, core)
        self.strides = (inner * core, core, 1)

    def place(self, index):
        return [index // s % n for s, n in zip(self.strides, self.dims)]

    def shifted(self, index, dim, by):
        at = index // self.strides[dim] % self.dims[dim]
        return index + ((at + by) % self.dims[dim] - at) * self.strides[dim]

    def move(self, x, dim, by):
        pairs = [(i, self.shifted(i, dim, by)) for i in range(self.size)]
        return lax.ppermute(x, "tensor", pairs)

    def gather(self, x, dim):
        return jnp.stack([x] + [self.move(x, dim, -k) for k in range(1, self.dims[dim])])

    def scatter_sum(self, x, dim):
        total = x[0].astype(F32)
        for k in range(1, self.dims[dim]):
            total = total + self.move(x[k], dim, k).astype(F32)
        return total

    def slot_devices(self, index):
        outer, inner, core = self.place(index)
        a, b, c = self.dims
        cs = lax.broadcasted_iota(jnp.int32, (c, b, a), 0)
        bs = lax.broadcasted_iota(jnp.int32, (c, b, a), 1)
        zs = lax.broadcasted_iota(jnp.int32, (c, b, a), 2)
        return (((outer + zs) % a * b + (inner + bs) % b) * c + (core + cs) % c).reshape(-1)

    def exchange_sum(self, x, dim):
        k = 1
        while k < self.dims[dim]:
            pairs = [
                (i, i + ((i // self.strides[dim] ^ k) - i // self.strides[dim]) * self.strides[dim])
                for i in range(self.size)
            ]
            x = x + lax.ppermute(x, "tensor", pairs)
            k *= 2
        return x

    def slots_of(self, index):
        outer, inner, core = self.place(index)
        a, b, c = self.dims
        zs = lax.broadcasted_iota(jnp.int32, (a, b, c), 0)
        bs = lax.broadcasted_iota(jnp.int32, (a, b, c), 1)
        cs = lax.broadcasted_iota(jnp.int32, (a, b, c), 2)
        return (((cs - core) % c * b + (bs - inner) % b) * a + (zs - outer) % a).reshape(-1)


def forward_kernel(near, far, w, *rest):
    out = rest[-1]
    x = jnp.concatenate([near[...], far[...]], axis=0)
    for i in range(2):
        part = dot(x, w[i])
        out[i] = part if len(rest) == 1 else rest[0][i] + part


def forward_chunk(near, far, frozen, start, first, tiles):
    half, step = near.shape
    hidden = frozen.shape[2]
    tile = tile_of(hidden, 256)
    low, high = tiles
    across = pl.BlockSpec((2, 2 * half, tile), lambda n: (0, 0, low + n))
    operands = [near, far, frozen]
    specs = [
        pl.BlockSpec((half, step), lambda n: (0, 0)),
        pl.BlockSpec((half, step), lambda n: (0, 0)),
        pl.BlockSpec((2, step, tile), lambda n: (0, first // step, low + n)),
    ]
    if start is not None:
        operands.append(start)
        specs.append(across)
    count = high - low
    return pl.pallas_call(
        forward_kernel,
        grid=(count,),
        in_specs=specs,
        out_specs=across,
        out_shape=jax.ShapeDtypeStruct((2, 2 * half, hidden), F32),
        input_output_aliases={} if start is None else {3: 0},
        compiler_params=params(32),
        cost_estimate=cost(8 * half * step * tile * count, 4 * step * tile * count),
    )(*operands)


def low_in_kernel(segments, rows, adapters, places, columns, seg, *rest):
    out = rest[-1]
    total = jnp.zeros((columns.shape[0], out.shape[1]), F32)
    for s in range(segments):
        part = dot(columns[...], rest[s][0])
        total = total + jnp.where(seg[...] == s, part, 0.0)
    put_rows(out, total, places, rows)


def put_rows(out, total, places, rows):
    if rows % 8:
        out[...] = total
        return
    for s in range(total.shape[0] // rows):
        out[pl.ds(pl.multiple_of(places[s] * rows, rows), rows), :] = total[s * rows : (s + 1) * rows]


def of_segment(shape, s):
    return pl.BlockSpec((1,) + shape[1:], lambda *a: (a[-2][s], 0, 0))


def low_in_partial(columns, seg, down, adapters, places, rows):
    segments = adapters.shape[0]
    tokens = columns.shape[0]
    full = lambda shape: pl.BlockSpec(shape, lambda *a: (0,) * len(shape))
    return pl.pallas_call(
        functools.partial(low_in_kernel, segments, rows),
        grid_spec=pltpu.PrefetchScalarGridSpec(
            num_scalar_prefetch=2,
            grid=(1,),
            in_specs=[full(columns.shape), full(seg.shape)]
            + [of_segment(down.shape, s) for s in range(segments)],
            out_specs=full((tokens, down.shape[2])),
        ),
        out_shape=jax.ShapeDtypeStruct((tokens, down.shape[2]), F32),
        compiler_params=params(16),
        cost_estimate=cost(2 * tokens * down[0].size * segments, 2 * down[0].size * segments),
    )(adapters, places, columns, seg, *([down] * segments))


def middle_kernel(segments, rows, adapters, places, base, dhidden, token_order, order, low, seg, *rest):
    factors = rest[:segments]
    dgate, dup, out, left, back = rest[segments:]
    rank = low.shape[1] // 2
    tokens = order.shape[0]
    n = pl.program_id(0)
    lane = lax.broadcasted_iota(jnp.int32, (tokens, segments * rank), 1) // rank
    mask = lane == seg[...]

    @pl.when(n == 0)
    def _():
        mine = dot(order[...], low[...])
        for i in range(2):
            wide = jnp.concatenate([mine[:, i * rank : (i + 1) * rank]] * segments, axis=1)
            left[i] = jnp.where(mask, wide, 0.0).astype(BF16)
        back[...] = jnp.zeros_like(back)

    up_g = jnp.concatenate([f[0, :rank] for f in factors], axis=0)
    up_u = jnp.concatenate([f[0, rank:] for f in factors], axis=0)
    gate = base[0] + dot(left[0], up_g)
    up = base[1] + dot(left[1], up_u)
    grad = dot(token_order[...], dhidden[...])
    sigma = 1.0 / (1.0 + jnp.exp(-gate))
    g = (grad * up * sigma * (1.0 + gate * (1.0 - sigma))).astype(BF16)
    u = (grad * gate * sigma).astype(BF16)
    dgate[...] = g
    dup[...] = u
    back[0] += dot(g, up_g, ((1,), (1,)))
    back[1] += dot(u, up_u, ((1,), (1,)))

    @pl.when(n == pl.num_programs(0) - 1)
    def _():
        parts = []
        for i in range(2):
            kept = jnp.where(mask, back[i], 0.0)
            parts.append(sum(kept[:, s * rank : (s + 1) * rank] for s in range(segments)))
        put_rows(out, jnp.concatenate(parts, axis=1), places, rows)


def middle(base, dhidden, token_order, order, low, seg, up, adapters, places, rows):
    segments = adapters.shape[0]
    tokens, hidden = dhidden.shape
    wide = up.shape[1]
    tile = tile_of(hidden, 256)
    full = lambda shape: pl.BlockSpec(shape, lambda *a: (0,) * len(shape))
    across = lambda lead: pl.BlockSpec(lead + (tokens, tile), lambda n, *a: (0,) * len(lead) + (0, n))

    def factor(s):
        return pl.BlockSpec((1, wide, tile), lambda n, adapters, places: (adapters[s], 0, n))

    return pl.pallas_call(
        functools.partial(middle_kernel, segments, rows),
        grid_spec=pltpu.PrefetchScalarGridSpec(
            num_scalar_prefetch=2,
            grid=(hidden // tile,),
            in_specs=[across((2,)), across(())]
            + [full(v.shape) for v in (token_order, order, low, seg)]
            + [factor(s) for s in range(segments)],
            out_specs=[across(()), across(()), full((tokens, wide))],
            scratch_shapes=[
                pltpu.VMEM((2, tokens, segments * wide // 2), BF16),
                pltpu.VMEM((2, tokens, segments * wide // 2), F32),
            ],
        ),
        out_shape=[
            jax.ShapeDtypeStruct((tokens, hidden), BF16),
            jax.ShapeDtypeStruct((tokens, hidden), BF16),
            jax.ShapeDtypeStruct((tokens, wide), F32),
        ],
        compiler_params=params(32),
        cost_estimate=cost(
            4 * tokens * hidden * segments * wide, hidden * (tokens * 14 + segments * wide * 2)
        ),
    )(adapters, places, base, dhidden, token_order, order, low, seg, *([up] * segments))


def grad_b_kernel(dgate, dup, order, low, adapter, *rest):
    out, left = rest[-2:]
    adapters, wide, tile = out.shape
    rank = wide // 2

    @pl.when(pl.program_id(0) == 0)
    def _():
        turned = dot(order[...], low[...]).T
        for a in range(adapters):
            kept = jnp.where(adapter[...] == a, turned, 0.0).astype(BF16)
            left[0, a * rank : (a + 1) * rank] = kept[:rank]
            left[1, a * rank : (a + 1) * rank] = kept[rank:]

    for i, grad in enumerate((dgate, dup)):
        part = dot(left[i], grad[...])
        out[:, i * rank : (i + 1) * rank, :] = part.reshape(adapters, rank, tile)


def grad_b_of(dgate, dup, order, low, adapter_row, adapters, start, tiles):
    tokens, hidden = dgate.shape
    wide = low.shape[1]
    tile = tile_of(hidden, 256)
    first, last = tiles
    full = lambda shape: pl.BlockSpec(shape, lambda n: (0,) * len(shape))
    across = pl.BlockSpec((tokens, tile), lambda n: (0, first + n))
    operands = [dgate, dup, order, low, adapter_row]
    specs = [across, across, full(order.shape), full(low.shape), full(adapter_row.shape)]
    if start is not None:
        operands.append(start)
        specs.append(pl.BlockSpec(memory_space=pl.ANY))
    part = tile * (last - first) * adapters * wide
    return pl.pallas_call(
        grad_b_kernel,
        grid=(last - first,),
        in_specs=specs,
        out_specs=pl.BlockSpec((adapters, wide, tile), lambda n: (0, 0, first + n)),
        out_shape=jax.ShapeDtypeStruct((adapters, wide, hidden), F32),
        scratch_shapes=[pltpu.VMEM((2, adapters * wide // 2, tokens), BF16)],
        input_output_aliases={} if start is None else {5: 0},
        compiler_params=params(32),
        cost_estimate=cost(2 * tokens * part, 4 * part),
    )(*operands)


def grad_a_kernel(per, columns, order, low, adapter, out, turned, mine):
    @pl.when(pl.program_id(0) == 0)
    def _():
        turned[...] = columns[...].astype(F32).T.astype(BF16)
        mine[...] = dot(order[...], low[...])

    for j in range(per):
        a = pl.program_id(0) * per + j
        kept = jnp.where(adapter[...] == a, mine[...], 0.0).astype(BF16)
        out[j] = dot(turned[...], kept)


def grad_a_of(columns, order, low, adapter, adapters):
    tokens, shard = columns.shape
    wide = low.shape[1]
    per = 4 if adapters % 4 == 0 else 1
    full = lambda shape: pl.BlockSpec(shape, lambda n: (0,) * len(shape))
    return pl.pallas_call(
        functools.partial(grad_a_kernel, per),
        grid=(adapters // per,),
        in_specs=[full(columns.shape), full(order.shape), full(low.shape), full(adapter.shape)],
        out_specs=pl.BlockSpec((per, shard, wide), lambda n: (n, 0, 0)),
        out_shape=jax.ShapeDtypeStruct((adapters, shard, wide), F32),
        scratch_shapes=[pltpu.VMEM((shard, tokens), BF16), pltpu.VMEM((tokens, wide), F32)],
        compiler_params=params(16),
        cost_estimate=cost(2 * tokens * shard * adapters * wide, 4 * shard * adapters * wide),
    )(columns, order, low, adapter)


def side_kernel(segments, adapters, places, order, low, seg, *rest):
    out = rest[-1]
    turned = dot(order[...], low[...]).T
    total = jnp.zeros(out.shape, F32)
    for s in range(segments):
        kept = jnp.where(seg[...] == s, turned, 0.0).astype(BF16)
        total = total + dot(rest[s][0], kept)
    out[...] = total


def side_of(order, low, seg_row, down, adapters, places):
    segments = adapters.shape[0]
    tokens = order.shape[0]
    shard = down.shape[1]
    full = lambda shape: pl.BlockSpec(shape, lambda *a: (0,) * len(shape))
    return pl.pallas_call(
        functools.partial(side_kernel, segments),
        grid_spec=pltpu.PrefetchScalarGridSpec(
            num_scalar_prefetch=2,
            grid=(1,),
            in_specs=[full(order.shape), full(low.shape), full(seg_row.shape)]
            + [of_segment(down.shape, s) for s in range(segments)],
            out_specs=full((shard, tokens)),
        ),
        out_shape=jax.ShapeDtypeStruct((shard, tokens), F32),
        compiler_params=params(16),
        cost_estimate=cost(2 * tokens * down[0].size * segments, 2 * down[0].size * segments),
    )(adapters, places, order, low, seg_row, *([down] * segments))


def backward_kernel(base, at, w, dgate, dup, side, out, total):
    block, tokens = total.shape
    shard = side.shape[0]
    part = tile_of(block, 256)
    first = at[0] * shard
    own = first // block == base + pl.program_id(0)

    def product(rows):
        return dot(w[0, rows], dgate[...], ((1,), (1,))) + dot(w[1, rows], dup[...], ((1,), (1,)))

    @pl.when(jnp.logical_not(own))
    def _():
        for n in range(0, block, part):
            rows = slice(n, n + part)
            out[:, rows] = product(rows).T.astype(BF16)

    @pl.when(own)
    def _():
        if shard == block:
            for n in range(0, block, part):
                rows = slice(n, n + part)
                out[:, rows] = (product(rows) + side[rows]).T.astype(BF16)
        else:
            total[...] = product(slice(None))
            here = pl.ds(pl.multiple_of(first % block, shard), shard)
            total[here, :] += side[...]
            out[...] = total[...].T.astype(BF16)


def backward_chunk(frozen, dgate, dup, side, at, first, step):
    tokens, hidden = dgate.shape
    block = tile_of(step, 512)
    base = first // block
    full = lambda shape: pl.BlockSpec(shape, lambda *a: (0,) * len(shape))
    return pl.pallas_call(
        functools.partial(backward_kernel, base),
        grid_spec=pltpu.PrefetchScalarGridSpec(
            num_scalar_prefetch=1,
            grid=(step // block,),
            in_specs=[
                pl.BlockSpec((2, block, hidden), lambda k, at: (0, base + k, 0)),
                full(dgate.shape),
                full(dup.shape),
                full(side.shape),
            ],
            out_specs=pl.BlockSpec((tokens, block), lambda k, at: (0, k)),
            scratch_shapes=[pltpu.VMEM((block, tokens), F32)],
        ),
        out_shape=jax.ShapeDtypeStruct((tokens, step), BF16),
        compiler_params=params(32),
        cost_estimate=cost(4 * tokens * step * hidden, 4 * step * hidden),
    )(at, frozen, dgate, dup, side)


def local(
    activations,
    dhidden,
    frozen,
    adapter_down_factors,
    adapter_up_factors,
    segment_adapter_index,
    segment_row_counts,
    ranks,
):
    adapter_list, shard_width, gate_and_up = adapter_down_factors.shape
    rank = gate_and_up // 2
    width = frozen.shape[1]
    rows = activations.shape[0]
    torus = Torus(width // shard_width)
    tokens = rows * torus.size
    a, b, c = torus.dims
    index = lax.axis_index("tensor")
    slots = torus.slot_devices(index)
    token = (slots[:, None] * rows + jnp.arange(rows, dtype=jnp.int32)[None, :]).reshape(-1)

    ends = jnp.cumsum(segment_row_counts[0])
    seg_adapter = segment_adapter_index[0]
    count = ends.shape[0]

    def segment_of(place):
        return jnp.sum((place[:, None] >= ends[None, :]).astype(jnp.int32), axis=1)

    def adapter_of(segment):
        match = segment[:, None] == jnp.arange(count, dtype=jnp.int32)[None, :]
        return jnp.sum(jnp.where(match, seg_adapter[None, :], 0), axis=1)

    column = jnp.arange(gate_and_up, dtype=jnp.int32) % rank
    chips = a * b
    core = index % c
    mine = (jnp.arange(chips, dtype=jnp.int32)[:, None] * c + core) * rows
    mine = (mine + jnp.arange(rows, dtype=jnp.int32)[None, :]).reshape(-1)
    my_adapter = adapter_of(segment_of(mine))
    hit = my_adapter[:, None] == jnp.arange(adapter_list, dtype=jnp.int32)[None, :]
    my_rank = jnp.sum(jnp.where(hit, ranks[None, :], 0), axis=1)[:, None]
    factor = jnp.where(column[None, :] < my_rank, 16.0 / my_rank.astype(F32), 0.0)

    places = (slots % c - core) % c * chips + slots // c
    spot = (places[:, None] * rows + jnp.arange(rows, dtype=jnp.int32)[None, :]).reshape(-1)
    count_up = jnp.arange(tokens, dtype=jnp.int32)[None, :]
    token_order = (token[:, None] == count_up).astype(BF16)
    order = (spot[:, None] == count_up).astype(BF16)

    segment = segment_of(token)
    adapter = adapter_of(segment)

    def whole_sum(partial):
        if rows % 8:
            at = jnp.arange(torus.size, dtype=jnp.int32)
            device = at % chips * c + (core + at // chips) % c
            partial = jnp.take(
                partial.reshape(torus.size, rows, -1),
                jnp.take(torus.slots_of(index), device),
                axis=0,
            )
        x = torus.scatter_sum(partial.reshape(c, chips * rows, gate_and_up), 2)
        x = torus.exchange_sum(torus.exchange_sum(x, 1), 0)
        return torus.gather((x * factor).astype(BF16), 2).reshape(tokens, gate_and_up)

    hidden = frozen.shape[2]
    tiles = hidden // tile_of(hidden, 256)
    step = width // GATHER_CHUNKS
    columns = None
    behind = None
    base = None
    for q in range(GATHER_CHUNKS):
        x = activations[:, q * step : (q + 1) * step]
        if q:
            x = after(x, behind)
        behind = torus.gather(x, 0)
        x = torus.gather(behind, 1).reshape(tokens // c, step)
        if q:
            x = after(x, base)
        y = torus.move(x, 2, -1)
        first = index * shard_width - q * step
        at = jnp.clip(first, 0, step - shard_width)
        cut = jnp.concatenate(
            [lax.dynamic_slice_in_dim(v, at, shard_width, 1) for v in (x, y)], axis=0
        )
        inside = (first >= 0) & (first < step)
        columns = cut if columns is None else jnp.where(inside, cut, columns)
        for cut in parts_of(tiles, 3) if q == GATHER_CHUNKS - 1 else [(0, tiles)]:
            base = forward_chunk(x, y, frozen, base, q * step, cut)

    partial_in = low_in_partial(
        columns, segment[:, None], adapter_down_factors, seg_adapter, places, rows
    )
    low_in = whole_sum(partial_in)
    dgate, dup, partial_out = middle(
        base, dhidden, token_order, order, low_in, segment[:, None], adapter_up_factors,
        seg_adapter, places, rows,
    )
    low_out = whole_sum(partial_out)
    grad_b = None
    for cut in parts_of(tiles, 2):
        grad_b = grad_b_of(
            dgate, dup, order, low_in, adapter[None, :], adapter_list, grad_b, cut
        )
    side = side_of(order, low_out, segment[None, :], adapter_down_factors, seg_adapter, places)
    blocks = []
    first = 0
    cores, inners = [], []
    for q, share in enumerate(SUM_SHARES):
        step = width * share // sum(SUM_SHARES)
        ready = index[None]
        if q:
            ready = after(ready, cores[q - 1])
        if q > 1:
            ready = after(ready, inners[q - 2])
        term = backward_chunk(frozen, dgate, dup, side, ready, first, step)
        cores.append(torus.scatter_sum(term.reshape(c, b, a, rows, step), 2).astype(BF16))
        inners.append(torus.scatter_sum(cores[q], 1).astype(BF16))
        blocks.append(torus.scatter_sum(inners[q], 0).astype(BF16))
        first += step
    dinput = jnp.concatenate(blocks, axis=1)
    grad_a = grad_a_of(columns, order, low_out, adapter[:, None], adapter_list)
    return (dinput, grad_a, grad_b)


def solution(mesh):
    placed = (
        P(("groups", "tensor"), None),
        P("groups", "tensor"),
        P(None, None, "tensor"),
        P(None, "tensor", None),
        P(None, None, "tensor"),
        P("groups", None),
        P("groups", None),
        P(),
    )
    return jax.shard_map(
        local,
        mesh=mesh,
        in_specs=placed,
        out_specs=(
            P(("groups", "tensor"), None),
            P("groups", "tensor", None),
            P("groups", None, "tensor"),
        ),
        check_vma=False,
    )
```

```python
import functools

import jax
import jax.numpy as jnp
from jax import lax
from jax.experimental import pallas as pl
from jax.experimental.pallas import tpu as pltpu
from jax.sharding import PartitionSpec as P

GATHER_CHUNKS = 2
SUM_SHARES = (3, 3, 2)
MIB = 1024 * 1024
BF16 = jnp.bfloat16
F32 = jnp.float32


def dot(left, right, dims=((1,), (0,))):
    return lax.dot_general(left, right, (dims, ((), ())), preferred_element_type=F32)


def params(mib):
    return pltpu.CompilerParams(vmem_limit_bytes=mib * MIB)


def cost(flops, moved):
    return pl.CostEstimate(flops=int(flops), bytes_accessed=int(moved), transcendentals=0)


def tile_of(size, most):
    return most if size % most == 0 else size


def parts_of(count, parts):
    parts = min(parts, count)
    ends = [count * k // parts for k in range(parts + 1)]
    return list(zip(ends[:-1], ends[1:]))


def after(x, other):
    return lax.optimization_barrier((x, other))[0]


class Torus:
    def __init__(self, size):
        core = 2 if size % 2 == 0 else 1
        chips = size // core
        inner = 1
        while inner * 2 * inner * 2 <= chips and chips % (inner * 2) == 0:
            inner *= 2
        self.size = size
        self.dims = (chips // inner, inner, core)
        self.strides = (inner * core, core, 1)

    def place(self, index):
        return [index // s % n for s, n in zip(self.strides, self.dims)]

    def shifted(self, index, dim, by):
        at = index // self.strides[dim] % self.dims[dim]
        return index + ((at + by) % self.dims[dim] - at) * self.strides[dim]

    def move(self, x, dim, by):
        pairs = [(i, self.shifted(i, dim, by)) for i in range(self.size)]
        return lax.ppermute(x, "tensor", pairs)

    def gather(self, x, dim):
        return jnp.stack([x] + [self.move(x, dim, -k) for k in range(1, self.dims[dim])])

    def scatter_sum(self, x, dim):
        total = x[0].astype(F32)
        for k in range(1, self.dims[dim]):
            total = total + self.move(x[k], dim, k).astype(F32)
        return total

    def slot_devices(self, index):
        outer, inner, core = self.place(index)
        a, b, c = self.dims
        cs = lax.broadcasted_iota(jnp.int32, (c, b, a), 0)
        bs = lax.broadcasted_iota(jnp.int32, (c, b, a), 1)
        zs = lax.broadcasted_iota(jnp.int32, (c, b, a), 2)
        return (((outer + zs) % a * b + (inner + bs) % b) * c + (core + cs) % c).reshape(-1)

    def exchange_sum(self, x, dims, beside):
        beside = list(beside)
        for dim in dims:
            k = 1
            while k < self.dims[dim]:
                stride = self.strides[dim]
                pairs = [(i, i + ((i // stride ^ k) - i // stride) * stride) for i in range(self.size)]
                x = x + lax.ppermute(x, "tensor", pairs)
                if beside:
                    x = after(x, beside.pop(0))
                k *= 2
        return x

    def slots_of(self, index):
        outer, inner, core = self.place(index)
        a, b, c = self.dims
        zs = lax.broadcasted_iota(jnp.int32, (a, b, c), 0)
        bs = lax.broadcasted_iota(jnp.int32, (a, b, c), 1)
        cs = lax.broadcasted_iota(jnp.int32, (a, b, c), 2)
        return (((cs - core) % c * b + (bs - inner) % b) * a + (zs - outer) % a).reshape(-1)


def forward_kernel(near, far, *rest):
    out = rest[-1]
    x = jnp.concatenate([near[...], far[...]], axis=0)
    depth = x.shape[1] // 2
    for i in range(2):
        part = dot(x[:, :depth], rest[2 * i][0]) + dot(x[:, depth:], rest[2 * i + 1][0])
        out[i] = part if len(rest) == 5 else rest[4][i] + part


def forward_chunk(near, far, frozen, start, first, tiles):
    half, step = near.shape
    hidden = frozen.shape[2]
    tile = tile_of(hidden, 256)
    depth = step // 2
    low, high = tiles
    across = pl.BlockSpec((2, 2 * half, tile), lambda n: (0, 0, low + n))

    def weight(i, h):
        return pl.BlockSpec((1, depth, tile), lambda n: (i, first // depth + h, low + n))

    operands = [near, far] + [frozen] * 4
    specs = [pl.BlockSpec((half, step), lambda n: (0, 0))] * 2
    specs += [weight(i, h) for i in range(2) for h in range(2)]
    if start is not None:
        operands.append(start)
        specs.append(across)
    count = high - low
    return pl.pallas_call(
        forward_kernel,
        grid=(count,),
        in_specs=specs,
        out_specs=across,
        out_shape=jax.ShapeDtypeStruct((2, 2 * half, hidden), F32),
        input_output_aliases={} if start is None else {6: 0},
        compiler_params=params(32),
        cost_estimate=cost(8 * half * step * tile * count, 4 * step * tile * count),
    )(*operands)


def low_in_kernel(segments, rows, adapters, places, which, seg, *rest):
    factors, rest = rest[:segments], rest[segments:]
    pairs, (columns, out) = rest[:-2], rest[-2:]
    half = columns.shape[0] // 2
    for q in range(len(pairs) // 2):

        @pl.when(which[0] == q)
        def _():
            columns[:half] = pairs[2 * q][...]
            columns[half:] = pairs[2 * q + 1][...]

    total = jnp.zeros(out.shape, F32)
    for s in range(segments):
        part = dot(columns[...], factors[s][0])
        total = total + jnp.where(seg[...] == s, part, 0.0)
    put_rows(out, total, places, rows)


def put_rows(out, total, places, rows):
    if rows % 8:
        out[...] = total
        return
    for s in range(total.shape[0] // rows):
        out[pl.ds(pl.multiple_of(places[s] * rows, rows), rows), :] = total[s * rows : (s + 1) * rows]


def of_segment(shape, s):
    return pl.BlockSpec((1,) + shape[1:], lambda *a: (a[-2][s], 0, 0))


def low_in_partial(pairs, seg, down, adapters, places, index, rows):
    segments = adapters.shape[0]
    shard, wide = down.shape[1:]
    half, step = pairs[0][0].shape
    per = step // shard
    if shard % 128:
        joined = [jnp.concatenate(side, axis=1) for side in zip(*pairs)]
        pairs = [[lax.dynamic_slice_in_dim(v, index * shard, shard, 1) for v in joined]]
        which = jnp.zeros((1,), jnp.int32)
        cuts = [pl.BlockSpec((half, shard), lambda *a: (0, 0))] * 2
    else:
        which = jnp.stack(
            [index // per] + [jnp.clip(index - q * per, 0, per - 1) for q in range(len(pairs))]
        ).astype(jnp.int32)
        cuts = []
        for q in range(len(pairs)):
            cuts += [pl.BlockSpec((half, shard), lambda i, a, p, w, q=q: (0, w[1 + q]))] * 2
    full = lambda shape: pl.BlockSpec(shape, lambda *a: (0,) * len(shape))
    factor = lambda s: pl.BlockSpec((1, shard, wide), lambda i, a, p, w: (a[s], 0, 0))
    return pl.pallas_call(
        functools.partial(low_in_kernel, segments, rows),
        grid_spec=pltpu.PrefetchScalarGridSpec(
            num_scalar_prefetch=3,
            grid=(1,),
            in_specs=[full(seg.shape)] + [factor(s) for s in range(segments)] + cuts,
            out_specs=[full((2 * half, shard)), full((2 * half, wide))],
        ),
        out_shape=[
            jax.ShapeDtypeStruct((2 * half, shard), BF16),
            jax.ShapeDtypeStruct((2 * half, wide), F32),
        ],
        compiler_params=params(16),
        cost_estimate=cost(4 * half * down[0].size * segments, 2 * down[0].size * segments),
    )(adapters, places, which, seg, *([down] * segments), *[v for pair in pairs for v in pair])


def middle_kernel(segments, rows, adapters, places, base, dhidden, token_order, order, low, seg, *rest):
    factors = rest[:segments]
    dgate, dup, out, left, back = rest[segments:]
    rank = low.shape[1] // 2
    tokens = order.shape[0]
    n = pl.program_id(0)
    lane = lax.broadcasted_iota(jnp.int32, (tokens, segments * rank), 1) // rank
    mask = lane == seg[...]

    @pl.when(n == 0)
    def _():
        mine = dot(order[...], low[...])
        for i in range(2):
            wide = jnp.concatenate([mine[:, i * rank : (i + 1) * rank]] * segments, axis=1)
            left[i] = jnp.where(mask, wide, 0.0).astype(BF16)
        back[...] = jnp.zeros_like(back)

    up_g = jnp.concatenate([f[0, :rank] for f in factors], axis=0)
    up_u = jnp.concatenate([f[0, rank:] for f in factors], axis=0)
    gate = base[0] + dot(left[0], up_g)
    up = base[1] + dot(left[1], up_u)
    grad = dot(token_order[...], dhidden[...])
    sigma = 1.0 / (1.0 + jnp.exp(-gate))
    g = (grad * up * sigma * (1.0 + gate * (1.0 - sigma))).astype(BF16)
    u = (grad * gate * sigma).astype(BF16)
    dgate[...] = g
    dup[...] = u
    back[0] += dot(g, up_g, ((1,), (1,)))
    back[1] += dot(u, up_u, ((1,), (1,)))

    @pl.when(n == pl.num_programs(0) - 1)
    def _():
        parts = []
        for i in range(2):
            kept = jnp.where(mask, back[i], 0.0)
            parts.append(sum(kept[:, s * rank : (s + 1) * rank] for s in range(segments)))
        put_rows(out, jnp.concatenate(parts, axis=1), places, rows)


def middle(base, dhidden, token_order, order, low, seg, up, adapters, places, rows):
    segments = adapters.shape[0]
    tokens, hidden = dhidden.shape
    wide = up.shape[1]
    tile = tile_of(hidden, 256)
    full = lambda shape: pl.BlockSpec(shape, lambda *a: (0,) * len(shape))
    across = lambda lead: pl.BlockSpec(lead + (tokens, tile), lambda n, *a: (0,) * len(lead) + (0, n))

    def factor(s):
        return pl.BlockSpec((1, wide, tile), lambda n, adapters, places: (adapters[s], 0, n))

    return pl.pallas_call(
        functools.partial(middle_kernel, segments, rows),
        grid_spec=pltpu.PrefetchScalarGridSpec(
            num_scalar_prefetch=2,
            grid=(hidden // tile,),
            in_specs=[across((2,)), across(())]
            + [full(v.shape) for v in (token_order, order, low, seg)]
            + [factor(s) for s in range(segments)],
            out_specs=[across(()), across(()), full((tokens, wide))],
            scratch_shapes=[
                pltpu.VMEM((2, tokens, segments * wide // 2), BF16),
                pltpu.VMEM((2, tokens, segments * wide // 2), F32),
            ],
        ),
        out_shape=[
            jax.ShapeDtypeStruct((tokens, hidden), BF16),
            jax.ShapeDtypeStruct((tokens, hidden), BF16),
            jax.ShapeDtypeStruct((tokens, wide), F32),
        ],
        compiler_params=params(32),
        cost_estimate=cost(
            4 * tokens * hidden * segments * wide, hidden * (tokens * 14 + segments * wide * 2)
        ),
    )(adapters, places, base, dhidden, token_order, order, low, seg, *([up] * segments))


def grad_b_kernel(dgate, dup, order, low, adapter, *rest):
    out, left = rest[-2:]
    adapters, wide, tile = out.shape
    rank = wide // 2

    @pl.when(pl.program_id(0) == 0)
    def _():
        turned = dot(order[...], low[...]).T
        for a in range(adapters):
            kept = jnp.where(adapter[...] == a, turned, 0.0).astype(BF16)
            left[0, a * rank : (a + 1) * rank] = kept[:rank]
            left[1, a * rank : (a + 1) * rank] = kept[rank:]

    for i, grad in enumerate((dgate, dup)):
        part = dot(left[i], grad[...])
        out[:, i * rank : (i + 1) * rank, :] = part.reshape(adapters, rank, tile)


def grad_b_of(dgate, dup, order, low, adapter_row, adapters, start, tiles):
    tokens, hidden = dgate.shape
    wide = low.shape[1]
    tile = tile_of(hidden, 256)
    first, last = tiles
    full = lambda shape: pl.BlockSpec(shape, lambda n: (0,) * len(shape))
    across = pl.BlockSpec((tokens, tile), lambda n: (0, first + n))
    operands = [dgate, dup, order, low, adapter_row]
    specs = [across, across, full(order.shape), full(low.shape), full(adapter_row.shape)]
    if start is not None:
        operands.append(start)
        specs.append(pl.BlockSpec(memory_space=pl.ANY))
    part = tile * (last - first) * adapters * wide
    return pl.pallas_call(
        grad_b_kernel,
        grid=(last - first,),
        in_specs=specs,
        out_specs=pl.BlockSpec((adapters, wide, tile), lambda n: (0, 0, first + n)),
        out_shape=jax.ShapeDtypeStruct((adapters, wide, hidden), F32),
        scratch_shapes=[pltpu.VMEM((2, adapters * wide // 2, tokens), BF16)],
        input_output_aliases={} if start is None else {5: 0},
        compiler_params=params(32),
        cost_estimate=cost(2 * tokens * part, 4 * part),
    )(*operands)


def grad_a_kernel(per, columns, order, low, adapter, out, turned, mine):
    @pl.when(pl.program_id(0) == 0)
    def _():
        turned[...] = columns[...].astype(F32).T.astype(BF16)
        mine[...] = dot(order[...], low[...])

    for j in range(per):
        a = pl.program_id(0) * per + j
        kept = jnp.where(adapter[...] == a, mine[...], 0.0).astype(BF16)
        out[j] = dot(turned[...], kept)


def grad_a_of(columns, order, low, adapter, adapters):
    tokens, shard = columns.shape
    wide = low.shape[1]
    per = 4 if adapters % 4 == 0 else 1
    full = lambda shape: pl.BlockSpec(shape, lambda n: (0,) * len(shape))
    return pl.pallas_call(
        functools.partial(grad_a_kernel, per),
        grid=(adapters // per,),
        in_specs=[full(columns.shape), full(order.shape), full(low.shape), full(adapter.shape)],
        out_specs=pl.BlockSpec((per, shard, wide), lambda n: (n, 0, 0)),
        out_shape=jax.ShapeDtypeStruct((adapters, shard, wide), F32),
        scratch_shapes=[pltpu.VMEM((shard, tokens), BF16), pltpu.VMEM((tokens, wide), F32)],
        compiler_params=params(16),
        cost_estimate=cost(2 * tokens * shard * adapters * wide, 4 * shard * adapters * wide),
    )(columns, order, low, adapter)


def side_kernel(segments, adapters, places, order, low, seg, *rest):
    out = rest[-1]
    turned = dot(order[...], low[...]).T
    total = jnp.zeros(out.shape, F32)
    for s in range(segments):
        kept = jnp.where(seg[...] == s, turned, 0.0).astype(BF16)
        total = total + dot(rest[s][0], kept)
    out[...] = total


def side_of(order, low, seg_row, down, adapters, places):
    segments = adapters.shape[0]
    tokens = order.shape[0]
    shard = down.shape[1]
    full = lambda shape: pl.BlockSpec(shape, lambda *a: (0,) * len(shape))
    return pl.pallas_call(
        functools.partial(side_kernel, segments),
        grid_spec=pltpu.PrefetchScalarGridSpec(
            num_scalar_prefetch=2,
            grid=(1,),
            in_specs=[full(order.shape), full(low.shape), full(seg_row.shape)]
            + [of_segment(down.shape, s) for s in range(segments)],
            out_specs=full((shard, tokens)),
        ),
        out_shape=jax.ShapeDtypeStruct((shard, tokens), F32),
        compiler_params=params(16),
        cost_estimate=cost(2 * tokens * down[0].size * segments, 2 * down[0].size * segments),
    )(adapters, places, order, low, seg_row, *([down] * segments))


def backward_kernel(base, at, g0, g1, u0, u1, dgate, dup, side, out, total):
    block, tokens = total.shape
    shard = side.shape[0]
    part = block // 2
    first = at[0] * shard
    own = first // block == base + pl.program_id(0)

    def product(h):
        gate, up = ((g0, u0), (g1, u1))[h]
        return dot(gate[0], dgate[...], ((1,), (1,))) + dot(up[0], dup[...], ((1,), (1,)))

    @pl.when(jnp.logical_not(own))
    def _():
        for h in range(2):
            out[:, h * part : (h + 1) * part] = product(h).T.astype(BF16)

    @pl.when(own)
    def _():
        if shard == block:
            for h in range(2):
                rows = slice(h * part, (h + 1) * part)
                out[:, rows] = (product(h) + side[rows]).T.astype(BF16)
        else:
            for h in range(2):
                total[h * part : (h + 1) * part] = product(h)
            here = pl.ds(pl.multiple_of(first % block, shard), shard)
            total[here, :] += side[...]
            out[...] = total[...].T.astype(BF16)


def backward_chunk(frozen, dgate, dup, side, at, first, step):
    tokens, hidden = dgate.shape
    block = tile_of(step, 512)
    base = first // block
    full = lambda shape: pl.BlockSpec(shape, lambda *a: (0,) * len(shape))

    def weight(i, h):
        return pl.BlockSpec((1, block // 2, hidden), lambda k, at: (i, 2 * (base + k) + h, 0))

    return pl.pallas_call(
        functools.partial(backward_kernel, base),
        grid_spec=pltpu.PrefetchScalarGridSpec(
            num_scalar_prefetch=1,
            grid=(step // block,),
            in_specs=[weight(i, h) for i in range(2) for h in range(2)]
            + [full(dgate.shape), full(dup.shape), full(side.shape)],
            out_specs=pl.BlockSpec((tokens, block), lambda k, at: (0, k)),
            scratch_shapes=[pltpu.VMEM((block, tokens), F32)],
        ),
        out_shape=jax.ShapeDtypeStruct((tokens, step), BF16),
        compiler_params=params(32),
        cost_estimate=cost(4 * tokens * step * hidden, 4 * step * hidden),
    )(at, *([frozen] * 4), dgate, dup, side)


def local(
    activations,
    dhidden,
    frozen,
    adapter_down_factors,
    adapter_up_factors,
    segment_adapter_index,
    segment_row_counts,
    ranks,
):
    adapter_list, shard_width, gate_and_up = adapter_down_factors.shape
    rank = gate_and_up // 2
    width = frozen.shape[1]
    rows = activations.shape[0]
    torus = Torus(width // shard_width)
    tokens = rows * torus.size
    a, b, c = torus.dims
    index = lax.axis_index("tensor")
    slots = torus.slot_devices(index)
    token = (slots[:, None] * rows + jnp.arange(rows, dtype=jnp.int32)[None, :]).reshape(-1)

    ends = jnp.cumsum(segment_row_counts[0])
    seg_adapter = segment_adapter_index[0]
    count = ends.shape[0]

    def segment_of(place):
        return jnp.sum((place[:, None] >= ends[None, :]).astype(jnp.int32), axis=1)

    def adapter_of(segment):
        match = segment[:, None] == jnp.arange(count, dtype=jnp.int32)[None, :]
        return jnp.sum(jnp.where(match, seg_adapter[None, :], 0), axis=1)

    column = jnp.arange(gate_and_up, dtype=jnp.int32) % rank
    chips = a * b
    core = index % c
    mine = (jnp.arange(chips, dtype=jnp.int32)[:, None] * c + core) * rows
    mine = (mine + jnp.arange(rows, dtype=jnp.int32)[None, :]).reshape(-1)
    my_adapter = adapter_of(segment_of(mine))
    hit = my_adapter[:, None] == jnp.arange(adapter_list, dtype=jnp.int32)[None, :]
    my_rank = jnp.sum(jnp.where(hit, ranks[None, :], 0), axis=1)[:, None]
    factor = jnp.where(column[None, :] < my_rank, 16.0 / my_rank.astype(F32), 0.0)

    places = (slots % c - core) % c * chips + slots // c
    spot = (places[:, None] * rows + jnp.arange(rows, dtype=jnp.int32)[None, :]).reshape(-1)
    count_up = jnp.arange(tokens, dtype=jnp.int32)[None, :]
    token_order = (token[:, None] == count_up).astype(BF16)
    order = (spot[:, None] == count_up).astype(BF16)

    segment = segment_of(token)
    adapter = adapter_of(segment)

    def whole_sum(partial, beside=()):
        if rows % 8:
            at = jnp.arange(torus.size, dtype=jnp.int32)
            device = at % chips * c + (core + at // chips) % c
            partial = jnp.take(
                partial.reshape(torus.size, rows, -1),
                jnp.take(torus.slots_of(index), device),
                axis=0,
            )
        x = torus.scatter_sum(partial.reshape(c, chips * rows, gate_and_up), 2)
        x = torus.exchange_sum(x, (1, 0), beside)
        return torus.gather((x * factor).astype(BF16), 2).reshape(tokens, gate_and_up)

    hidden = frozen.shape[2]
    tiles = hidden // tile_of(hidden, 256)
    step = width // GATHER_CHUNKS
    behind = None
    base = None
    pairs = []
    for q in range(GATHER_CHUNKS):
        x = activations[:, q * step : (q + 1) * step]
        if q:
            x = after(x, behind)
        behind = torus.gather(x, 0)
        parts = [behind] + [torus.move(behind, 1, -k) for k in range(1, b)]
        if q:
            parts = list(lax.optimization_barrier((*parts, base))[:-1])
        x = jnp.stack(parts).reshape(tokens // c, step)
        y = torus.move(x, 2, -1)
        pairs.append((x, y))
        for cut in parts_of(tiles, 3) if q == GATHER_CHUNKS - 1 else [(0, tiles)]:
            base = forward_chunk(x, y, frozen, base, q * step, cut)

    columns, partial_in = low_in_partial(
        pairs, segment[:, None], adapter_down_factors, seg_adapter, places, index, rows
    )
    low_in = whole_sum(partial_in)
    dgate, dup, partial_out = middle(
        base, dhidden, token_order, order, low_in, segment[:, None], adapter_up_factors,
        seg_adapter, places, rows,
    )
    grad_b = []
    for cut in parts_of(tiles, 3):
        grad_b.append(
            grad_b_of(
                dgate, dup, order, low_in, adapter[None, :], adapter_list,
                grad_b[-1] if grad_b else None, cut,
            )
        )
    low_out = whole_sum(partial_out, grad_b)
    grad_b = grad_b[-1]
    side = side_of(order, low_out, segment[None, :], adapter_down_factors, seg_adapter, places)
    blocks = []
    first = 0
    cores, inners = [], []
    for q, share in enumerate(SUM_SHARES):
        step = width * share // sum(SUM_SHARES)
        ready = index[None]
        if q:
            ready = after(ready, cores[q - 1])
        if q > 1:
            ready = after(ready, inners[q - 2])
        term = backward_chunk(frozen, dgate, dup, side, ready, first, step)
        cores.append(torus.scatter_sum(term.reshape(c, b, a, rows, step), 2).astype(BF16))
        inners.append(torus.scatter_sum(cores[q], 1).astype(BF16))
        blocks.append(torus.scatter_sum(inners[q], 0).astype(BF16))
        first += step
    dinput = jnp.concatenate(blocks, axis=1)
    grad_a = grad_a_of(columns, order, after(low_out, term), adapter[:, None], adapter_list)
    return (dinput, grad_a, grad_b)


def solution(mesh):
    placed = (
        P(("groups", "tensor"), None),
        P("groups", "tensor"),
        P(None, None, "tensor"),
        P(None, "tensor", None),
        P(None, None, "tensor"),
        P("groups", None),
        P("groups", None),
        P(),
    )
    return jax.shard_map(
        local,
        mesh=mesh,
        in_specs=placed,
        out_specs=(
            P(("groups", "tensor"), None),
            P("groups", "tensor", None),
            P("groups", None, "tensor"),
        ),
        check_vma=False,
    )
```

```python
import functools

import jax
import jax.numpy as jnp
from jax import lax
from jax.experimental import pallas as pl
from jax.experimental.pallas import tpu as pltpu
from jax.sharding import PartitionSpec as P

GATHER_CHUNKS = 2
SUM_SHARES = (4, 2, 2)
MIB = 1024 * 1024
BF16 = jnp.bfloat16
F32 = jnp.float32


def dot(left, right, dims=((1,), (0,))):
    return lax.dot_general(left, right, (dims, ((), ())), preferred_element_type=F32)


def params(mib):
    return pltpu.CompilerParams(vmem_limit_bytes=mib * MIB)


def cost(flops, moved):
    return pl.CostEstimate(flops=int(flops), bytes_accessed=int(moved), transcendentals=0)


def tile_of(size, most):
    return most if size % most == 0 else size


def parts_of(count, parts):
    parts = min(parts, count)
    ends = [count * k // parts for k in range(parts + 1)]
    return list(zip(ends[:-1], ends[1:]))


def after(x, other):
    return lax.optimization_barrier((x, other))[0]


class Torus:
    def __init__(self, size):
        core = 2 if size % 2 == 0 else 1
        chips = size // core
        inner = 1
        while inner * 2 * inner * 2 <= chips and chips % (inner * 2) == 0:
            inner *= 2
        self.size = size
        self.dims = (chips // inner, inner, core)
        self.strides = (inner * core, core, 1)

    def place(self, index):
        return [index // s % n for s, n in zip(self.strides, self.dims)]

    def shifted(self, index, dim, by):
        at = index // self.strides[dim] % self.dims[dim]
        return index + ((at + by) % self.dims[dim] - at) * self.strides[dim]

    def move(self, x, dim, by):
        pairs = [(i, self.shifted(i, dim, by)) for i in range(self.size)]
        return lax.ppermute(x, "tensor", pairs)

    def gather(self, x, dim):
        return jnp.stack([x] + [self.move(x, dim, -k) for k in range(1, self.dims[dim])])

    def scatter_sum(self, x, dim):
        total = x[0].astype(F32)
        for k in range(1, self.dims[dim]):
            total = total + self.move(x[k], dim, k).astype(F32)
        return total

    def slot_devices(self, index):
        outer, inner, core = self.place(index)
        a, b, c = self.dims
        cs = lax.broadcasted_iota(jnp.int32, (c, b, a), 0)
        bs = lax.broadcasted_iota(jnp.int32, (c, b, a), 1)
        zs = lax.broadcasted_iota(jnp.int32, (c, b, a), 2)
        return (((outer + zs) % a * b + (inner + bs) % b) * c + (core + cs) % c).reshape(-1)

    def exchange_sum(self, x, dims, beside):
        beside = list(beside)
        for dim in dims:
            k = 1
            while k < self.dims[dim]:
                stride = self.strides[dim]
                pairs = [(i, i + ((i // stride ^ k) - i // stride) * stride) for i in range(self.size)]
                x = x + lax.ppermute(x, "tensor", pairs)
                if beside:
                    x = after(x, beside.pop(0))
                k *= 2
        return x

    def slots_of(self, index):
        outer, inner, core = self.place(index)
        a, b, c = self.dims
        zs = lax.broadcasted_iota(jnp.int32, (a, b, c), 0)
        bs = lax.broadcasted_iota(jnp.int32, (a, b, c), 1)
        cs = lax.broadcasted_iota(jnp.int32, (a, b, c), 2)
        return (((cs - core) % c * b + (bs - inner) % b) * a + (zs - outer) % a).reshape(-1)


def forward_kernel(near, far, *rest):
    out = rest[-1]
    x = jnp.concatenate([near[...], far[...]], axis=0)
    depth = x.shape[1] // 2
    for i in range(2):
        part = dot(x[:, :depth], rest[2 * i][0]) + dot(x[:, depth:], rest[2 * i + 1][0])
        out[i] = part if len(rest) == 5 else rest[4][i] + part


def forward_chunk(near, far, frozen, start, first, tiles):
    half, step = near.shape
    hidden = frozen.shape[2]
    tile = tile_of(hidden, 256)
    depth = step // 2
    low, high = tiles
    across = pl.BlockSpec((2, 2 * half, tile), lambda n: (0, 0, low + n))

    def weight(i, h):
        return pl.BlockSpec((1, depth, tile), lambda n: (i, first // depth + h, low + n))

    operands = [near, far] + [frozen] * 4
    specs = [pl.BlockSpec((half, step), lambda n: (0, 0))] * 2
    specs += [weight(i, h) for i in range(2) for h in range(2)]
    if start is not None:
        operands.append(start)
        specs.append(across)
    count = high - low
    return pl.pallas_call(
        forward_kernel,
        grid=(count,),
        in_specs=specs,
        out_specs=across,
        out_shape=jax.ShapeDtypeStruct((2, 2 * half, hidden), F32),
        input_output_aliases={} if start is None else {6: 0},
        compiler_params=params(32),
        cost_estimate=cost(8 * half * step * tile * count, 4 * step * tile * count),
    )(*operands)


def low_in_kernel(segments, rows, adapters, places, which, seg, *rest):
    factors, rest = rest[:segments], rest[segments:]
    pairs, (columns, out) = rest[:-2], rest[-2:]
    half = columns.shape[0] // 2
    for q in range(len(pairs) // 2):

        @pl.when(which[0] == q)
        def _():
            columns[:half] = pairs[2 * q][...]
            columns[half:] = pairs[2 * q + 1][...]

    total = jnp.zeros(out.shape, F32)
    for s in range(segments):
        part = dot(columns[...], factors[s][0])
        total = total + jnp.where(seg[...] == s, part, 0.0)
    put_rows(out, total, places, rows)


def put_rows(out, total, places, rows):
    if rows % 8:
        out[...] = total
        return
    for s in range(total.shape[0] // rows):
        out[pl.ds(pl.multiple_of(places[s] * rows, rows), rows), :] = total[s * rows : (s + 1) * rows]


def of_segment(shape, s):
    return pl.BlockSpec((1,) + shape[1:], lambda *a: (a[-2][s], 0, 0))


def low_in_partial(pairs, seg, down, adapters, places, index, rows):
    segments = adapters.shape[0]
    shard, wide = down.shape[1:]
    half, step = pairs[0][0].shape
    per = step // shard
    if shard % 128:
        joined = [jnp.concatenate(side, axis=1) for side in zip(*pairs)]
        pairs = [[lax.dynamic_slice_in_dim(v, index * shard, shard, 1) for v in joined]]
        which = jnp.zeros((1,), jnp.int32)
        cuts = [pl.BlockSpec((half, shard), lambda *a: (0, 0))] * 2
    else:
        which = jnp.stack(
            [index // per] + [jnp.clip(index - q * per, 0, per - 1) for q in range(len(pairs))]
        ).astype(jnp.int32)
        cuts = []
        for q in range(len(pairs)):
            cuts += [pl.BlockSpec((half, shard), lambda i, a, p, w, q=q: (0, w[1 + q]))] * 2
    full = lambda shape: pl.BlockSpec(shape, lambda *a: (0,) * len(shape))
    factor = lambda s: pl.BlockSpec((1, shard, wide), lambda i, a, p, w: (a[s], 0, 0))
    return pl.pallas_call(
        functools.partial(low_in_kernel, segments, rows),
        grid_spec=pltpu.PrefetchScalarGridSpec(
            num_scalar_prefetch=3,
            grid=(1,),
            in_specs=[full(seg.shape)] + [factor(s) for s in range(segments)] + cuts,
            out_specs=[full((2 * half, shard)), full((2 * half, wide))],
        ),
        out_shape=[
            jax.ShapeDtypeStruct((2 * half, shard), BF16),
            jax.ShapeDtypeStruct((2 * half, wide), F32),
        ],
        compiler_params=params(16),
        cost_estimate=cost(4 * half * down[0].size * segments, 2 * down[0].size * segments),
    )(adapters, places, which, seg, *([down] * segments), *[v for pair in pairs for v in pair])


def middle_kernel(segments, rows, adapters, places, base, dhidden, token_order, order, low, seg, *rest):
    factors = rest[:segments]
    dgate, dup, out, left, back = rest[segments:]
    rank = low.shape[1] // 2
    tokens = order.shape[0]
    n = pl.program_id(0)
    lane = lax.broadcasted_iota(jnp.int32, (tokens, segments * rank), 1) // rank
    mask = lane == seg[...]

    @pl.when(n == 0)
    def _():
        mine = dot(order[...], low[...])
        for i in range(2):
            wide = jnp.concatenate([mine[:, i * rank : (i + 1) * rank]] * segments, axis=1)
            left[i] = jnp.where(mask, wide, 0.0).astype(BF16)
        back[...] = jnp.zeros_like(back)

    up_g = jnp.concatenate([f[0, :rank] for f in factors], axis=0)
    up_u = jnp.concatenate([f[0, rank:] for f in factors], axis=0)
    gate = base[0] + dot(left[0], up_g)
    up = base[1] + dot(left[1], up_u)
    grad = dot(token_order[...], dhidden[...])
    sigma = 1.0 / (1.0 + jnp.exp(-gate))
    g = (grad * up * sigma * (1.0 + gate * (1.0 - sigma))).astype(BF16)
    u = (grad * gate * sigma).astype(BF16)
    dgate[...] = g
    dup[...] = u
    back[0] += dot(g, up_g, ((1,), (1,)))
    back[1] += dot(u, up_u, ((1,), (1,)))

    @pl.when(n == pl.num_programs(0) - 1)
    def _():
        parts = []
        for i in range(2):
            kept = jnp.where(mask, back[i], 0.0)
            parts.append(sum(kept[:, s * rank : (s + 1) * rank] for s in range(segments)))
        put_rows(out, jnp.concatenate(parts, axis=1), places, rows)


def middle(base, dhidden, token_order, order, low, seg, up, adapters, places, rows):
    segments = adapters.shape[0]
    tokens, hidden = dhidden.shape
    wide = up.shape[1]
    tile = tile_of(hidden, 256)
    full = lambda shape: pl.BlockSpec(shape, lambda *a: (0,) * len(shape))
    across = lambda lead: pl.BlockSpec(lead + (tokens, tile), lambda n, *a: (0,) * len(lead) + (0, n))

    def factor(s):
        return pl.BlockSpec((1, wide, tile), lambda n, adapters, places: (adapters[s], 0, n))

    return pl.pallas_call(
        functools.partial(middle_kernel, segments, rows),
        grid_spec=pltpu.PrefetchScalarGridSpec(
            num_scalar_prefetch=2,
            grid=(hidden // tile,),
            in_specs=[across((2,)), across(())]
            + [full(v.shape) for v in (token_order, order, low, seg)]
            + [factor(s) for s in range(segments)],
            out_specs=[across(()), across(()), full((tokens, wide))],
            scratch_shapes=[
                pltpu.VMEM((2, tokens, segments * wide // 2), BF16),
                pltpu.VMEM((2, tokens, segments * wide // 2), F32),
            ],
        ),
        out_shape=[
            jax.ShapeDtypeStruct((tokens, hidden), BF16),
            jax.ShapeDtypeStruct((tokens, hidden), BF16),
            jax.ShapeDtypeStruct((tokens, wide), F32),
        ],
        compiler_params=params(32),
        cost_estimate=cost(
            4 * tokens * hidden * segments * wide, hidden * (tokens * 14 + segments * wide * 2)
        ),
    )(adapters, places, base, dhidden, token_order, order, low, seg, *([up] * segments))


def grad_b_kernel(dgate, dup, order, low, adapter, *rest):
    out, left = rest[-2:]
    adapters, wide, tile = out.shape
    rank = wide // 2

    @pl.when(pl.program_id(0) == 0)
    def _():
        turned = dot(order[...], low[...]).T
        for a in range(adapters):
            kept = jnp.where(adapter[...] == a, turned, 0.0).astype(BF16)
            left[0, a * rank : (a + 1) * rank] = kept[:rank]
            left[1, a * rank : (a + 1) * rank] = kept[rank:]

    for i, grad in enumerate((dgate, dup)):
        part = dot(left[i], grad[...])
        out[:, i * rank : (i + 1) * rank, :] = part.reshape(adapters, rank, tile)


def grad_b_of(dgate, dup, order, low, adapter_row, adapters, start, tiles):
    tokens, hidden = dgate.shape
    wide = low.shape[1]
    tile = tile_of(hidden, 256)
    first, last = tiles
    full = lambda shape: pl.BlockSpec(shape, lambda n: (0,) * len(shape))
    across = pl.BlockSpec((tokens, tile), lambda n: (0, first + n))
    operands = [dgate, dup, order, low, adapter_row]
    specs = [across, across, full(order.shape), full(low.shape), full(adapter_row.shape)]
    if start is not None:
        operands.append(start)
        specs.append(pl.BlockSpec(memory_space=pl.ANY))
    part = tile * (last - first) * adapters * wide
    return pl.pallas_call(
        grad_b_kernel,
        grid=(last - first,),
        in_specs=specs,
        out_specs=pl.BlockSpec((adapters, wide, tile), lambda n: (0, 0, first + n)),
        out_shape=jax.ShapeDtypeStruct((adapters, wide, hidden), F32),
        scratch_shapes=[pltpu.VMEM((2, adapters * wide // 2, tokens), BF16)],
        input_output_aliases={} if start is None else {5: 0},
        compiler_params=params(32),
        cost_estimate=cost(2 * tokens * part, 4 * part),
    )(*operands)


def grad_a_kernel(per, columns, order, low, adapter, out, turned, mine):
    @pl.when(pl.program_id(0) == 0)
    def _():
        turned[...] = columns[...].astype(F32).T.astype(BF16)
        mine[...] = dot(order[...], low[...])

    for j in range(per):
        a = pl.program_id(0) * per + j
        kept = jnp.where(adapter[...] == a, mine[...], 0.0).astype(BF16)
        out[j] = dot(turned[...], kept)


def grad_a_of(columns, order, low, adapter, adapters):
    tokens, shard = columns.shape
    wide = low.shape[1]
    per = 4 if adapters % 4 == 0 else 1
    full = lambda shape: pl.BlockSpec(shape, lambda n: (0,) * len(shape))
    return pl.pallas_call(
        functools.partial(grad_a_kernel, per),
        grid=(adapters // per,),
        in_specs=[full(columns.shape), full(order.shape), full(low.shape), full(adapter.shape)],
        out_specs=pl.BlockSpec((per, shard, wide), lambda n: (n, 0, 0)),
        out_shape=jax.ShapeDtypeStruct((adapters, shard, wide), F32),
        scratch_shapes=[pltpu.VMEM((shard, tokens), BF16), pltpu.VMEM((tokens, wide), F32)],
        compiler_params=params(16),
        cost_estimate=cost(2 * tokens * shard * adapters * wide, 4 * shard * adapters * wide),
    )(columns, order, low, adapter)


def side_kernel(segments, adapters, places, order, low, seg, *rest):
    out = rest[-1]
    turned = dot(order[...], low[...]).T
    total = jnp.zeros(out.shape, F32)
    for s in range(segments):
        kept = jnp.where(seg[...] == s, turned, 0.0).astype(BF16)
        total = total + dot(rest[s][0], kept)
    out[...] = total


def side_of(order, low, seg_row, down, adapters, places):
    segments = adapters.shape[0]
    tokens = order.shape[0]
    shard = down.shape[1]
    full = lambda shape: pl.BlockSpec(shape, lambda *a: (0,) * len(shape))
    return pl.pallas_call(
        functools.partial(side_kernel, segments),
        grid_spec=pltpu.PrefetchScalarGridSpec(
            num_scalar_prefetch=2,
            grid=(1,),
            in_specs=[full(order.shape), full(low.shape), full(seg_row.shape)]
            + [of_segment(down.shape, s) for s in range(segments)],
            out_specs=full((shard, tokens)),
        ),
        out_shape=jax.ShapeDtypeStruct((shard, tokens), F32),
        compiler_params=params(16),
        cost_estimate=cost(2 * tokens * down[0].size * segments, 2 * down[0].size * segments),
    )(adapters, places, order, low, seg_row, *([down] * segments))


def backward_kernel(base, at, gate, up, dgate, dup, side, out, total):
    block, tokens = total.shape[1:]
    shard = side.shape[0]
    k = pl.program_id(0)
    first = at[0] * shard
    now, before = k % 2, (k + 1) % 2

    @pl.when(k < pl.num_programs(0) - 1)
    def _():
        out[...] = total[before].T.astype(BF16)
        total[now] = dot(gate[0], dgate[...], ((1,), (1,))) + dot(up[0], dup[...], ((1,), (1,)))

    @pl.when(jnp.logical_and(first // block == base + k, k < pl.num_programs(0) - 1))
    def _():
        here = pl.ds(pl.multiple_of(first % block, shard), shard)
        total[now, here, :] += side[...]

    @pl.when(k == pl.num_programs(0) - 1)
    def _():
        out[...] = total[before].T.astype(BF16)


def backward_chunk(frozen, dgate, dup, side, at, first, step):
    tokens, hidden = dgate.shape
    block = tile_of(step, 512)
    base = first // block
    count = step // block
    full = lambda shape: pl.BlockSpec(shape, lambda *a: (0,) * len(shape))

    def weight(i):
        return pl.BlockSpec(
            (1, block, hidden), lambda k, at: (i, base + jnp.minimum(k, count - 1), 0)
        )

    return pl.pallas_call(
        functools.partial(backward_kernel, base),
        grid_spec=pltpu.PrefetchScalarGridSpec(
            num_scalar_prefetch=1,
            grid=(count + 1,),
            in_specs=[weight(0), weight(1), full(dgate.shape), full(dup.shape), full(side.shape)],
            out_specs=pl.BlockSpec((tokens, block), lambda k, at: (0, jnp.maximum(k - 1, 0))),
            scratch_shapes=[pltpu.VMEM((2, block, tokens), F32)],
        ),
        out_shape=jax.ShapeDtypeStruct((tokens, step), BF16),
        compiler_params=params(32),
        cost_estimate=cost(4 * tokens * step * hidden, 4 * step * hidden),
    )(at, frozen, frozen, dgate, dup, side)


def local(
    activations,
    dhidden,
    frozen,
    adapter_down_factors,
    adapter_up_factors,
    segment_adapter_index,
    segment_row_counts,
    ranks,
):
    adapter_list, shard_width, gate_and_up = adapter_down_factors.shape
    rank = gate_and_up // 2
    width = frozen.shape[1]
    rows = activations.shape[0]
    torus = Torus(width // shard_width)
    tokens = rows * torus.size
    a, b, c = torus.dims
    index = lax.axis_index("tensor")
    slots = torus.slot_devices(index)
    token = (slots[:, None] * rows + jnp.arange(rows, dtype=jnp.int32)[None, :]).reshape(-1)

    ends = jnp.cumsum(segment_row_counts[0])
    seg_adapter = segment_adapter_index[0]
    count = ends.shape[0]

    def segment_of(place):
        return jnp.sum((place[:, None] >= ends[None, :]).astype(jnp.int32), axis=1)

    def adapter_of(segment):
        match = segment[:, None] == jnp.arange(count, dtype=jnp.int32)[None, :]
        return jnp.sum(jnp.where(match, seg_adapter[None, :], 0), axis=1)

    column = jnp.arange(gate_and_up, dtype=jnp.int32) % rank
    chips = a * b
    core = index % c
    mine = (jnp.arange(chips, dtype=jnp.int32)[:, None] * c + core) * rows
    mine = (mine + jnp.arange(rows, dtype=jnp.int32)[None, :]).reshape(-1)
    my_adapter = adapter_of(segment_of(mine))
    hit = my_adapter[:, None] == jnp.arange(adapter_list, dtype=jnp.int32)[None, :]
    my_rank = jnp.sum(jnp.where(hit, ranks[None, :], 0), axis=1)[:, None]
    factor = jnp.where(column[None, :] < my_rank, 16.0 / my_rank.astype(F32), 0.0)

    places = (slots % c - core) % c * chips + slots // c
    spot = (places[:, None] * rows + jnp.arange(rows, dtype=jnp.int32)[None, :]).reshape(-1)
    count_up = jnp.arange(tokens, dtype=jnp.int32)[None, :]
    token_order = (token[:, None] == count_up).astype(BF16)
    order = (spot[:, None] == count_up).astype(BF16)

    segment = segment_of(token)
    adapter = adapter_of(segment)

    def whole_sum(partial, beside=()):
        if rows % 8:
            at = jnp.arange(torus.size, dtype=jnp.int32)
            device = at % chips * c + (core + at // chips) % c
            partial = jnp.take(
                partial.reshape(torus.size, rows, -1),
                jnp.take(torus.slots_of(index), device),
                axis=0,
            )
        x = torus.scatter_sum(partial.reshape(c, chips * rows, gate_and_up), 2)
        x = torus.exchange_sum(x, (1, 0), beside)
        return torus.gather((x * factor).astype(BF16), 2).reshape(tokens, gate_and_up)

    hidden = frozen.shape[2]
    tiles = hidden // tile_of(hidden, 256)
    step = width // GATHER_CHUNKS
    outer = []
    for q in range(GATHER_CHUNKS):
        x = activations[:, q * step : (q + 1) * step]
        outer.append(torus.gather(after(x, outer[-1]) if q else x, 0))
    base = None
    pairs = []
    for q in range(GATHER_CHUNKS):
        parts = [outer[q]] + [torus.move(outer[q], 1, -k) for k in range(1, b)]
        ahead = base if q else outer[-1]
        parts = lax.optimization_barrier((*parts, ahead))[:-1]
        x = jnp.stack(parts).reshape(tokens // c, step)
        y = torus.move(x, 2, -1)
        pairs.append((x, y))
        for cut in parts_of(tiles, 4) if q == GATHER_CHUNKS - 1 else [(0, tiles)]:
            base = forward_chunk(x, y, frozen, base, q * step, cut)

    columns, partial_in = low_in_partial(
        pairs, segment[:, None], adapter_down_factors, seg_adapter, places, index, rows
    )
    low_in = whole_sum(partial_in)
    dgate, dup, partial_out = middle(
        base, dhidden, token_order, order, low_in, segment[:, None], adapter_up_factors,
        seg_adapter, places, rows,
    )
    grad_b = []
    for cut in parts_of(tiles, 3):
        grad_b.append(
            grad_b_of(
                dgate, dup, order, low_in, adapter[None, :], adapter_list,
                grad_b[-1] if grad_b else None, cut,
            )
        )
    low_out = whole_sum(partial_out, grad_b)
    grad_b = grad_b[-1]
    side = side_of(order, low_out, segment[None, :], adapter_down_factors, seg_adapter, places)
    blocks = []
    first = 0
    cores, inners = [], []
    for q, share in enumerate(SUM_SHARES):
        step = width * share // sum(SUM_SHARES)
        ready = index[None]
        if q == 1:
            ready = after(ready, cores[0])
        if q > 1:
            ready = after(ready, inners[q - 2])
        term = backward_chunk(frozen, dgate, dup, side, ready, first, step)
        cores.append(torus.scatter_sum(term.reshape(c, b, a, rows, step), 2).astype(BF16))
        inners.append(torus.scatter_sum(cores[q], 1).astype(BF16))
        blocks.append(torus.scatter_sum(inners[q], 0).astype(BF16))
        first += step
    dinput = jnp.concatenate(blocks, axis=1)
    grad_a = grad_a_of(columns, order, after(low_out, term), adapter[:, None], adapter_list)
    return (dinput, grad_a, grad_b)


def solution(mesh):
    placed = (
        P(("groups", "tensor"), None),
        P("groups", "tensor"),
        P(None, None, "tensor"),
        P(None, "tensor", None),
        P(None, None, "tensor"),
        P("groups", None),
        P("groups", None),
        P(),
    )
    return jax.shard_map(
        local,
        mesh=mesh,
        in_specs=placed,
        out_specs=(
            P(("groups", "tensor"), None),
            P("groups", "tensor", None),
            P("groups", None, "tensor"),
        ),
        check_vma=False,
    )
```

```python
import functools
import math

import jax
import jax.numpy as jnp
from jax import lax
from jax.experimental import pallas as pl
from jax.experimental.pallas import tpu as pltpu
from jax.sharding import PartitionSpec as P

GATHER_SHARES = (3, 5)
SUM_SHARES = (3, 3, 2)
MIB = 1024 * 1024
BF16 = jnp.bfloat16
F32 = jnp.float32


def dot(left, right, dims=((1,), (0,))):
    return lax.dot_general(left, right, (dims, ((), ())), preferred_element_type=F32)


def params(mib):
    return pltpu.CompilerParams(vmem_limit_bytes=mib * MIB)


def cost(flops, moved):
    return pl.CostEstimate(flops=int(flops), bytes_accessed=int(moved), transcendentals=0)


def tile_of(size, most):
    return most if size % most == 0 else size


def parts_of(count, parts):
    parts = min(parts, count)
    ends = [count * k // parts for k in range(parts + 1)]
    return list(zip(ends[:-1], ends[1:]))


def after(x, other):
    return lax.optimization_barrier((x, other))[0]


class Torus:
    def __init__(self, size):
        core = 2 if size % 2 == 0 else 1
        chips = size // core
        inner = 1
        while inner * 2 * inner * 2 <= chips and chips % (inner * 2) == 0:
            inner *= 2
        self.size = size
        self.dims = (chips // inner, inner, core)
        self.strides = (inner * core, core, 1)

    def place(self, index):
        return [index // s % n for s, n in zip(self.strides, self.dims)]

    def shifted(self, index, dim, by):
        at = index // self.strides[dim] % self.dims[dim]
        return index + ((at + by) % self.dims[dim] - at) * self.strides[dim]

    def move(self, x, dim, by):
        pairs = [(i, self.shifted(i, dim, by)) for i in range(self.size)]
        return lax.ppermute(x, "tensor", pairs)

    def gather(self, x, dim):
        return jnp.stack([x] + [self.move(x, dim, -k) for k in range(1, self.dims[dim])])

    def scatter_sum(self, x, dim):
        total = x[0].astype(F32)
        for k in range(1, self.dims[dim]):
            total = total + self.move(x[k], dim, k).astype(F32)
        return total

    def slot_devices(self, index):
        outer, inner, core = self.place(index)
        a, b, c = self.dims
        cs = lax.broadcasted_iota(jnp.int32, (c, b, a), 0)
        bs = lax.broadcasted_iota(jnp.int32, (c, b, a), 1)
        zs = lax.broadcasted_iota(jnp.int32, (c, b, a), 2)
        return (((outer + zs) % a * b + (inner + bs) % b) * c + (core + cs) % c).reshape(-1)

    def exchange_sum(self, x, dims, beside):
        beside = list(beside)
        for dim in dims:
            k = 1
            while k < self.dims[dim]:
                stride = self.strides[dim]
                pairs = [(i, i + ((i // stride ^ k) - i // stride) * stride) for i in range(self.size)]
                x = x + lax.ppermute(x, "tensor", pairs)
                if beside:
                    x = after(x, beside.pop(0))
                k *= 2
        return x

    def slots_of(self, index):
        outer, inner, core = self.place(index)
        a, b, c = self.dims
        zs = lax.broadcasted_iota(jnp.int32, (a, b, c), 0)
        bs = lax.broadcasted_iota(jnp.int32, (a, b, c), 1)
        cs = lax.broadcasted_iota(jnp.int32, (a, b, c), 2)
        return (((cs - core) % c * b + (bs - inner) % b) * a + (zs - outer) % a).reshape(-1)


def forward_kernel(pieces, blocks, *rest):
    x = jnp.concatenate([v[...] for v in rest[:pieces]], axis=0)
    weights = rest[pieces : pieces + 2 * blocks]
    rest = rest[pieces + 2 * blocks :]
    out = rest[-1]
    depth = weights[0].shape[1]
    for i in range(2):
        part = sum(
            dot(x[:, h * depth : (h + 1) * depth], weights[i * blocks + h][0])
            for h in range(blocks)
        )
        out[i] = part if len(rest) == 1 else rest[0][i] + part


def forward_chunk(pieces, frozen, start, first, tiles):
    step = pieces[0].shape[1]
    tokens = sum(v.shape[0] for v in pieces)
    hidden = frozen.shape[2]
    tile = tile_of(hidden, 256)
    depth = math.gcd(first, step)
    blocks = step // depth
    low, high = tiles
    across = pl.BlockSpec((2, tokens, tile), lambda n: (0, 0, low + n))

    def weight(i, h):
        return pl.BlockSpec((1, depth, tile), lambda n: (i, first // depth + h, low + n))

    operands = [*pieces] + [frozen] * (2 * blocks)
    specs = [pl.BlockSpec(v.shape, lambda n: (0, 0)) for v in pieces]
    specs += [weight(i, h) for i in range(2) for h in range(blocks)]
    if start is not None:
        operands.append(start)
        specs.append(across)
    count = high - low
    return pl.pallas_call(
        functools.partial(forward_kernel, len(pieces), blocks),
        grid=(count,),
        in_specs=specs,
        out_specs=across,
        out_shape=jax.ShapeDtypeStruct((2, tokens, hidden), F32),
        input_output_aliases={} if start is None else {len(operands) - 1: 0},
        compiler_params=params(24),
        cost_estimate=cost(4 * tokens * step * tile * count, 4 * step * tile * count),
    )(*operands)


def low_in_kernel(segments, chunks, rows, adapters, places, which, seg, *rest):
    factors, rest = rest[:segments], rest[segments:]
    cuts, (columns, out) = rest[:-2], rest[-2:]
    pieces = len(cuts) // chunks
    for q in range(chunks):

        @pl.when(which[0] == q)
        def _():
            first = 0
            for v in cuts[q * pieces : (q + 1) * pieces]:
                columns[first : first + v.shape[0]] = v[...]
                first += v.shape[0]

    total = jnp.zeros(out.shape, F32)
    for s in range(segments):
        part = dot(columns[...], factors[s][0])
        total = total + jnp.where(seg[...] == s, part, 0.0)
    put_rows(out, total, places, rows)


def put_rows(out, total, places, rows):
    if rows % 8:
        out[...] = total
        return
    for s in range(total.shape[0] // rows):
        out[pl.ds(pl.multiple_of(places[s] * rows, rows), rows), :] = total[s * rows : (s + 1) * rows]


def of_segment(shape, s):
    return pl.BlockSpec((1,) + shape[1:], lambda *a: (a[-2][s], 0, 0))


def low_in_partial(chunks, seg, down, adapters, places, index, rows):
    segments = adapters.shape[0]
    shard, wide = down.shape[1:]
    tokens = seg.shape[0]
    if shard % 128:
        joined = [jnp.concatenate(piece, axis=1) for piece in zip(*chunks)]
        chunks = [[lax.dynamic_slice_in_dim(v, index * shard, shard, 1) for v in joined]]
        which = jnp.zeros((1,), jnp.int32)
        cuts = [pl.BlockSpec(v.shape, lambda *a: (0, 0)) for v in chunks[0]]
    else:
        inside, at, cuts, first = [], [], [], 0
        for q, pieces in enumerate(chunks):
            per = pieces[0].shape[1] // shard
            inside.append(index >= first)
            at.append(jnp.clip(index - first, 0, per - 1))
            cuts += [
                pl.BlockSpec((v.shape[0], shard), lambda i, a, p, w, q=q: (0, w[1 + q])) for v in pieces
            ]
            first += per
        which = jnp.stack([sum(v.astype(jnp.int32) for v in inside) - 1] + at).astype(jnp.int32)
    full = lambda shape: pl.BlockSpec(shape, lambda *a: (0,) * len(shape))
    factor = lambda s: pl.BlockSpec((1, shard, wide), lambda i, a, p, w: (a[s], 0, 0))
    return pl.pallas_call(
        functools.partial(low_in_kernel, segments, len(chunks), rows),
        grid_spec=pltpu.PrefetchScalarGridSpec(
            num_scalar_prefetch=3,
            grid=(1,),
            in_specs=[full(seg.shape)] + [factor(s) for s in range(segments)] + cuts,
            out_specs=[full((tokens, shard)), full((tokens, wide))],
        ),
        out_shape=[
            jax.ShapeDtypeStruct((tokens, shard), BF16),
            jax.ShapeDtypeStruct((tokens, wide), F32),
        ],
        compiler_params=params(16),
        cost_estimate=cost(2 * tokens * down[0].size * segments, 2 * down[0].size * segments),
    )(adapters, places, which, seg, *([down] * segments), *[v for pieces in chunks for v in pieces])


def middle_kernel(segments, rows, adapters, places, base, dhidden, token_order, order, low, seg, *rest):
    factors = rest[:segments]
    dgate, dup, out, left, back = rest[segments:]
    rank = low.shape[1] // 2
    tokens = order.shape[0]
    n = pl.program_id(0)
    lane = lax.broadcasted_iota(jnp.int32, (tokens, segments * rank), 1) // rank
    mask = lane == seg[...]

    @pl.when(n == 0)
    def _():
        mine = dot(order[...], low[...])
        for i in range(2):
            wide = jnp.concatenate([mine[:, i * rank : (i + 1) * rank]] * segments, axis=1)
            left[i] = jnp.where(mask, wide, 0.0).astype(BF16)
        back[...] = jnp.zeros_like(back)

    up_g = jnp.concatenate([f[0, :rank] for f in factors], axis=0)
    up_u = jnp.concatenate([f[0, rank:] for f in factors], axis=0)
    gate = base[0] + dot(left[0], up_g)
    up = base[1] + dot(left[1], up_u)
    grad = dot(token_order[...], dhidden[...])
    sigma = 1.0 / (1.0 + jnp.exp(-gate))
    g = (grad * up * sigma * (1.0 + gate * (1.0 - sigma))).astype(BF16)
    u = (grad * gate * sigma).astype(BF16)
    dgate[...] = g
    dup[...] = u
    back[0] += dot(g, up_g, ((1,), (1,)))
    back[1] += dot(u, up_u, ((1,), (1,)))

    @pl.when(n == pl.num_programs(0) - 1)
    def _():
        parts = []
        for i in range(2):
            kept = jnp.where(mask, back[i], 0.0)
            parts.append(sum(kept[:, s * rank : (s + 1) * rank] for s in range(segments)))
        put_rows(out, jnp.concatenate(parts, axis=1), places, rows)


def middle(base, dhidden, token_order, order, low, seg, up, adapters, places, rows):
    segments = adapters.shape[0]
    tokens, hidden = dhidden.shape
    wide = up.shape[1]
    tile = tile_of(hidden, 256)
    full = lambda shape: pl.BlockSpec(shape, lambda *a: (0,) * len(shape))
    across = lambda lead: pl.BlockSpec(lead + (tokens, tile), lambda n, *a: (0,) * len(lead) + (0, n))

    def factor(s):
        return pl.BlockSpec((1, wide, tile), lambda n, adapters, places: (adapters[s], 0, n))

    return pl.pallas_call(
        functools.partial(middle_kernel, segments, rows),
        grid_spec=pltpu.PrefetchScalarGridSpec(
            num_scalar_prefetch=2,
            grid=(hidden // tile,),
            in_specs=[across((2,)), across(())]
            + [full(v.shape) for v in (token_order, order, low, seg)]
            + [factor(s) for s in range(segments)],
            out_specs=[across(()), across(()), full((tokens, wide))],
            scratch_shapes=[
                pltpu.VMEM((2, tokens, segments * wide // 2), BF16),
                pltpu.VMEM((2, tokens, segments * wide // 2), F32),
            ],
        ),
        out_shape=[
            jax.ShapeDtypeStruct((tokens, hidden), BF16),
            jax.ShapeDtypeStruct((tokens, hidden), BF16),
            jax.ShapeDtypeStruct((tokens, wide), F32),
        ],
        compiler_params=params(20),
        cost_estimate=cost(
            4 * tokens * hidden * segments * wide, hidden * (tokens * 14 + segments * wide * 2)
        ),
    )(adapters, places, base, dhidden, token_order, order, low, seg, *([up] * segments))


def grad_b_kernel(dgate, dup, order, low, adapter, *rest):
    out, left = rest[-2:]
    adapters, wide, tile = out.shape
    rank = wide // 2

    @pl.when(pl.program_id(0) == 0)
    def _():
        turned = dot(order[...], low[...]).T
        for a in range(adapters):
            kept = jnp.where(adapter[...] == a, turned, 0.0).astype(BF16)
            left[0, a * rank : (a + 1) * rank] = kept[:rank]
            left[1, a * rank : (a + 1) * rank] = kept[rank:]

    for i, grad in enumerate((dgate, dup)):
        part = dot(left[i], grad[...])
        out[:, i * rank : (i + 1) * rank, :] = part.reshape(adapters, rank, tile)


def grad_b_of(dgate, dup, order, low, adapter_row, adapters, start, tiles):
    tokens, hidden = dgate.shape
    wide = low.shape[1]
    tile = tile_of(hidden, 256)
    first, last = tiles
    full = lambda shape: pl.BlockSpec(shape, lambda n: (0,) * len(shape))
    across = pl.BlockSpec((tokens, tile), lambda n: (0, first + n))
    operands = [dgate, dup, order, low, adapter_row]
    specs = [across, across, full(order.shape), full(low.shape), full(adapter_row.shape)]
    if start is not None:
        operands.append(start)
        specs.append(pl.BlockSpec(memory_space=pl.ANY))
    part = tile * (last - first) * adapters * wide
    return pl.pallas_call(
        grad_b_kernel,
        grid=(last - first,),
        in_specs=specs,
        out_specs=pl.BlockSpec((adapters, wide, tile), lambda n: (0, 0, first + n)),
        out_shape=jax.ShapeDtypeStruct((adapters, wide, hidden), F32),
        scratch_shapes=[pltpu.VMEM((2, adapters * wide // 2, tokens), BF16)],
        input_output_aliases={} if start is None else {5: 0},
        compiler_params=params(20),
        cost_estimate=cost(2 * tokens * part, 4 * part),
    )(*operands)


def grad_a_kernel(per, columns, order, low, adapter, out, turned, mine):
    @pl.when(pl.program_id(0) == 0)
    def _():
        turned[...] = columns[...].astype(F32).T.astype(BF16)
        mine[...] = dot(order[...], low[...])

    for j in range(per):
        a = pl.program_id(0) * per + j
        kept = jnp.where(adapter[...] == a, mine[...], 0.0).astype(BF16)
        out[j] = dot(turned[...], kept)


def grad_a_of(columns, order, low, adapter, adapters):
    tokens, shard = columns.shape
    wide = low.shape[1]
    per = 4 if adapters % 4 == 0 else 1
    full = lambda shape: pl.BlockSpec(shape, lambda n: (0,) * len(shape))
    return pl.pallas_call(
        functools.partial(grad_a_kernel, per),
        grid=(adapters // per,),
        in_specs=[full(columns.shape), full(order.shape), full(low.shape), full(adapter.shape)],
        out_specs=pl.BlockSpec((per, shard, wide), lambda n: (n, 0, 0)),
        out_shape=jax.ShapeDtypeStruct((adapters, shard, wide), F32),
        scratch_shapes=[pltpu.VMEM((shard, tokens), BF16), pltpu.VMEM((tokens, wide), F32)],
        compiler_params=params(16),
        cost_estimate=cost(2 * tokens * shard * adapters * wide, 4 * shard * adapters * wide),
    )(columns, order, low, adapter)


def side_kernel(segments, adapters, places, order, low, seg, *rest):
    near, far = rest[-2:]
    half = near.shape[0]
    mine = dot(order[...], low[...])
    total = jnp.zeros((2 * half, near.shape[1]), F32)
    for s in range(segments):
        kept = jnp.where(seg[...] == s, mine, 0.0).astype(BF16)
        total = total + dot(kept, rest[s][0], ((1,), (1,)))
    near[...] = total[:half]
    far[...] = total[half:]


def side_of(order, low, seg, down, adapters, places):
    segments = adapters.shape[0]
    tokens = order.shape[0]
    shard = down.shape[1]
    full = lambda shape: pl.BlockSpec(shape, lambda *a: (0,) * len(shape))
    return pl.pallas_call(
        functools.partial(side_kernel, segments),
        grid_spec=pltpu.PrefetchScalarGridSpec(
            num_scalar_prefetch=2,
            grid=(1,),
            in_specs=[full(order.shape), full(low.shape), full(seg.shape)]
            + [of_segment(down.shape, s) for s in range(segments)],
            out_specs=[full((tokens // 2, shard))] * 2,
        ),
        out_shape=[jax.ShapeDtypeStruct((tokens // 2, shard), F32)] * 2,
        compiler_params=params(16),
        cost_estimate=cost(2 * tokens * down[0].size * segments, 2 * down[0].size * segments),
    )(adapters, places, order, low, seg, *([down] * segments))


def backward_kernel(gate, up, dgate, dup, near, far, total):
    k = pl.program_id(0)
    now, before = k % 2, (k + 1) % 2
    half = near.shape[0]

    def store():
        block = total[before].T.astype(BF16)
        near[...] = block[:half]
        far[...] = block[half:]

    @pl.when(k < pl.num_programs(0) - 1)
    def _():
        store()
        total[now] = dot(gate[0], dgate[...], ((1,), (1,))) + dot(up[0], dup[...], ((1,), (1,)))

    @pl.when(k == pl.num_programs(0) - 1)
    def _():
        store()


def backward_chunk(frozen, dgate, dup, first, step):
    tokens, hidden = dgate.shape
    block = tile_of(step, 512)
    base = first // block
    count = step // block
    full = lambda shape: pl.BlockSpec(shape, lambda *a: (0,) * len(shape))
    out = pl.BlockSpec((tokens // 2, block), lambda k: (0, jnp.maximum(k - 1, 0)))

    def weight(i):
        return pl.BlockSpec((1, block, hidden), lambda k: (i, base + jnp.minimum(k, count - 1), 0))

    return pl.pallas_call(
        backward_kernel,
        grid=(count + 1,),
        in_specs=[weight(0), weight(1), full(dgate.shape), full(dup.shape)],
        out_specs=[out, out],
        out_shape=[jax.ShapeDtypeStruct((tokens // 2, step), BF16)] * 2,
        scratch_shapes=[pltpu.VMEM((2, block, tokens), F32)],
        compiler_params=params(20),
        cost_estimate=cost(4 * tokens * step * hidden, 4 * step * hidden),
    )(frozen, frozen, dgate, dup)


def core_sum_kernel(base, at, near, far, side, side_far, *outs):
    total = near[...].astype(F32) + far[...].astype(F32)
    rows = outs[0].shape[0]
    own = at[0] == base + pl.program_id(0)

    def store(total):
        for s, out in enumerate(outs):
            out[...] = total[s * rows : (s + 1) * rows].astype(BF16)

    @pl.when(jnp.logical_not(own))
    def _():
        store(total)

    @pl.when(jnp.logical_and(own, at[1] == 0))
    def _():
        store(total + jnp.concatenate([side[...], side_far[...]], axis=1))

    @pl.when(jnp.logical_and(own, at[1] != 0))
    def _():
        store(total + jnp.concatenate([side_far[...], side[...]], axis=1))


def core_sum(near, far, side, side_far, at, first, slots):
    half, step = near.shape
    block = 2 * side.shape[1]
    full = lambda shape: pl.BlockSpec(shape, lambda *a: (0,) * len(shape))
    across = lambda rows: pl.BlockSpec((rows, block), lambda k, at: (0, k))
    return pl.pallas_call(
        functools.partial(core_sum_kernel, first // block),
        grid_spec=pltpu.PrefetchScalarGridSpec(
            num_scalar_prefetch=1,
            grid=(step // block,),
            in_specs=[across(half), across(half), full(side.shape), full(side_far.shape)],
            out_specs=[across(half // slots)] * slots,
        ),
        out_shape=[jax.ShapeDtypeStruct((half // slots, step), BF16)] * slots,
        compiler_params=params(16),
        cost_estimate=cost(2 * half * step, 6 * half * step),
    )(at, near, far, side, side_far)


def local(
    activations,
    dhidden,
    frozen,
    adapter_down_factors,
    adapter_up_factors,
    segment_adapter_index,
    segment_row_counts,
    ranks,
):
    adapter_list, shard_width, gate_and_up = adapter_down_factors.shape
    rank = gate_and_up // 2
    width = frozen.shape[1]
    rows = activations.shape[0]
    torus = Torus(width // shard_width)
    tokens = rows * torus.size
    a, b, c = torus.dims
    index = lax.axis_index("tensor")
    slots = torus.slot_devices(index)
    token = (slots[:, None] * rows + jnp.arange(rows, dtype=jnp.int32)[None, :]).reshape(-1)

    ends = jnp.cumsum(segment_row_counts[0])
    seg_adapter = segment_adapter_index[0]
    count = ends.shape[0]

    def segment_of(place):
        return jnp.sum((place[:, None] >= ends[None, :]).astype(jnp.int32), axis=1)

    def adapter_of(segment):
        match = segment[:, None] == jnp.arange(count, dtype=jnp.int32)[None, :]
        return jnp.sum(jnp.where(match, seg_adapter[None, :], 0), axis=1)

    column = jnp.arange(gate_and_up, dtype=jnp.int32) % rank
    chips = a * b
    core = index % c
    mine = (jnp.arange(chips, dtype=jnp.int32)[:, None] * c + core) * rows
    mine = (mine + jnp.arange(rows, dtype=jnp.int32)[None, :]).reshape(-1)
    my_adapter = adapter_of(segment_of(mine))
    hit = my_adapter[:, None] == jnp.arange(adapter_list, dtype=jnp.int32)[None, :]
    my_rank = jnp.sum(jnp.where(hit, ranks[None, :], 0), axis=1)[:, None]
    factor = jnp.where(column[None, :] < my_rank, 16.0 / my_rank.astype(F32), 0.0)

    places = (slots % c - core) % c * chips + slots // c
    spot = (places[:, None] * rows + jnp.arange(rows, dtype=jnp.int32)[None, :]).reshape(-1)
    count_up = jnp.arange(tokens, dtype=jnp.int32)[None, :]
    token_order = (token[:, None] == count_up).astype(BF16)
    order = (spot[:, None] == count_up).astype(BF16)

    segment = segment_of(token)
    adapter = adapter_of(segment)

    def whole_sum(partial, beside=()):
        if rows % 8:
            at = jnp.arange(torus.size, dtype=jnp.int32)
            device = at % chips * c + (core + at // chips) % c
            partial = jnp.take(
                partial.reshape(torus.size, rows, -1),
                jnp.take(torus.slots_of(index), device),
                axis=0,
            )
        x = torus.scatter_sum(partial.reshape(c, chips * rows, gate_and_up), 2)
        x = torus.exchange_sum(x, (1, 0), beside)
        return torus.gather((x * factor).astype(BF16), 2).reshape(tokens, gate_and_up)

    hidden = frozen.shape[2]
    tiles = hidden // tile_of(hidden, 256)
    chunks = []
    for share in GATHER_SHARES:
        first = sum(v.shape[1] for v in chunks)
        chunks.append(activations[:, first : first + width * share // sum(GATHER_SHARES)])
    outer = []
    for x in chunks:
        x = torus.gather(after(x, outer[-1]) if outer else x, 0)
        outer.append(x.reshape(a * rows, -1))
    base = None
    gathered = []
    for q, x in enumerate(outer):
        near = [x] + [torus.move(x, 1, -k) for k in range(1, b)]
        near[1:] = lax.optimization_barrier((*near[1:], base if q else outer[-1]))[:-1]
        far = [torus.move(v, 2, -1) for v in near]
        gathered.append([*near, *far])
        first = sum(v.shape[1] for v in chunks[:q])
        for cut in parts_of(tiles, 4 if q else 1):
            base = forward_chunk(gathered[q], frozen, base, first, cut)

    columns, partial_in = low_in_partial(
        gathered, segment[:, None], adapter_down_factors, seg_adapter, places, index, rows
    )
    low_in = whole_sum(partial_in)
    dgate, dup, partial_out = middle(
        base, dhidden, token_order, order, low_in, segment[:, None], adapter_up_factors,
        seg_adapter, places, rows,
    )
    grad_b = []
    thirds = parts_of(tiles, 3)
    for cut in thirds[:-1]:
        grad_b.append(
            grad_b_of(
                dgate, dup, order, low_in, adapter[None, :], adapter_list,
                grad_b[-1] if grad_b else None, cut,
            )
        )
    cuts = []
    for share in SUM_SHARES:
        cuts.append((sum(v[1] for v in cuts), width * share // sum(SUM_SHARES)))
    near, far = backward_chunk(frozen, dgate, dup, *cuts[0])
    low_out = whole_sum(partial_out, [*grad_b, near])
    side, side_far = side_of(
        order, low_out, segment[:, None], adapter_down_factors, seg_adapter, places
    )
    side_far = torus.move(side_far, 2, 1)
    at = jnp.stack([index // c, core]).astype(jnp.int32)
    blocks, sums = [], []
    for q, (first, step) in enumerate(cuts):
        if q:
            ready = after(dgate, sums[0][0] if q > 1 else near)
            near, far = backward_chunk(frozen, ready, dup, first, step)
        sent = core_sum(near, torus.move(far, 2, 1), side, side_far, at, first, b)
        sums.append(sent)
    for q, (first, step) in enumerate(cuts):
        hold = lambda v, wait: after(v, sums[-1][0]) if wait else v
        last = q == len(cuts) - 1
        total = sums[q][0].astype(F32)
        for k in range(1, b):
            total = total + hold(torus.move(sums[q][k], 1, k), q and not last).astype(F32)
        inner = total.astype(BF16).reshape(a, rows, step)
        total = inner[0].astype(F32)
        for k in range(1, a):
            total = total + hold(torus.move(inner[k], 0, k), not last).astype(F32)
        blocks.append(total.astype(BF16))
    dinput = jnp.concatenate(blocks, axis=1)
    grad_b = grad_b_of(
        dgate, dup, order, after(low_in, near), adapter[None, :], adapter_list,
        grad_b[-1] if grad_b else None, thirds[-1],
    )
    grad_a = grad_a_of(
        columns, order, after(low_out, sent[0]), adapter[:, None], adapter_list
    )
    return (dinput, grad_a, grad_b)


def solution(mesh):
    placed = (
        P(("groups", "tensor"), None),
        P("groups", "tensor"),
        P(None, None, "tensor"),
        P(None, "tensor", None),
        P(None, None, "tensor"),
        P("groups", None),
        P("groups", None),
        P(),
    )
    return jax.shard_map(
        local,
        mesh=mesh,
        in_specs=placed,
        out_specs=(
            P(("groups", "tensor"), None),
            P("groups", "tensor", None),
            P("groups", None, "tensor"),
        ),
        check_vma=False,
    )
```

```python
import functools
import math

import jax
import jax.numpy as jnp
from jax import lax
from jax.experimental import pallas as pl
from jax.experimental.pallas import tpu as pltpu
from jax.sharding import PartitionSpec as P

GATHER_SHARES = (2, 3, 3)
SUM_SHARES = (3, 3, 2)
MIB = 1024 * 1024
BF16 = jnp.bfloat16
F32 = jnp.float32


def dot(left, right, dims=((1,), (0,))):
    return lax.dot_general(left, right, (dims, ((), ())), preferred_element_type=F32)


def params(mib):
    return pltpu.CompilerParams(vmem_limit_bytes=mib * MIB)


def cost(flops, moved):
    return pl.CostEstimate(flops=int(flops), bytes_accessed=int(moved), transcendentals=0)


def tile_of(size, most):
    return most if size % most == 0 else size


def parts_of(count, parts):
    parts = min(parts, count)
    ends = [count * k // parts for k in range(parts + 1)]
    return list(zip(ends[:-1], ends[1:]))


def after(x, other):
    return lax.optimization_barrier((x, other))[0]


class Torus:
    def __init__(self, size):
        core = 2 if size % 2 == 0 else 1
        chips = size // core
        inner = 1
        while inner * 2 * inner * 2 <= chips and chips % (inner * 2) == 0:
            inner *= 2
        self.size = size
        self.dims = (chips // inner, inner, core)
        self.strides = (inner * core, core, 1)

    def place(self, index):
        return [index // s % n for s, n in zip(self.strides, self.dims)]

    def shifted(self, index, dim, by):
        at = index // self.strides[dim] % self.dims[dim]
        return index + ((at + by) % self.dims[dim] - at) * self.strides[dim]

    def move(self, x, dim, by):
        pairs = [(i, self.shifted(i, dim, by)) for i in range(self.size)]
        return lax.ppermute(x, "tensor", pairs)

    def gather(self, x, dim):
        return jnp.stack([x] + [self.move(x, dim, -k) for k in range(1, self.dims[dim])])

    def scatter_sum(self, x, dim):
        total = x[0].astype(F32)
        for k in range(1, self.dims[dim]):
            total = total + self.move(x[k], dim, k).astype(F32)
        return total

    def slot_devices(self, index):
        outer, inner, core = self.place(index)
        a, b, c = self.dims
        cs = lax.broadcasted_iota(jnp.int32, (c, b, a), 0)
        bs = lax.broadcasted_iota(jnp.int32, (c, b, a), 1)
        zs = lax.broadcasted_iota(jnp.int32, (c, b, a), 2)
        return (((outer + zs) % a * b + (inner + bs) % b) * c + (core + cs) % c).reshape(-1)

    def exchange_sum(self, x, dims, beside):
        beside = list(beside)
        for dim in dims:
            k = 1
            while k < self.dims[dim]:
                stride = self.strides[dim]
                pairs = [(i, i + ((i // stride ^ k) - i // stride) * stride) for i in range(self.size)]
                x = x + lax.ppermute(x, "tensor", pairs)
                if beside:
                    x = after(x, beside.pop(0))
                k *= 2
        return x

    def slots_of(self, index):
        outer, inner, core = self.place(index)
        a, b, c = self.dims
        zs = lax.broadcasted_iota(jnp.int32, (a, b, c), 0)
        bs = lax.broadcasted_iota(jnp.int32, (a, b, c), 1)
        cs = lax.broadcasted_iota(jnp.int32, (a, b, c), 2)
        return (((cs - core) % c * b + (bs - inner) % b) * a + (zs - outer) % a).reshape(-1)


def forward_kernel(pieces, blocks, *rest):
    x = jnp.concatenate([v[...] for v in rest[:pieces]], axis=0)
    weights = rest[pieces : pieces + 2 * blocks]
    rest = rest[pieces + 2 * blocks :]
    out = rest[-1]
    depth = weights[0].shape[1]
    tile = out.shape[2]
    part = sum(
        dot(
            x[:, h * depth : (h + 1) * depth],
            jnp.concatenate([weights[h][0], weights[blocks + h][0]], axis=1),
        )
        for h in range(blocks)
    )
    for i in range(2):
        now = part[:, i * tile : (i + 1) * tile]
        out[i] = now if len(rest) == 1 else rest[0][i] + now


def forward_chunk(pieces, frozen, start, first, tiles):
    step = pieces[0].shape[1]
    tokens = sum(v.shape[0] for v in pieces)
    hidden = frozen.shape[2]
    tile = tile_of(hidden, 256)
    depth = math.gcd(first, step)
    blocks = step // depth
    low, high = tiles
    across = pl.BlockSpec((2, tokens, tile), lambda n: (0, 0, low + n))

    def weight(i, h):
        return pl.BlockSpec((1, depth, tile), lambda n: (i, first // depth + h, low + n))

    operands = [*pieces] + [frozen] * (2 * blocks)
    specs = [pl.BlockSpec(v.shape, lambda n: (0, 0)) for v in pieces]
    specs += [weight(i, h) for i in range(2) for h in range(blocks)]
    if start is not None:
        operands.append(start)
        specs.append(across)
    count = high - low
    return pl.pallas_call(
        functools.partial(forward_kernel, len(pieces), blocks),
        grid=(count,),
        in_specs=specs,
        out_specs=across,
        out_shape=jax.ShapeDtypeStruct((2, tokens, hidden), F32),
        input_output_aliases={} if start is None else {len(operands) - 1: 0},
        compiler_params=params(24),
        cost_estimate=cost(4 * tokens * step * tile * count, 4 * step * tile * count),
    )(*operands)


def low_in_kernel(segments, chunks, rows, adapters, places, which, seg, *rest):
    factors, rest = rest[:segments], rest[segments:]
    cuts, (columns, out) = rest[:-2], rest[-2:]
    pieces = len(cuts) // chunks
    for q in range(chunks):

        @pl.when(which[0] == q)
        def _():
            first = 0
            for v in cuts[q * pieces : (q + 1) * pieces]:
                columns[first : first + v.shape[0]] = v[...]
                first += v.shape[0]

    total = jnp.zeros(out.shape, F32)
    for s in range(segments):
        part = dot(columns[...], factors[s][0])
        total = total + jnp.where(seg[...] == s, part, 0.0)
    put_rows(out, total, places, rows)


def put_rows(out, total, places, rows):
    if rows % 8:
        out[...] = total
        return
    for s in range(total.shape[0] // rows):
        out[pl.ds(pl.multiple_of(places[s] * rows, rows), rows), :] = total[s * rows : (s + 1) * rows]


def of_segment(shape, s):
    return pl.BlockSpec((1,) + shape[1:], lambda *a: (a[-2][s], 0, 0))


def low_in_partial(chunks, seg, down, adapters, places, index, rows):
    segments = adapters.shape[0]
    shard, wide = down.shape[1:]
    tokens = seg.shape[0]
    if shard % 128:
        joined = [jnp.concatenate(piece, axis=1) for piece in zip(*chunks)]
        chunks = [[lax.dynamic_slice_in_dim(v, index * shard, shard, 1) for v in joined]]
        which = jnp.zeros((1,), jnp.int32)
        cuts = [pl.BlockSpec(v.shape, lambda *a: (0, 0)) for v in chunks[0]]
    else:
        inside, at, cuts, first = [], [], [], 0
        for q, pieces in enumerate(chunks):
            per = pieces[0].shape[1] // shard
            inside.append(index >= first)
            at.append(jnp.clip(index - first, 0, per - 1))
            cuts += [
                pl.BlockSpec((v.shape[0], shard), lambda i, a, p, w, q=q: (0, w[1 + q])) for v in pieces
            ]
            first += per
        which = jnp.stack([sum(v.astype(jnp.int32) for v in inside) - 1] + at).astype(jnp.int32)
    full = lambda shape: pl.BlockSpec(shape, lambda *a: (0,) * len(shape))
    factor = lambda s: pl.BlockSpec((1, shard, wide), lambda i, a, p, w: (a[s], 0, 0))
    return pl.pallas_call(
        functools.partial(low_in_kernel, segments, len(chunks), rows),
        grid_spec=pltpu.PrefetchScalarGridSpec(
            num_scalar_prefetch=3,
            grid=(1,),
            in_specs=[full(seg.shape)] + [factor(s) for s in range(segments)] + cuts,
            out_specs=[full((tokens, shard)), full((tokens, wide))],
        ),
        out_shape=[
            jax.ShapeDtypeStruct((tokens, shard), BF16),
            jax.ShapeDtypeStruct((tokens, wide), F32),
        ],
        compiler_params=params(16),
        cost_estimate=cost(2 * tokens * down[0].size * segments, 2 * down[0].size * segments),
    )(adapters, places, which, seg, *([down] * segments), *[v for pieces in chunks for v in pieces])


def middle_kernel(segments, rows, adapters, places, base, dhidden, token_order, order, low, seg, *rest):
    factors = rest[:segments]
    dgate, dup, out, left, back = rest[segments:]
    rank = low.shape[1] // 2
    tokens = order.shape[0]
    n = pl.program_id(0)
    lane = lax.broadcasted_iota(jnp.int32, (tokens, segments * rank), 1) // rank
    mask = lane == seg[...]

    @pl.when(n == 0)
    def _():
        mine = dot(order[...], low[...])
        for i in range(2):
            wide = jnp.concatenate([mine[:, i * rank : (i + 1) * rank]] * segments, axis=1)
            left[i] = jnp.where(mask, wide, 0.0).astype(BF16)
        back[...] = jnp.zeros_like(back)

    up_g = jnp.concatenate([f[0, :rank] for f in factors], axis=0)
    up_u = jnp.concatenate([f[0, rank:] for f in factors], axis=0)
    gate = base[0] + dot(left[0], up_g)
    up = base[1] + dot(left[1], up_u)
    grad = dot(token_order[...], dhidden[...])
    sigma = 1.0 / (1.0 + jnp.exp(-gate))
    g = (grad * up * sigma * (1.0 + gate * (1.0 - sigma))).astype(BF16)
    u = (grad * gate * sigma).astype(BF16)
    dgate[...] = g
    dup[...] = u
    back[0] += dot(g, up_g, ((1,), (1,)))
    back[1] += dot(u, up_u, ((1,), (1,)))

    @pl.when(n == pl.num_programs(0) - 1)
    def _():
        parts = []
        for i in range(2):
            kept = jnp.where(mask, back[i], 0.0)
            parts.append(sum(kept[:, s * rank : (s + 1) * rank] for s in range(segments)))
        put_rows(out, jnp.concatenate(parts, axis=1), places, rows)


def middle(base, dhidden, token_order, order, low, seg, up, adapters, places, rows):
    segments = adapters.shape[0]
    tokens, hidden = dhidden.shape
    wide = up.shape[1]
    tile = tile_of(hidden, 256)
    full = lambda shape: pl.BlockSpec(shape, lambda *a: (0,) * len(shape))
    across = lambda lead: pl.BlockSpec(lead + (tokens, tile), lambda n, *a: (0,) * len(lead) + (0, n))

    def factor(s):
        return pl.BlockSpec((1, wide, tile), lambda n, adapters, places: (adapters[s], 0, n))

    return pl.pallas_call(
        functools.partial(middle_kernel, segments, rows),
        grid_spec=pltpu.PrefetchScalarGridSpec(
            num_scalar_prefetch=2,
            grid=(hidden // tile,),
            in_specs=[across((2,)), across(())]
            + [full(v.shape) for v in (token_order, order, low, seg)]
            + [factor(s) for s in range(segments)],
            out_specs=[across(()), across(()), full((tokens, wide))],
            scratch_shapes=[
                pltpu.VMEM((2, tokens, segments * wide // 2), BF16),
                pltpu.VMEM((2, tokens, segments * wide // 2), F32),
            ],
        ),
        out_shape=[
            jax.ShapeDtypeStruct((tokens, hidden), BF16),
            jax.ShapeDtypeStruct((tokens, hidden), BF16),
            jax.ShapeDtypeStruct((tokens, wide), F32),
        ],
        compiler_params=params(44),
        cost_estimate=cost(
            4 * tokens * hidden * segments * wide, hidden * (tokens * 14 + segments * wide * 2)
        ),
    )(adapters, places, base, dhidden, token_order, order, low, seg, *([up] * segments))


def grad_b_kernel(dgate, dup, order, low, adapter, *rest):
    out, left = rest[-2:]
    adapters, wide, tile = out.shape
    rank = wide // 2

    @pl.when(pl.program_id(0) == 0)
    def _():
        turned = dot(order[...], low[...]).T
        for a in range(adapters):
            kept = jnp.where(adapter[...] == a, turned, 0.0).astype(BF16)
            left[0, a * rank : (a + 1) * rank] = kept[:rank]
            left[1, a * rank : (a + 1) * rank] = kept[rank:]

    for i, grad in enumerate((dgate, dup)):
        part = dot(left[i], grad[...])
        out[:, i * rank : (i + 1) * rank, :] = part.reshape(adapters, rank, tile)


def grad_b_of(dgate, dup, order, low, adapter_row, adapters, start, tiles):
    tokens, hidden = dgate.shape
    wide = low.shape[1]
    tile = tile_of(hidden, 256)
    first, last = tiles
    full = lambda shape: pl.BlockSpec(shape, lambda n: (0,) * len(shape))
    across = pl.BlockSpec((tokens, tile), lambda n: (0, first + n))
    operands = [dgate, dup, order, low, adapter_row]
    specs = [across, across, full(order.shape), full(low.shape), full(adapter_row.shape)]
    if start is not None:
        operands.append(start)
        specs.append(pl.BlockSpec(memory_space=pl.ANY))
    part = tile * (last - first) * adapters * wide
    return pl.pallas_call(
        grad_b_kernel,
        grid=(last - first,),
        in_specs=specs,
        out_specs=pl.BlockSpec((adapters, wide, tile), lambda n: (0, 0, first + n)),
        out_shape=jax.ShapeDtypeStruct((adapters, wide, hidden), F32),
        scratch_shapes=[pltpu.VMEM((2, adapters * wide // 2, tokens), BF16)],
        input_output_aliases={} if start is None else {5: 0},
        compiler_params=params(20),
        cost_estimate=cost(2 * tokens * part, 4 * part),
    )(*operands)


def grad_a_kernel(per, columns, order, low, adapter, out, turned, mine):
    @pl.when(pl.program_id(0) == 0)
    def _():
        turned[...] = columns[...].astype(F32).T.astype(BF16)
        mine[...] = dot(order[...], low[...])

    for j in range(per):
        a = pl.program_id(0) * per + j
        kept = jnp.where(adapter[...] == a, mine[...], 0.0).astype(BF16)
        out[j] = dot(turned[...], kept)


def grad_a_of(columns, order, low, adapter, adapters):
    tokens, shard = columns.shape
    wide = low.shape[1]
    per = 4 if adapters % 4 == 0 else 1
    full = lambda shape: pl.BlockSpec(shape, lambda n: (0,) * len(shape))
    return pl.pallas_call(
        functools.partial(grad_a_kernel, per),
        grid=(adapters // per,),
        in_specs=[full(columns.shape), full(order.shape), full(low.shape), full(adapter.shape)],
        out_specs=pl.BlockSpec((per, shard, wide), lambda n: (n, 0, 0)),
        out_shape=jax.ShapeDtypeStruct((adapters, shard, wide), F32),
        scratch_shapes=[pltpu.VMEM((shard, tokens), BF16), pltpu.VMEM((tokens, wide), F32)],
        compiler_params=params(16),
        cost_estimate=cost(2 * tokens * shard * adapters * wide, 4 * shard * adapters * wide),
    )(columns, order, low, adapter)


def side_kernel(segments, adapters, places, order, low, seg, *rest):
    near, far = rest[-2:]
    half = near.shape[0]
    mine = dot(order[...], low[...])
    total = jnp.zeros((2 * half, near.shape[1]), F32)
    for s in range(segments):
        kept = jnp.where(seg[...] == s, mine, 0.0).astype(BF16)
        total = total + dot(kept, rest[s][0], ((1,), (1,)))
    near[...] = total[:half]
    far[...] = total[half:]


def side_of(order, low, seg, down, adapters, places):
    segments = adapters.shape[0]
    tokens = order.shape[0]
    shard = down.shape[1]
    full = lambda shape: pl.BlockSpec(shape, lambda *a: (0,) * len(shape))
    return pl.pallas_call(
        functools.partial(side_kernel, segments),
        grid_spec=pltpu.PrefetchScalarGridSpec(
            num_scalar_prefetch=2,
            grid=(1,),
            in_specs=[full(order.shape), full(low.shape), full(seg.shape)]
            + [of_segment(down.shape, s) for s in range(segments)],
            out_specs=[full((tokens // 2, shard))] * 2,
        ),
        out_shape=[jax.ShapeDtypeStruct((tokens // 2, shard), F32)] * 2,
        compiler_params=params(16),
        cost_estimate=cost(2 * tokens * down[0].size * segments, 2 * down[0].size * segments),
    )(adapters, places, order, low, seg, *([down] * segments))


def backward_kernel(gate, up, dgate, dup, near, far):
    half = near.shape[0]
    term = dot(dgate[...], gate[0], ((1,), (1,))) + dot(dup[...], up[0], ((1,), (1,)))
    near[...] = term[:half].astype(BF16)
    far[...] = term[half:].astype(BF16)


def backward_chunk(frozen, dgate, dup, first, step):
    tokens, hidden = dgate.shape
    block = tile_of(step, 512)
    base = first // block
    full = lambda shape: pl.BlockSpec(shape, lambda *a: (0,) * len(shape))
    out = pl.BlockSpec((tokens // 2, block), lambda k: (0, k))

    def weight(i):
        return pl.BlockSpec((1, block, hidden), lambda k: (i, base + k, 0))

    return pl.pallas_call(
        backward_kernel,
        grid=(step // block,),
        in_specs=[weight(0), weight(1), full(dgate.shape), full(dup.shape)],
        out_specs=[out, out],
        out_shape=[jax.ShapeDtypeStruct((tokens // 2, step), BF16)] * 2,
        compiler_params=params(20),
        cost_estimate=cost(4 * tokens * step * hidden, 4 * step * hidden),
    )(frozen, frozen, dgate, dup)


def core_sum_kernel(base, at, near, far, side, side_far, *outs):
    total = near[...].astype(F32) + far[...].astype(F32)
    rows = outs[0].shape[0]
    own = at[0] == base + pl.program_id(0)

    def store(total):
        for s, out in enumerate(outs):
            out[...] = total[s * rows : (s + 1) * rows].astype(BF16)

    @pl.when(jnp.logical_not(own))
    def _():
        store(total)

    @pl.when(jnp.logical_and(own, at[1] == 0))
    def _():
        store(total + jnp.concatenate([side[...], side_far[...]], axis=1))

    @pl.when(jnp.logical_and(own, at[1] != 0))
    def _():
        store(total + jnp.concatenate([side_far[...], side[...]], axis=1))


def core_sum(near, far, side, side_far, at, first, slots):
    half, step = near.shape
    block = 2 * side.shape[1]
    full = lambda shape: pl.BlockSpec(shape, lambda *a: (0,) * len(shape))
    across = lambda rows: pl.BlockSpec((rows, block), lambda k, at: (0, k))
    return pl.pallas_call(
        functools.partial(core_sum_kernel, first // block),
        grid_spec=pltpu.PrefetchScalarGridSpec(
            num_scalar_prefetch=1,
            grid=(step // block,),
            in_specs=[across(half), across(half), full(side.shape), full(side_far.shape)],
            out_specs=[across(half // slots)] * slots,
        ),
        out_shape=[jax.ShapeDtypeStruct((half // slots, step), BF16)] * slots,
        compiler_params=params(16),
        cost_estimate=cost(2 * half * step, 6 * half * step),
    )(at, near, far, side, side_far)


def local(
    activations,
    dhidden,
    frozen,
    adapter_down_factors,
    adapter_up_factors,
    segment_adapter_index,
    segment_row_counts,
    ranks,
):
    adapter_list, shard_width, gate_and_up = adapter_down_factors.shape
    rank = gate_and_up // 2
    width = frozen.shape[1]
    rows = activations.shape[0]
    torus = Torus(width // shard_width)
    tokens = rows * torus.size
    a, b, c = torus.dims
    index = lax.axis_index("tensor")
    slots = torus.slot_devices(index)
    token = (slots[:, None] * rows + jnp.arange(rows, dtype=jnp.int32)[None, :]).reshape(-1)

    ends = jnp.cumsum(segment_row_counts[0])
    seg_adapter = segment_adapter_index[0]
    count = ends.shape[0]

    def segment_of(place):
        return jnp.sum((place[:, None] >= ends[None, :]).astype(jnp.int32), axis=1)

    def adapter_of(segment):
        match = segment[:, None] == jnp.arange(count, dtype=jnp.int32)[None, :]
        return jnp.sum(jnp.where(match, seg_adapter[None, :], 0), axis=1)

    column = jnp.arange(gate_and_up, dtype=jnp.int32) % rank
    chips = a * b
    core = index % c
    mine = (jnp.arange(chips, dtype=jnp.int32)[:, None] * c + core) * rows
    mine = (mine + jnp.arange(rows, dtype=jnp.int32)[None, :]).reshape(-1)
    my_adapter = adapter_of(segment_of(mine))
    hit = my_adapter[:, None] == jnp.arange(adapter_list, dtype=jnp.int32)[None, :]
    my_rank = jnp.sum(jnp.where(hit, ranks[None, :], 0), axis=1)[:, None]
    factor = jnp.where(column[None, :] < my_rank, 16.0 / my_rank.astype(F32), 0.0)

    places = (slots % c - core) % c * chips + slots // c
    spot = (places[:, None] * rows + jnp.arange(rows, dtype=jnp.int32)[None, :]).reshape(-1)
    count_up = jnp.arange(tokens, dtype=jnp.int32)[None, :]
    token_order = (token[:, None] == count_up).astype(BF16)
    order = (spot[:, None] == count_up).astype(BF16)

    segment = segment_of(token)
    adapter = adapter_of(segment)

    def whole_sum(partial, beside=()):
        if rows % 8:
            at = jnp.arange(torus.size, dtype=jnp.int32)
            device = at % chips * c + (core + at // chips) % c
            partial = jnp.take(
                partial.reshape(torus.size, rows, -1),
                jnp.take(torus.slots_of(index), device),
                axis=0,
            )
        x = torus.scatter_sum(partial.reshape(c, chips * rows, gate_and_up), 2)
        x = torus.exchange_sum(x, (1, 0), beside)
        return torus.gather((x * factor).astype(BF16), 2).reshape(tokens, gate_and_up)

    hidden = frozen.shape[2]
    tiles = hidden // tile_of(hidden, 256)
    outer = torus.gather(activations, 0).reshape(a * rows, width)
    base = None
    gathered = []
    first = 0
    for share in GATHER_SHARES:
        step = width * share // sum(GATHER_SHARES)
        x = outer[:, first : first + step]
        if gathered:
            x = after(x, gathered[-1][1])
        inner = [torus.move(x, 1, -k) for k in range(1, b)]
        if gathered:
            inner = list(lax.optimization_barrier((*inner, base))[:-1])
        near = [x, *inner]
        gathered.append([*near, *[torus.move(v, 2, -1) for v in near]])
        last = len(gathered) == len(GATHER_SHARES)
        for cut in parts_of(tiles, 3 if last else 1):
            base = forward_chunk(gathered[-1], frozen, base, first, cut)
        first += step

    columns, partial_in = low_in_partial(
        gathered, segment[:, None], adapter_down_factors, seg_adapter, places, index, rows
    )
    low_in = whole_sum(partial_in)
    dgate, dup, partial_out = middle(
        base, dhidden, token_order, order, low_in, segment[:, None], adapter_up_factors,
        seg_adapter, places, rows,
    )
    grad_b = []
    thirds = parts_of(tiles, 3)
    for cut in thirds[:-1]:
        grad_b.append(
            grad_b_of(
                dgate, dup, order, low_in, adapter[None, :], adapter_list,
                grad_b[-1] if grad_b else None, cut,
            )
        )
    cuts = []
    for share in SUM_SHARES:
        cuts.append((sum(v[1] for v in cuts), width * share // sum(SUM_SHARES)))
    near, far = backward_chunk(frozen, dgate, dup, *cuts[0])
    low_out = whole_sum(partial_out, [*grad_b, near])
    side, side_far = side_of(
        order, low_out, segment[:, None], adapter_down_factors, seg_adapter, places
    )
    side_far = torus.move(side_far, 2, 1)
    at = jnp.stack([index // c, core]).astype(jnp.int32)
    sums, inners, inner_moves, outer_moves, blocks = [], [], [], [], []
    for q, (first, step) in enumerate(cuts):
        if q:
            near, far = backward_chunk(frozen, after(dgate, sums[-1][0]), dup, first, step)
            ahead = inner_moves[q - 1] + (outer_moves[q - 2] if q > 1 else [])
            far = lax.optimization_barrier((far, *ahead))[0]
        far = torus.move(far, 2, 1)
        sums.append(core_sum(near, far, side, side_far, at, first, b))
        inner_moves.append([torus.move(sums[q][k], 1, k) for k in range(1, b)])
        total = sums[q][0].astype(F32)
        for v in inner_moves[q]:
            total = total + v.astype(F32)
        inners.append(total.astype(BF16).reshape(a, rows, step))
        outer_moves.append([torus.move(inners[q][k], 0, k) for k in range(1, a)])
    for q, inner in enumerate(inners):
        total = inner[0].astype(F32)
        for v in outer_moves[q]:
            v = lax.optimization_barrier((v, *inner_moves[-1]))[0] if q < len(cuts) - 1 else v
            total = total + v.astype(F32)
        blocks.append(total.astype(BF16))
    dinput = jnp.concatenate(blocks, axis=1)
    grad_b = grad_b_of(
        dgate, dup, order, after(low_in, sums[-1][0]), adapter[None, :], adapter_list,
        grad_b[-1] if grad_b else None, thirds[-1],
    )
    grad_a = grad_a_of(
        columns, order, after(low_out, sums[-1][0]), adapter[:, None], adapter_list
    )
    return (dinput, grad_a, grad_b)


def solution(mesh):
    placed = (
        P(("groups", "tensor"), None),
        P("groups", "tensor"),
        P(None, None, "tensor"),
        P(None, "tensor", None),
        P(None, None, "tensor"),
        P("groups", None),
        P("groups", None),
        P(),
    )
    return jax.shard_map(
        local,
        mesh=mesh,
        in_specs=placed,
        out_specs=(
            P(("groups", "tensor"), None),
            P("groups", "tensor", None),
            P("groups", None, "tensor"),
        ),
        check_vma=False,
    )
```

```python
import functools

import jax
import jax.numpy as jnp
from jax import lax
from jax.experimental import pallas as pl
from jax.experimental.pallas import tpu as pltpu
from jax.sharding import PartitionSpec as P

GATHER_SHARES = (3, 5)
SUM_SHARES = (3, 3, 2)
MIB = 1024 * 1024
BF16 = jnp.bfloat16
DEPTH = 3
ONCE = pl.Buffered(1)
F32 = jnp.float32


def dot(left, right, dims=((1,), (0,))):
    return lax.dot_general(left, right, (dims, ((), ())), preferred_element_type=F32)


def params(mib):
    return pltpu.CompilerParams(vmem_limit_bytes=mib * MIB)


def cost(flops, moved):
    return pl.CostEstimate(flops=int(flops), bytes_accessed=int(moved), transcendentals=0)


def tile_of(size, most):
    return most if size % most == 0 else size


def parts_of(count, parts):
    parts = min(parts, count)
    ends = [count * k // parts for k in range(parts + 1)]
    return list(zip(ends[:-1], ends[1:]))


def after(x, other):
    return lax.optimization_barrier((x, other))[0]


class Torus:
    def __init__(self, size):
        core = 2 if size % 2 == 0 else 1
        chips = size // core
        inner = 1
        while inner * 2 * inner * 2 <= chips and chips % (inner * 2) == 0:
            inner *= 2
        self.size = size
        self.dims = (chips // inner, inner, core)
        self.strides = (inner * core, core, 1)

    def place(self, index):
        return [index // s % n for s, n in zip(self.strides, self.dims)]

    def shifted(self, index, dim, by):
        at = index // self.strides[dim] % self.dims[dim]
        return index + ((at + by) % self.dims[dim] - at) * self.strides[dim]

    def move(self, x, dim, by):
        pairs = [(i, self.shifted(i, dim, by)) for i in range(self.size)]
        return lax.ppermute(x, "tensor", pairs)

    def gather(self, x, dim):
        return jnp.stack([x] + [self.move(x, dim, -k) for k in range(1, self.dims[dim])])

    def scatter_sum(self, x, dim):
        total = x[0].astype(F32)
        for k in range(1, self.dims[dim]):
            total = total + self.move(x[k], dim, k).astype(F32)
        return total

    def slot_devices(self, index):
        outer, inner, core = self.place(index)
        a, b, c = self.dims
        cs = lax.broadcasted_iota(jnp.int32, (c, b, a), 0)
        bs = lax.broadcasted_iota(jnp.int32, (c, b, a), 1)
        zs = lax.broadcasted_iota(jnp.int32, (c, b, a), 2)
        return (((outer + zs) % a * b + (inner + bs) % b) * c + (core + cs) % c).reshape(-1)

    def exchange_sum(self, x, dims, beside):
        beside = list(beside)
        for dim in dims:
            k = 1
            while k < self.dims[dim]:
                stride = self.strides[dim]
                pairs = [(i, i + ((i // stride ^ k) - i // stride) * stride) for i in range(self.size)]
                x = x + lax.ppermute(x, "tensor", pairs)
                if beside:
                    x = after(x, beside.pop(0))
                k *= 2
        return x

    def slots_of(self, index):
        outer, inner, core = self.place(index)
        a, b, c = self.dims
        zs = lax.broadcasted_iota(jnp.int32, (a, b, c), 0)
        bs = lax.broadcasted_iota(jnp.int32, (a, b, c), 1)
        cs = lax.broadcasted_iota(jnp.int32, (a, b, c), 2)
        return (((cs - core) % c * b + (bs - inner) % b) * a + (zs - outer) % a).reshape(-1)


def tile_at(ref, n, tile):
    if ref.shape[1] == tile:
        return ref
    return ref.at[:, pl.ds(pl.multiple_of(n * tile, tile), tile)]


def ring(fetch, k, count):
    @pl.when(k == 0)
    def _():
        for j in range(min(DEPTH - 1, count)):
            for copy in fetch(j, j):
                copy.start()

    @pl.when(k + DEPTH - 1 < count)
    def _():
        for copy in fetch(k + DEPTH - 1, (k + DEPTH - 1) % DEPTH):
            copy.start()

    for copy in fetch(k, k % DEPTH):
        copy.wait()
    return k % DEPTH


def forward_kernel(pieces, low, count, first, *rest):
    parts, frozen, rest = rest[:pieces], rest[pieces], rest[pieces + 1 :]
    out, held, arrived = rest[-3:]
    step, tile = held.shape[2:]

    def fetch(n, slot):
        return [
            pltpu.make_async_copy(
                tile_at(frozen.at[i, pl.ds(first, step)], low + n, tile),
                held.at[slot, i],
                arrived.at[slot, i],
            )
            for i in range(2)
        ]

    slot = ring(fetch, pl.program_id(0), count)
    x = jnp.concatenate([v[...] for v in parts], axis=0)
    for i in range(2):
        part = dot(x, held[slot, i])
        out[i] = part if len(rest) == 3 else rest[0][i] + part


def forward_chunk(pieces, frozen, start, first, tiles):
    step = pieces[0].shape[1]
    tokens = sum(v.shape[0] for v in pieces)
    hidden = frozen.shape[2]
    tile = tile_of(hidden, 256)
    low, high = tiles
    across = pl.BlockSpec((2, tokens, tile), lambda n: (0, 0, low + n))
    operands = [*pieces, frozen]
    specs = [pl.BlockSpec(v.shape, lambda n: (0, 0), pipeline_mode=ONCE) for v in pieces]
    specs.append(pl.BlockSpec(memory_space=pltpu.HBM))
    if start is not None:
        operands.append(start)
        specs.append(across)
    count = high - low
    return pl.pallas_call(
        functools.partial(forward_kernel, len(pieces), low, count, first),
        grid=(count,),
        in_specs=specs,
        out_specs=across,
        out_shape=jax.ShapeDtypeStruct((2, tokens, hidden), F32),
        scratch_shapes=[
            pltpu.VMEM((DEPTH, 2, step, tile), BF16),
            pltpu.SemaphoreType.DMA((DEPTH, 2)),
        ],
        input_output_aliases={} if start is None else {len(operands) - 1: 0},
        compiler_params=params(24),
        cost_estimate=cost(4 * tokens * step * tile * count, 4 * step * tile * count),
    )(*operands)


def low_in_kernel(segments, chunks, rows, adapters, places, which, seg, *rest):
    factors, rest = rest[:segments], rest[segments:]
    cuts, (columns, out) = rest[:-2], rest[-2:]
    pieces = len(cuts) // chunks
    for q in range(chunks):

        @pl.when(which[0] == q)
        def _():
            first = 0
            for v in cuts[q * pieces : (q + 1) * pieces]:
                columns[first : first + v.shape[0]] = v[...]
                first += v.shape[0]

    total = jnp.zeros(out.shape, F32)
    for s in range(segments):
        part = dot(columns[...], factors[s][0])
        total = total + jnp.where(seg[...] == s, part, 0.0)
    put_rows(out, total, places, rows)


def put_rows(out, total, places, rows):
    if rows % 8:
        out[...] = total
        return
    for s in range(total.shape[0] // rows):
        out[pl.ds(pl.multiple_of(places[s] * rows, rows), rows), :] = total[s * rows : (s + 1) * rows]


def of_segment(shape, s):
    return pl.BlockSpec((1,) + shape[1:], lambda *a: (a[-2][s], 0, 0))


def low_in_partial(chunks, seg, down, adapters, places, index, rows):
    segments = adapters.shape[0]
    shard, wide = down.shape[1:]
    tokens = seg.shape[0]
    if shard % 128:
        joined = [jnp.concatenate(piece, axis=1) for piece in zip(*chunks)]
        chunks = [[lax.dynamic_slice_in_dim(v, index * shard, shard, 1) for v in joined]]
        which = jnp.zeros((1,), jnp.int32)
        cuts = [pl.BlockSpec(v.shape, lambda *a: (0, 0)) for v in chunks[0]]
    else:
        inside, at, cuts, first = [], [], [], 0
        for q, pieces in enumerate(chunks):
            per = pieces[0].shape[1] // shard
            inside.append(index >= first)
            at.append(jnp.clip(index - first, 0, per - 1))
            cuts += [
                pl.BlockSpec((v.shape[0], shard), lambda i, a, p, w, q=q: (0, w[1 + q])) for v in pieces
            ]
            first += per
        which = jnp.stack([sum(v.astype(jnp.int32) for v in inside) - 1] + at).astype(jnp.int32)
    full = lambda shape: pl.BlockSpec(shape, lambda *a: (0,) * len(shape))
    factor = lambda s: pl.BlockSpec((1, shard, wide), lambda i, a, p, w: (a[s], 0, 0))
    return pl.pallas_call(
        functools.partial(low_in_kernel, segments, len(chunks), rows),
        grid_spec=pltpu.PrefetchScalarGridSpec(
            num_scalar_prefetch=3,
            grid=(1,),
            in_specs=[full(seg.shape)] + [factor(s) for s in range(segments)] + cuts,
            out_specs=[full((tokens, shard)), full((tokens, wide))],
        ),
        out_shape=[
            jax.ShapeDtypeStruct((tokens, shard), BF16),
            jax.ShapeDtypeStruct((tokens, wide), F32),
        ],
        compiler_params=params(16),
        cost_estimate=cost(2 * tokens * down[0].size * segments, 2 * down[0].size * segments),
    )(adapters, places, which, seg, *([down] * segments), *[v for pieces in chunks for v in pieces])


def middle_kernel(rows, adapters, places, base, dhidden, token_order, order, low, seg, up, *rest):
    dgate, dup, out, left, back, factors, arrived = rest
    segments, wide, tile = factors.shape[1:]
    rank = wide // 2
    tokens = order.shape[0]
    n = pl.program_id(0)
    slot = n % 2
    lane = lax.broadcasted_iota(jnp.int32, (tokens, segments * rank), 1) // rank
    mask = lane == seg[...]

    def fetch(n, slot, s):
        return pltpu.make_async_copy(
            tile_at(up.at[adapters[s]], n, tile), factors.at[slot, s], arrived.at[slot, s]
        )

    @pl.when(n == 0)
    def _():
        for s in range(segments):
            fetch(0, 0, s).start()
        mine = dot(order[...], low[...])
        for i in range(2):
            block = jnp.concatenate([mine[:, i * rank : (i + 1) * rank]] * segments, axis=1)
            left[i] = jnp.where(mask, block, 0.0).astype(BF16)
        back[...] = jnp.zeros_like(back)

    @pl.when(n + 1 < pl.num_programs(0))
    def _():
        for s in range(segments):
            fetch(n + 1, 1 - slot, s).start()

    for s in range(segments):
        fetch(n, slot, s).wait()
    up_g = jnp.concatenate([factors[slot, s, :rank] for s in range(segments)], axis=0)
    up_u = jnp.concatenate([factors[slot, s, rank:] for s in range(segments)], axis=0)
    gate = base[0] + dot(left[0], up_g)
    up_sum = base[1] + dot(left[1], up_u)
    grad = dot(token_order[...], dhidden[...])
    sigma = 1.0 / (1.0 + jnp.exp(-gate))
    g = (grad * up_sum * sigma * (1.0 + gate * (1.0 - sigma))).astype(BF16)
    u = (grad * gate * sigma).astype(BF16)
    dgate[...] = g
    dup[...] = u
    back[0] += dot(g, up_g, ((1,), (1,)))
    back[1] += dot(u, up_u, ((1,), (1,)))

    @pl.when(n == pl.num_programs(0) - 1)
    def _():
        parts = []
        for i in range(2):
            kept = jnp.where(mask, back[i], 0.0)
            parts.append(sum(kept[:, s * rank : (s + 1) * rank] for s in range(segments)))
        put_rows(out, jnp.concatenate(parts, axis=1), places, rows)


def middle(base, dhidden, token_order, order, low, seg, up, adapters, places, rows):
    segments = adapters.shape[0]
    tokens, hidden = dhidden.shape
    wide = up.shape[1]
    tile = tile_of(hidden, 256)
    full = lambda shape: pl.BlockSpec(shape, lambda *a: (0,) * len(shape))
    across = lambda lead: pl.BlockSpec(lead + (tokens, tile), lambda n, *a: (0,) * len(lead) + (0, n))
    return pl.pallas_call(
        functools.partial(middle_kernel, rows),
        grid_spec=pltpu.PrefetchScalarGridSpec(
            num_scalar_prefetch=2,
            grid=(hidden // tile,),
            in_specs=[across((2,)), across(())]
            + [full(v.shape) for v in (token_order, order, low, seg)]
            + [pl.BlockSpec(memory_space=pltpu.HBM)],
            out_specs=[across(()), across(()), full((tokens, wide))],
            scratch_shapes=[
                pltpu.VMEM((2, tokens, segments * wide // 2), BF16),
                pltpu.VMEM((2, tokens, segments * wide // 2), F32),
                pltpu.VMEM((2, segments, wide, tile), BF16),
                pltpu.SemaphoreType.DMA((2, segments)),
            ],
        ),
        out_shape=[
            jax.ShapeDtypeStruct((tokens, hidden), BF16),
            jax.ShapeDtypeStruct((tokens, hidden), BF16),
            jax.ShapeDtypeStruct((tokens, wide), F32),
        ],
        compiler_params=params(20),
        cost_estimate=cost(
            4 * tokens * hidden * segments * wide, hidden * (tokens * 14 + segments * wide * 2)
        ),
    )(adapters, places, base, dhidden, token_order, order, low, seg, up)


def grad_b_kernel(dgate, dup, order, low, adapter, *rest):
    out, left = rest[-2:]
    adapters, wide, tile = out.shape
    rank = wide // 2

    @pl.when(pl.program_id(0) == 0)
    def _():
        turned = dot(order[...], low[...]).T
        for a in range(adapters):
            kept = jnp.where(adapter[...] == a, turned, 0.0).astype(BF16)
            left[0, a * rank : (a + 1) * rank] = kept[:rank]
            left[1, a * rank : (a + 1) * rank] = kept[rank:]

    for i, grad in enumerate((dgate, dup)):
        part = dot(left[i], grad[...])
        out[:, i * rank : (i + 1) * rank, :] = part.reshape(adapters, rank, tile)


def grad_b_of(dgate, dup, order, low, adapter_row, adapters, start, tiles):
    tokens, hidden = dgate.shape
    wide = low.shape[1]
    tile = tile_of(hidden, 256)
    first, last = tiles
    full = lambda shape: pl.BlockSpec(shape, lambda n: (0,) * len(shape))
    across = pl.BlockSpec((tokens, tile), lambda n: (0, first + n))
    operands = [dgate, dup, order, low, adapter_row]
    specs = [across, across, full(order.shape), full(low.shape), full(adapter_row.shape)]
    if start is not None:
        operands.append(start)
        specs.append(pl.BlockSpec(memory_space=pl.ANY))
    part = tile * (last - first) * adapters * wide
    return pl.pallas_call(
        grad_b_kernel,
        grid=(last - first,),
        in_specs=specs,
        out_specs=pl.BlockSpec((adapters, wide, tile), lambda n: (0, 0, first + n)),
        out_shape=jax.ShapeDtypeStruct((adapters, wide, hidden), F32),
        scratch_shapes=[pltpu.VMEM((2, adapters * wide // 2, tokens), BF16)],
        input_output_aliases={} if start is None else {5: 0},
        compiler_params=params(20),
        cost_estimate=cost(2 * tokens * part, 4 * part),
    )(*operands)


def grad_a_kernel(per, columns, order, low, adapter, out, turned, mine):
    @pl.when(pl.program_id(0) == 0)
    def _():
        turned[...] = columns[...].astype(F32).T.astype(BF16)
        mine[...] = dot(order[...], low[...])

    for j in range(per):
        a = pl.program_id(0) * per + j
        kept = jnp.where(adapter[...] == a, mine[...], 0.0).astype(BF16)
        out[j] = dot(turned[...], kept)


def grad_a_of(columns, order, low, adapter, adapters):
    tokens, shard = columns.shape
    wide = low.shape[1]
    per = 4 if adapters % 4 == 0 else 1
    full = lambda shape: pl.BlockSpec(shape, lambda n: (0,) * len(shape))
    return pl.pallas_call(
        functools.partial(grad_a_kernel, per),
        grid=(adapters // per,),
        in_specs=[full(columns.shape), full(order.shape), full(low.shape), full(adapter.shape)],
        out_specs=pl.BlockSpec((per, shard, wide), lambda n: (n, 0, 0)),
        out_shape=jax.ShapeDtypeStruct((adapters, shard, wide), F32),
        scratch_shapes=[pltpu.VMEM((shard, tokens), BF16), pltpu.VMEM((tokens, wide), F32)],
        compiler_params=params(16),
        cost_estimate=cost(2 * tokens * shard * adapters * wide, 4 * shard * adapters * wide),
    )(columns, order, low, adapter)


def side_kernel(segments, adapters, places, order, low, seg, *rest):
    near, far = rest[-2:]
    half = near.shape[0]
    mine = dot(order[...], low[...])
    total = jnp.zeros((2 * half, near.shape[1]), F32)
    for s in range(segments):
        kept = jnp.where(seg[...] == s, mine, 0.0).astype(BF16)
        total = total + dot(kept, rest[s][0], ((1,), (1,)))
    near[...] = total[:half]
    far[...] = total[half:]


def side_of(order, low, seg, down, adapters, places):
    segments = adapters.shape[0]
    tokens = order.shape[0]
    shard = down.shape[1]
    full = lambda shape: pl.BlockSpec(shape, lambda *a: (0,) * len(shape))
    return pl.pallas_call(
        functools.partial(side_kernel, segments),
        grid_spec=pltpu.PrefetchScalarGridSpec(
            num_scalar_prefetch=2,
            grid=(1,),
            in_specs=[full(order.shape), full(low.shape), full(seg.shape)]
            + [of_segment(down.shape, s) for s in range(segments)],
            out_specs=[full((tokens // 2, shard))] * 2,
        ),
        out_shape=[jax.ShapeDtypeStruct((tokens // 2, shard), F32)] * 2,
        compiler_params=params(16),
        cost_estimate=cost(2 * tokens * down[0].size * segments, 2 * down[0].size * segments),
    )(adapters, places, order, low, seg, *([down] * segments))


def backward_kernel(count, first, frozen, dgate, dup, near, far, held, arrived):
    half = near.shape[0]
    block = held.shape[2]

    def fetch(k, slot):
        rows = pl.ds(pl.multiple_of(first + k * block, block), block)
        return [
            pltpu.make_async_copy(frozen.at[i, rows, :], held.at[slot, i], arrived.at[slot, i])
            for i in range(2)
        ]

    slot = ring(fetch, pl.program_id(0), count)
    term = dot(dgate[...], held[slot, 0], ((1,), (1,))) + dot(dup[...], held[slot, 1], ((1,), (1,)))
    near[...] = term[:half].astype(BF16)
    far[...] = term[half:].astype(BF16)


def backward_chunk(frozen, dgate, dup, first, step):
    tokens, hidden = dgate.shape
    block = tile_of(step, 512)
    count = step // block
    full = lambda shape: pl.BlockSpec(shape, lambda k: (0, 0), pipeline_mode=ONCE)
    out = pl.BlockSpec((tokens // 2, block), lambda k: (0, k))
    return pl.pallas_call(
        functools.partial(backward_kernel, count, first),
        grid=(count,),
        in_specs=[pl.BlockSpec(memory_space=pltpu.HBM), full(dgate.shape), full(dup.shape)],
        out_specs=[out, out],
        out_shape=[jax.ShapeDtypeStruct((tokens // 2, step), BF16)] * 2,
        scratch_shapes=[
            pltpu.VMEM((DEPTH, 2, block, hidden), BF16),
            pltpu.SemaphoreType.DMA((DEPTH, 2)),
        ],
        compiler_params=params(20),
        cost_estimate=cost(4 * tokens * step * hidden, 4 * step * hidden),
    )(frozen, dgate, dup)


def core_sum_kernel(base, at, near, far, side, side_far, *outs):
    total = near[...].astype(F32) + far[...].astype(F32)
    rows = outs[0].shape[0]
    own = at[0] == base + pl.program_id(0)

    def store(total):
        for s, out in enumerate(outs):
            out[...] = total[s * rows : (s + 1) * rows].astype(BF16)

    @pl.when(jnp.logical_not(own))
    def _():
        store(total)

    @pl.when(jnp.logical_and(own, at[1] == 0))
    def _():
        store(total + jnp.concatenate([side[...], side_far[...]], axis=1))

    @pl.when(jnp.logical_and(own, at[1] != 0))
    def _():
        store(total + jnp.concatenate([side_far[...], side[...]], axis=1))


def core_sum(near, far, side, side_far, at, first, slots):
    half, step = near.shape
    block = 2 * side.shape[1]
    full = lambda shape: pl.BlockSpec(shape, lambda *a: (0,) * len(shape))
    across = lambda rows: pl.BlockSpec((rows, block), lambda k, at: (0, k))
    return pl.pallas_call(
        functools.partial(core_sum_kernel, first // block),
        grid_spec=pltpu.PrefetchScalarGridSpec(
            num_scalar_prefetch=1,
            grid=(step // block,),
            in_specs=[across(half), across(half), full(side.shape), full(side_far.shape)],
            out_specs=[across(half // slots)] * slots,
        ),
        out_shape=[jax.ShapeDtypeStruct((half // slots, step), BF16)] * slots,
        compiler_params=params(16),
        cost_estimate=cost(2 * half * step, 6 * half * step),
    )(at, near, far, side, side_far)


def local(
    activations,
    dhidden,
    frozen,
    adapter_down_factors,
    adapter_up_factors,
    segment_adapter_index,
    segment_row_counts,
    ranks,
):
    adapter_list, shard_width, gate_and_up = adapter_down_factors.shape
    rank = gate_and_up // 2
    width = frozen.shape[1]
    rows = activations.shape[0]
    torus = Torus(width // shard_width)
    tokens = rows * torus.size
    a, b, c = torus.dims
    index = lax.axis_index("tensor")
    slots = torus.slot_devices(index)
    token = (slots[:, None] * rows + jnp.arange(rows, dtype=jnp.int32)[None, :]).reshape(-1)

    ends = jnp.cumsum(segment_row_counts[0])
    seg_adapter = segment_adapter_index[0]
    count = ends.shape[0]

    def segment_of(place):
        return jnp.sum((place[:, None] >= ends[None, :]).astype(jnp.int32), axis=1)

    def adapter_of(segment):
        match = segment[:, None] == jnp.arange(count, dtype=jnp.int32)[None, :]
        return jnp.sum(jnp.where(match, seg_adapter[None, :], 0), axis=1)

    column = jnp.arange(gate_and_up, dtype=jnp.int32) % rank
    chips = a * b
    core = index % c
    mine = (jnp.arange(chips, dtype=jnp.int32)[:, None] * c + core) * rows
    mine = (mine + jnp.arange(rows, dtype=jnp.int32)[None, :]).reshape(-1)
    my_adapter = adapter_of(segment_of(mine))
    hit = my_adapter[:, None] == jnp.arange(adapter_list, dtype=jnp.int32)[None, :]
    my_rank = jnp.sum(jnp.where(hit, ranks[None, :], 0), axis=1)[:, None]
    factor = jnp.where(column[None, :] < my_rank, 16.0 / my_rank.astype(F32), 0.0)

    places = (slots % c - core) % c * chips + slots // c
    spot = (places[:, None] * rows + jnp.arange(rows, dtype=jnp.int32)[None, :]).reshape(-1)
    count_up = jnp.arange(tokens, dtype=jnp.int32)[None, :]
    token_order = (token[:, None] == count_up).astype(BF16)
    order = (spot[:, None] == count_up).astype(BF16)

    segment = segment_of(token)
    adapter = adapter_of(segment)

    def whole_sum(partial, beside=()):
        if rows % 8:
            at = jnp.arange(torus.size, dtype=jnp.int32)
            device = at % chips * c + (core + at // chips) % c
            partial = jnp.take(
                partial.reshape(torus.size, rows, -1),
                jnp.take(torus.slots_of(index), device),
                axis=0,
            )
        x = torus.scatter_sum(partial.reshape(c, chips * rows, gate_and_up), 2)
        x = torus.exchange_sum(x, (1, 0), beside)
        return torus.gather((x * factor).astype(BF16), 2).reshape(tokens, gate_and_up)

    hidden = frozen.shape[2]
    tiles = hidden // tile_of(hidden, 256)
    chunks = []
    for share in GATHER_SHARES:
        first = sum(v.shape[1] for v in chunks)
        chunks.append(activations[:, first : first + width * share // sum(GATHER_SHARES)])
    outer = []
    for x in chunks:
        x = torus.gather(after(x, outer[-1]) if outer else x, 0)
        outer.append(x.reshape(a * rows, -1))
    base = None
    gathered = []
    for q, x in enumerate(outer):
        near = [x] + [torus.move(x, 1, -k) for k in range(1, b)]
        near[1:] = lax.optimization_barrier((*near[1:], base if q else outer[-1]))[:-1]
        far = [torus.move(v, 2, -1) for v in near]
        gathered.append([*near, *far])
        first = sum(v.shape[1] for v in chunks[:q])
        for cut in parts_of(tiles, 4 if q else 1):
            base = forward_chunk(gathered[q], frozen, base, first, cut)

    columns, partial_in = low_in_partial(
        gathered, segment[:, None], adapter_down_factors, seg_adapter, places, index, rows
    )
    low_in = whole_sum(partial_in)
    dgate, dup, partial_out = middle(
        base, dhidden, token_order, order, low_in, segment[:, None], adapter_up_factors,
        seg_adapter, places, rows,
    )
    grad_b = []
    thirds = parts_of(tiles, 3)
    for cut in thirds[:-1]:
        grad_b.append(
            grad_b_of(
                dgate, dup, order, low_in, adapter[None, :], adapter_list,
                grad_b[-1] if grad_b else None, cut,
            )
        )
    cuts = []
    for share in SUM_SHARES:
        cuts.append((sum(v[1] for v in cuts), width * share // sum(SUM_SHARES)))
    near, far = backward_chunk(frozen, dgate, dup, *cuts[0])
    low_out = whole_sum(partial_out, [*grad_b, near])
    side, side_far = side_of(
        order, low_out, segment[:, None], adapter_down_factors, seg_adapter, places
    )
    side_far = torus.move(side_far, 2, 1)
    at = jnp.stack([index // c, core]).astype(jnp.int32)
    sums, inners, inner_moves, outer_moves, blocks = [], [], [], [], []
    for q, (first, step) in enumerate(cuts):
        if q:
            near, far = backward_chunk(frozen, after(dgate, sums[-1][0]), dup, first, step)
            ahead = inner_moves[q - 1] + (outer_moves[q - 2] if q > 1 else [])
            far = lax.optimization_barrier((far, *ahead))[0]
        far = torus.move(far, 2, 1)
        sums.append(core_sum(near, far, side, side_far, at, first, b))
        inner_moves.append([torus.move(sums[q][k], 1, k) for k in range(1, b)])
        total = sums[q][0].astype(F32)
        for v in inner_moves[q]:
            total = total + v.astype(F32)
        inners.append(total.astype(BF16).reshape(a, rows, step))
        outer_moves.append([torus.move(inners[q][k], 0, k) for k in range(1, a)])
    for q, inner in enumerate(inners):
        total = inner[0].astype(F32)
        for v in outer_moves[q]:
            v = lax.optimization_barrier((v, *inner_moves[-1]))[0] if q < len(cuts) - 1 else v
            total = total + v.astype(F32)
        blocks.append(total.astype(BF16))
    dinput = jnp.concatenate(blocks, axis=1)
    grad_b = grad_b_of(
        dgate, dup, order, after(low_in, sums[-1][0]), adapter[None, :], adapter_list,
        grad_b[-1] if grad_b else None, thirds[-1],
    )
    grad_a = grad_a_of(
        columns, order, after(low_out, sums[-1][0]), adapter[:, None], adapter_list
    )
    return (dinput, grad_a, grad_b)


def solution(mesh):
    placed = (
        P(("groups", "tensor"), None),
        P("groups", "tensor"),
        P(None, None, "tensor"),
        P(None, "tensor", None),
        P(None, None, "tensor"),
        P("groups", None),
        P("groups", None),
        P(),
    )
    return jax.shard_map(
        local,
        mesh=mesh,
        in_specs=placed,
        out_specs=(
            P(("groups", "tensor"), None),
            P("groups", "tensor", None),
            P("groups", None, "tensor"),
        ),
        check_vma=False,
    )
```

```python
import functools

import jax
import jax.numpy as jnp
from jax import lax
from jax.experimental import pallas as pl
from jax.experimental.pallas import tpu as pltpu
from jax.sharding import PartitionSpec as P

OUTER_SHARES = (3, 5)
INNER_CUTS = (1, 2)
SUM_SHARES = (5, 3)
MIB = 1024 * 1024
BF16 = jnp.bfloat16
DEPTH = 3
SLOTS = 4
ONCE = pl.Buffered(1)
F32 = jnp.float32


def dot(left, right, dims=((1,), (0,))):
    return lax.dot_general(left, right, (dims, ((), ())), preferred_element_type=F32)


def params(mib):
    return pltpu.CompilerParams(vmem_limit_bytes=mib * MIB)


def cost(flops, moved):
    return pl.CostEstimate(flops=int(flops), bytes_accessed=int(moved), transcendentals=0)


def tile_of(size, most):
    return most if size % most == 0 else size


def parts_of(count, parts):
    parts = min(parts, count)
    ends = [count * k // parts for k in range(parts + 1)]
    return list(zip(ends[:-1], ends[1:]))


def after(x, other):
    return lax.optimization_barrier((x, other))[0]


class Torus:
    def __init__(self, size):
        core = 2 if size % 2 == 0 else 1
        chips = size // core
        inner = 1
        while inner * 2 * inner * 2 <= chips and chips % (inner * 2) == 0:
            inner *= 2
        self.size = size
        self.dims = (chips // inner, inner, core)
        self.strides = (inner * core, core, 1)

    def place(self, index):
        return [index // s % n for s, n in zip(self.strides, self.dims)]

    def shifted(self, index, dim, by):
        at = index // self.strides[dim] % self.dims[dim]
        return index + ((at + by) % self.dims[dim] - at) * self.strides[dim]

    def move(self, x, dim, by):
        pairs = [(i, self.shifted(i, dim, by)) for i in range(self.size)]
        return lax.ppermute(x, "tensor", pairs)

    def gather(self, x, dim):
        return jnp.stack([x] + [self.move(x, dim, -k) for k in range(1, self.dims[dim])])

    def scatter_sum(self, x, dim):
        total = x[0].astype(F32)
        for k in range(1, self.dims[dim]):
            total = total + self.move(x[k], dim, k).astype(F32)
        return total

    def slot_devices(self, index):
        outer, inner, core = self.place(index)
        a, b, c = self.dims
        cs = lax.broadcasted_iota(jnp.int32, (c, b, a), 0)
        bs = lax.broadcasted_iota(jnp.int32, (c, b, a), 1)
        zs = lax.broadcasted_iota(jnp.int32, (c, b, a), 2)
        return (((outer + zs) % a * b + (inner + bs) % b) * c + (core + cs) % c).reshape(-1)

    def exchange_sum(self, x, dims, beside):
        beside = list(beside)
        for dim in dims:
            k = 1
            while k < self.dims[dim]:
                stride = self.strides[dim]
                pairs = [(i, i + ((i // stride ^ k) - i // stride) * stride) for i in range(self.size)]
                done = beside.pop(0)(x) if beside else None
                x = x + lax.ppermute(x, "tensor", pairs)
                x = x if done is None else after(x, done)
                k *= 2
        return x

    def slots_of(self, index):
        outer, inner, core = self.place(index)
        a, b, c = self.dims
        zs = lax.broadcasted_iota(jnp.int32, (a, b, c), 0)
        bs = lax.broadcasted_iota(jnp.int32, (a, b, c), 1)
        cs = lax.broadcasted_iota(jnp.int32, (a, b, c), 2)
        return (((cs - core) % c * b + (bs - inner) % b) * a + (zs - outer) % a).reshape(-1)


def tile_at(ref, n, tile):
    if ref.shape[1] == tile:
        return ref
    return ref.at[:, pl.ds(pl.multiple_of(n * tile, tile), tile)]


def ring(fetch, k, count):
    @pl.when(k == 0)
    def _():
        for j in range(min(DEPTH - 1, count)):
            for copy in fetch(j, j):
                copy.start()

    @pl.when(k + DEPTH - 1 < count)
    def _():
        for copy in fetch(k + DEPTH - 1, (k + DEPTH - 1) % DEPTH):
            copy.start()

    return k % DEPTH, fetch(k, k % DEPTH)


def send(copy_of, k, count, fill):
    @pl.when(k >= SLOTS)
    def _():
        copy_of(k - SLOTS).wait()

    fill(k % SLOTS)
    copy_of(k).start()

    @pl.when(k == count - 1)
    def _():
        for j in range(min(SLOTS, count)):
            copy_of(k - j).wait()


def forward_kernel(pieces, low, count, first, *rest):
    parts, frozen, rest = rest[:pieces], rest[pieces], rest[pieces + 1 :]
    out, held, arrived = rest[-3:]
    step, tile = held.shape[2:]

    depth = step // 2

    def fetch(n, slot):
        return [
            pltpu.make_async_copy(
                tile_at(frozen.at[i, pl.ds(first + h * depth, depth)], low + n, tile),
                held.at[slot, i, pl.ds(h * depth, depth)],
                arrived.at[slot, i, h],
            )
            for i in range(2)
            for h in range(2)
        ]

    slot, copies = ring(fetch, pl.program_id(0), count)
    x = jnp.concatenate([v[...] for v in parts], axis=0)
    for i in range(2):
        part = 0.0 if len(rest) == 3 else rest[0][i]
        for h in range(2):
            rows = slice(h * depth, (h + 1) * depth)
            copies[2 * i + h].wait()
            part = part + dot(x[:, rows], held[slot, i, rows])
        out[i] = part


def forward_chunk(pieces, frozen, start, first, tiles):
    step = pieces[0].shape[1]
    tokens = sum(v.shape[0] for v in pieces)
    hidden = frozen.shape[2]
    tile = tile_of(hidden, 256)
    low, high = tiles
    across = pl.BlockSpec((2, tokens, tile), lambda n: (0, 0, low + n))
    operands = [*pieces, frozen]
    specs = [pl.BlockSpec(v.shape, lambda n: (0, 0), pipeline_mode=ONCE) for v in pieces]
    specs.append(pl.BlockSpec(memory_space=pltpu.HBM))
    if start is not None:
        operands.append(start)
        specs.append(across)
    count = high - low
    return pl.pallas_call(
        functools.partial(forward_kernel, len(pieces), low, count, first),
        grid=(count,),
        in_specs=specs,
        out_specs=across,
        out_shape=jax.ShapeDtypeStruct((2, tokens, hidden), F32),
        scratch_shapes=[
            pltpu.VMEM((DEPTH, 2, step, tile), BF16),
            pltpu.SemaphoreType.DMA((DEPTH, 2, 2)),
        ],
        input_output_aliases={} if start is None else {len(operands) - 1: 0},
        compiler_params=params(24),
        cost_estimate=cost(4 * tokens * step * tile * count, 4 * step * tile * count),
    )(*operands)


def low_in_kernel(segments, chunks, rows, adapters, places, which, seg, *rest):
    factors, rest = rest[:segments], rest[segments:]
    cuts, (columns, out) = rest[:-2], rest[-2:]
    pieces = len(cuts) // chunks
    for q in range(chunks):

        @pl.when(which[0] == q)
        def _():
            first = 0
            for v in cuts[q * pieces : (q + 1) * pieces]:
                columns[first : first + v.shape[0]] = v[...]
                first += v.shape[0]

    total = jnp.zeros(out.shape, F32)
    for s in range(segments):
        part = dot(columns[...], factors[s][0])
        total = total + jnp.where(seg[...] == s, part, 0.0)
    put_rows(out, total, places, rows)


def put_rows(out, total, places, rows):
    if rows % 8:
        out[...] = total
        return
    for s in range(total.shape[0] // rows):
        out[pl.ds(pl.multiple_of(places[s] * rows, rows), rows), :] = total[s * rows : (s + 1) * rows]


def of_segment(shape, s):
    return pl.BlockSpec((1,) + shape[1:], lambda *a: (a[-2][s], 0, 0))


def low_in_partial(chunks, seg, down, adapters, places, index, rows):
    segments = adapters.shape[0]
    shard, wide = down.shape[1:]
    tokens = seg.shape[0]
    if shard % 128:
        joined = [jnp.concatenate(piece, axis=1) for piece in zip(*chunks)]
        chunks = [[lax.dynamic_slice_in_dim(v, index * shard, shard, 1) for v in joined]]
        which = jnp.zeros((1,), jnp.int32)
        cuts = [pl.BlockSpec(v.shape, lambda *a: (0, 0)) for v in chunks[0]]
    else:
        inside, at, cuts, first = [], [], [], 0
        for q, pieces in enumerate(chunks):
            per = pieces[0].shape[1] // shard
            inside.append(index >= first)
            at.append(jnp.clip(index - first, 0, per - 1))
            cuts += [
                pl.BlockSpec((v.shape[0], shard), lambda i, a, p, w, q=q: (0, w[1 + q])) for v in pieces
            ]
            first += per
        which = jnp.stack([sum(v.astype(jnp.int32) for v in inside) - 1] + at).astype(jnp.int32)
    full = lambda shape: pl.BlockSpec(shape, lambda *a: (0,) * len(shape))
    factor = lambda s: pl.BlockSpec((1, shard, wide), lambda i, a, p, w: (a[s], 0, 0))
    return pl.pallas_call(
        functools.partial(low_in_kernel, segments, len(chunks), rows),
        grid_spec=pltpu.PrefetchScalarGridSpec(
            num_scalar_prefetch=3,
            grid=(1,),
            in_specs=[full(seg.shape)] + [factor(s) for s in range(segments)] + cuts,
            out_specs=[full((tokens, shard)), full((tokens, wide))],
        ),
        out_shape=[
            jax.ShapeDtypeStruct((tokens, shard), BF16),
            jax.ShapeDtypeStruct((tokens, wide), F32),
        ],
        compiler_params=params(16),
        cost_estimate=cost(2 * tokens * down[0].size * segments, 2 * down[0].size * segments),
    )(adapters, places, which, seg, *([down] * segments), *[v for pieces in chunks for v in pieces])


def middle_kernel(rows, adapters, places, base, dhidden, token_order, order, low, seg, up, *rest):
    dgate, dup, out, left, back, factors, arrived = rest
    segments, wide, tile = factors.shape[1:]
    rank = wide // 2
    tokens = order.shape[0]
    n = pl.program_id(0)
    slot = n % 2
    lane = lax.broadcasted_iota(jnp.int32, (tokens, segments * rank), 1) // rank
    mask = lane == seg[...]

    def fetch(n, slot, s):
        return pltpu.make_async_copy(
            tile_at(up.at[adapters[s]], n, tile), factors.at[slot, s], arrived.at[slot, s]
        )

    @pl.when(n == 0)
    def _():
        for s in range(segments):
            fetch(0, 0, s).start()
        mine = dot(order[...], low[...])
        for i in range(2):
            block = jnp.concatenate([mine[:, i * rank : (i + 1) * rank]] * segments, axis=1)
            left[i] = jnp.where(mask, block, 0.0).astype(BF16)
        back[...] = jnp.zeros_like(back)

    @pl.when(n + 1 < pl.num_programs(0))
    def _():
        for s in range(segments):
            fetch(n + 1, 1 - slot, s).start()

    for s in range(segments):
        fetch(n, slot, s).wait()
    up_g = jnp.concatenate([factors[slot, s, :rank] for s in range(segments)], axis=0)
    up_u = jnp.concatenate([factors[slot, s, rank:] for s in range(segments)], axis=0)
    gate = base[0] + dot(left[0], up_g)
    up_sum = base[1] + dot(left[1], up_u)
    grad = dot(token_order[...], dhidden[...])
    sigma = 1.0 / (1.0 + jnp.exp(-gate))
    g = (grad * up_sum * sigma * (1.0 + gate * (1.0 - sigma))).astype(BF16)
    u = (grad * gate * sigma).astype(BF16)
    dgate[...] = g
    dup[...] = u
    back[0] += dot(g, up_g, ((1,), (1,)))
    back[1] += dot(u, up_u, ((1,), (1,)))

    @pl.when(n == pl.num_programs(0) - 1)
    def _():
        parts = []
        for i in range(2):
            kept = jnp.where(mask, back[i], 0.0)
            parts.append(sum(kept[:, s * rank : (s + 1) * rank] for s in range(segments)))
        put_rows(out, jnp.concatenate(parts, axis=1), places, rows)


def middle(base, dhidden, token_order, order, low, seg, up, adapters, places, rows):
    segments = adapters.shape[0]
    tokens, hidden = dhidden.shape
    wide = up.shape[1]
    tile = tile_of(hidden, 256)
    full = lambda shape: pl.BlockSpec(shape, lambda *a: (0,) * len(shape))
    across = lambda lead: pl.BlockSpec(lead + (tokens, tile), lambda n, *a: (0,) * len(lead) + (0, n))
    return pl.pallas_call(
        functools.partial(middle_kernel, rows),
        grid_spec=pltpu.PrefetchScalarGridSpec(
            num_scalar_prefetch=2,
            grid=(hidden // tile,),
            in_specs=[across((2,)), across(())]
            + [full(v.shape) for v in (token_order, order, low, seg)]
            + [pl.BlockSpec(memory_space=pltpu.HBM)],
            out_specs=[across(()), across(()), full((tokens, wide))],
            scratch_shapes=[
                pltpu.VMEM((2, tokens, segments * wide // 2), BF16),
                pltpu.VMEM((2, tokens, segments * wide // 2), F32),
                pltpu.VMEM((2, segments, wide, tile), BF16),
                pltpu.SemaphoreType.DMA((2, segments)),
            ],
        ),
        out_shape=[
            jax.ShapeDtypeStruct((tokens, hidden), BF16),
            jax.ShapeDtypeStruct((tokens, hidden), BF16),
            jax.ShapeDtypeStruct((tokens, wide), F32),
        ],
        compiler_params=params(20),
        cost_estimate=cost(
            4 * tokens * hidden * segments * wide, hidden * (tokens * 14 + segments * wide * 2)
        ),
    )(adapters, places, base, dhidden, token_order, order, low, seg, up)


def grad_b_kernel(first, count, dgate, dup, order, low, adapter, *rest):
    out, left, staged, sent = rest[-4:]
    group, wide, tile = staged.shape[1:]
    groups = left.shape[1]
    rank = wide // 2
    g = pl.program_id(1)
    k = pl.program_id(0) * groups + g

    @pl.when(k == 0)
    def _():
        turned = dot(order[...], low[...]).T
        for a in range(groups * group):
            kept = jnp.where(adapter[...] == a, turned, 0.0).astype(BF16)
            at = (a // group, slice(a % group * rank, (a % group + 1) * rank))
            left[(0, *at)] = kept[:rank]
            left[(1, *at)] = kept[rank:]

    def copy_of(k):
        block = out.at[pl.ds(k % groups * group, group)]
        if out.shape[2] != tile:
            at = pl.multiple_of((first + k // groups) * tile, tile)
            block = block.at[:, :, pl.ds(at, tile)]
        return pltpu.make_async_copy(staged.at[k % SLOTS], block, sent.at[k % SLOTS])

    def fill(slot):
        for i, grad in enumerate((dgate, dup)):
            part = dot(left[i, g], grad[...])
            staged[slot, :, i * rank : (i + 1) * rank, :] = part.reshape(group, rank, tile)

    send(copy_of, k, count * groups, fill)


def grad_b_of(dgate, dup, order, low, adapter_row, adapters, start, tiles):
    tokens, hidden = dgate.shape
    wide = low.shape[1]
    tile = tile_of(hidden, 256)
    first, last = tiles
    groups = 2 if adapters % 2 == 0 else 1
    group = adapters // groups
    full = lambda shape: pl.BlockSpec(shape, lambda n, g: (0,) * len(shape))
    across = pl.BlockSpec((tokens, tile), lambda n, g: (0, first + n))
    operands = [dgate, dup, order, low, adapter_row]
    specs = [across, across, full(order.shape), full(low.shape), full(adapter_row.shape)]
    if start is not None:
        operands.append(start)
        specs.append(pl.BlockSpec(memory_space=pltpu.HBM))
    part = tile * (last - first) * adapters * wide
    return pl.pallas_call(
        functools.partial(grad_b_kernel, first, last - first),
        grid=(last - first, groups),
        in_specs=specs,
        out_specs=pl.BlockSpec(memory_space=pltpu.HBM),
        out_shape=jax.ShapeDtypeStruct((adapters, wide, hidden), F32),
        scratch_shapes=[
            pltpu.VMEM((2, groups, group * wide // 2, tokens), BF16),
            pltpu.VMEM((SLOTS, group, wide, tile), F32),
            pltpu.SemaphoreType.DMA((SLOTS,)),
        ],
        input_output_aliases={} if start is None else {5: 0},
        compiler_params=params(20),
        cost_estimate=cost(2 * tokens * part, 4 * part),
    )(*operands)


def grad_a_kernel(columns, order, low, adapter, out, turned, mine, staged, sent):
    per = staged.shape[1]
    k = pl.program_id(0)

    @pl.when(k == 0)
    def _():
        turned[...] = columns[...].astype(F32).T.astype(BF16)
        mine[...] = dot(order[...], low[...])

    def copy_of(k):
        return pltpu.make_async_copy(
            staged.at[k % SLOTS], out.at[pl.ds(k * per, per)], sent.at[k % SLOTS]
        )

    def fill(slot):
        for j in range(per):
            kept = jnp.where(adapter[...] == k * per + j, mine[...], 0.0).astype(BF16)
            staged[slot, j] = dot(turned[...], kept)

    send(copy_of, k, out.shape[0] // per, fill)


def grad_a_of(columns, order, low, adapter, adapters):
    tokens, shard = columns.shape
    wide = low.shape[1]
    per = 4 if adapters % 4 == 0 else 1
    full = lambda shape: pl.BlockSpec(shape, lambda n: (0,) * len(shape))
    return pl.pallas_call(
        grad_a_kernel,
        grid=(adapters // per,),
        in_specs=[full(columns.shape), full(order.shape), full(low.shape), full(adapter.shape)],
        out_specs=pl.BlockSpec(memory_space=pltpu.HBM),
        out_shape=jax.ShapeDtypeStruct((adapters, shard, wide), F32),
        scratch_shapes=[
            pltpu.VMEM((shard, tokens), BF16),
            pltpu.VMEM((tokens, wide), F32),
            pltpu.VMEM((SLOTS, per, shard, wide), F32),
            pltpu.SemaphoreType.DMA((SLOTS,)),
        ],
        compiler_params=params(16),
        cost_estimate=cost(2 * tokens * shard * adapters * wide, 4 * shard * adapters * wide),
    )(columns, order, low, adapter)


def side_kernel(segments, adapters, places, order, low, seg, *rest):
    near, far = rest[-2:]
    half = near.shape[0]
    mine = dot(order[...], low[...])
    total = jnp.zeros((2 * half, near.shape[1]), F32)
    for s in range(segments):
        kept = jnp.where(seg[...] == s, mine, 0.0).astype(BF16)
        total = total + dot(kept, rest[s][0], ((1,), (1,)))
    near[...] = total[:half]
    far[...] = total[half:]


def side_of(order, low, seg, down, adapters, places):
    segments = adapters.shape[0]
    tokens = order.shape[0]
    shard = down.shape[1]
    full = lambda shape: pl.BlockSpec(shape, lambda *a: (0,) * len(shape))
    return pl.pallas_call(
        functools.partial(side_kernel, segments),
        grid_spec=pltpu.PrefetchScalarGridSpec(
            num_scalar_prefetch=2,
            grid=(1,),
            in_specs=[full(order.shape), full(low.shape), full(seg.shape)]
            + [of_segment(down.shape, s) for s in range(segments)],
            out_specs=[full((tokens // 2, shard))] * 2,
        ),
        out_shape=[jax.ShapeDtypeStruct((tokens // 2, shard), F32)] * 2,
        compiler_params=params(16),
        cost_estimate=cost(2 * tokens * down[0].size * segments, 2 * down[0].size * segments),
    )(adapters, places, order, low, seg, *([down] * segments))


def backward_kernel(count, first, frozen, dgate, dup, near, far, held, arrived):
    half = near.shape[0]
    block = held.shape[2]

    part = block // 2

    def fetch(k, slot):
        at = pl.multiple_of(first + k * block, block)
        return [
            pltpu.make_async_copy(
                frozen.at[i, pl.ds(at + h * part, part)],
                held.at[slot, i, pl.ds(h * part, part)],
                arrived.at[slot, i, h],
            )
            for h in range(2)
            for i in range(2)
        ]

    slot, copies = ring(fetch, pl.program_id(0), count)
    for h in range(2):
        rows = slice(h * part, (h + 1) * part)
        copies[2 * h].wait()
        term = dot(dgate[...], held[slot, 0, rows], ((1,), (1,)))
        copies[2 * h + 1].wait()
        term = term + dot(dup[...], held[slot, 1, rows], ((1,), (1,)))
        near[:, rows] = term[:half].astype(BF16)
        far[:, rows] = term[half:].astype(BF16)


def backward_chunk(frozen, dgate, dup, first, step):
    tokens, hidden = dgate.shape
    block = tile_of(step, 512)
    count = step // block
    full = lambda shape: pl.BlockSpec(shape, lambda k: (0, 0), pipeline_mode=ONCE)
    out = pl.BlockSpec((tokens // 2, block), lambda k: (0, k))
    return pl.pallas_call(
        functools.partial(backward_kernel, count, first),
        grid=(count,),
        in_specs=[pl.BlockSpec(memory_space=pltpu.HBM), full(dgate.shape), full(dup.shape)],
        out_specs=[out, out],
        out_shape=[jax.ShapeDtypeStruct((tokens // 2, step), BF16)] * 2,
        scratch_shapes=[
            pltpu.VMEM((DEPTH, 2, block, hidden), BF16),
            pltpu.SemaphoreType.DMA((DEPTH, 2, 2)),
        ],
        compiler_params=params(20),
        cost_estimate=cost(4 * tokens * step * hidden, 4 * step * hidden),
    )(frozen, dgate, dup)


def core_sum_kernel(base, at, near, far, side, side_far, *outs):
    total = near[...].astype(F32) + far[...].astype(F32)
    rows = outs[0].shape[0]
    own = at[0] == base + pl.program_id(0)

    def store(total):
        for s, out in enumerate(outs):
            out[...] = total[s * rows : (s + 1) * rows].astype(BF16)

    @pl.when(jnp.logical_not(own))
    def _():
        store(total)

    @pl.when(jnp.logical_and(own, at[1] == 0))
    def _():
        store(total + jnp.concatenate([side[...], side_far[...]], axis=1))

    @pl.when(jnp.logical_and(own, at[1] != 0))
    def _():
        store(total + jnp.concatenate([side_far[...], side[...]], axis=1))


def core_sum(near, far, side, side_far, at, first, slots):
    half, step = near.shape
    block = 2 * side.shape[1]
    full = lambda shape: pl.BlockSpec(shape, lambda *a: (0,) * len(shape))
    across = lambda rows: pl.BlockSpec((rows, block), lambda k, at: (0, k))
    return pl.pallas_call(
        functools.partial(core_sum_kernel, first // block),
        grid_spec=pltpu.PrefetchScalarGridSpec(
            num_scalar_prefetch=1,
            grid=(step // block,),
            in_specs=[across(half), across(half), full(side.shape), full(side_far.shape)],
            out_specs=[across(half // slots)] * slots,
        ),
        out_shape=[jax.ShapeDtypeStruct((half // slots, step), BF16)] * slots,
        compiler_params=params(16),
        cost_estimate=cost(2 * half * step, 6 * half * step),
    )(at, near, far, side, side_far)


def local(
    activations,
    dhidden,
    frozen,
    adapter_down_factors,
    adapter_up_factors,
    segment_adapter_index,
    segment_row_counts,
    ranks,
):
    adapter_list, shard_width, gate_and_up = adapter_down_factors.shape
    rank = gate_and_up // 2
    width = frozen.shape[1]
    rows = activations.shape[0]
    torus = Torus(width // shard_width)
    tokens = rows * torus.size
    a, b, c = torus.dims
    index = lax.axis_index("tensor")
    slots = torus.slot_devices(index)
    token = (slots[:, None] * rows + jnp.arange(rows, dtype=jnp.int32)[None, :]).reshape(-1)

    ends = jnp.cumsum(segment_row_counts[0])
    seg_adapter = segment_adapter_index[0]
    count = ends.shape[0]

    def segment_of(place):
        return jnp.sum((place[:, None] >= ends[None, :]).astype(jnp.int32), axis=1)

    def adapter_of(segment):
        match = segment[:, None] == jnp.arange(count, dtype=jnp.int32)[None, :]
        return jnp.sum(jnp.where(match, seg_adapter[None, :], 0), axis=1)

    column = jnp.arange(gate_and_up, dtype=jnp.int32) % rank
    chips = a * b
    core = index % c
    mine = (jnp.arange(chips, dtype=jnp.int32)[:, None] * c + core) * rows
    mine = (mine + jnp.arange(rows, dtype=jnp.int32)[None, :]).reshape(-1)
    my_adapter = adapter_of(segment_of(mine))
    hit = my_adapter[:, None] == jnp.arange(adapter_list, dtype=jnp.int32)[None, :]
    my_rank = jnp.sum(jnp.where(hit, ranks[None, :], 0), axis=1)[:, None]
    factor = jnp.where(column[None, :] < my_rank, 16.0 / my_rank.astype(F32), 0.0)

    places = (slots % c - core) % c * chips + slots // c
    spot = (places[:, None] * rows + jnp.arange(rows, dtype=jnp.int32)[None, :]).reshape(-1)
    count_up = jnp.arange(tokens, dtype=jnp.int32)[None, :]
    token_order = (token[:, None] == count_up).astype(BF16)
    order = (spot[:, None] == count_up).astype(BF16)

    segment = segment_of(token)
    adapter = adapter_of(segment)

    def whole_sum(partial, beside=()):
        if rows % 8:
            at = jnp.arange(torus.size, dtype=jnp.int32)
            device = at % chips * c + (core + at // chips) % c
            partial = jnp.take(
                partial.reshape(torus.size, rows, -1),
                jnp.take(torus.slots_of(index), device),
                axis=0,
            )
        x = torus.scatter_sum(partial.reshape(c, chips * rows, gate_and_up), 2)
        x = torus.exchange_sum(x, (1, 0), beside)
        return torus.gather((x * factor).astype(BF16), 2).reshape(tokens, gate_and_up)

    hidden = frozen.shape[2]
    tiles = hidden // tile_of(hidden, 256)
    chunks = []
    for share in OUTER_SHARES:
        first = sum(v.shape[1] for v in chunks)
        chunks.append(activations[:, first : first + width * share // sum(OUTER_SHARES)])
    outer = []
    for x in chunks:
        x = torus.gather(after(x, outer[-1]) if outer else x, 0)
        outer.append(x.reshape(a * rows, -1))
    parts = []
    for x, cuts in zip(outer, INNER_CUTS):
        step = x.shape[1] // cuts
        parts += [x[:, j * step : (j + 1) * step] for j in range(cuts)]
    base = None
    gathered = []
    first = 0
    for q, x in enumerate(parts):
        near = [x] + [torus.move(x, 1, -k) for k in range(1, b)]
        near[1:] = lax.optimization_barrier((*near[1:], base if q else outer[-1]))[:-1]
        far = [torus.move(v, 2, -1) for v in near]
        gathered.append([*near, *far])
        for cut in parts_of(tiles, 4 if q == len(parts) - 1 else 1):
            base = forward_chunk(gathered[q], frozen, base, first, cut)
        first += x.shape[1]

    columns, partial_in = low_in_partial(
        gathered, segment[:, None], adapter_down_factors, seg_adapter, places, index, rows
    )
    low_in = whole_sum(partial_in)
    dgate, dup, partial_out = middle(
        base, dhidden, token_order, order, low_in, segment[:, None], adapter_up_factors,
        seg_adapter, places, rows,
    )
    thirds = parts_of(tiles, 3)
    grad_b = []

    def grad_b_part(token):
        grad_b.append(
            grad_b_of(
                dgate, dup, order, after(low_in, token), adapter[None, :], adapter_list,
                grad_b[-1] if grad_b else None, thirds[len(grad_b)],
            )
        )
        return grad_b[-1]

    cuts = []
    for share in SUM_SHARES:
        cuts.append((sum(v[1] for v in cuts), width * share // sum(SUM_SHARES)))
    terms = []

    def first_term(token):
        terms.append(backward_chunk(frozen, after(dgate, token), dup, *cuts[0]))
        return terms[0][0]

    low_out = whole_sum(partial_out, [grad_b_part] * (len(thirds) - 1) + [first_term])
    near, far = terms[0][0], after(terms[0][1], low_out)
    side, side_far = side_of(
        order, low_out, segment[:, None], adapter_down_factors, seg_adapter, places
    )
    side_far = torus.move(side_far, 2, 1)
    at = jnp.stack([index // c, core]).astype(jnp.int32)
    sums, inners, inner_moves, outer_moves, blocks = [], [], [], [], []
    for q, (first, step) in enumerate(cuts):
        if q:
            near, far = backward_chunk(frozen, after(dgate, sums[-1][0]), dup, first, step)
            ahead = inner_moves[q - 1] + (outer_moves[q - 2] if q > 1 else [])
            far = lax.optimization_barrier((far, *ahead))[0]
        far = torus.move(far, 2, 1)
        sums.append(core_sum(near, far, side, side_far, at, first, b))
        inner_moves.append([torus.move(sums[q][k], 1, k) for k in range(1, b)])
        total = sums[q][0].astype(F32)
        for v in inner_moves[q]:
            total = total + v.astype(F32)
        inners.append(total.astype(BF16).reshape(a, rows, step))
        outer_moves.append([torus.move(inners[q][k], 0, k) for k in range(1, a)])
    grad_b = grad_b_part(inner_moves[-1][0])
    for q, inner in enumerate(inners):
        total = inner[0].astype(F32)
        for v in outer_moves[q]:
            behind = (v, *inner_moves[-1], grad_b)
            v = lax.optimization_barrier(behind)[0] if q < len(cuts) - 1 else v
            total = total + v.astype(F32)
        blocks.append(total.astype(BF16))
    dinput = jnp.concatenate(blocks, axis=1)
    grad_a = grad_a_of(
        columns, order, after(low_out, sums[-1][0]), adapter[:, None], adapter_list
    )
    return (dinput, grad_a, grad_b)


def solution(mesh):
    placed = (
        P(("groups", "tensor"), None),
        P("groups", "tensor"),
        P(None, None, "tensor"),
        P(None, "tensor", None),
        P(None, None, "tensor"),
        P("groups", None),
        P("groups", None),
        P(),
    )
    return jax.shard_map(
        local,
        mesh=mesh,
        in_specs=placed,
        out_specs=(
            P(("groups", "tensor"), None),
            P("groups", "tensor", None),
            P("groups", None, "tensor"),
        ),
        check_vma=False,
    )
```

```python
import functools

import jax
import jax.numpy as jnp
from jax import lax
from jax.experimental import pallas as pl
from jax.experimental.pallas import tpu as pltpu
from jax.sharding import PartitionSpec as P

OUTER_SHARES = (3, 5)
INNER_CUTS = (1, 2)
SUM_SHARES = (4, 4)
MIB = 1024 * 1024
BF16 = jnp.bfloat16
DEPTH = 3
SLOTS = 4
ONCE = pl.Buffered(1)
F32 = jnp.float32


def dot(left, right, dims=((1,), (0,))):
    return lax.dot_general(left, right, (dims, ((), ())), preferred_element_type=F32)


def params(mib):
    return pltpu.CompilerParams(vmem_limit_bytes=mib * MIB)


def cost(flops, moved):
    return pl.CostEstimate(flops=int(flops), bytes_accessed=int(moved), transcendentals=0)


def tile_of(size, most):
    return most if size % most == 0 else size


def parts_of(count, parts):
    parts = min(parts, count)
    ends = [count * k // parts for k in range(parts + 1)]
    return list(zip(ends[:-1], ends[1:]))


def after(x, other):
    return lax.optimization_barrier((x, other))[0]


class Torus:
    def __init__(self, size):
        core = 2 if size % 2 == 0 else 1
        chips = size // core
        inner = 1
        while inner * 2 * inner * 2 <= chips and chips % (inner * 2) == 0:
            inner *= 2
        self.size = size
        self.dims = (chips // inner, inner, core)
        self.strides = (inner * core, core, 1)

    def place(self, index):
        return [index // s % n for s, n in zip(self.strides, self.dims)]

    def shifted(self, index, dim, by):
        at = index // self.strides[dim] % self.dims[dim]
        return index + ((at + by) % self.dims[dim] - at) * self.strides[dim]

    def move(self, x, dim, by):
        pairs = [(i, self.shifted(i, dim, by)) for i in range(self.size)]
        return lax.ppermute(x, "tensor", pairs)

    def gather(self, x, dim):
        return jnp.stack([x] + [self.move(x, dim, -k) for k in range(1, self.dims[dim])])

    def scatter_sum(self, x, dim):
        total = x[0].astype(F32)
        for k in range(1, self.dims[dim]):
            total = total + self.move(x[k], dim, k).astype(F32)
        return total

    def slot_devices(self, index):
        outer, inner, core = self.place(index)
        a, b, c = self.dims
        cs = lax.broadcasted_iota(jnp.int32, (c, b, a), 0)
        bs = lax.broadcasted_iota(jnp.int32, (c, b, a), 1)
        zs = lax.broadcasted_iota(jnp.int32, (c, b, a), 2)
        return (((outer + zs) % a * b + (inner + bs) % b) * c + (core + cs) % c).reshape(-1)

    def exchange_sum(self, x, dims, beside):
        beside = list(beside)
        for dim in dims:
            k = 1
            while k < self.dims[dim]:
                stride = self.strides[dim]
                pairs = [(i, i + ((i // stride ^ k) - i // stride) * stride) for i in range(self.size)]
                done = beside.pop(0)(x) if beside else None
                x = x + lax.ppermute(x, "tensor", pairs)
                x = x if done is None else after(x, done)
                k *= 2
        return x

    def slots_of(self, index):
        outer, inner, core = self.place(index)
        a, b, c = self.dims
        zs = lax.broadcasted_iota(jnp.int32, (a, b, c), 0)
        bs = lax.broadcasted_iota(jnp.int32, (a, b, c), 1)
        cs = lax.broadcasted_iota(jnp.int32, (a, b, c), 2)
        return (((cs - core) % c * b + (bs - inner) % b) * a + (zs - outer) % a).reshape(-1)


def tile_at(ref, n, tile):
    if ref.shape[1] == tile:
        return ref
    return ref.at[:, pl.ds(pl.multiple_of(n * tile, tile), tile)]


def ring(fetch, k, count):
    @pl.when(k == 0)
    def _():
        for j in range(min(DEPTH - 1, count)):
            for copy in fetch(j, j):
                copy.start()

    @pl.when(k + DEPTH - 1 < count)
    def _():
        for copy in fetch(k + DEPTH - 1, (k + DEPTH - 1) % DEPTH):
            copy.start()

    for copy in fetch(k, k % DEPTH):
        copy.wait()
    return k % DEPTH


def send(copy_of, k, count, fill):
    @pl.when(k >= SLOTS)
    def _():
        copy_of(k - SLOTS).wait()

    fill(k % SLOTS)
    copy_of(k).start()

    @pl.when(k == count - 1)
    def _():
        for j in range(min(SLOTS, count)):
            copy_of(k - j).wait()


def forward_kernel(pieces, low, count, first, *rest):
    parts, frozen, rest = rest[:pieces], rest[pieces], rest[pieces + 1 :]
    out, held, arrived = rest[-3:]
    step, tile = held.shape[2:]

    def fetch(n, slot):
        return [
            pltpu.make_async_copy(
                tile_at(frozen.at[i, pl.ds(first, step)], low + n, tile),
                held.at[slot, i],
                arrived.at[slot, i],
            )
            for i in range(2)
        ]

    slot = ring(fetch, pl.program_id(0), count)
    x = jnp.concatenate([v[...] for v in parts], axis=0)
    for i in range(2):
        part = dot(x, held[slot, i])
        out[i] = part if len(rest) == 3 else rest[0][i] + part


def forward_chunk(pieces, frozen, start, first, tiles):
    step = pieces[0].shape[1]
    tokens = sum(v.shape[0] for v in pieces)
    hidden = frozen.shape[2]
    tile = tile_of(hidden, 256)
    low, high = tiles
    across = pl.BlockSpec((2, tokens, tile), lambda n: (0, 0, low + n))
    operands = [*pieces, frozen]
    specs = [pl.BlockSpec(v.shape, lambda n: (0, 0), pipeline_mode=ONCE) for v in pieces]
    specs.append(pl.BlockSpec(memory_space=pltpu.HBM))
    if start is not None:
        operands.append(start)
        specs.append(across)
    count = high - low
    return pl.pallas_call(
        functools.partial(forward_kernel, len(pieces), low, count, first),
        grid=(count,),
        in_specs=specs,
        out_specs=across,
        out_shape=jax.ShapeDtypeStruct((2, tokens, hidden), F32),
        scratch_shapes=[
            pltpu.VMEM((DEPTH, 2, step, tile), BF16),
            pltpu.SemaphoreType.DMA((DEPTH, 2)),
        ],
        input_output_aliases={} if start is None else {len(operands) - 1: 0},
        compiler_params=params(24),
        cost_estimate=cost(4 * tokens * step * tile * count, 4 * step * tile * count),
    )(*operands)


def low_in_kernel(segments, chunks, rows, adapters, places, which, seg, *rest):
    factors, rest = rest[:segments], rest[segments:]
    cuts, (columns, out) = rest[:-2], rest[-2:]
    pieces = len(cuts) // chunks
    for q in range(chunks):

        @pl.when(which[0] == q)
        def _():
            first = 0
            for v in cuts[q * pieces : (q + 1) * pieces]:
                columns[first : first + v.shape[0]] = v[...]
                first += v.shape[0]

    total = jnp.zeros(out.shape, F32)
    for s in range(segments):
        part = dot(columns[...], factors[s][0])
        total = total + jnp.where(seg[...] == s, part, 0.0)
    put_rows(out, total, places, rows)


def put_rows(out, total, places, rows):
    if rows % 8:
        out[...] = total
        return
    for s in range(total.shape[0] // rows):
        out[pl.ds(pl.multiple_of(places[s] * rows, rows), rows), :] = total[s * rows : (s + 1) * rows]


def of_segment(shape, s):
    return pl.BlockSpec((1,) + shape[1:], lambda *a: (a[-2][s], 0, 0))


def low_in_partial(chunks, seg, down, adapters, places, index, rows):
    segments = adapters.shape[0]
    shard, wide = down.shape[1:]
    tokens = seg.shape[0]
    if shard % 128:
        joined = [jnp.concatenate(piece, axis=1) for piece in zip(*chunks)]
        chunks = [[lax.dynamic_slice_in_dim(v, index * shard, shard, 1) for v in joined]]
        which = jnp.zeros((1,), jnp.int32)
        cuts = [pl.BlockSpec(v.shape, lambda *a: (0, 0)) for v in chunks[0]]
    else:
        inside, at, cuts, first = [], [], [], 0
        for q, pieces in enumerate(chunks):
            per = pieces[0].shape[1] // shard
            inside.append(index >= first)
            at.append(jnp.clip(index - first, 0, per - 1))
            cuts += [
                pl.BlockSpec((v.shape[0], shard), lambda i, a, p, w, q=q: (0, w[1 + q])) for v in pieces
            ]
            first += per
        which = jnp.stack([sum(v.astype(jnp.int32) for v in inside) - 1] + at).astype(jnp.int32)
    full = lambda shape: pl.BlockSpec(shape, lambda *a: (0,) * len(shape))
    factor = lambda s: pl.BlockSpec((1, shard, wide), lambda i, a, p, w: (a[s], 0, 0))
    return pl.pallas_call(
        functools.partial(low_in_kernel, segments, len(chunks), rows),
        grid_spec=pltpu.PrefetchScalarGridSpec(
            num_scalar_prefetch=3,
            grid=(1,),
            in_specs=[full(seg.shape)] + [factor(s) for s in range(segments)] + cuts,
            out_specs=[full((tokens, shard)), full((tokens, wide))],
        ),
        out_shape=[
            jax.ShapeDtypeStruct((tokens, shard), BF16),
            jax.ShapeDtypeStruct((tokens, wide), F32),
        ],
        compiler_params=params(16),
        cost_estimate=cost(2 * tokens * down[0].size * segments, 2 * down[0].size * segments),
    )(adapters, places, which, seg, *([down] * segments), *[v for pieces in chunks for v in pieces])


def middle_kernel(rows, adapters, places, base, dhidden, token_order, order, low, seg, up, *rest):
    dgate, dup, out, left, back, factors, arrived = rest
    segments, wide, tile = factors.shape[1:]
    rank = wide // 2
    tokens = order.shape[0]
    n = pl.program_id(0)
    slot = n % 2
    lane = lax.broadcasted_iota(jnp.int32, (tokens, segments * rank), 1) // rank
    mask = lane == seg[...]

    def fetch(n, slot, s):
        return pltpu.make_async_copy(
            tile_at(up.at[adapters[s]], n, tile), factors.at[slot, s], arrived.at[slot, s]
        )

    @pl.when(n == 0)
    def _():
        for s in range(segments):
            fetch(0, 0, s).start()
        mine = dot(order[...], low[...])
        for i in range(2):
            block = jnp.concatenate([mine[:, i * rank : (i + 1) * rank]] * segments, axis=1)
            left[i] = jnp.where(mask, block, 0.0).astype(BF16)
        back[...] = jnp.zeros_like(back)

    @pl.when(n + 1 < pl.num_programs(0))
    def _():
        for s in range(segments):
            fetch(n + 1, 1 - slot, s).start()

    for s in range(segments):
        fetch(n, slot, s).wait()
    up_g = jnp.concatenate([factors[slot, s, :rank] for s in range(segments)], axis=0)
    up_u = jnp.concatenate([factors[slot, s, rank:] for s in range(segments)], axis=0)
    gate = base[0] + dot(left[0], up_g)
    up_sum = base[1] + dot(left[1], up_u)
    grad = dot(token_order[...], dhidden[...])
    sigma = 1.0 / (1.0 + jnp.exp(-gate))
    g = (grad * up_sum * sigma * (1.0 + gate * (1.0 - sigma))).astype(BF16)
    u = (grad * gate * sigma).astype(BF16)
    dgate[...] = g
    dup[...] = u
    back[0] += dot(g, up_g, ((1,), (1,)))
    back[1] += dot(u, up_u, ((1,), (1,)))

    @pl.when(n == pl.num_programs(0) - 1)
    def _():
        parts = []
        for i in range(2):
            kept = jnp.where(mask, back[i], 0.0)
            parts.append(sum(kept[:, s * rank : (s + 1) * rank] for s in range(segments)))
        put_rows(out, jnp.concatenate(parts, axis=1), places, rows)


def middle(base, dhidden, token_order, order, low, seg, up, adapters, places, rows):
    segments = adapters.shape[0]
    tokens, hidden = dhidden.shape
    wide = up.shape[1]
    tile = tile_of(hidden, 256)
    full = lambda shape: pl.BlockSpec(shape, lambda *a: (0,) * len(shape))
    across = lambda lead: pl.BlockSpec(lead + (tokens, tile), lambda n, *a: (0,) * len(lead) + (0, n))
    return pl.pallas_call(
        functools.partial(middle_kernel, rows),
        grid_spec=pltpu.PrefetchScalarGridSpec(
            num_scalar_prefetch=2,
            grid=(hidden // tile,),
            in_specs=[across((2,)), across(())]
            + [full(v.shape) for v in (token_order, order, low, seg)]
            + [pl.BlockSpec(memory_space=pltpu.HBM)],
            out_specs=[across(()), across(()), full((tokens, wide))],
            scratch_shapes=[
                pltpu.VMEM((2, tokens, segments * wide // 2), BF16),
                pltpu.VMEM((2, tokens, segments * wide // 2), F32),
                pltpu.VMEM((2, segments, wide, tile), BF16),
                pltpu.SemaphoreType.DMA((2, segments)),
            ],
        ),
        out_shape=[
            jax.ShapeDtypeStruct((tokens, hidden), BF16),
            jax.ShapeDtypeStruct((tokens, hidden), BF16),
            jax.ShapeDtypeStruct((tokens, wide), F32),
        ],
        compiler_params=params(20),
        cost_estimate=cost(
            4 * tokens * hidden * segments * wide, hidden * (tokens * 14 + segments * wide * 2)
        ),
    )(adapters, places, base, dhidden, token_order, order, low, seg, up)


def grad_b_kernel(first, count, dgate, dup, order, low, adapter, *rest):
    out, left, staged, sent = rest[-4:]
    group, wide, tile = staged.shape[1:]
    groups = left.shape[1]
    rank = wide // 2
    g = pl.program_id(1)
    k = pl.program_id(0) * groups + g

    @pl.when(k == 0)
    def _():
        turned = dot(order[...], low[...]).T
        for a in range(groups * group):
            kept = jnp.where(adapter[...] == a, turned, 0.0).astype(BF16)
            at = (a // group, slice(a % group * rank, (a % group + 1) * rank))
            left[(0, *at)] = kept[:rank]
            left[(1, *at)] = kept[rank:]

    def copy_of(k):
        block = out.at[pl.ds(k % groups * group, group)]
        if out.shape[2] != tile:
            at = pl.multiple_of((first + k // groups) * tile, tile)
            block = block.at[:, :, pl.ds(at, tile)]
        return pltpu.make_async_copy(staged.at[k % SLOTS], block, sent.at[k % SLOTS])

    def fill(slot):
        for i, grad in enumerate((dgate, dup)):
            part = dot(left[i, g], grad[...])
            staged[slot, :, i * rank : (i + 1) * rank, :] = part.reshape(group, rank, tile)

    send(copy_of, k, count * groups, fill)


def grad_b_of(dgate, dup, order, low, adapter_row, adapters, start, tiles):
    tokens, hidden = dgate.shape
    wide = low.shape[1]
    tile = tile_of(hidden, 256)
    first, last = tiles
    groups = 2 if adapters % 2 == 0 else 1
    group = adapters // groups
    full = lambda shape: pl.BlockSpec(shape, lambda n, g: (0,) * len(shape))
    across = pl.BlockSpec((tokens, tile), lambda n, g: (0, first + n))
    operands = [dgate, dup, order, low, adapter_row]
    specs = [across, across, full(order.shape), full(low.shape), full(adapter_row.shape)]
    if start is not None:
        operands.append(start)
        specs.append(pl.BlockSpec(memory_space=pltpu.HBM))
    part = tile * (last - first) * adapters * wide
    return pl.pallas_call(
        functools.partial(grad_b_kernel, first, last - first),
        grid=(last - first, groups),
        in_specs=specs,
        out_specs=pl.BlockSpec(memory_space=pltpu.HBM),
        out_shape=jax.ShapeDtypeStruct((adapters, wide, hidden), F32),
        scratch_shapes=[
            pltpu.VMEM((2, groups, group * wide // 2, tokens), BF16),
            pltpu.VMEM((SLOTS, group, wide, tile), F32),
            pltpu.SemaphoreType.DMA((SLOTS,)),
        ],
        input_output_aliases={} if start is None else {5: 0},
        compiler_params=params(20),
        cost_estimate=cost(2 * tokens * part, 4 * part),
    )(*operands)


def grad_a_kernel(columns, order, low, adapter, out, turned, mine, staged, sent):
    per = staged.shape[1]
    k = pl.program_id(0)

    @pl.when(k == 0)
    def _():
        turned[...] = columns[...].astype(F32).T.astype(BF16)
        mine[...] = dot(order[...], low[...])

    def copy_of(k):
        return pltpu.make_async_copy(
            staged.at[k % SLOTS], out.at[pl.ds(k * per, per)], sent.at[k % SLOTS]
        )

    def fill(slot):
        for j in range(per):
            kept = jnp.where(adapter[...] == k * per + j, mine[...], 0.0).astype(BF16)
            staged[slot, j] = dot(turned[...], kept)

    send(copy_of, k, out.shape[0] // per, fill)


def grad_a_of(columns, order, low, adapter, adapters):
    tokens, shard = columns.shape
    wide = low.shape[1]
    per = 4 if adapters % 4 == 0 else 1
    full = lambda shape: pl.BlockSpec(shape, lambda n: (0,) * len(shape))
    return pl.pallas_call(
        grad_a_kernel,
        grid=(adapters // per,),
        in_specs=[full(columns.shape), full(order.shape), full(low.shape), full(adapter.shape)],
        out_specs=pl.BlockSpec(memory_space=pltpu.HBM),
        out_shape=jax.ShapeDtypeStruct((adapters, shard, wide), F32),
        scratch_shapes=[
            pltpu.VMEM((shard, tokens), BF16),
            pltpu.VMEM((tokens, wide), F32),
            pltpu.VMEM((SLOTS, per, shard, wide), F32),
            pltpu.SemaphoreType.DMA((SLOTS,)),
        ],
        compiler_params=params(16),
        cost_estimate=cost(2 * tokens * shard * adapters * wide, 4 * shard * adapters * wide),
    )(columns, order, low, adapter)


def side_kernel(segments, adapters, places, order, low, seg, *rest):
    near, far = rest[-2:]
    half = near.shape[0]
    mine = dot(order[...], low[...])
    total = jnp.zeros((2 * half, near.shape[1]), F32)
    for s in range(segments):
        kept = jnp.where(seg[...] == s, mine, 0.0).astype(BF16)
        total = total + dot(kept, rest[s][0], ((1,), (1,)))
    near[...] = total[:half]
    far[...] = total[half:]


def side_of(order, low, seg, down, adapters, places):
    segments = adapters.shape[0]
    tokens = order.shape[0]
    shard = down.shape[1]
    full = lambda shape: pl.BlockSpec(shape, lambda *a: (0,) * len(shape))
    return pl.pallas_call(
        functools.partial(side_kernel, segments),
        grid_spec=pltpu.PrefetchScalarGridSpec(
            num_scalar_prefetch=2,
            grid=(1,),
            in_specs=[full(order.shape), full(low.shape), full(seg.shape)]
            + [of_segment(down.shape, s) for s in range(segments)],
            out_specs=[full((tokens // 2, shard))] * 2,
        ),
        out_shape=[jax.ShapeDtypeStruct((tokens // 2, shard), F32)] * 2,
        compiler_params=params(16),
        cost_estimate=cost(2 * tokens * down[0].size * segments, 2 * down[0].size * segments),
    )(adapters, places, order, low, seg, *([down] * segments))


def backward_kernel(count, first, frozen, dgate, dup, near, far, held, arrived):
    half = near.shape[0]
    block = held.shape[2]

    def fetch(k, slot):
        rows = pl.ds(pl.multiple_of(first + k * block, block), block)
        return [
            pltpu.make_async_copy(frozen.at[i, rows, :], held.at[slot, i], arrived.at[slot, i])
            for i in range(2)
        ]

    slot = ring(fetch, pl.program_id(0), count)
    term = dot(dgate[...], held[slot, 0], ((1,), (1,))) + dot(dup[...], held[slot, 1], ((1,), (1,)))
    near[...] = term[:half].astype(BF16)
    far[...] = term[half:].astype(BF16)


def backward_chunk(frozen, dgate, dup, first, step):
    tokens, hidden = dgate.shape
    block = tile_of(step, 512)
    count = step // block
    full = lambda shape: pl.BlockSpec(shape, lambda k: (0, 0), pipeline_mode=ONCE)
    out = pl.BlockSpec((tokens // 2, block), lambda k: (0, k))
    return pl.pallas_call(
        functools.partial(backward_kernel, count, first),
        grid=(count,),
        in_specs=[pl.BlockSpec(memory_space=pltpu.HBM), full(dgate.shape), full(dup.shape)],
        out_specs=[out, out],
        out_shape=[jax.ShapeDtypeStruct((tokens // 2, step), BF16)] * 2,
        scratch_shapes=[
            pltpu.VMEM((DEPTH, 2, block, hidden), BF16),
            pltpu.SemaphoreType.DMA((DEPTH, 2)),
        ],
        compiler_params=params(20),
        cost_estimate=cost(4 * tokens * step * hidden, 4 * step * hidden),
    )(frozen, dgate, dup)


def core_sum_kernel(base, at, near, far, side, side_far, *outs):
    total = near[...].astype(F32) + far[...].astype(F32)
    rows = outs[0].shape[0]
    own = at[0] == base + pl.program_id(0)

    def store(total):
        for s, out in enumerate(outs):
            out[...] = total[s * rows : (s + 1) * rows].astype(BF16)

    @pl.when(jnp.logical_not(own))
    def _():
        store(total)

    @pl.when(jnp.logical_and(own, at[1] == 0))
    def _():
        store(total + jnp.concatenate([side[...], side_far[...]], axis=1))

    @pl.when(jnp.logical_and(own, at[1] != 0))
    def _():
        store(total + jnp.concatenate([side_far[...], side[...]], axis=1))


def core_sum(near, far, side, side_far, at, first, slots):
    half, step = near.shape
    block = 2 * side.shape[1]
    full = lambda shape: pl.BlockSpec(shape, lambda *a: (0,) * len(shape))
    across = lambda rows: pl.BlockSpec((rows, block), lambda k, at: (0, k))
    return pl.pallas_call(
        functools.partial(core_sum_kernel, first // block),
        grid_spec=pltpu.PrefetchScalarGridSpec(
            num_scalar_prefetch=1,
            grid=(step // block,),
            in_specs=[across(half), across(half), full(side.shape), full(side_far.shape)],
            out_specs=[across(half // slots)] * slots,
        ),
        out_shape=[jax.ShapeDtypeStruct((half // slots, step), BF16)] * slots,
        compiler_params=params(16),
        cost_estimate=cost(2 * half * step, 6 * half * step),
    )(at, near, far, side, side_far)


def local(
    activations,
    dhidden,
    frozen,
    adapter_down_factors,
    adapter_up_factors,
    segment_adapter_index,
    segment_row_counts,
    ranks,
):
    adapter_list, shard_width, gate_and_up = adapter_down_factors.shape
    rank = gate_and_up // 2
    width = frozen.shape[1]
    rows = activations.shape[0]
    torus = Torus(width // shard_width)
    tokens = rows * torus.size
    a, b, c = torus.dims
    index = lax.axis_index("tensor")
    slots = torus.slot_devices(index)
    token = (slots[:, None] * rows + jnp.arange(rows, dtype=jnp.int32)[None, :]).reshape(-1)

    ends = jnp.cumsum(segment_row_counts[0])
    seg_adapter = segment_adapter_index[0]
    count = ends.shape[0]

    def segment_of(place):
        return jnp.sum((place[:, None] >= ends[None, :]).astype(jnp.int32), axis=1)

    def adapter_of(segment):
        match = segment[:, None] == jnp.arange(count, dtype=jnp.int32)[None, :]
        return jnp.sum(jnp.where(match, seg_adapter[None, :], 0), axis=1)

    column = jnp.arange(gate_and_up, dtype=jnp.int32) % rank
    chips = a * b
    core = index % c
    mine = (jnp.arange(chips, dtype=jnp.int32)[:, None] * c + core) * rows
    mine = (mine + jnp.arange(rows, dtype=jnp.int32)[None, :]).reshape(-1)
    my_adapter = adapter_of(segment_of(mine))
    hit = my_adapter[:, None] == jnp.arange(adapter_list, dtype=jnp.int32)[None, :]
    my_rank = jnp.sum(jnp.where(hit, ranks[None, :], 0), axis=1)[:, None]
    factor = jnp.where(column[None, :] < my_rank, 16.0 / my_rank.astype(F32), 0.0)

    places = (slots % c - core) % c * chips + slots // c
    spot = (places[:, None] * rows + jnp.arange(rows, dtype=jnp.int32)[None, :]).reshape(-1)
    count_up = jnp.arange(tokens, dtype=jnp.int32)[None, :]
    token_order = (token[:, None] == count_up).astype(BF16)
    order = (spot[:, None] == count_up).astype(BF16)

    segment = segment_of(token)
    adapter = adapter_of(segment)

    def whole_sum(partial, beside=()):
        if rows % 8:
            at = jnp.arange(torus.size, dtype=jnp.int32)
            device = at % chips * c + (core + at // chips) % c
            partial = jnp.take(
                partial.reshape(torus.size, rows, -1),
                jnp.take(torus.slots_of(index), device),
                axis=0,
            )
        x = torus.scatter_sum(partial.reshape(c, chips * rows, gate_and_up), 2)
        x = torus.exchange_sum(x, (1, 0), beside)
        return torus.gather((x * factor).astype(BF16), 2).reshape(tokens, gate_and_up)

    hidden = frozen.shape[2]
    tiles = hidden // tile_of(hidden, 256)
    chunks = []
    for share in OUTER_SHARES:
        first = sum(v.shape[1] for v in chunks)
        chunks.append(activations[:, first : first + width * share // sum(OUTER_SHARES)])
    outer = []
    for x in chunks:
        x = torus.gather(after(x, outer[-1]) if outer else x, 0)
        outer.append(x.reshape(a * rows, -1))
    parts = []
    for x, cuts in zip(outer, INNER_CUTS):
        step = x.shape[1] // cuts
        parts += [x[:, j * step : (j + 1) * step] for j in range(cuts)]
    base = None
    gathered = []
    first = 0
    for q, x in enumerate(parts):
        near = [x] + [torus.move(x, 1, -k) for k in range(1, b)]
        near[1:] = lax.optimization_barrier((*near[1:], base if q else outer[-1]))[:-1]
        far = [torus.move(v, 2, -1) for v in near]
        gathered.append([*near, *far])
        for cut in parts_of(tiles, 2 if q == len(parts) - 1 else 1):
            base = forward_chunk(gathered[q], frozen, base, first, cut)
        first += x.shape[1]

    columns, partial_in = low_in_partial(
        gathered, segment[:, None], adapter_down_factors, seg_adapter, places, index, rows
    )
    low_in = whole_sum(partial_in)
    dgate, dup, partial_out = middle(
        base, dhidden, token_order, order, low_in, segment[:, None], adapter_up_factors,
        seg_adapter, places, rows,
    )
    thirds = parts_of(tiles, 3)
    grad_b = []

    def grad_b_part(token):
        grad_b.append(
            grad_b_of(
                dgate, dup, order, after(low_in, token), adapter[None, :], adapter_list,
                grad_b[-1] if grad_b else None, thirds[len(grad_b)],
            )
        )
        return grad_b[-1]

    cuts = []
    for share in SUM_SHARES:
        cuts.append((sum(v[1] for v in cuts), width * share // sum(SUM_SHARES)))
    terms = []

    def first_term(token):
        terms.append(backward_chunk(frozen, after(dgate, token), dup, *cuts[0]))
        return terms[0][0]

    low_out = whole_sum(partial_out, [grad_b_part] * (len(thirds) - 1) + [first_term])
    near, far = terms[0][0], after(terms[0][1], low_out)
    side, side_far = side_of(
        order, low_out, segment[:, None], adapter_down_factors, seg_adapter, places
    )
    side_far = torus.move(side_far, 2, 1)
    at = jnp.stack([index // c, core]).astype(jnp.int32)
    sums, inners, inner_moves, outer_moves, blocks = [], [], [], [], []
    for q, (first, step) in enumerate(cuts):
        if q:
            near, far = backward_chunk(frozen, after(dgate, sums[-1][0]), dup, first, step)
            ahead = inner_moves[q - 1] + (outer_moves[q - 2] if q > 1 else [])
            far = lax.optimization_barrier((far, *ahead))[0]
        far = torus.move(far, 2, 1)
        sums.append(core_sum(near, far, side, side_far, at, first, b))
        inner_moves.append([torus.move(sums[q][k], 1, k) for k in range(1, b)])
        total = sums[q][0].astype(F32)
        for v in inner_moves[q]:
            total = total + v.astype(F32)
        inners.append(total.astype(BF16).reshape(a, rows, step))
        outer_moves.append([torus.move(inners[q][k], 0, k) for k in range(1, a)])
    grad_b = grad_b_part(sums[-1][0])
    for q, inner in enumerate(inners):
        total = inner[0].astype(F32)
        for v in outer_moves[q]:
            behind = (v, *inner_moves[-1], grad_b)
            v = lax.optimization_barrier(behind)[0] if q < len(cuts) - 1 else v
            total = total + v.astype(F32)
        blocks.append(total.astype(BF16))
    dinput = jnp.concatenate(blocks, axis=1)
    grad_a = grad_a_of(
        columns, order, after(low_out, sums[-1][0]), adapter[:, None], adapter_list
    )
    return (dinput, grad_a, grad_b)


def solution(mesh):
    placed = (
        P(("groups", "tensor"), None),
        P("groups", "tensor"),
        P(None, None, "tensor"),
        P(None, "tensor", None),
        P(None, None, "tensor"),
        P("groups", None),
        P("groups", None),
        P(),
    )
    return jax.shard_map(
        local,
        mesh=mesh,
        in_specs=placed,
        out_specs=(
            P(("groups", "tensor"), None),
            P("groups", "tensor", None),
            P("groups", None, "tensor"),
        ),
        check_vma=False,
    )
```

```python
import functools

import jax
import jax.numpy as jnp
from jax import lax
from jax.experimental import pallas as pl
from jax.experimental.pallas import tpu as pltpu
from jax.sharding import PartitionSpec as P

SUM_SHARES = (4, 4)
MIB = 1024 * 1024
BF16 = jnp.bfloat16
DEPTH = 3
SLOTS = 4
ONCE = pl.Buffered(1)
F32 = jnp.float32


def dot(left, right, dims=((1,), (0,))):
    return lax.dot_general(left, right, (dims, ((), ())), preferred_element_type=F32)


def params(mib):
    return pltpu.CompilerParams(vmem_limit_bytes=mib * MIB)


def cost(flops, moved):
    return pl.CostEstimate(flops=int(flops), bytes_accessed=int(moved), transcendentals=0)


def tile_of(size, most):
    return most if size % most == 0 else size


def parts_of(count, parts):
    parts = min(parts, count)
    ends = [count * k // parts for k in range(parts + 1)]
    return list(zip(ends[:-1], ends[1:]))


def after(x, other):
    return lax.optimization_barrier((x, other))[0]


class Torus:
    def __init__(self, size):
        core = 2 if size % 2 == 0 else 1
        chips = size // core
        inner = 1
        while inner * 2 * inner * 2 <= chips and chips % (inner * 2) == 0:
            inner *= 2
        self.size = size
        self.dims = (chips // inner, inner, core)
        self.strides = (inner * core, core, 1)

    def place(self, index):
        return [index // s % n for s, n in zip(self.strides, self.dims)]

    def shifted(self, index, dim, by):
        at = index // self.strides[dim] % self.dims[dim]
        return index + ((at + by) % self.dims[dim] - at) * self.strides[dim]

    def move(self, x, dim, by):
        pairs = [(i, self.shifted(i, dim, by)) for i in range(self.size)]
        return lax.ppermute(x, "tensor", pairs)

    def gather(self, x, dim):
        return jnp.stack([x] + [self.move(x, dim, -k) for k in range(1, self.dims[dim])])

    def scatter_sum(self, x, dim):
        total = x[0].astype(F32)
        for k in range(1, self.dims[dim]):
            total = total + self.move(x[k], dim, k).astype(F32)
        return total

    def slot_devices(self, index):
        outer, inner, core = self.place(index)
        a, b, c = self.dims
        cs = lax.broadcasted_iota(jnp.int32, (c, b, a), 0)
        bs = lax.broadcasted_iota(jnp.int32, (c, b, a), 1)
        zs = lax.broadcasted_iota(jnp.int32, (c, b, a), 2)
        return (((outer + zs) % a * b + (inner + bs) % b) * c + (core + cs) % c).reshape(-1)

    def exchange_sum(self, x, dims, beside):
        beside = list(beside)
        for dim in dims:
            k = 1
            while k < self.dims[dim]:
                stride = self.strides[dim]
                pairs = [(i, i + ((i // stride ^ k) - i // stride) * stride) for i in range(self.size)]
                done = beside.pop(0)(x) if beside else None
                x = x + lax.ppermute(x, "tensor", pairs)
                x = x if done is None else after(x, done)
                k *= 2
        return x

    def slots_of(self, index):
        outer, inner, core = self.place(index)
        a, b, c = self.dims
        zs = lax.broadcasted_iota(jnp.int32, (a, b, c), 0)
        bs = lax.broadcasted_iota(jnp.int32, (a, b, c), 1)
        cs = lax.broadcasted_iota(jnp.int32, (a, b, c), 2)
        return (((cs - core) % c * b + (bs - inner) % b) * a + (zs - outer) % a).reshape(-1)


def tile_at(ref, n, tile):
    if ref.shape[1] == tile:
        return ref
    return ref.at[:, pl.ds(pl.multiple_of(n * tile, tile), tile)]


def ring(fetch, k, count):
    @pl.when(k == 0)
    def _():
        for j in range(min(DEPTH - 1, count)):
            for copy in fetch(j, j):
                copy.start()

    @pl.when(k + DEPTH - 1 < count)
    def _():
        for copy in fetch(k + DEPTH - 1, (k + DEPTH - 1) % DEPTH):
            copy.start()

    for copy in fetch(k, k % DEPTH):
        copy.wait()
    return k % DEPTH


def send(copy_of, k, count, fill):
    @pl.when(k >= SLOTS)
    def _():
        copy_of(k - SLOTS).wait()

    fill(k % SLOTS)
    copy_of(k).start()

    @pl.when(k == count - 1)
    def _():
        for j in range(min(SLOTS, count)):
            copy_of(k - j).wait()


def forward_kernel(pieces, low, count, first, *rest):
    parts, frozen, rest = rest[:pieces], rest[pieces], rest[pieces + 1 :]
    out, held, arrived = rest[-3:]
    step, tile = held.shape[2:]

    def fetch(n, slot):
        return [
            pltpu.make_async_copy(
                tile_at(frozen.at[i, pl.ds(first, step)], low + n, tile),
                held.at[slot, i],
                arrived.at[slot, i],
            )
            for i in range(2)
        ]

    slot = ring(fetch, pl.program_id(0), count)
    x = jnp.concatenate([v[...] for v in parts], axis=0)
    for i in range(2):
        part = dot(x, held[slot, i])
        out[i] = part if len(rest) == 3 else rest[0][i] + part


def forward_chunk(pieces, frozen, start, first, tiles, share=1):
    step = pieces[0].shape[1]
    tokens = sum(v.shape[0] for v in pieces)
    hidden = frozen.shape[2]
    tile = tile_of(hidden, 256)
    low, high = tiles
    across = pl.BlockSpec((2, tokens, tile), lambda n: (0, 0, low + n))
    operands = [*pieces, frozen]
    specs = [pl.BlockSpec(v.shape, lambda n: (0, 0), pipeline_mode=ONCE) for v in pieces]
    specs.append(pl.BlockSpec(memory_space=pltpu.HBM))
    if start is not None:
        operands.append(start)
        specs.append(across)
    count = high - low
    return pl.pallas_call(
        functools.partial(forward_kernel, len(pieces), low, count, first),
        grid=(count,),
        in_specs=specs,
        out_specs=across,
        out_shape=jax.ShapeDtypeStruct((2, tokens, hidden), F32),
        scratch_shapes=[
            pltpu.VMEM((DEPTH, 2, step, tile), BF16),
            pltpu.SemaphoreType.DMA((DEPTH, 2)),
        ],
        input_output_aliases={} if start is None else {len(operands) - 1: 0},
        compiler_params=params(24),
        cost_estimate=cost(4 * tokens * step * tile * count // share, 4 * step * tile * count // share),
    )(*operands)


def low_in_kernel(segments, chunks, rows, adapters, places, which, seg, *rest):
    factors, rest = rest[:segments], rest[segments:]
    cuts, (columns, out) = rest[:-2], rest[-2:]
    pieces = len(cuts) // chunks
    for q in range(chunks):

        @pl.when(which[0] == q)
        def _():
            first = 0
            for v in cuts[q * pieces : (q + 1) * pieces]:
                columns[first : first + v.shape[0]] = v[...]
                first += v.shape[0]

    total = jnp.zeros(out.shape, F32)
    for s in range(segments):
        part = dot(columns[...], factors[s][0])
        total = total + jnp.where(seg[...] == s, part, 0.0)
    put_rows(out, total, places, rows)


def put_rows(out, total, places, rows):
    if rows % 8:
        out[...] = total
        return
    for s in range(total.shape[0] // rows):
        out[pl.ds(pl.multiple_of(places[s] * rows, rows), rows), :] = total[s * rows : (s + 1) * rows]


def of_segment(shape, s):
    return pl.BlockSpec((1,) + shape[1:], lambda *a: (a[-2][s], 0, 0))


def low_in_partial(chunks, seg, down, adapters, places, index, rows):
    segments = adapters.shape[0]
    shard, wide = down.shape[1:]
    tokens = seg.shape[0]
    if shard % 128:
        joined = [jnp.concatenate(piece, axis=1) for piece in zip(*chunks)]
        chunks = [[lax.dynamic_slice_in_dim(v, index * shard, shard, 1) for v in joined]]
        which = jnp.zeros((1,), jnp.int32)
        cuts = [pl.BlockSpec(v.shape, lambda *a: (0, 0)) for v in chunks[0]]
    else:
        inside, at, cuts, first = [], [], [], 0
        for q, pieces in enumerate(chunks):
            per = pieces[0].shape[1] // shard
            inside.append(index >= first)
            at.append(jnp.clip(index - first, 0, per - 1))
            cuts += [
                pl.BlockSpec((v.shape[0], shard), lambda i, a, p, w, q=q: (0, w[1 + q])) for v in pieces
            ]
            first += per
        which = jnp.stack([sum(v.astype(jnp.int32) for v in inside) - 1] + at).astype(jnp.int32)
    full = lambda shape: pl.BlockSpec(shape, lambda *a: (0,) * len(shape))
    factor = lambda s: pl.BlockSpec((1, shard, wide), lambda i, a, p, w: (a[s], 0, 0))
    return pl.pallas_call(
        functools.partial(low_in_kernel, segments, len(chunks), rows),
        grid_spec=pltpu.PrefetchScalarGridSpec(
            num_scalar_prefetch=3,
            grid=(1,),
            in_specs=[full(seg.shape)] + [factor(s) for s in range(segments)] + cuts,
            out_specs=[full((tokens, shard)), full((tokens, wide))],
        ),
        out_shape=[
            jax.ShapeDtypeStruct((tokens, shard), BF16),
            jax.ShapeDtypeStruct((tokens, wide), F32),
        ],
        compiler_params=params(16),
        cost_estimate=cost(2 * tokens * down[0].size * segments, 2 * down[0].size * segments),
    )(adapters, places, which, seg, *([down] * segments), *[v for pieces in chunks for v in pieces])


def middle_kernel(rows, adapters, places, base, dhidden, token_order, order, low, seg, up, *rest):
    dgate, dup, out, left, back, factors, arrived = rest
    segments, wide, tile = factors.shape[1:]
    rank = wide // 2
    tokens = order.shape[0]
    n = pl.program_id(0)
    slot = n % 2
    lane = lax.broadcasted_iota(jnp.int32, (tokens, segments * rank), 1) // rank
    mask = lane == seg[...]

    def fetch(n, slot, s):
        return pltpu.make_async_copy(
            tile_at(up.at[adapters[s]], n, tile), factors.at[slot, s], arrived.at[slot, s]
        )

    @pl.when(n == 0)
    def _():
        for s in range(segments):
            fetch(0, 0, s).start()
        mine = dot(order[...], low[...])
        for i in range(2):
            block = jnp.concatenate([mine[:, i * rank : (i + 1) * rank]] * segments, axis=1)
            left[i] = jnp.where(mask, block, 0.0).astype(BF16)
        back[...] = jnp.zeros_like(back)

    @pl.when(n + 1 < pl.num_programs(0))
    def _():
        for s in range(segments):
            fetch(n + 1, 1 - slot, s).start()

    for s in range(segments):
        fetch(n, slot, s).wait()
    up_g = jnp.concatenate([factors[slot, s, :rank] for s in range(segments)], axis=0)
    up_u = jnp.concatenate([factors[slot, s, rank:] for s in range(segments)], axis=0)
    gate = base[0] + dot(left[0], up_g)
    up_sum = base[1] + dot(left[1], up_u)
    grad = dot(token_order[...], dhidden[...])
    sigma = 1.0 / (1.0 + jnp.exp(-gate))
    g = (grad * up_sum * sigma * (1.0 + gate * (1.0 - sigma))).astype(BF16)
    u = (grad * gate * sigma).astype(BF16)
    dgate[...] = g
    dup[...] = u
    back[0] += dot(g, up_g, ((1,), (1,)))
    back[1] += dot(u, up_u, ((1,), (1,)))

    @pl.when(n == pl.num_programs(0) - 1)
    def _():
        parts = []
        for i in range(2):
            kept = jnp.where(mask, back[i], 0.0)
            parts.append(sum(kept[:, s * rank : (s + 1) * rank] for s in range(segments)))
        put_rows(out, jnp.concatenate(parts, axis=1), places, rows)


def middle(base, dhidden, token_order, order, low, seg, up, adapters, places, rows):
    segments = adapters.shape[0]
    tokens, hidden = dhidden.shape
    wide = up.shape[1]
    tile = tile_of(hidden, 256)
    full = lambda shape: pl.BlockSpec(shape, lambda *a: (0,) * len(shape))
    across = lambda lead: pl.BlockSpec(lead + (tokens, tile), lambda n, *a: (0,) * len(lead) + (0, n))
    return pl.pallas_call(
        functools.partial(middle_kernel, rows),
        grid_spec=pltpu.PrefetchScalarGridSpec(
            num_scalar_prefetch=2,
            grid=(hidden // tile,),
            in_specs=[across((2,)), across(())]
            + [full(v.shape) for v in (token_order, order, low, seg)]
            + [pl.BlockSpec(memory_space=pltpu.HBM)],
            out_specs=[across(()), across(()), full((tokens, wide))],
            scratch_shapes=[
                pltpu.VMEM((2, tokens, segments * wide // 2), BF16),
                pltpu.VMEM((2, tokens, segments * wide // 2), F32),
                pltpu.VMEM((2, segments, wide, tile), BF16),
                pltpu.SemaphoreType.DMA((2, segments)),
            ],
        ),
        out_shape=[
            jax.ShapeDtypeStruct((tokens, hidden), BF16),
            jax.ShapeDtypeStruct((tokens, hidden), BF16),
            jax.ShapeDtypeStruct((tokens, wide), F32),
        ],
        compiler_params=params(20),
        cost_estimate=cost(
            4 * tokens * hidden * segments * wide, hidden * (tokens * 14 + segments * wide * 2)
        ),
    )(adapters, places, base, dhidden, token_order, order, low, seg, up)


def grad_b_kernel(first, count, dgate, dup, order, low, adapter, *rest):
    out, left, staged, sent = rest[-4:]
    group, wide, tile = staged.shape[1:]
    groups = left.shape[1]
    rank = wide // 2
    g = pl.program_id(1)
    k = pl.program_id(0) * groups + g

    @pl.when(k == 0)
    def _():
        turned = dot(order[...], low[...]).T
        for a in range(groups * group):
            kept = jnp.where(adapter[...] == a, turned, 0.0).astype(BF16)
            at = (a // group, slice(a % group * rank, (a % group + 1) * rank))
            left[(0, *at)] = kept[:rank]
            left[(1, *at)] = kept[rank:]

    def copy_of(k):
        block = out.at[pl.ds(k % groups * group, group)]
        if out.shape[2] != tile:
            at = pl.multiple_of((first + k // groups) * tile, tile)
            block = block.at[:, :, pl.ds(at, tile)]
        return pltpu.make_async_copy(staged.at[k % SLOTS], block, sent.at[k % SLOTS])

    def fill(slot):
        for i, grad in enumerate((dgate, dup)):
            part = dot(left[i, g], grad[...])
            staged[slot, :, i * rank : (i + 1) * rank, :] = part.reshape(group, rank, tile)

    send(copy_of, k, count * groups, fill)


def grad_b_of(dgate, dup, order, low, adapter_row, adapters, start, tiles):
    tokens, hidden = dgate.shape
    wide = low.shape[1]
    tile = tile_of(hidden, 256)
    first, last = tiles
    groups = 2 if adapters % 2 == 0 else 1
    group = adapters // groups
    full = lambda shape: pl.BlockSpec(shape, lambda n, g: (0,) * len(shape))
    across = pl.BlockSpec((tokens, tile), lambda n, g: (0, first + n))
    operands = [dgate, dup, order, low, adapter_row]
    specs = [across, across, full(order.shape), full(low.shape), full(adapter_row.shape)]
    if start is not None:
        operands.append(start)
        specs.append(pl.BlockSpec(memory_space=pltpu.HBM))
    part = tile * (last - first) * adapters * wide
    return pl.pallas_call(
        functools.partial(grad_b_kernel, first, last - first),
        grid=(last - first, groups),
        in_specs=specs,
        out_specs=pl.BlockSpec(memory_space=pltpu.HBM),
        out_shape=jax.ShapeDtypeStruct((adapters, wide, hidden), F32),
        scratch_shapes=[
            pltpu.VMEM((2, groups, group * wide // 2, tokens), BF16),
            pltpu.VMEM((SLOTS, group, wide, tile), F32),
            pltpu.SemaphoreType.DMA((SLOTS,)),
        ],
        input_output_aliases={} if start is None else {5: 0},
        compiler_params=params(20),
        cost_estimate=cost(2 * tokens * part, 4 * part),
    )(*operands)


def grad_a_kernel(columns, order, low, adapter, out, turned, mine, staged, sent):
    per = staged.shape[1]
    k = pl.program_id(0)

    @pl.when(k == 0)
    def _():
        turned[...] = columns[...].astype(F32).T.astype(BF16)
        mine[...] = dot(order[...], low[...])

    def copy_of(k):
        return pltpu.make_async_copy(
            staged.at[k % SLOTS], out.at[pl.ds(k * per, per)], sent.at[k % SLOTS]
        )

    def fill(slot):
        for j in range(per):
            kept = jnp.where(adapter[...] == k * per + j, mine[...], 0.0).astype(BF16)
            staged[slot, j] = dot(turned[...], kept)

    send(copy_of, k, out.shape[0] // per, fill)


def grad_a_of(columns, order, low, adapter, adapters):
    tokens, shard = columns.shape
    wide = low.shape[1]
    per = 4 if adapters % 4 == 0 else 1
    full = lambda shape: pl.BlockSpec(shape, lambda n: (0,) * len(shape))
    return pl.pallas_call(
        grad_a_kernel,
        grid=(adapters // per,),
        in_specs=[full(columns.shape), full(order.shape), full(low.shape), full(adapter.shape)],
        out_specs=pl.BlockSpec(memory_space=pltpu.HBM),
        out_shape=jax.ShapeDtypeStruct((adapters, shard, wide), F32),
        scratch_shapes=[
            pltpu.VMEM((shard, tokens), BF16),
            pltpu.VMEM((tokens, wide), F32),
            pltpu.VMEM((SLOTS, per, shard, wide), F32),
            pltpu.SemaphoreType.DMA((SLOTS,)),
        ],
        compiler_params=params(16),
        cost_estimate=cost(2 * tokens * shard * adapters * wide, 4 * shard * adapters * wide),
    )(columns, order, low, adapter)


def side_kernel(segments, adapters, places, order, low, seg, *rest):
    near, far = rest[-2:]
    half = near.shape[0]
    mine = dot(order[...], low[...])
    total = jnp.zeros((2 * half, near.shape[1]), F32)
    for s in range(segments):
        kept = jnp.where(seg[...] == s, mine, 0.0).astype(BF16)
        total = total + dot(kept, rest[s][0], ((1,), (1,)))
    near[...] = total[:half]
    far[...] = total[half:]


def side_of(order, low, seg, down, adapters, places):
    segments = adapters.shape[0]
    tokens = order.shape[0]
    shard = down.shape[1]
    full = lambda shape: pl.BlockSpec(shape, lambda *a: (0,) * len(shape))
    return pl.pallas_call(
        functools.partial(side_kernel, segments),
        grid_spec=pltpu.PrefetchScalarGridSpec(
            num_scalar_prefetch=2,
            grid=(1,),
            in_specs=[full(order.shape), full(low.shape), full(seg.shape)]
            + [of_segment(down.shape, s) for s in range(segments)],
            out_specs=[full((tokens // 2, shard))] * 2,
        ),
        out_shape=[jax.ShapeDtypeStruct((tokens // 2, shard), F32)] * 2,
        compiler_params=params(16),
        cost_estimate=cost(2 * tokens * down[0].size * segments, 2 * down[0].size * segments),
    )(adapters, places, order, low, seg, *([down] * segments))


def backward_kernel(count, first, frozen, dgate, dup, near, far, held, arrived):
    half = near.shape[0]
    block = held.shape[2]

    def fetch(k, slot):
        rows = pl.ds(pl.multiple_of(first + k * block, block), block)
        return [
            pltpu.make_async_copy(frozen.at[i, rows, :], held.at[slot, i], arrived.at[slot, i])
            for i in range(2)
        ]

    slot = ring(fetch, pl.program_id(0), count)
    term = dot(dgate[...], held[slot, 0], ((1,), (1,))) + dot(dup[...], held[slot, 1], ((1,), (1,)))
    near[...] = term[:half].astype(BF16)
    far[...] = term[half:].astype(BF16)


def backward_chunk(frozen, dgate, dup, first, step):
    tokens, hidden = dgate.shape
    block = tile_of(step, 512)
    count = step // block
    full = lambda shape: pl.BlockSpec(shape, lambda k: (0, 0), pipeline_mode=ONCE)
    out = pl.BlockSpec((tokens // 2, block), lambda k: (0, k))
    return pl.pallas_call(
        functools.partial(backward_kernel, count, first),
        grid=(count,),
        in_specs=[pl.BlockSpec(memory_space=pltpu.HBM), full(dgate.shape), full(dup.shape)],
        out_specs=[out, out],
        out_shape=[jax.ShapeDtypeStruct((tokens // 2, step), BF16)] * 2,
        scratch_shapes=[
            pltpu.VMEM((DEPTH, 2, block, hidden), BF16),
            pltpu.SemaphoreType.DMA((DEPTH, 2)),
        ],
        compiler_params=params(20),
        cost_estimate=cost(4 * tokens * step * hidden, 4 * step * hidden),
    )(frozen, dgate, dup)


def core_sum_kernel(base, at, near, far, side, side_far, *outs):
    total = near[...].astype(F32) + far[...].astype(F32)
    rows = outs[0].shape[0]
    own = at[0] == base + pl.program_id(0)

    def store(total):
        for s, out in enumerate(outs):
            out[...] = total[s * rows : (s + 1) * rows].astype(BF16)

    @pl.when(jnp.logical_not(own))
    def _():
        store(total)

    @pl.when(jnp.logical_and(own, at[1] == 0))
    def _():
        store(total + jnp.concatenate([side[...], side_far[...]], axis=1))

    @pl.when(jnp.logical_and(own, at[1] != 0))
    def _():
        store(total + jnp.concatenate([side_far[...], side[...]], axis=1))


def core_sum(near, far, side, side_far, at, first, slots):
    half, step = near.shape
    block = 2 * side.shape[1]
    full = lambda shape: pl.BlockSpec(shape, lambda *a: (0,) * len(shape))
    across = lambda rows: pl.BlockSpec((rows, block), lambda k, at: (0, k))
    return pl.pallas_call(
        functools.partial(core_sum_kernel, first // block),
        grid_spec=pltpu.PrefetchScalarGridSpec(
            num_scalar_prefetch=1,
            grid=(step // block,),
            in_specs=[across(half), across(half), full(side.shape), full(side_far.shape)],
            out_specs=[across(half // slots)] * slots,
        ),
        out_shape=[jax.ShapeDtypeStruct((half // slots, step), BF16)] * slots,
        compiler_params=params(16),
        cost_estimate=cost(2 * half * step, 6 * half * step),
    )(at, near, far, side, side_far)


def local(
    activations,
    dhidden,
    frozen,
    adapter_down_factors,
    adapter_up_factors,
    segment_adapter_index,
    segment_row_counts,
    ranks,
):
    adapter_list, shard_width, gate_and_up = adapter_down_factors.shape
    rank = gate_and_up // 2
    width = frozen.shape[1]
    rows = activations.shape[0]
    torus = Torus(width // shard_width)
    tokens = rows * torus.size
    a, b, c = torus.dims
    index = lax.axis_index("tensor")
    slots = torus.slot_devices(index)
    token = (slots[:, None] * rows + jnp.arange(rows, dtype=jnp.int32)[None, :]).reshape(-1)

    ends = jnp.cumsum(segment_row_counts[0])
    seg_adapter = segment_adapter_index[0]
    count = ends.shape[0]

    def segment_of(place):
        return jnp.sum((place[:, None] >= ends[None, :]).astype(jnp.int32), axis=1)

    def adapter_of(segment):
        match = segment[:, None] == jnp.arange(count, dtype=jnp.int32)[None, :]
        return jnp.sum(jnp.where(match, seg_adapter[None, :], 0), axis=1)

    column = jnp.arange(gate_and_up, dtype=jnp.int32) % rank
    chips = a * b
    core = index % c
    mine = (jnp.arange(chips, dtype=jnp.int32)[:, None] * c + core) * rows
    mine = (mine + jnp.arange(rows, dtype=jnp.int32)[None, :]).reshape(-1)
    my_adapter = adapter_of(segment_of(mine))
    hit = my_adapter[:, None] == jnp.arange(adapter_list, dtype=jnp.int32)[None, :]
    my_rank = jnp.sum(jnp.where(hit, ranks[None, :], 0), axis=1)[:, None]
    factor = jnp.where(column[None, :] < my_rank, 16.0 / my_rank.astype(F32), 0.0)

    places = (slots % c - core) % c * chips + slots // c
    spot = (places[:, None] * rows + jnp.arange(rows, dtype=jnp.int32)[None, :]).reshape(-1)
    count_up = jnp.arange(tokens, dtype=jnp.int32)[None, :]
    token_order = (token[:, None] == count_up).astype(BF16)
    order = (spot[:, None] == count_up).astype(BF16)

    segment = segment_of(token)
    adapter = adapter_of(segment)

    def whole_sum(partial, beside=()):
        if rows % 8:
            at = jnp.arange(torus.size, dtype=jnp.int32)
            device = at % chips * c + (core + at // chips) % c
            partial = jnp.take(
                partial.reshape(torus.size, rows, -1),
                jnp.take(torus.slots_of(index), device),
                axis=0,
            )
        x = torus.scatter_sum(partial.reshape(c, chips * rows, gate_and_up), 2)
        x = torus.exchange_sum(x, (1, 0), beside)
        return torus.gather((x * factor).astype(BF16), 2).reshape(tokens, gate_and_up)

    hidden = frozen.shape[2]
    tiles = hidden // tile_of(hidden, 256)
    split = width * 3 // 8
    last, main = activations[:, :split], activations[:, split:]
    pair = [torus.move(last, 1, -k) for k in range(1, b)]
    main = torus.gather(main, 0).reshape(a * rows, -1)
    step = main.shape[1] // 2
    parts = []
    for j in range(2):
        x = main[:, j * step : (j + 1) * step]
        x = lax.optimization_barrier((x, *pair))[0] if j else x
        parts.append((split + j * step, [x] + [torus.move(x, 1, -k) for k in range(1, b)]))
    pair = after(jnp.stack([last, *pair]), main)
    outer = [pair] + [torus.move(pair, 0, -k) for k in range(1, a)]

    base = None
    gathered = []
    for first, near in parts:
        if gathered:
            near[1:] = lax.optimization_barrier((*near[1:], base, *outer[1:]))[: b - 1]
        gathered.append([*near, *[torus.move(v, 2, -1) for v in near]])
        share = 64 if base is not None else 1
        base = forward_chunk(gathered[-1], frozen, base, first, (0, tiles), share)
    outer = lax.optimization_barrier((*outer, base))[:-1]
    near = [jnp.stack([v[k] for v in outer]).reshape(a * rows, split) for k in range(b)]
    gathered.insert(0, [*near, *[torus.move(v, 2, -1) for v in near]])

    columns, partial_in = low_in_partial(
        gathered, segment[:, None], adapter_down_factors, seg_adapter, places, index, rows
    )
    ends_at = [cut[1] for cut in parts_of(tiles, 3)]
    bases = [base]

    def forward_part(token):
        cut = (ends_at[len(bases) - 2] if len(bases) > 1 else 0, ends_at[len(bases) - 1])
        pieces = [after(gathered[0][0], token), *gathered[0][1:]]
        bases.append(forward_chunk(pieces, frozen, bases[-1], 0, cut))
        return bases[-1]

    low_in = whole_sum(partial_in, [forward_part] * len(ends_at))
    base = bases[-1]
    dgate, dup, partial_out = middle(
        base, dhidden, token_order, order, low_in, segment[:, None], adapter_up_factors,
        seg_adapter, places, rows,
    )
    thirds = parts_of(tiles, 3)
    grad_b = []

    def grad_b_part(token):
        grad_b.append(
            grad_b_of(
                dgate, dup, order, after(low_in, token), adapter[None, :], adapter_list,
                grad_b[-1] if grad_b else None, thirds[len(grad_b)],
            )
        )
        return grad_b[-1]

    cuts = []
    for share in SUM_SHARES:
        cuts.append((sum(v[1] for v in cuts), width * share // sum(SUM_SHARES)))
    terms = []

    def first_term(token):
        terms.append(backward_chunk(frozen, after(dgate, token), dup, *cuts[0]))
        return terms[0][0]

    low_out = whole_sum(partial_out, [grad_b_part] * (len(thirds) - 1) + [first_term])
    near, far = terms[0][0], after(terms[0][1], low_out)
    side, side_far = side_of(
        order, low_out, segment[:, None], adapter_down_factors, seg_adapter, places
    )
    side_far = torus.move(side_far, 2, 1)
    at = jnp.stack([index // c, core]).astype(jnp.int32)
    sums, inners, inner_moves, outer_moves, blocks = [], [], [], [], []
    for q, (first, step) in enumerate(cuts):
        if q:
            near, far = backward_chunk(frozen, after(dgate, sums[-1][0]), dup, first, step)
            ahead = inner_moves[q - 1] + (outer_moves[q - 2] if q > 1 else [])
            far = lax.optimization_barrier((far, *ahead))[0]
        far = torus.move(far, 2, 1)
        sums.append(core_sum(near, far, side, side_far, at, first, b))
        inner_moves.append([torus.move(sums[q][k], 1, k) for k in range(1, b)])
        total = sums[q][0].astype(F32)
        for v in inner_moves[q]:
            total = total + v.astype(F32)
        inners.append(total.astype(BF16).reshape(a, rows, step))
        outer_moves.append([torus.move(inners[q][k], 0, k) for k in range(1, a)])
    grad_b = grad_b_part(outer_moves[-1][0])
    for q, inner in enumerate(inners):
        total = inner[0].astype(F32)
        for v in outer_moves[q]:
            v = lax.optimization_barrier((v, *inner_moves[-1]))[0] if q < len(cuts) - 1 else v
            total = total + v.astype(F32)
        blocks.append(total.astype(BF16))
    dinput = jnp.concatenate(blocks, axis=1)
    grad_a = grad_a_of(
        columns, order, after(low_out, sums[-1][0]), adapter[:, None], adapter_list
    )
    return (dinput, grad_a, grad_b)


def solution(mesh):
    placed = (
        P(("groups", "tensor"), None),
        P("groups", "tensor"),
        P(None, None, "tensor"),
        P(None, "tensor", None),
        P(None, None, "tensor"),
        P("groups", None),
        P("groups", None),
        P(),
    )
    return jax.shard_map(
        local,
        mesh=mesh,
        in_specs=placed,
        out_specs=(
            P(("groups", "tensor"), None),
            P("groups", "tensor", None),
            P("groups", None, "tensor"),
        ),
        check_vma=False,
    )
```

```python
import functools

import jax
import jax.numpy as jnp
from jax import lax
from jax.experimental import pallas as pl
from jax.experimental.pallas import tpu as pltpu
from jax.sharding import PartitionSpec as P

OUTER_SHARES = (3, 5)
INNER_CUTS = (1, 2)
SUM_SHARES = (4, 4)
MIB = 1024 * 1024
BF16 = jnp.bfloat16
DEPTH = 3
SLOTS = 4
ONCE = pl.Buffered(1)
F32 = jnp.float32


def dot(left, right, dims=((1,), (0,))):
    return lax.dot_general(left, right, (dims, ((), ())), preferred_element_type=F32)


def params(mib):
    return pltpu.CompilerParams(vmem_limit_bytes=mib * MIB)


def cost(flops, moved):
    return pl.CostEstimate(flops=int(flops), bytes_accessed=int(moved), transcendentals=0)


def tile_of(size, most):
    return most if size % most == 0 else size


def parts_of(count, parts):
    parts = min(parts, count)
    ends = [count * k // parts for k in range(parts + 1)]
    return list(zip(ends[:-1], ends[1:]))


def after(x, other):
    return lax.optimization_barrier((x, other))[0]


class Torus:
    def __init__(self, size):
        core = 2 if size % 2 == 0 else 1
        chips = size // core
        inner = 1
        while inner * 2 * inner * 2 <= chips and chips % (inner * 2) == 0:
            inner *= 2
        self.size = size
        self.dims = (chips // inner, inner, core)
        self.strides = (inner * core, core, 1)

    def place(self, index):
        return [index // s % n for s, n in zip(self.strides, self.dims)]

    def shifted(self, index, dim, by):
        at = index // self.strides[dim] % self.dims[dim]
        return index + ((at + by) % self.dims[dim] - at) * self.strides[dim]

    def move(self, x, dim, by):
        pairs = [(i, self.shifted(i, dim, by)) for i in range(self.size)]
        return lax.ppermute(x, "tensor", pairs)

    def gather(self, x, dim):
        return jnp.stack([x] + [self.move(x, dim, -k) for k in range(1, self.dims[dim])])

    def scatter_sum(self, x, dim):
        total = x[0].astype(F32)
        for k in range(1, self.dims[dim]):
            total = total + self.move(x[k], dim, k).astype(F32)
        return total

    def slot_devices(self, index):
        outer, inner, core = self.place(index)
        a, b, c = self.dims
        cs = lax.broadcasted_iota(jnp.int32, (c, b, a), 0)
        bs = lax.broadcasted_iota(jnp.int32, (c, b, a), 1)
        zs = lax.broadcasted_iota(jnp.int32, (c, b, a), 2)
        return (((outer + zs) % a * b + (inner + bs) % b) * c + (core + cs) % c).reshape(-1)

    def exchange_sum(self, x, dims, beside):
        beside = list(beside)
        for dim in dims:
            k = 1
            while k < self.dims[dim]:
                stride = self.strides[dim]
                pairs = [(i, i + ((i // stride ^ k) - i // stride) * stride) for i in range(self.size)]
                done = beside.pop(0)(x) if beside else None
                x = x + lax.ppermute(x, "tensor", pairs)
                x = x if done is None else after(x, done)
                k *= 2
        return x

    def slots_of(self, index):
        outer, inner, core = self.place(index)
        a, b, c = self.dims
        zs = lax.broadcasted_iota(jnp.int32, (a, b, c), 0)
        bs = lax.broadcasted_iota(jnp.int32, (a, b, c), 1)
        cs = lax.broadcasted_iota(jnp.int32, (a, b, c), 2)
        return (((cs - core) % c * b + (bs - inner) % b) * a + (zs - outer) % a).reshape(-1)


def tile_at(ref, n, tile):
    if ref.shape[1] == tile:
        return ref
    return ref.at[:, pl.ds(pl.multiple_of(n * tile, tile), tile)]


def ring(fetch, k, count):
    @pl.when(k == 0)
    def _():
        for j in range(min(DEPTH - 1, count)):
            for copy in fetch(j, j):
                copy.start()

    @pl.when(k + DEPTH - 1 < count)
    def _():
        for copy in fetch(k + DEPTH - 1, (k + DEPTH - 1) % DEPTH):
            copy.start()

    for copy in fetch(k, k % DEPTH):
        copy.wait()
    return k % DEPTH


def send(copy_of, k, count, fill):
    @pl.when(k >= SLOTS)
    def _():
        copy_of(k - SLOTS).wait()

    fill(k % SLOTS)
    copy_of(k).start()

    @pl.when(k == count - 1)
    def _():
        for j in range(min(SLOTS, count)):
            copy_of(k - j).wait()


def forward_kernel(pieces, low, count, first, *rest):
    parts, frozen, rest = rest[:pieces], rest[pieces], rest[pieces + 1 :]
    out, held, arrived = rest[-3:]
    step, tile = held.shape[2:]

    def fetch(n, slot):
        return [
            pltpu.make_async_copy(
                tile_at(frozen.at[i, pl.ds(first, step)], low + n, tile),
                held.at[slot, i],
                arrived.at[slot, i],
            )
            for i in range(2)
        ]

    slot = ring(fetch, pl.program_id(0), count)
    x = jnp.concatenate([v[...] for v in parts], axis=0)
    for i in range(2):
        part = dot(x, held[slot, i])
        out[i] = part if len(rest) == 3 else rest[0][i] + part


def forward_chunk(pieces, frozen, start, first, tiles):
    step = pieces[0].shape[1]
    tokens = sum(v.shape[0] for v in pieces)
    hidden = frozen.shape[2]
    tile = tile_of(hidden, 256)
    low, high = tiles
    across = pl.BlockSpec((2, tokens, tile), lambda n: (0, 0, low + n))
    operands = [*pieces, frozen]
    specs = [pl.BlockSpec(v.shape, lambda n: (0, 0), pipeline_mode=ONCE) for v in pieces]
    specs.append(pl.BlockSpec(memory_space=pltpu.HBM))
    if start is not None:
        operands.append(start)
        specs.append(across)
    count = high - low
    return pl.pallas_call(
        functools.partial(forward_kernel, len(pieces), low, count, first),
        grid=(count,),
        in_specs=specs,
        out_specs=across,
        out_shape=jax.ShapeDtypeStruct((2, tokens, hidden), F32),
        scratch_shapes=[
            pltpu.VMEM((DEPTH, 2, step, tile), BF16),
            pltpu.SemaphoreType.DMA((DEPTH, 2)),
        ],
        input_output_aliases={} if start is None else {len(operands) - 1: 0},
        compiler_params=params(16),
        cost_estimate=cost(4 * tokens * step * tile * count, 4 * step * tile * count),
    )(*operands)


def low_in_kernel(segments, chunks, rows, adapters, places, which, seg, *rest):
    factors, rest = rest[:segments], rest[segments:]
    cuts, (columns, out) = rest[:-2], rest[-2:]
    pieces = len(cuts) // chunks
    for q in range(chunks):

        @pl.when(which[0] == q)
        def _():
            first = 0
            for v in cuts[q * pieces : (q + 1) * pieces]:
                columns[first : first + v.shape[0]] = v[...]
                first += v.shape[0]

    total = jnp.zeros(out.shape, F32)
    for s in range(segments):
        part = dot(columns[...], factors[s][0])
        total = total + jnp.where(seg[...] == s, part, 0.0)
    put_rows(out, total, places, rows)


def put_rows(out, total, places, rows):
    if rows % 8:
        out[...] = total
        return
    for s in range(total.shape[0] // rows):
        out[pl.ds(pl.multiple_of(places[s] * rows, rows), rows), :] = total[s * rows : (s + 1) * rows]


def of_segment(shape, s):
    return pl.BlockSpec((1,) + shape[1:], lambda *a: (a[-2][s], 0, 0))


def low_in_partial(chunks, seg, down, adapters, places, index, rows):
    segments = adapters.shape[0]
    shard, wide = down.shape[1:]
    tokens = seg.shape[0]
    if shard % 128:
        joined = [jnp.concatenate(piece, axis=1) for piece in zip(*chunks)]
        chunks = [[lax.dynamic_slice_in_dim(v, index * shard, shard, 1) for v in joined]]
        which = jnp.zeros((1,), jnp.int32)
        cuts = [pl.BlockSpec(v.shape, lambda *a: (0, 0)) for v in chunks[0]]
    else:
        inside, at, cuts, first = [], [], [], 0
        for q, pieces in enumerate(chunks):
            per = pieces[0].shape[1] // shard
            inside.append(index >= first)
            at.append(jnp.clip(index - first, 0, per - 1))
            cuts += [
                pl.BlockSpec((v.shape[0], shard), lambda i, a, p, w, q=q: (0, w[1 + q])) for v in pieces
            ]
            first += per
        which = jnp.stack([sum(v.astype(jnp.int32) for v in inside) - 1] + at).astype(jnp.int32)
    full = lambda shape: pl.BlockSpec(shape, lambda *a: (0,) * len(shape))
    factor = lambda s: pl.BlockSpec((1, shard, wide), lambda i, a, p, w: (a[s], 0, 0))
    return pl.pallas_call(
        functools.partial(low_in_kernel, segments, len(chunks), rows),
        grid_spec=pltpu.PrefetchScalarGridSpec(
            num_scalar_prefetch=3,
            grid=(1,),
            in_specs=[full(seg.shape)] + [factor(s) for s in range(segments)] + cuts,
            out_specs=[full((tokens, shard)), full((tokens, wide))],
        ),
        out_shape=[
            jax.ShapeDtypeStruct((tokens, shard), BF16),
            jax.ShapeDtypeStruct((tokens, wide), F32),
        ],
        compiler_params=params(16),
        cost_estimate=cost(2 * tokens * down[0].size * segments, 2 * down[0].size * segments),
    )(adapters, places, which, seg, *([down] * segments), *[v for pieces in chunks for v in pieces])


def middle_kernel(rows, adapters, places, base, dhidden, token_order, order, low, seg, up, *rest):
    dgate, dup, out, left, back, factors, arrived = rest
    segments, wide, tile = factors.shape[1:]
    rank = wide // 2
    tokens = order.shape[0]
    n = pl.program_id(0)
    slot = n % 2
    lane = lax.broadcasted_iota(jnp.int32, (tokens, segments * rank), 1) // rank
    mask = lane == seg[...]

    def fetch(n, slot, s):
        return pltpu.make_async_copy(
            tile_at(up.at[adapters[s]], n, tile), factors.at[slot, s], arrived.at[slot, s]
        )

    @pl.when(n == 0)
    def _():
        for s in range(segments):
            fetch(0, 0, s).start()
        mine = dot(order[...], low[...])
        for i in range(2):
            block = jnp.concatenate([mine[:, i * rank : (i + 1) * rank]] * segments, axis=1)
            left[i] = jnp.where(mask, block, 0.0).astype(BF16)
        back[...] = jnp.zeros_like(back)

    @pl.when(n + 1 < pl.num_programs(0))
    def _():
        for s in range(segments):
            fetch(n + 1, 1 - slot, s).start()

    for s in range(segments):
        fetch(n, slot, s).wait()
    up_g = jnp.concatenate([factors[slot, s, :rank] for s in range(segments)], axis=0)
    up_u = jnp.concatenate([factors[slot, s, rank:] for s in range(segments)], axis=0)
    gate = base[0] + dot(left[0], up_g)
    up_sum = base[1] + dot(left[1], up_u)
    grad = dot(token_order[...], dhidden[...])
    sigma = 1.0 / (1.0 + jnp.exp(-gate))
    g = (grad * up_sum * sigma * (1.0 + gate * (1.0 - sigma))).astype(BF16)
    u = (grad * gate * sigma).astype(BF16)
    dgate[...] = g
    dup[...] = u
    back[0] += dot(g, up_g, ((1,), (1,)))
    back[1] += dot(u, up_u, ((1,), (1,)))

    @pl.when(n == pl.num_programs(0) - 1)
    def _():
        parts = []
        for i in range(2):
            kept = jnp.where(mask, back[i], 0.0)
            parts.append(sum(kept[:, s * rank : (s + 1) * rank] for s in range(segments)))
        put_rows(out, jnp.concatenate(parts, axis=1), places, rows)


def middle(base, dhidden, token_order, order, low, seg, up, adapters, places, rows):
    segments = adapters.shape[0]
    tokens, hidden = dhidden.shape
    wide = up.shape[1]
    tile = tile_of(hidden, 256)
    full = lambda shape: pl.BlockSpec(shape, lambda *a: (0,) * len(shape))
    across = lambda lead: pl.BlockSpec(lead + (tokens, tile), lambda n, *a: (0,) * len(lead) + (0, n))
    return pl.pallas_call(
        functools.partial(middle_kernel, rows),
        grid_spec=pltpu.PrefetchScalarGridSpec(
            num_scalar_prefetch=2,
            grid=(hidden // tile,),
            in_specs=[across((2,)), across(())]
            + [full(v.shape) for v in (token_order, order, low, seg)]
            + [pl.BlockSpec(memory_space=pltpu.HBM)],
            out_specs=[across(()), across(()), full((tokens, wide))],
            scratch_shapes=[
                pltpu.VMEM((2, tokens, segments * wide // 2), BF16),
                pltpu.VMEM((2, tokens, segments * wide // 2), F32),
                pltpu.VMEM((2, segments, wide, tile), BF16),
                pltpu.SemaphoreType.DMA((2, segments)),
            ],
        ),
        out_shape=[
            jax.ShapeDtypeStruct((tokens, hidden), BF16),
            jax.ShapeDtypeStruct((tokens, hidden), BF16),
            jax.ShapeDtypeStruct((tokens, wide), F32),
        ],
        compiler_params=params(16),
        cost_estimate=cost(
            4 * tokens * hidden * segments * wide, hidden * (tokens * 14 + segments * wide * 2)
        ),
    )(adapters, places, base, dhidden, token_order, order, low, seg, up)


def grad_b_kernel(first, count, dgate, dup, order, low, adapter, *rest):
    out, left, staged, sent = rest[-4:]
    group, wide, tile = staged.shape[1:]
    groups = left.shape[1]
    rank = wide // 2
    g = pl.program_id(1)
    k = pl.program_id(0) * groups + g

    @pl.when(k == 0)
    def _():
        turned = dot(order[...], low[...]).T
        for a in range(groups * group):
            kept = jnp.where(adapter[...] == a, turned, 0.0).astype(BF16)
            at = (a // group, slice(a % group * rank, (a % group + 1) * rank))
            left[(0, *at)] = kept[:rank]
            left[(1, *at)] = kept[rank:]

    def copy_of(k):
        block = out.at[pl.ds(k % groups * group, group)]
        if out.shape[2] != tile:
            at = pl.multiple_of((first + k // groups) * tile, tile)
            block = block.at[:, :, pl.ds(at, tile)]
        return pltpu.make_async_copy(staged.at[k % SLOTS], block, sent.at[k % SLOTS])

    def fill(slot):
        for i, grad in enumerate((dgate, dup)):
            part = dot(left[i, g], grad[...])
            staged[slot, :, i * rank : (i + 1) * rank, :] = part.reshape(group, rank, tile)

    send(copy_of, k, count * groups, fill)


def grad_b_of(dgate, dup, order, low, adapter_row, adapters, start, tiles):
    tokens, hidden = dgate.shape
    wide = low.shape[1]
    tile = tile_of(hidden, 256)
    first, last = tiles
    groups = 2 if adapters % 2 == 0 else 1
    group = adapters // groups
    full = lambda shape: pl.BlockSpec(shape, lambda n, g: (0,) * len(shape))
    across = pl.BlockSpec((tokens, tile), lambda n, g: (0, first + n))
    operands = [dgate, dup, order, low, adapter_row]
    specs = [across, across, full(order.shape), full(low.shape), full(adapter_row.shape)]
    if start is not None:
        operands.append(start)
        specs.append(pl.BlockSpec(memory_space=pltpu.HBM))
    part = tile * (last - first) * adapters * wide
    return pl.pallas_call(
        functools.partial(grad_b_kernel, first, last - first),
        grid=(last - first, groups),
        in_specs=specs,
        out_specs=pl.BlockSpec(memory_space=pltpu.HBM),
        out_shape=jax.ShapeDtypeStruct((adapters, wide, hidden), F32),
        scratch_shapes=[
            pltpu.VMEM((2, groups, group * wide // 2, tokens), BF16),
            pltpu.VMEM((SLOTS, group, wide, tile), F32),
            pltpu.SemaphoreType.DMA((SLOTS,)),
        ],
        input_output_aliases={} if start is None else {5: 0},
        compiler_params=params(16),
        cost_estimate=cost(2 * tokens * part, 4 * part),
    )(*operands)


def grad_a_kernel(columns, order, low, adapter, out, turned, mine, staged, sent):
    per = staged.shape[1]
    k = pl.program_id(0)

    @pl.when(k == 0)
    def _():
        turned[...] = columns[...].astype(F32).T.astype(BF16)
        mine[...] = dot(order[...], low[...])

    def copy_of(k):
        return pltpu.make_async_copy(
            staged.at[k % SLOTS], out.at[pl.ds(k * per, per)], sent.at[k % SLOTS]
        )

    def fill(slot):
        for j in range(per):
            kept = jnp.where(adapter[...] == k * per + j, mine[...], 0.0).astype(BF16)
            staged[slot, j] = dot(turned[...], kept)

    send(copy_of, k, out.shape[0] // per, fill)


def grad_a_of(columns, order, low, adapter, adapters):
    tokens, shard = columns.shape
    wide = low.shape[1]
    per = 4 if adapters % 4 == 0 else 1
    full = lambda shape: pl.BlockSpec(shape, lambda n: (0,) * len(shape))
    return pl.pallas_call(
        grad_a_kernel,
        grid=(adapters // per,),
        in_specs=[full(columns.shape), full(order.shape), full(low.shape), full(adapter.shape)],
        out_specs=pl.BlockSpec(memory_space=pltpu.HBM),
        out_shape=jax.ShapeDtypeStruct((adapters, shard, wide), F32),
        scratch_shapes=[
            pltpu.VMEM((shard, tokens), BF16),
            pltpu.VMEM((tokens, wide), F32),
            pltpu.VMEM((SLOTS, per, shard, wide), F32),
            pltpu.SemaphoreType.DMA((SLOTS,)),
        ],
        compiler_params=params(16),
        cost_estimate=cost(2 * tokens * shard * adapters * wide, 4 * shard * adapters * wide),
    )(columns, order, low, adapter)


def side_kernel(segments, adapters, places, order, low, seg, *rest):
    near, far = rest[-2:]
    half = near.shape[0]
    mine = dot(order[...], low[...])
    total = jnp.zeros((2 * half, near.shape[1]), F32)
    for s in range(segments):
        kept = jnp.where(seg[...] == s, mine, 0.0).astype(BF16)
        total = total + dot(kept, rest[s][0], ((1,), (1,)))
    near[...] = total[:half]
    far[...] = total[half:]


def side_of(order, low, seg, down, adapters, places):
    segments = adapters.shape[0]
    tokens = order.shape[0]
    shard = down.shape[1]
    full = lambda shape: pl.BlockSpec(shape, lambda *a: (0,) * len(shape))
    return pl.pallas_call(
        functools.partial(side_kernel, segments),
        grid_spec=pltpu.PrefetchScalarGridSpec(
            num_scalar_prefetch=2,
            grid=(1,),
            in_specs=[full(order.shape), full(low.shape), full(seg.shape)]
            + [of_segment(down.shape, s) for s in range(segments)],
            out_specs=[full((tokens // 2, shard))] * 2,
        ),
        out_shape=[jax.ShapeDtypeStruct((tokens // 2, shard), F32)] * 2,
        compiler_params=params(16),
        cost_estimate=cost(2 * tokens * down[0].size * segments, 2 * down[0].size * segments),
    )(adapters, places, order, low, seg, *([down] * segments))


def backward_kernel(count, first, frozen, dgate, dup, near, far, held, arrived):
    half = near.shape[0]
    block = held.shape[2]

    def fetch(k, slot):
        rows = pl.ds(pl.multiple_of(first + k * block, block), block)
        return [
            pltpu.make_async_copy(frozen.at[i, rows, :], held.at[slot, i], arrived.at[slot, i])
            for i in range(2)
        ]

    slot = ring(fetch, pl.program_id(0), count)
    term = dot(dgate[...], held[slot, 0], ((1,), (1,))) + dot(dup[...], held[slot, 1], ((1,), (1,)))
    near[...] = term[:half].astype(BF16)
    far[...] = term[half:].astype(BF16)


def backward_chunk(frozen, dgate, dup, first, step):
    tokens, hidden = dgate.shape
    block = tile_of(step, 512)
    count = step // block
    full = lambda shape: pl.BlockSpec(shape, lambda k: (0, 0), pipeline_mode=ONCE)
    out = pl.BlockSpec((tokens // 2, block), lambda k: (0, k))
    return pl.pallas_call(
        functools.partial(backward_kernel, count, first),
        grid=(count,),
        in_specs=[pl.BlockSpec(memory_space=pltpu.HBM), full(dgate.shape), full(dup.shape)],
        out_specs=[out, out],
        out_shape=[jax.ShapeDtypeStruct((tokens // 2, step), BF16)] * 2,
        scratch_shapes=[
            pltpu.VMEM((DEPTH, 2, block, hidden), BF16),
            pltpu.SemaphoreType.DMA((DEPTH, 2)),
        ],
        compiler_params=params(16),
        cost_estimate=cost(4 * tokens * step * hidden, 4 * step * hidden),
    )(frozen, dgate, dup)


def core_sum_kernel(base, at, near, far, side, side_far, *outs):
    total = near[...].astype(F32) + far[...].astype(F32)
    rows = outs[0].shape[0]
    own = at[0] == base + pl.program_id(0)

    def store(total):
        for s, out in enumerate(outs):
            out[...] = total[s * rows : (s + 1) * rows].astype(BF16)

    @pl.when(jnp.logical_not(own))
    def _():
        store(total)

    @pl.when(jnp.logical_and(own, at[1] == 0))
    def _():
        store(total + jnp.concatenate([side[...], side_far[...]], axis=1))

    @pl.when(jnp.logical_and(own, at[1] != 0))
    def _():
        store(total + jnp.concatenate([side_far[...], side[...]], axis=1))


def core_sum(near, far, side, side_far, at, first, slots):
    half, step = near.shape
    block = 2 * side.shape[1]
    full = lambda shape: pl.BlockSpec(shape, lambda *a: (0,) * len(shape))
    across = lambda rows: pl.BlockSpec((rows, block), lambda k, at: (0, k))
    return pl.pallas_call(
        functools.partial(core_sum_kernel, first // block),
        grid_spec=pltpu.PrefetchScalarGridSpec(
            num_scalar_prefetch=1,
            grid=(step // block,),
            in_specs=[across(half), across(half), full(side.shape), full(side_far.shape)],
            out_specs=[across(half // slots)] * slots,
        ),
        out_shape=[jax.ShapeDtypeStruct((half // slots, step), BF16)] * slots,
        compiler_params=params(16),
        cost_estimate=cost(2 * half * step, 6 * half * step),
    )(at, near, far, side, side_far)


def local(
    activations,
    dhidden,
    frozen,
    adapter_down_factors,
    adapter_up_factors,
    segment_adapter_index,
    segment_row_counts,
    ranks,
):
    adapter_list, shard_width, gate_and_up = adapter_down_factors.shape
    rank = gate_and_up // 2
    width = frozen.shape[1]
    rows = activations.shape[0]
    torus = Torus(width // shard_width)
    tokens = rows * torus.size
    a, b, c = torus.dims
    index = lax.axis_index("tensor")
    slots = torus.slot_devices(index)
    token = (slots[:, None] * rows + jnp.arange(rows, dtype=jnp.int32)[None, :]).reshape(-1)

    ends = jnp.cumsum(segment_row_counts[0])
    seg_adapter = segment_adapter_index[0]
    count = ends.shape[0]

    def segment_of(place):
        return jnp.sum((place[:, None] >= ends[None, :]).astype(jnp.int32), axis=1)

    def adapter_of(segment):
        match = segment[:, None] == jnp.arange(count, dtype=jnp.int32)[None, :]
        return jnp.sum(jnp.where(match, seg_adapter[None, :], 0), axis=1)

    column = jnp.arange(gate_and_up, dtype=jnp.int32) % rank
    chips = a * b
    core = index % c
    mine = (jnp.arange(chips, dtype=jnp.int32)[:, None] * c + core) * rows
    mine = (mine + jnp.arange(rows, dtype=jnp.int32)[None, :]).reshape(-1)
    my_adapter = adapter_of(segment_of(mine))
    hit = my_adapter[:, None] == jnp.arange(adapter_list, dtype=jnp.int32)[None, :]
    my_rank = jnp.sum(jnp.where(hit, ranks[None, :], 0), axis=1)[:, None]
    factor = jnp.where(column[None, :] < my_rank, 16.0 / my_rank.astype(F32), 0.0)

    places = (slots % c - core) % c * chips + slots // c
    spot = (places[:, None] * rows + jnp.arange(rows, dtype=jnp.int32)[None, :]).reshape(-1)
    count_up = jnp.arange(tokens, dtype=jnp.int32)[None, :]
    token_order = (token[:, None] == count_up).astype(BF16)
    order = (spot[:, None] == count_up).astype(BF16)

    segment = segment_of(token)
    adapter = adapter_of(segment)

    def whole_sum(partial, beside=()):
        if rows % 8:
            at = jnp.arange(torus.size, dtype=jnp.int32)
            device = at % chips * c + (core + at // chips) % c
            partial = jnp.take(
                partial.reshape(torus.size, rows, -1),
                jnp.take(torus.slots_of(index), device),
                axis=0,
            )
        x = torus.scatter_sum(partial.reshape(c, chips * rows, gate_and_up), 2)
        x = torus.exchange_sum(x, (1, 0), beside)
        return torus.gather((x * factor).astype(BF16), 2).reshape(tokens, gate_and_up)

    hidden = frozen.shape[2]
    tiles = hidden // tile_of(hidden, 256)
    chunks = []
    for share in OUTER_SHARES:
        first = sum(v.shape[1] for v in chunks)
        chunks.append(activations[:, first : first + width * share // sum(OUTER_SHARES)])
    outer = []
    for x in chunks:
        x = torus.gather(after(x, outer[-1]) if outer else x, 0)
        outer.append(x.reshape(a * rows, -1))
    parts = []
    for x, cuts in zip(outer, INNER_CUTS):
        step = x.shape[1] // cuts
        parts += [x[:, j * step : (j + 1) * step] for j in range(cuts)]
    base = None
    gathered = []
    first = 0
    for q, x in enumerate(parts):
        near = [x] + [torus.move(x, 1, -k) for k in range(1, b)]
        near[1:] = lax.optimization_barrier((*near[1:], base if q else outer[-1]))[:-1]
        far = [torus.move(v, 2, -1) for v in near]
        gathered.append([*near, *far])
        if q < len(parts) - 1:
            base = forward_chunk(gathered[q], frozen, base, first, (0, tiles))
            first += x.shape[1]

    columns, partial_in = low_in_partial(
        gathered, segment[:, None], adapter_down_factors, seg_adapter, places, index, rows
    )
    thirds = parts_of(tiles, 3)
    bases = [base]

    def forward_part(token):
        pieces = [after(gathered[-1][0], token), *gathered[-1][1:]]
        bases.append(forward_chunk(pieces, frozen, bases[-1], first, thirds[len(bases) - 1]))
        return bases[-1]

    low_in = whole_sum(partial_in, [forward_part] * len(thirds))
    base = bases[-1]
    dgate, dup, partial_out = middle(
        base, dhidden, token_order, order, low_in, segment[:, None], adapter_up_factors,
        seg_adapter, places, rows,
    )
    grad_b = []

    def grad_b_part(token):
        grad_b.append(
            grad_b_of(
                dgate, dup, order, after(low_in, token), adapter[None, :], adapter_list,
                grad_b[-1] if grad_b else None, thirds[len(grad_b)],
            )
        )
        return grad_b[-1]

    cuts = []
    for share in SUM_SHARES:
        cuts.append((sum(v[1] for v in cuts), width * share // sum(SUM_SHARES)))
    terms = []

    def first_term(token):
        terms.append(backward_chunk(frozen, after(dgate, token), dup, *cuts[0]))
        return terms[0][0]

    low_out = whole_sum(partial_out, [grad_b_part] * (len(thirds) - 1) + [first_term])
    near, far = terms[0][0], after(terms[0][1], low_out)
    side, side_far = side_of(
        order, low_out, segment[:, None], adapter_down_factors, seg_adapter, places
    )
    side_far = torus.move(side_far, 2, 1)
    at = jnp.stack([index // c, core]).astype(jnp.int32)
    sums, inners, inner_moves, outer_moves, blocks = [], [], [], [], []
    for q, (first, step) in enumerate(cuts):
        if q:
            near, far = backward_chunk(frozen, after(dgate, sums[-1][0]), dup, first, step)
            ahead = inner_moves[q - 1] + (outer_moves[q - 2] if q > 1 else [])
            far = lax.optimization_barrier((far, *ahead))[0]
        far = torus.move(far, 2, 1)
        sums.append(core_sum(near, far, side, side_far, at, first, b))
        inner_moves.append([torus.move(sums[q][k], 1, k) for k in range(1, b)])
        total = sums[q][0].astype(F32)
        for v in inner_moves[q]:
            total = total + v.astype(F32)
        inners.append(total.astype(BF16).reshape(a, rows, step))
        outer_moves.append([torus.move(inners[q][k], 0, k) for k in range(1, a)])
    grad_b = grad_b_part(outer_moves[-1][0])
    for q, inner in enumerate(inners):
        total = inner[0].astype(F32)
        for v in outer_moves[q]:
            v = lax.optimization_barrier((v, *inner_moves[-1]))[0] if q < len(cuts) - 1 else v
            total = total + v.astype(F32)
        blocks.append(total.astype(BF16))
    dinput = jnp.concatenate(blocks, axis=1)
    grad_a = grad_a_of(
        columns, order, after(low_out, sums[-1][0]), adapter[:, None], adapter_list
    )
    return (dinput, grad_a, grad_b)


def solution(mesh):
    placed = (
        P(("groups", "tensor"), None),
        P("groups", "tensor"),
        P(None, None, "tensor"),
        P(None, "tensor", None),
        P(None, None, "tensor"),
        P("groups", None),
        P("groups", None),
        P(),
    )
    return jax.shard_map(
        local,
        mesh=mesh,
        in_specs=placed,
        out_specs=(
            P(("groups", "tensor"), None),
            P("groups", "tensor", None),
            P("groups", None, "tensor"),
        ),
        check_vma=False,
    )
```

```python
import functools

import jax
import jax.numpy as jnp
from jax import lax
from jax.experimental import pallas as pl
from jax.experimental.pallas import tpu as pltpu
from jax.sharding import PartitionSpec as P

OUTER_SHARES = (3, 5)
INNER_CUTS = (1, 2)
SUM_SHARES = (4, 4)
MIB = 1024 * 1024
BF16 = jnp.bfloat16
DEPTH = 3
SLOTS = 4
ONCE = pl.Buffered(1)
F32 = jnp.float32


def dot(left, right, dims=((1,), (0,))):
    return lax.dot_general(left, right, (dims, ((), ())), preferred_element_type=F32)


def params(mib):
    return pltpu.CompilerParams(vmem_limit_bytes=mib * MIB)


def cost(flops, moved):
    return pl.CostEstimate(flops=int(flops), bytes_accessed=int(moved), transcendentals=0)


def tile_of(size, most):
    return most if size % most == 0 else size


def parts_of(count, parts):
    parts = min(parts, count)
    ends = [count * k // parts for k in range(parts + 1)]
    return list(zip(ends[:-1], ends[1:]))


def after(x, other):
    return lax.optimization_barrier((x, other))[0]


class Torus:
    def __init__(self, size):
        core = 2 if size % 2 == 0 else 1
        chips = size // core
        inner = 1
        while inner * 2 * inner * 2 <= chips and chips % (inner * 2) == 0:
            inner *= 2
        self.size = size
        self.dims = (chips // inner, inner, core)
        self.strides = (inner * core, core, 1)

    def place(self, index):
        return [index // s % n for s, n in zip(self.strides, self.dims)]

    def shifted(self, index, dim, by):
        at = index // self.strides[dim] % self.dims[dim]
        return index + ((at + by) % self.dims[dim] - at) * self.strides[dim]

    def move(self, x, dim, by):
        pairs = [(i, self.shifted(i, dim, by)) for i in range(self.size)]
        return lax.ppermute(x, "tensor", pairs)

    def gather(self, x, dim):
        return jnp.stack([x] + [self.move(x, dim, -k) for k in range(1, self.dims[dim])])

    def scatter_sum(self, x, dim):
        total = x[0].astype(F32)
        for k in range(1, self.dims[dim]):
            total = total + self.move(x[k], dim, k).astype(F32)
        return total

    def slot_devices(self, index):
        outer, inner, core = self.place(index)
        a, b, c = self.dims
        cs = lax.broadcasted_iota(jnp.int32, (c, b, a), 0)
        bs = lax.broadcasted_iota(jnp.int32, (c, b, a), 1)
        zs = lax.broadcasted_iota(jnp.int32, (c, b, a), 2)
        return (((outer + zs) % a * b + (inner + bs) % b) * c + (core + cs) % c).reshape(-1)

    def exchange_sum(self, x, dims, beside):
        beside = list(beside)
        for dim in dims:
            k = 1
            while k < self.dims[dim]:
                stride = self.strides[dim]
                pairs = [(i, i + ((i // stride ^ k) - i // stride) * stride) for i in range(self.size)]
                done = beside.pop(0)(x) if beside else None
                x = x + lax.ppermute(x, "tensor", pairs)
                x = x if done is None else after(x, done)
                k *= 2
        return x

    def slots_of(self, index):
        outer, inner, core = self.place(index)
        a, b, c = self.dims
        zs = lax.broadcasted_iota(jnp.int32, (a, b, c), 0)
        bs = lax.broadcasted_iota(jnp.int32, (a, b, c), 1)
        cs = lax.broadcasted_iota(jnp.int32, (a, b, c), 2)
        return (((cs - core) % c * b + (bs - inner) % b) * a + (zs - outer) % a).reshape(-1)


def tile_at(ref, n, tile):
    if ref.shape[1] == tile:
        return ref
    return ref.at[:, pl.ds(pl.multiple_of(n * tile, tile), tile)]


def ring(fetch, k, count):
    @pl.when(k == 0)
    def _():
        for j in range(min(DEPTH - 1, count)):
            for copy in fetch(j, j):
                copy.start()

    @pl.when(k + DEPTH - 1 < count)
    def _():
        for copy in fetch(k + DEPTH - 1, (k + DEPTH - 1) % DEPTH):
            copy.start()

    for copy in fetch(k, k % DEPTH):
        copy.wait()
    return k % DEPTH


def send(copy_of, k, count, fill):
    @pl.when(k >= SLOTS)
    def _():
        copy_of(k - SLOTS).wait()

    fill(k % SLOTS)
    copy_of(k).start()

    @pl.when(k == count - 1)
    def _():
        for j in range(min(SLOTS, count)):
            copy_of(k - j).wait()


def forward_kernel(pieces, low, count, first, *rest):
    parts, frozen, rest = rest[:pieces], rest[pieces], rest[pieces + 1 :]
    out, held, arrived = rest[-3:]
    step, tile = held.shape[2:]

    def fetch(n, slot):
        return [
            pltpu.make_async_copy(
                tile_at(frozen.at[i, pl.ds(first, step)], low + n, tile),
                held.at[slot, i],
                arrived.at[slot, i],
            )
            for i in range(2)
        ]

    slot = ring(fetch, pl.program_id(0), count)
    x = jnp.concatenate([v[...] for v in parts], axis=0)
    for i in range(2):
        part = dot(x, held[slot, i])
        out[i] = part if len(rest) == 3 else rest[0][i] + part


def forward_chunk(pieces, frozen, start, first, tiles):
    step = pieces[0].shape[1]
    tokens = sum(v.shape[0] for v in pieces)
    hidden = frozen.shape[2]
    tile = tile_of(hidden, 256)
    low, high = tiles
    across = pl.BlockSpec((2, tokens, tile), lambda n: (0, 0, low + n))
    operands = [*pieces, frozen]
    specs = [pl.BlockSpec(v.shape, lambda n: (0, 0), pipeline_mode=ONCE) for v in pieces]
    specs.append(pl.BlockSpec(memory_space=pltpu.HBM))
    if start is not None:
        operands.append(start)
        specs.append(across)
    count = high - low
    return pl.pallas_call(
        functools.partial(forward_kernel, len(pieces), low, count, first),
        grid=(count,),
        in_specs=specs,
        out_specs=across,
        out_shape=jax.ShapeDtypeStruct((2, tokens, hidden), F32),
        scratch_shapes=[
            pltpu.VMEM((DEPTH, 2, step, tile), BF16),
            pltpu.SemaphoreType.DMA((DEPTH, 2)),
        ],
        input_output_aliases={} if start is None else {len(operands) - 1: 0},
        compiler_params=params(24),
        cost_estimate=cost(4 * tokens * step * tile * count, 4 * step * tile * count),
    )(*operands)


def low_in_kernel(segments, chunks, rows, adapters, places, which, seg, *rest):
    factors, rest = rest[:segments], rest[segments:]
    cuts, (columns, out) = rest[:-2], rest[-2:]
    pieces = len(cuts) // chunks
    for q in range(chunks):

        @pl.when(which[0] == q)
        def _():
            first = 0
            for v in cuts[q * pieces : (q + 1) * pieces]:
                columns[first : first + v.shape[0]] = v[...]
                first += v.shape[0]

    total = jnp.zeros(out.shape, F32)
    for s in range(segments):
        part = dot(columns[...], factors[s][0])
        total = total + jnp.where(seg[...] == s, part, 0.0)
    put_rows(out, total, places, rows)


def put_rows(out, total, places, rows):
    if rows % 8:
        out[...] = total
        return
    for s in range(total.shape[0] // rows):
        out[pl.ds(pl.multiple_of(places[s] * rows, rows), rows), :] = total[s * rows : (s + 1) * rows]


def of_segment(shape, s):
    return pl.BlockSpec((1,) + shape[1:], lambda *a: (a[-2][s], 0, 0))


def low_in_partial(chunks, seg, down, adapters, places, index, rows):
    segments = adapters.shape[0]
    shard, wide = down.shape[1:]
    tokens = seg.shape[0]
    if shard % 128:
        joined = [jnp.concatenate(piece, axis=1) for piece in zip(*chunks)]
        chunks = [[lax.dynamic_slice_in_dim(v, index * shard, shard, 1) for v in joined]]
        which = jnp.zeros((1,), jnp.int32)
        cuts = [pl.BlockSpec(v.shape, lambda *a: (0, 0)) for v in chunks[0]]
    else:
        inside, at, cuts, first = [], [], [], 0
        for q, pieces in enumerate(chunks):
            per = pieces[0].shape[1] // shard
            inside.append(index >= first)
            at.append(jnp.clip(index - first, 0, per - 1))
            cuts += [
                pl.BlockSpec((v.shape[0], shard), lambda i, a, p, w, q=q: (0, w[1 + q])) for v in pieces
            ]
            first += per
        which = jnp.stack([sum(v.astype(jnp.int32) for v in inside) - 1] + at).astype(jnp.int32)
    full = lambda shape: pl.BlockSpec(shape, lambda *a: (0,) * len(shape))
    factor = lambda s: pl.BlockSpec((1, shard, wide), lambda i, a, p, w: (a[s], 0, 0))
    return pl.pallas_call(
        functools.partial(low_in_kernel, segments, len(chunks), rows),
        grid_spec=pltpu.PrefetchScalarGridSpec(
            num_scalar_prefetch=3,
            grid=(1,),
            in_specs=[full(seg.shape)] + [factor(s) for s in range(segments)] + cuts,
            out_specs=[full((tokens, shard)), full((tokens, wide))],
        ),
        out_shape=[
            jax.ShapeDtypeStruct((tokens, shard), BF16),
            jax.ShapeDtypeStruct((tokens, wide), F32),
        ],
        compiler_params=params(16),
        cost_estimate=cost(2 * tokens * down[0].size * segments, 2 * down[0].size * segments),
    )(adapters, places, which, seg, *([down] * segments), *[v for pieces in chunks for v in pieces])


def middle_kernel(rows, adapters, places, base, dhidden, token_order, order, low, seg, up, *rest):
    dgate, dup, out, left, back, factors, arrived = rest
    segments, wide, tile = factors.shape[1:]
    rank = wide // 2
    tokens = order.shape[0]
    n = pl.program_id(0)
    slot = n % 2
    lane = lax.broadcasted_iota(jnp.int32, (tokens, segments * rank), 1) // rank
    mask = lane == seg[...]

    def fetch(n, slot, s):
        return pltpu.make_async_copy(
            tile_at(up.at[adapters[s]], n, tile), factors.at[slot, s], arrived.at[slot, s]
        )

    @pl.when(n == 0)
    def _():
        for s in range(segments):
            fetch(0, 0, s).start()
        mine = dot(order[...], low[...])
        for i in range(2):
            block = jnp.concatenate([mine[:, i * rank : (i + 1) * rank]] * segments, axis=1)
            left[i] = jnp.where(mask, block, 0.0).astype(BF16)
        back[...] = jnp.zeros_like(back)

    @pl.when(n + 1 < pl.num_programs(0))
    def _():
        for s in range(segments):
            fetch(n + 1, 1 - slot, s).start()

    for s in range(segments):
        fetch(n, slot, s).wait()
    up_g = jnp.concatenate([factors[slot, s, :rank] for s in range(segments)], axis=0)
    up_u = jnp.concatenate([factors[slot, s, rank:] for s in range(segments)], axis=0)
    gate = base[0] + dot(left[0], up_g)
    up_sum = base[1] + dot(left[1], up_u)
    grad = dot(token_order[...], dhidden[...])
    sigma = 1.0 / (1.0 + jnp.exp(-gate))
    g = (grad * up_sum * sigma * (1.0 + gate * (1.0 - sigma))).astype(BF16)
    u = (grad * gate * sigma).astype(BF16)
    dgate[...] = g
    dup[...] = u
    back[0] += dot(g, up_g, ((1,), (1,)))
    back[1] += dot(u, up_u, ((1,), (1,)))

    @pl.when(n == pl.num_programs(0) - 1)
    def _():
        parts = []
        for i in range(2):
            kept = jnp.where(mask, back[i], 0.0)
            parts.append(sum(kept[:, s * rank : (s + 1) * rank] for s in range(segments)))
        put_rows(out, jnp.concatenate(parts, axis=1), places, rows)


def middle(base, dhidden, token_order, order, low, seg, up, adapters, places, rows):
    segments = adapters.shape[0]
    tokens, hidden = dhidden.shape
    wide = up.shape[1]
    tile = tile_of(hidden, 256)
    full = lambda shape: pl.BlockSpec(shape, lambda *a: (0,) * len(shape))
    across = lambda lead: pl.BlockSpec(lead + (tokens, tile), lambda n, *a: (0,) * len(lead) + (0, n))
    return pl.pallas_call(
        functools.partial(middle_kernel, rows),
        grid_spec=pltpu.PrefetchScalarGridSpec(
            num_scalar_prefetch=2,
            grid=(hidden // tile,),
            in_specs=[across((2,)), across(())]
            + [full(v.shape) for v in (token_order, order, low, seg)]
            + [pl.BlockSpec(memory_space=pltpu.HBM)],
            out_specs=[across(()), across(()), full((tokens, wide))],
            scratch_shapes=[
                pltpu.VMEM((2, tokens, segments * wide // 2), BF16),
                pltpu.VMEM((2, tokens, segments * wide // 2), F32),
                pltpu.VMEM((2, segments, wide, tile), BF16),
                pltpu.SemaphoreType.DMA((2, segments)),
            ],
        ),
        out_shape=[
            jax.ShapeDtypeStruct((tokens, hidden), BF16),
            jax.ShapeDtypeStruct((tokens, hidden), BF16),
            jax.ShapeDtypeStruct((tokens, wide), F32),
        ],
        compiler_params=params(20),
        cost_estimate=cost(
            4 * tokens * hidden * segments * wide, hidden * (tokens * 14 + segments * wide * 2)
        ),
    )(adapters, places, base, dhidden, token_order, order, low, seg, up)


def grad_b_kernel(first, count, dgate, dup, order, low, adapter, *rest):
    out, left, staged, sent = rest[-4:]
    group, wide, tile = staged.shape[1:]
    groups = left.shape[1]
    rank = wide // 2
    g = pl.program_id(1)
    k = pl.program_id(0) * groups + g

    @pl.when(k == 0)
    def _():
        turned = dot(order[...], low[...]).T
        for a in range(groups * group):
            kept = jnp.where(adapter[...] == a, turned, 0.0).astype(BF16)
            at = (a // group, slice(a % group * rank, (a % group + 1) * rank))
            left[(0, *at)] = kept[:rank]
            left[(1, *at)] = kept[rank:]

    def copy_of(k):
        block = out.at[pl.ds(k % groups * group, group)]
        if out.shape[2] != tile:
            at = pl.multiple_of((first + k // groups) * tile, tile)
            block = block.at[:, :, pl.ds(at, tile)]
        return pltpu.make_async_copy(staged.at[k % SLOTS], block, sent.at[k % SLOTS])

    def fill(slot):
        for i, grad in enumerate((dgate, dup)):
            part = dot(left[i, g], grad[...])
            staged[slot, :, i * rank : (i + 1) * rank, :] = part.reshape(group, rank, tile)

    send(copy_of, k, count * groups, fill)


def grad_b_of(dgate, dup, order, low, adapter_row, adapters, start, tiles):
    tokens, hidden = dgate.shape
    wide = low.shape[1]
    tile = tile_of(hidden, 256)
    first, last = tiles
    groups = 2 if adapters % 2 == 0 else 1
    group = adapters // groups
    full = lambda shape: pl.BlockSpec(shape, lambda n, g: (0,) * len(shape))
    across = pl.BlockSpec((tokens, tile), lambda n, g: (0, first + n))
    operands = [dgate, dup, order, low, adapter_row]
    specs = [across, across, full(order.shape), full(low.shape), full(adapter_row.shape)]
    if start is not None:
        operands.append(start)
        specs.append(pl.BlockSpec(memory_space=pltpu.HBM))
    part = tile * (last - first) * adapters * wide
    return pl.pallas_call(
        functools.partial(grad_b_kernel, first, last - first),
        grid=(last - first, groups),
        in_specs=specs,
        out_specs=pl.BlockSpec(memory_space=pltpu.HBM),
        out_shape=jax.ShapeDtypeStruct((adapters, wide, hidden), F32),
        scratch_shapes=[
            pltpu.VMEM((2, groups, group * wide // 2, tokens), BF16),
            pltpu.VMEM((SLOTS, group, wide, tile), F32),
            pltpu.SemaphoreType.DMA((SLOTS,)),
        ],
        input_output_aliases={} if start is None else {5: 0},
        compiler_params=params(20),
        cost_estimate=cost(2 * tokens * part, 4 * part),
    )(*operands)


def grad_a_kernel(columns, order, low, adapter, out, turned, mine, staged, sent):
    per = staged.shape[1]
    k = pl.program_id(0)

    @pl.when(k == 0)
    def _():
        turned[...] = columns[...].astype(F32).T.astype(BF16)
        mine[...] = dot(order[...], low[...])

    def copy_of(k):
        return pltpu.make_async_copy(
            staged.at[k % SLOTS], out.at[pl.ds(k * per, per)], sent.at[k % SLOTS]
        )

    def fill(slot):
        for j in range(per):
            kept = jnp.where(adapter[...] == k * per + j, mine[...], 0.0).astype(BF16)
            staged[slot, j] = dot(turned[...], kept)

    send(copy_of, k, out.shape[0] // per, fill)


def grad_a_of(columns, order, low, adapter, adapters):
    tokens, shard = columns.shape
    wide = low.shape[1]
    per = 4 if adapters % 4 == 0 else 1
    full = lambda shape: pl.BlockSpec(shape, lambda n: (0,) * len(shape))
    return pl.pallas_call(
        grad_a_kernel,
        grid=(adapters // per,),
        in_specs=[full(columns.shape), full(order.shape), full(low.shape), full(adapter.shape)],
        out_specs=pl.BlockSpec(memory_space=pltpu.HBM),
        out_shape=jax.ShapeDtypeStruct((adapters, shard, wide), F32),
        scratch_shapes=[
            pltpu.VMEM((shard, tokens), BF16),
            pltpu.VMEM((tokens, wide), F32),
            pltpu.VMEM((SLOTS, per, shard, wide), F32),
            pltpu.SemaphoreType.DMA((SLOTS,)),
        ],
        compiler_params=params(16),
        cost_estimate=cost(2 * tokens * shard * adapters * wide, 4 * shard * adapters * wide),
    )(columns, order, low, adapter)


def side_kernel(segments, adapters, places, order, low, seg, *rest):
    near, far = rest[-2:]
    half = near.shape[0]
    mine = dot(order[...], low[...])
    total = jnp.zeros((2 * half, near.shape[1]), F32)
    for s in range(segments):
        kept = jnp.where(seg[...] == s, mine, 0.0).astype(BF16)
        total = total + dot(kept, rest[s][0], ((1,), (1,)))
    near[...] = total[:half]
    far[...] = total[half:]


def side_of(order, low, seg, down, adapters, places):
    segments = adapters.shape[0]
    tokens = order.shape[0]
    shard = down.shape[1]
    full = lambda shape: pl.BlockSpec(shape, lambda *a: (0,) * len(shape))
    return pl.pallas_call(
        functools.partial(side_kernel, segments),
        grid_spec=pltpu.PrefetchScalarGridSpec(
            num_scalar_prefetch=2,
            grid=(1,),
            in_specs=[full(order.shape), full(low.shape), full(seg.shape)]
            + [of_segment(down.shape, s) for s in range(segments)],
            out_specs=[full((tokens // 2, shard))] * 2,
        ),
        out_shape=[jax.ShapeDtypeStruct((tokens // 2, shard), F32)] * 2,
        compiler_params=params(16),
        cost_estimate=cost(2 * tokens * down[0].size * segments, 2 * down[0].size * segments),
    )(adapters, places, order, low, seg, *([down] * segments))


def backward_kernel(count, first, frozen, dgate, dup, near, far, held, arrived):
    half = near.shape[0]
    block = held.shape[2]

    def fetch(k, slot):
        rows = pl.ds(pl.multiple_of(first + k * block, block), block)
        return [
            pltpu.make_async_copy(frozen.at[i, rows, :], held.at[slot, i], arrived.at[slot, i])
            for i in range(2)
        ]

    slot = ring(fetch, pl.program_id(0), count)
    term = dot(dgate[...], held[slot, 0], ((1,), (1,))) + dot(dup[...], held[slot, 1], ((1,), (1,)))
    near[...] = term[:half].astype(BF16)
    far[...] = term[half:].astype(BF16)


def backward_chunk(frozen, dgate, dup, first, step):
    tokens, hidden = dgate.shape
    block = tile_of(step, 512)
    count = step // block
    full = lambda shape: pl.BlockSpec(shape, lambda k: (0, 0), pipeline_mode=ONCE)
    out = pl.BlockSpec((tokens // 2, block), lambda k: (0, k))
    return pl.pallas_call(
        functools.partial(backward_kernel, count, first),
        grid=(count,),
        in_specs=[pl.BlockSpec(memory_space=pltpu.HBM), full(dgate.shape), full(dup.shape)],
        out_specs=[out, out],
        out_shape=[jax.ShapeDtypeStruct((tokens // 2, step), BF16)] * 2,
        scratch_shapes=[
            pltpu.VMEM((DEPTH, 2, block, hidden), BF16),
            pltpu.SemaphoreType.DMA((DEPTH, 2)),
        ],
        compiler_params=params(20),
        cost_estimate=cost(4 * tokens * step * hidden, 4 * step * hidden),
    )(frozen, dgate, dup)


def core_sum_kernel(base, at, near, far, side, side_far, *outs):
    total = near[...].astype(F32) + far[...].astype(F32)
    rows = outs[0].shape[0]
    own = at[0] == base + pl.program_id(0)

    def store(total):
        for s, out in enumerate(outs):
            out[...] = total[s * rows : (s + 1) * rows].astype(BF16)

    @pl.when(jnp.logical_not(own))
    def _():
        store(total)

    @pl.when(jnp.logical_and(own, at[1] == 0))
    def _():
        store(total + jnp.concatenate([side[...], side_far[...]], axis=1))

    @pl.when(jnp.logical_and(own, at[1] != 0))
    def _():
        store(total + jnp.concatenate([side_far[...], side[...]], axis=1))


def core_sum(near, far, side, side_far, at, first, slots):
    half, step = near.shape
    block = 2 * side.shape[1]
    full = lambda shape: pl.BlockSpec(shape, lambda *a: (0,) * len(shape))
    across = lambda rows: pl.BlockSpec((rows, block), lambda k, at: (0, k))
    return pl.pallas_call(
        functools.partial(core_sum_kernel, first // block),
        grid_spec=pltpu.PrefetchScalarGridSpec(
            num_scalar_prefetch=1,
            grid=(step // block,),
            in_specs=[across(half), across(half), full(side.shape), full(side_far.shape)],
            out_specs=[across(half // slots)] * slots,
        ),
        out_shape=[jax.ShapeDtypeStruct((half // slots, step), BF16)] * slots,
        compiler_params=params(16),
        cost_estimate=cost(2 * half * step, 6 * half * step),
    )(at, near, far, side, side_far)


def local(
    activations,
    dhidden,
    frozen,
    adapter_down_factors,
    adapter_up_factors,
    segment_adapter_index,
    segment_row_counts,
    ranks,
):
    adapter_list, shard_width, gate_and_up = adapter_down_factors.shape
    rank = gate_and_up // 2
    width = frozen.shape[1]
    rows = activations.shape[0]
    torus = Torus(width // shard_width)
    tokens = rows * torus.size
    a, b, c = torus.dims
    index = lax.axis_index("tensor")
    slots = torus.slot_devices(index)
    token = (slots[:, None] * rows + jnp.arange(rows, dtype=jnp.int32)[None, :]).reshape(-1)

    ends = jnp.cumsum(segment_row_counts[0])
    seg_adapter = segment_adapter_index[0]
    count = ends.shape[0]

    def segment_of(place):
        return jnp.sum((place[:, None] >= ends[None, :]).astype(jnp.int32), axis=1)

    def adapter_of(segment):
        match = segment[:, None] == jnp.arange(count, dtype=jnp.int32)[None, :]
        return jnp.sum(jnp.where(match, seg_adapter[None, :], 0), axis=1)

    column = jnp.arange(gate_and_up, dtype=jnp.int32) % rank
    chips = a * b
    core = index % c
    mine = (jnp.arange(chips, dtype=jnp.int32)[:, None] * c + core) * rows
    mine = (mine + jnp.arange(rows, dtype=jnp.int32)[None, :]).reshape(-1)
    my_adapter = adapter_of(segment_of(mine))
    hit = my_adapter[:, None] == jnp.arange(adapter_list, dtype=jnp.int32)[None, :]
    my_rank = jnp.sum(jnp.where(hit, ranks[None, :], 0), axis=1)[:, None]
    factor = jnp.where(column[None, :] < my_rank, 16.0 / my_rank.astype(F32), 0.0)

    places = (slots % c - core) % c * chips + slots // c
    spot = (places[:, None] * rows + jnp.arange(rows, dtype=jnp.int32)[None, :]).reshape(-1)
    count_up = jnp.arange(tokens, dtype=jnp.int32)[None, :]
    token_order = (token[:, None] == count_up).astype(BF16)
    order = (spot[:, None] == count_up).astype(BF16)

    segment = segment_of(token)
    adapter = adapter_of(segment)

    def whole_sum(partial, beside=()):
        if rows % 8:
            at = jnp.arange(torus.size, dtype=jnp.int32)
            device = at % chips * c + (core + at // chips) % c
            partial = jnp.take(
                partial.reshape(torus.size, rows, -1),
                jnp.take(torus.slots_of(index), device),
                axis=0,
            )
        x = torus.scatter_sum(partial.reshape(c, chips * rows, gate_and_up), 2)
        x = torus.exchange_sum(x, (1, 0), beside)
        return torus.gather((x * factor).astype(BF16), 2).reshape(tokens, gate_and_up)

    hidden = frozen.shape[2]
    tiles = hidden // tile_of(hidden, 256)
    chunks = []
    for share in OUTER_SHARES:
        first = sum(v.shape[1] for v in chunks)
        chunks.append(activations[:, first : first + width * share // sum(OUTER_SHARES)])
    outer = []
    for x in chunks:
        x = torus.gather(after(x, outer[-1]) if outer else x, 0)
        outer.append(x.reshape(a * rows, -1))
    parts = []
    for x, cuts in zip(outer, INNER_CUTS):
        step = x.shape[1] // cuts
        parts += [x[:, j * step : (j + 1) * step] for j in range(cuts)]
    base = None
    gathered = []
    first = 0
    for q, x in enumerate(parts):
        near = [x] + [torus.move(x, 1, -k) for k in range(1, b)]
        near[1:] = lax.optimization_barrier((*near[1:], base if q else outer[-1]))[:-1]
        far = [torus.move(v, 2, -1) for v in near]
        gathered.append([*near, *far])
        for cut in parts_of(tiles, 4 if q == len(parts) - 1 else 1):
            base = forward_chunk(gathered[q], frozen, base, first, cut)
        first += x.shape[1]

    columns, partial_in = low_in_partial(
        gathered, segment[:, None], adapter_down_factors, seg_adapter, places, index, rows
    )
    low_in = whole_sum(partial_in)
    dgate, dup, partial_out = middle(
        base, dhidden, token_order, order, low_in, segment[:, None], adapter_up_factors,
        seg_adapter, places, rows,
    )
    thirds = parts_of(tiles, 3)
    grad_b = []

    def grad_b_part(token):
        grad_b.append(
            grad_b_of(
                dgate, dup, order, after(low_in, token), adapter[None, :], adapter_list,
                grad_b[-1] if grad_b else None, thirds[len(grad_b)],
            )
        )
        return grad_b[-1]

    cuts = []
    for share in SUM_SHARES:
        cuts.append((sum(v[1] for v in cuts), width * share // sum(SUM_SHARES)))
    terms = []

    def first_term(token):
        terms.append(backward_chunk(frozen, after(dgate, token), dup, *cuts[0]))
        return terms[0][0]

    low_out = whole_sum(partial_out, [grad_b_part] * (len(thirds) - 1) + [first_term])
    near, far = terms[0][0], after(terms[0][1], low_out)
    side, side_far = side_of(
        order, low_out, segment[:, None], adapter_down_factors, seg_adapter, places
    )
    side_far = torus.move(side_far, 2, 1)
    at = jnp.stack([index // c, core]).astype(jnp.int32)
    sums, inners, inner_moves, outer_moves, blocks = [], [], [], [], []
    for q, (first, step) in enumerate(cuts):
        if q:
            near, far = backward_chunk(frozen, after(dgate, sums[-1][0]), dup, first, step)
            ahead = inner_moves[q - 1] + (outer_moves[q - 2] if q > 1 else [])
            far = lax.optimization_barrier((far, *ahead))[0]
        far = torus.move(far, 2, 1)
        sums.append(core_sum(near, far, side, side_far, at, first, b))
        inner_moves.append([torus.move(sums[q][k], 1, k) for k in range(1, b)])
        total = sums[q][0].astype(F32)
        for v in inner_moves[q]:
            total = total + v.astype(F32)
        inners.append(total.astype(BF16).reshape(a, rows, step))
        outer_moves.append([torus.move(inners[q][k], 0, k) for k in range(1, a)])
    grad_b = grad_b_part(outer_moves[-1][0])
    for q, inner in enumerate(inners):
        total = inner[0].astype(F32)
        for v in outer_moves[q]:
            v = lax.optimization_barrier((v, *inner_moves[-1]))[0] if q < len(cuts) - 1 else v
            total = total + v.astype(F32)
        blocks.append(total.astype(BF16))
    dinput = jnp.concatenate(blocks, axis=1)
    grad_a = grad_a_of(
        columns, order, after(low_out, sums[-1][0]), adapter[:, None], adapter_list
    )
    return (dinput, grad_a, grad_b)


def solution(mesh):
    placed = (
        P(("groups", "tensor"), None),
        P("groups", "tensor"),
        P(None, None, "tensor"),
        P(None, "tensor", None),
        P(None, None, "tensor"),
        P("groups", None),
        P("groups", None),
        P(),
    )
    return jax.shard_map(
        local,
        mesh=mesh,
        in_specs=placed,
        out_specs=(
            P(("groups", "tensor"), None),
            P("groups", "tensor", None),
            P("groups", None, "tensor"),
        ),
        check_vma=False,
    )
```

```python
import functools

import jax
import jax.numpy as jnp
from jax import lax
from jax.experimental import pallas as pl
from jax.experimental.pallas import tpu as pltpu
from jax.sharding import PartitionSpec as P

OUTER_SHARES = (3, 5)
INNER_CUTS = (1, 2)
SUM_SHARES = (5, 3)
MIB = 1024 * 1024
BF16 = jnp.bfloat16
DEPTH = 3
SLOTS = 4
ONCE = pl.Buffered(1)
F32 = jnp.float32


def dot(left, right, dims=((1,), (0,))):
    return lax.dot_general(left, right, (dims, ((), ())), preferred_element_type=F32)


def params(mib):
    return pltpu.CompilerParams(vmem_limit_bytes=mib * MIB)


def cost(flops, moved):
    return pl.CostEstimate(flops=int(flops), bytes_accessed=int(moved), transcendentals=0)


def tile_of(size, most):
    return most if size % most == 0 else size


def parts_of(count, parts):
    parts = min(parts, count)
    ends = [count * k // parts for k in range(parts + 1)]
    return list(zip(ends[:-1], ends[1:]))


def after(x, other):
    return lax.optimization_barrier((x, other))[0]


class Torus:
    def __init__(self, size):
        core = 2 if size % 2 == 0 else 1
        chips = size // core
        inner = 1
        while inner * 2 * inner * 2 <= chips and chips % (inner * 2) == 0:
            inner *= 2
        self.size = size
        self.dims = (chips // inner, inner, core)
        self.strides = (inner * core, core, 1)

    def place(self, index):
        return [index // s % n for s, n in zip(self.strides, self.dims)]

    def shifted(self, index, dim, by):
        at = index // self.strides[dim] % self.dims[dim]
        return index + ((at + by) % self.dims[dim] - at) * self.strides[dim]

    def move(self, x, dim, by):
        pairs = [(i, self.shifted(i, dim, by)) for i in range(self.size)]
        return lax.ppermute(x, "tensor", pairs)

    def gather(self, x, dim):
        return jnp.stack([x] + [self.move(x, dim, -k) for k in range(1, self.dims[dim])])

    def scatter_sum(self, x, dim):
        total = x[0].astype(F32)
        for k in range(1, self.dims[dim]):
            total = total + self.move(x[k], dim, k).astype(F32)
        return total

    def slot_devices(self, index):
        outer, inner, core = self.place(index)
        a, b, c = self.dims
        cs = lax.broadcasted_iota(jnp.int32, (c, b, a), 0)
        bs = lax.broadcasted_iota(jnp.int32, (c, b, a), 1)
        zs = lax.broadcasted_iota(jnp.int32, (c, b, a), 2)
        return (((outer + zs) % a * b + (inner + bs) % b) * c + (core + cs) % c).reshape(-1)

    def exchange_sum(self, x, dims, beside):
        beside = list(beside)
        for dim in dims:
            k = 1
            while k < self.dims[dim]:
                stride = self.strides[dim]
                pairs = [(i, i + ((i // stride ^ k) - i // stride) * stride) for i in range(self.size)]
                done = beside.pop(0)(x) if beside else None
                x = x + lax.ppermute(x, "tensor", pairs)
                x = x if done is None else after(x, done)
                k *= 2
        return x

    def slots_of(self, index):
        outer, inner, core = self.place(index)
        a, b, c = self.dims
        zs = lax.broadcasted_iota(jnp.int32, (a, b, c), 0)
        bs = lax.broadcasted_iota(jnp.int32, (a, b, c), 1)
        cs = lax.broadcasted_iota(jnp.int32, (a, b, c), 2)
        return (((cs - core) % c * b + (bs - inner) % b) * a + (zs - outer) % a).reshape(-1)


def tile_at(ref, n, tile):
    if ref.shape[1] == tile:
        return ref
    return ref.at[:, pl.ds(pl.multiple_of(n * tile, tile), tile)]


def ring(fetch, k, count):
    @pl.when(k == 0)
    def _():
        for j in range(min(DEPTH - 1, count)):
            for copy in fetch(j, j):
                copy.start()

    @pl.when(k + DEPTH - 1 < count)
    def _():
        for copy in fetch(k + DEPTH - 1, (k + DEPTH - 1) % DEPTH):
            copy.start()

    for copy in fetch(k, k % DEPTH):
        copy.wait()
    return k % DEPTH


def send(copy_of, k, count, fill):
    @pl.when(k >= SLOTS)
    def _():
        copy_of(k - SLOTS).wait()

    fill(k % SLOTS)
    copy_of(k).start()

    @pl.when(k == count - 1)
    def _():
        for j in range(min(SLOTS, count)):
            copy_of(k - j).wait()


def forward_kernel(pieces, low, count, first, *rest):
    parts, frozen, rest = rest[:pieces], rest[pieces], rest[pieces + 1 :]
    out, held, arrived = rest[-3:]
    step, tile = held.shape[2:]

    def fetch(n, slot):
        return [
            pltpu.make_async_copy(
                tile_at(frozen.at[i, pl.ds(first, step)], low + n, tile),
                held.at[slot, i],
                arrived.at[slot, i],
            )
            for i in range(2)
        ]

    slot = ring(fetch, pl.program_id(0), count)
    x = jnp.concatenate([v[...] for v in parts], axis=0)
    for i in range(2):
        part = dot(x, held[slot, i])
        out[i] = part if len(rest) == 3 else rest[0][i] + part


def forward_chunk(pieces, frozen, start, first, tiles):
    step = pieces[0].shape[1]
    tokens = sum(v.shape[0] for v in pieces)
    hidden = frozen.shape[2]
    tile = tile_of(hidden, 256)
    low, high = tiles
    across = pl.BlockSpec((2, tokens, tile), lambda n: (0, 0, low + n))
    operands = [*pieces, frozen]
    specs = [pl.BlockSpec(v.shape, lambda n: (0, 0), pipeline_mode=ONCE) for v in pieces]
    specs.append(pl.BlockSpec(memory_space=pltpu.HBM))
    if start is not None:
        operands.append(start)
        specs.append(across)
    count = high - low
    return pl.pallas_call(
        functools.partial(forward_kernel, len(pieces), low, count, first),
        grid=(count,),
        in_specs=specs,
        out_specs=across,
        out_shape=jax.ShapeDtypeStruct((2, tokens, hidden), F32),
        scratch_shapes=[
            pltpu.VMEM((DEPTH, 2, step, tile), BF16),
            pltpu.SemaphoreType.DMA((DEPTH, 2)),
        ],
        input_output_aliases={} if start is None else {len(operands) - 1: 0},
        compiler_params=params(24),
        cost_estimate=cost(4 * tokens * step * tile * count, 4 * step * tile * count),
    )(*operands)


def low_in_kernel(segments, chunks, rows, adapters, places, which, seg, *rest):
    factors, rest = rest[:segments], rest[segments:]
    cuts, (columns, out) = rest[:-2], rest[-2:]
    pieces = len(cuts) // chunks
    for q in range(chunks):

        @pl.when(which[0] == q)
        def _():
            first = 0
            for v in cuts[q * pieces : (q + 1) * pieces]:
                columns[first : first + v.shape[0]] = v[...]
                first += v.shape[0]

    total = jnp.zeros(out.shape, F32)
    for s in range(segments):
        part = dot(columns[...], factors[s][0])
        total = total + jnp.where(seg[...] == s, part, 0.0)
    put_rows(out, total, places, rows)


def put_rows(out, total, places, rows):
    if rows % 8:
        out[...] = total
        return
    for s in range(total.shape[0] // rows):
        out[pl.ds(pl.multiple_of(places[s] * rows, rows), rows), :] = total[s * rows : (s + 1) * rows]


def of_segment(shape, s):
    return pl.BlockSpec((1,) + shape[1:], lambda *a: (a[-2][s], 0, 0))


def low_in_partial(chunks, seg, down, adapters, places, index, rows):
    segments = adapters.shape[0]
    shard, wide = down.shape[1:]
    tokens = seg.shape[0]
    if shard % 128:
        joined = [jnp.concatenate(piece, axis=1) for piece in zip(*chunks)]
        chunks = [[lax.dynamic_slice_in_dim(v, index * shard, shard, 1) for v in joined]]
        which = jnp.zeros((1,), jnp.int32)
        cuts = [pl.BlockSpec(v.shape, lambda *a: (0, 0)) for v in chunks[0]]
    else:
        inside, at, cuts, first = [], [], [], 0
        for q, pieces in enumerate(chunks):
            per = pieces[0].shape[1] // shard
            inside.append(index >= first)
            at.append(jnp.clip(index - first, 0, per - 1))
            cuts += [
                pl.BlockSpec((v.shape[0], shard), lambda i, a, p, w, q=q: (0, w[1 + q])) for v in pieces
            ]
            first += per
        which = jnp.stack([sum(v.astype(jnp.int32) for v in inside) - 1] + at).astype(jnp.int32)
    full = lambda shape: pl.BlockSpec(shape, lambda *a: (0,) * len(shape))
    factor = lambda s: pl.BlockSpec((1, shard, wide), lambda i, a, p, w: (a[s], 0, 0))
    return pl.pallas_call(
        functools.partial(low_in_kernel, segments, len(chunks), rows),
        grid_spec=pltpu.PrefetchScalarGridSpec(
            num_scalar_prefetch=3,
            grid=(1,),
            in_specs=[full(seg.shape)] + [factor(s) for s in range(segments)] + cuts,
            out_specs=[full((tokens, shard)), full((tokens, wide))],
        ),
        out_shape=[
            jax.ShapeDtypeStruct((tokens, shard), BF16),
            jax.ShapeDtypeStruct((tokens, wide), F32),
        ],
        compiler_params=params(16),
        cost_estimate=cost(2 * tokens * down[0].size * segments, 2 * down[0].size * segments),
    )(adapters, places, which, seg, *([down] * segments), *[v for pieces in chunks for v in pieces])


def middle_kernel(rows, adapters, places, base, dhidden, token_order, order, low, seg, up, *rest):
    dgate, dup, out, left, back, factors, arrived = rest
    segments, wide, tile = factors.shape[1:]
    rank = wide // 2
    tokens = order.shape[0]
    n = pl.program_id(0)
    slot = n % 2
    lane = lax.broadcasted_iota(jnp.int32, (tokens, segments * rank), 1) // rank
    mask = lane == seg[...]

    def fetch(n, slot, s):
        return pltpu.make_async_copy(
            tile_at(up.at[adapters[s]], n, tile), factors.at[slot, s], arrived.at[slot, s]
        )

    @pl.when(n == 0)
    def _():
        for s in range(segments):
            fetch(0, 0, s).start()
        mine = dot(order[...], low[...])
        for i in range(2):
            block = jnp.concatenate([mine[:, i * rank : (i + 1) * rank]] * segments, axis=1)
            left[i] = jnp.where(mask, block, 0.0).astype(BF16)
        back[...] = jnp.zeros_like(back)

    @pl.when(n + 1 < pl.num_programs(0))
    def _():
        for s in range(segments):
            fetch(n + 1, 1 - slot, s).start()

    for s in range(segments):
        fetch(n, slot, s).wait()
    up_g = jnp.concatenate([factors[slot, s, :rank] for s in range(segments)], axis=0)
    up_u = jnp.concatenate([factors[slot, s, rank:] for s in range(segments)], axis=0)
    gate = base[0] + dot(left[0], up_g)
    up_sum = base[1] + dot(left[1], up_u)
    grad = dot(token_order[...], dhidden[...])
    sigma = 1.0 / (1.0 + jnp.exp(-gate))
    g = (grad * up_sum * sigma * (1.0 + gate * (1.0 - sigma))).astype(BF16)
    u = (grad * gate * sigma).astype(BF16)
    dgate[...] = g
    dup[...] = u
    back[0] += dot(g, up_g, ((1,), (1,)))
    back[1] += dot(u, up_u, ((1,), (1,)))

    @pl.when(n == pl.num_programs(0) - 1)
    def _():
        parts = []
        for i in range(2):
            kept = jnp.where(mask, back[i], 0.0)
            parts.append(sum(kept[:, s * rank : (s + 1) * rank] for s in range(segments)))
        put_rows(out, jnp.concatenate(parts, axis=1), places, rows)


def middle(base, dhidden, token_order, order, low, seg, up, adapters, places, rows):
    segments = adapters.shape[0]
    tokens, hidden = dhidden.shape
    wide = up.shape[1]
    tile = tile_of(hidden, 256)
    full = lambda shape: pl.BlockSpec(shape, lambda *a: (0,) * len(shape))
    across = lambda lead: pl.BlockSpec(lead + (tokens, tile), lambda n, *a: (0,) * len(lead) + (0, n))
    return pl.pallas_call(
        functools.partial(middle_kernel, rows),
        grid_spec=pltpu.PrefetchScalarGridSpec(
            num_scalar_prefetch=2,
            grid=(hidden // tile,),
            in_specs=[across((2,)), across(())]
            + [full(v.shape) for v in (token_order, order, low, seg)]
            + [pl.BlockSpec(memory_space=pltpu.HBM)],
            out_specs=[across(()), across(()), full((tokens, wide))],
            scratch_shapes=[
                pltpu.VMEM((2, tokens, segments * wide // 2), BF16),
                pltpu.VMEM((2, tokens, segments * wide // 2), F32),
                pltpu.VMEM((2, segments, wide, tile), BF16),
                pltpu.SemaphoreType.DMA((2, segments)),
            ],
        ),
        out_shape=[
            jax.ShapeDtypeStruct((tokens, hidden), BF16),
            jax.ShapeDtypeStruct((tokens, hidden), BF16),
            jax.ShapeDtypeStruct((tokens, wide), F32),
        ],
        compiler_params=params(20),
        cost_estimate=cost(
            4 * tokens * hidden * segments * wide, hidden * (tokens * 14 + segments * wide * 2)
        ),
    )(adapters, places, base, dhidden, token_order, order, low, seg, up)


def grad_b_kernel(first, count, dgate, dup, order, low, adapter, *rest):
    out, left, staged, sent = rest[-4:]
    group, wide, tile = staged.shape[1:]
    groups = left.shape[1]
    rank = wide // 2
    g = pl.program_id(1)
    k = pl.program_id(0) * groups + g

    @pl.when(k == 0)
    def _():
        turned = dot(order[...], low[...]).T
        for a in range(groups * group):
            kept = jnp.where(adapter[...] == a, turned, 0.0).astype(BF16)
            at = (a // group, slice(a % group * rank, (a % group + 1) * rank))
            left[(0, *at)] = kept[:rank]
            left[(1, *at)] = kept[rank:]

    def copy_of(k):
        block = out.at[pl.ds(k % groups * group, group)]
        if out.shape[2] != tile:
            at = pl.multiple_of((first + k // groups) * tile, tile)
            block = block.at[:, :, pl.ds(at, tile)]
        return pltpu.make_async_copy(staged.at[k % SLOTS], block, sent.at[k % SLOTS])

    def fill(slot):
        for i, grad in enumerate((dgate, dup)):
            part = dot(left[i, g], grad[...])
            staged[slot, :, i * rank : (i + 1) * rank, :] = part.reshape(group, rank, tile)

    send(copy_of, k, count * groups, fill)


def grad_b_of(dgate, dup, order, low, adapter_row, adapters, start, tiles):
    tokens, hidden = dgate.shape
    wide = low.shape[1]
    tile = tile_of(hidden, 256)
    first, last = tiles
    groups = 2 if adapters % 2 == 0 else 1
    group = adapters // groups
    full = lambda shape: pl.BlockSpec(shape, lambda n, g: (0,) * len(shape))
    across = pl.BlockSpec((tokens, tile), lambda n, g: (0, first + n))
    operands = [dgate, dup, order, low, adapter_row]
    specs = [across, across, full(order.shape), full(low.shape), full(adapter_row.shape)]
    if start is not None:
        operands.append(start)
        specs.append(pl.BlockSpec(memory_space=pltpu.HBM))
    part = tile * (last - first) * adapters * wide
    return pl.pallas_call(
        functools.partial(grad_b_kernel, first, last - first),
        grid=(last - first, groups),
        in_specs=specs,
        out_specs=pl.BlockSpec(memory_space=pltpu.HBM),
        out_shape=jax.ShapeDtypeStruct((adapters, wide, hidden), F32),
        scratch_shapes=[
            pltpu.VMEM((2, groups, group * wide // 2, tokens), BF16),
            pltpu.VMEM((SLOTS, group, wide, tile), F32),
            pltpu.SemaphoreType.DMA((SLOTS,)),
        ],
        input_output_aliases={} if start is None else {5: 0},
        compiler_params=params(20),
        cost_estimate=cost(2 * tokens * part, 4 * part),
    )(*operands)


def grad_a_kernel(columns, order, low, adapter, out, turned, mine, staged, sent):
    per = staged.shape[1]
    k = pl.program_id(0)

    @pl.when(k == 0)
    def _():
        turned[...] = columns[...].astype(F32).T.astype(BF16)
        mine[...] = dot(order[...], low[...])

    def copy_of(k):
        return pltpu.make_async_copy(
            staged.at[k % SLOTS], out.at[pl.ds(k * per, per)], sent.at[k % SLOTS]
        )

    def fill(slot):
        for j in range(per):
            kept = jnp.where(adapter[...] == k * per + j, mine[...], 0.0).astype(BF16)
            staged[slot, j] = dot(turned[...], kept)

    send(copy_of, k, out.shape[0] // per, fill)


def grad_a_of(columns, order, low, adapter, adapters):
    tokens, shard = columns.shape
    wide = low.shape[1]
    per = 4 if adapters % 4 == 0 else 1
    full = lambda shape: pl.BlockSpec(shape, lambda n: (0,) * len(shape))
    return pl.pallas_call(
        grad_a_kernel,
        grid=(adapters // per,),
        in_specs=[full(columns.shape), full(order.shape), full(low.shape), full(adapter.shape)],
        out_specs=pl.BlockSpec(memory_space=pltpu.HBM),
        out_shape=jax.ShapeDtypeStruct((adapters, shard, wide), F32),
        scratch_shapes=[
            pltpu.VMEM((shard, tokens), BF16),
            pltpu.VMEM((tokens, wide), F32),
            pltpu.VMEM((SLOTS, per, shard, wide), F32),
            pltpu.SemaphoreType.DMA((SLOTS,)),
        ],
        compiler_params=params(16),
        cost_estimate=cost(2 * tokens * shard * adapters * wide, 4 * shard * adapters * wide),
    )(columns, order, low, adapter)


def side_kernel(segments, adapters, places, order, low, seg, *rest):
    near, far = rest[-2:]
    half = near.shape[0]
    mine = dot(order[...], low[...])
    total = jnp.zeros((2 * half, near.shape[1]), F32)
    for s in range(segments):
        kept = jnp.where(seg[...] == s, mine, 0.0).astype(BF16)
        total = total + dot(kept, rest[s][0], ((1,), (1,)))
    near[...] = total[:half]
    far[...] = total[half:]


def side_of(order, low, seg, down, adapters, places):
    segments = adapters.shape[0]
    tokens = order.shape[0]
    shard = down.shape[1]
    full = lambda shape: pl.BlockSpec(shape, lambda *a: (0,) * len(shape))
    return pl.pallas_call(
        functools.partial(side_kernel, segments),
        grid_spec=pltpu.PrefetchScalarGridSpec(
            num_scalar_prefetch=2,
            grid=(1,),
            in_specs=[full(order.shape), full(low.shape), full(seg.shape)]
            + [of_segment(down.shape, s) for s in range(segments)],
            out_specs=[full((tokens // 2, shard))] * 2,
        ),
        out_shape=[jax.ShapeDtypeStruct((tokens // 2, shard), F32)] * 2,
        compiler_params=params(16),
        cost_estimate=cost(2 * tokens * down[0].size * segments, 2 * down[0].size * segments),
    )(adapters, places, order, low, seg, *([down] * segments))


def backward_kernel(count, first, frozen, dgate, dup, near, far, held, arrived):
    half = near.shape[0]
    block = held.shape[2]

    def fetch(k, slot):
        rows = pl.ds(pl.multiple_of(first + k * block, block), block)
        return [
            pltpu.make_async_copy(frozen.at[i, rows, :], held.at[slot, i], arrived.at[slot, i])
            for i in range(2)
        ]

    slot = ring(fetch, pl.program_id(0), count)
    term = dot(dgate[...], held[slot, 0], ((1,), (1,))) + dot(dup[...], held[slot, 1], ((1,), (1,)))
    near[...] = term[:half].astype(BF16)
    far[...] = term[half:].astype(BF16)


def backward_chunk(frozen, dgate, dup, first, step):
    tokens, hidden = dgate.shape
    block = tile_of(step, 512)
    count = step // block
    full = lambda shape: pl.BlockSpec(shape, lambda k: (0, 0), pipeline_mode=ONCE)
    out = pl.BlockSpec((tokens // 2, block), lambda k: (0, k))
    return pl.pallas_call(
        functools.partial(backward_kernel, count, first),
        grid=(count,),
        in_specs=[pl.BlockSpec(memory_space=pltpu.HBM), full(dgate.shape), full(dup.shape)],
        out_specs=[out, out],
        out_shape=[jax.ShapeDtypeStruct((tokens // 2, step), BF16)] * 2,
        scratch_shapes=[
            pltpu.VMEM((DEPTH, 2, block, hidden), BF16),
            pltpu.SemaphoreType.DMA((DEPTH, 2)),
        ],
        compiler_params=params(20),
        cost_estimate=cost(4 * tokens * step * hidden, 4 * step * hidden),
    )(frozen, dgate, dup)


def core_sum_kernel(base, at, near, far, side, side_far, *outs):
    total = near[...].astype(F32) + far[...].astype(F32)
    rows = outs[0].shape[0]
    own = at[0] == base + pl.program_id(0)

    def store(total):
        for s, out in enumerate(outs):
            out[...] = total[s * rows : (s + 1) * rows].astype(BF16)

    @pl.when(jnp.logical_not(own))
    def _():
        store(total)

    @pl.when(jnp.logical_and(own, at[1] == 0))
    def _():
        store(total + jnp.concatenate([side[...], side_far[...]], axis=1))

    @pl.when(jnp.logical_and(own, at[1] != 0))
    def _():
        store(total + jnp.concatenate([side_far[...], side[...]], axis=1))


def core_sum(near, far, side, side_far, at, first, slots):
    half, step = near.shape
    block = 2 * side.shape[1]
    full = lambda shape: pl.BlockSpec(shape, lambda *a: (0,) * len(shape))
    across = lambda rows: pl.BlockSpec((rows, block), lambda k, at: (0, k))
    return pl.pallas_call(
        functools.partial(core_sum_kernel, first // block),
        grid_spec=pltpu.PrefetchScalarGridSpec(
            num_scalar_prefetch=1,
            grid=(step // block,),
            in_specs=[across(half), across(half), full(side.shape), full(side_far.shape)],
            out_specs=[across(half // slots)] * slots,
        ),
        out_shape=[jax.ShapeDtypeStruct((half // slots, step), BF16)] * slots,
        compiler_params=params(16),
        cost_estimate=cost(2 * half * step, 6 * half * step),
    )(at, near, far, side, side_far)


def local(
    activations,
    dhidden,
    frozen,
    adapter_down_factors,
    adapter_up_factors,
    segment_adapter_index,
    segment_row_counts,
    ranks,
):
    adapter_list, shard_width, gate_and_up = adapter_down_factors.shape
    rank = gate_and_up // 2
    width = frozen.shape[1]
    rows = activations.shape[0]
    torus = Torus(width // shard_width)
    tokens = rows * torus.size
    a, b, c = torus.dims
    index = lax.axis_index("tensor")
    slots = torus.slot_devices(index)
    token = (slots[:, None] * rows + jnp.arange(rows, dtype=jnp.int32)[None, :]).reshape(-1)

    ends = jnp.cumsum(segment_row_counts[0])
    seg_adapter = segment_adapter_index[0]
    count = ends.shape[0]

    def segment_of(place):
        return jnp.sum((place[:, None] >= ends[None, :]).astype(jnp.int32), axis=1)

    def adapter_of(segment):
        match = segment[:, None] == jnp.arange(count, dtype=jnp.int32)[None, :]
        return jnp.sum(jnp.where(match, seg_adapter[None, :], 0), axis=1)

    column = jnp.arange(gate_and_up, dtype=jnp.int32) % rank
    chips = a * b
    core = index % c
    mine = (jnp.arange(chips, dtype=jnp.int32)[:, None] * c + core) * rows
    mine = (mine + jnp.arange(rows, dtype=jnp.int32)[None, :]).reshape(-1)
    my_adapter = adapter_of(segment_of(mine))
    hit = my_adapter[:, None] == jnp.arange(adapter_list, dtype=jnp.int32)[None, :]
    my_rank = jnp.sum(jnp.where(hit, ranks[None, :], 0), axis=1)[:, None]
    factor = jnp.where(column[None, :] < my_rank, 16.0 / my_rank.astype(F32), 0.0)

    places = (slots % c - core) % c * chips + slots // c
    spot = (places[:, None] * rows + jnp.arange(rows, dtype=jnp.int32)[None, :]).reshape(-1)
    count_up = jnp.arange(tokens, dtype=jnp.int32)[None, :]
    token_order = (token[:, None] == count_up).astype(BF16)
    order = (spot[:, None] == count_up).astype(BF16)

    segment = segment_of(token)
    adapter = adapter_of(segment)

    def whole_sum(partial, beside=()):
        if rows % 8:
            at = jnp.arange(torus.size, dtype=jnp.int32)
            device = at % chips * c + (core + at // chips) % c
            partial = jnp.take(
                partial.reshape(torus.size, rows, -1),
                jnp.take(torus.slots_of(index), device),
                axis=0,
            )
        x = torus.scatter_sum(partial.reshape(c, chips * rows, gate_and_up), 2)
        x = torus.exchange_sum(x, (1, 0), beside)
        return torus.gather((x * factor).astype(BF16), 2).reshape(tokens, gate_and_up)

    hidden = frozen.shape[2]
    tiles = hidden // tile_of(hidden, 256)
    chunks = []
    for share in OUTER_SHARES:
        first = sum(v.shape[1] for v in chunks)
        chunks.append(activations[:, first : first + width * share // sum(OUTER_SHARES)])
    outer = []
    for x in chunks:
        x = torus.gather(after(x, outer[-1]) if outer else x, 0)
        outer.append(x.reshape(a * rows, -1))
    parts = []
    for x, cuts in zip(outer, INNER_CUTS):
        step = x.shape[1] // cuts
        parts += [x[:, j * step : (j + 1) * step] for j in range(cuts)]
    base = None
    gathered = []
    first = 0
    for q, x in enumerate(parts):
        near = [x] + [torus.move(x, 1, -k) for k in range(1, b)]
        near[1:] = lax.optimization_barrier((*near[1:], base if q else outer[-1]))[:-1]
        far = [torus.move(v, 2, -1) for v in near]
        gathered.append([*near, *far])
        for cut in parts_of(tiles, 4 if q == len(parts) - 1 else 1):
            base = forward_chunk(gathered[q], frozen, base, first, cut)
        first += x.shape[1]

    columns, partial_in = low_in_partial(
        gathered, segment[:, None], adapter_down_factors, seg_adapter, places, index, rows
    )
    low_in = whole_sum(partial_in)
    dgate, dup, partial_out = middle(
        base, dhidden, token_order, order, low_in, segment[:, None], adapter_up_factors,
        seg_adapter, places, rows,
    )
    thirds = parts_of(tiles, 3)
    grad_b = []

    def grad_b_part(token):
        grad_b.append(
            grad_b_of(
                dgate, dup, order, after(low_in, token), adapter[None, :], adapter_list,
                grad_b[-1] if grad_b else None, thirds[len(grad_b)],
            )
        )
        return grad_b[-1]

    cuts = []
    for share in SUM_SHARES:
        cuts.append((sum(v[1] for v in cuts), width * share // sum(SUM_SHARES)))
    terms = []

    def first_term(token):
        terms.append(backward_chunk(frozen, after(dgate, token), dup, *cuts[0]))
        return terms[0][0]

    low_out = whole_sum(partial_out, [grad_b_part] * (len(thirds) - 1) + [first_term])
    near, far = terms[0][0], after(terms[0][1], low_out)
    side, side_far = side_of(
        order, low_out, segment[:, None], adapter_down_factors, seg_adapter, places
    )
    side_far = torus.move(side_far, 2, 1)
    at = jnp.stack([index // c, core]).astype(jnp.int32)
    sums, inners, inner_moves, outer_moves, blocks = [], [], [], [], []
    for q, (first, step) in enumerate(cuts):
        if q:
            near, far = backward_chunk(frozen, after(dgate, sums[-1][0]), dup, first, step)
            ahead = inner_moves[q - 1] + (outer_moves[q - 2] if q > 1 else [])
            if q == len(cuts) - 1:
                grad_a = grad_a_of(
                    columns, order, after(low_out, near), adapter[:, None], adapter_list
                )
                ahead = ahead + [grad_a]
            far = lax.optimization_barrier((far, *ahead))[0]
        far = torus.move(far, 2, 1)
        sums.append(core_sum(near, far, side, side_far, at, first, b))
        inner_moves.append([torus.move(sums[q][k], 1, k) for k in range(1, b)])
        total = sums[q][0].astype(F32)
        for v in inner_moves[q]:
            total = total + v.astype(F32)
        inners.append(total.astype(BF16).reshape(a, rows, step))
        outer_moves.append([torus.move(inners[q][k], 0, k) for k in range(1, a)])
    grad_b = grad_b_part(sums[-1][0])
    for q, inner in enumerate(inners):
        total = inner[0].astype(F32)
        for v in outer_moves[q]:
            v = lax.optimization_barrier((v, *inner_moves[-1]))[0] if q < len(cuts) - 1 else v
            total = total + v.astype(F32)
        blocks.append(total.astype(BF16))
    dinput = jnp.concatenate(blocks, axis=1)
    return (dinput, grad_a, grad_b)


def solution(mesh):
    placed = (
        P(("groups", "tensor"), None),
        P("groups", "tensor"),
        P(None, None, "tensor"),
        P(None, "tensor", None),
        P(None, None, "tensor"),
        P("groups", None),
        P("groups", None),
        P(),
    )
    return jax.shard_map(
        local,
        mesh=mesh,
        in_specs=placed,
        out_specs=(
            P(("groups", "tensor"), None),
            P("groups", "tensor", None),
            P("groups", None, "tensor"),
        ),
        check_vma=False,
    )
```

```python
import functools

import jax
import jax.numpy as jnp
from jax import lax
from jax.experimental import pallas as pl
from jax.experimental.pallas import tpu as pltpu
from jax.sharding import PartitionSpec as P

OUTER_SHARES = (3, 5)
INNER_CUTS = (1, 2)
SUM_SHARES = (5, 3)
MIB = 1024 * 1024
BF16 = jnp.bfloat16
DEPTH = 3
SLOTS = 4
ONCE = pl.Buffered(1)
F32 = jnp.float32


def dot(left, right, dims=((1,), (0,))):
    return lax.dot_general(left, right, (dims, ((), ())), preferred_element_type=F32)


def params(mib):
    return pltpu.CompilerParams(vmem_limit_bytes=mib * MIB)


def cost(flops, moved):
    return pl.CostEstimate(flops=int(flops), bytes_accessed=int(moved), transcendentals=0)


def tile_of(size, most):
    return most if size % most == 0 else size


def parts_of(count, parts):
    parts = min(parts, count)
    ends = [count * k // parts for k in range(parts + 1)]
    return list(zip(ends[:-1], ends[1:]))


def after(x, other):
    return lax.optimization_barrier((x, other))[0]


class Torus:
    def __init__(self, size):
        core = 2 if size % 2 == 0 else 1
        chips = size // core
        inner = 1
        while inner * 2 * inner * 2 <= chips and chips % (inner * 2) == 0:
            inner *= 2
        self.size = size
        self.dims = (chips // inner, inner, core)
        self.strides = (inner * core, core, 1)

    def place(self, index):
        return [index // s % n for s, n in zip(self.strides, self.dims)]

    def shifted(self, index, dim, by):
        at = index // self.strides[dim] % self.dims[dim]
        return index + ((at + by) % self.dims[dim] - at) * self.strides[dim]

    def move(self, x, dim, by):
        pairs = [(i, self.shifted(i, dim, by)) for i in range(self.size)]
        return lax.ppermute(x, "tensor", pairs)

    def gather(self, x, dim):
        return jnp.stack([x] + [self.move(x, dim, -k) for k in range(1, self.dims[dim])])

    def scatter_sum(self, x, dim):
        total = x[0].astype(F32)
        for k in range(1, self.dims[dim]):
            total = total + self.move(x[k], dim, k).astype(F32)
        return total

    def slot_devices(self, index):
        outer, inner, core = self.place(index)
        a, b, c = self.dims
        cs = lax.broadcasted_iota(jnp.int32, (c, b, a), 0)
        bs = lax.broadcasted_iota(jnp.int32, (c, b, a), 1)
        zs = lax.broadcasted_iota(jnp.int32, (c, b, a), 2)
        return (((outer + zs) % a * b + (inner + bs) % b) * c + (core + cs) % c).reshape(-1)

    def exchange_sum(self, x, dims, beside):
        beside = list(beside)
        for dim in dims:
            k = 1
            while k < self.dims[dim]:
                stride = self.strides[dim]
                pairs = [(i, i + ((i // stride ^ k) - i // stride) * stride) for i in range(self.size)]
                done = beside.pop(0)(x) if beside else None
                x = x + lax.ppermute(x, "tensor", pairs)
                x = x if done is None else after(x, done)
                k *= 2
        return x

    def slots_of(self, index):
        outer, inner, core = self.place(index)
        a, b, c = self.dims
        zs = lax.broadcasted_iota(jnp.int32, (a, b, c), 0)
        bs = lax.broadcasted_iota(jnp.int32, (a, b, c), 1)
        cs = lax.broadcasted_iota(jnp.int32, (a, b, c), 2)
        return (((cs - core) % c * b + (bs - inner) % b) * a + (zs - outer) % a).reshape(-1)


def tile_at(ref, n, tile):
    if ref.shape[1] == tile:
        return ref
    return ref.at[:, pl.ds(pl.multiple_of(n * tile, tile), tile)]


def ring(fetch, k, count):
    @pl.when(k == 0)
    def _():
        for j in range(min(DEPTH - 1, count)):
            for copy in fetch(j, j):
                copy.start()

    @pl.when(k + DEPTH - 1 < count)
    def _():
        for copy in fetch(k + DEPTH - 1, (k + DEPTH - 1) % DEPTH):
            copy.start()

    for copy in fetch(k, k % DEPTH):
        copy.wait()
    return k % DEPTH


def send(copy_of, k, count, fill):
    @pl.when(k >= SLOTS)
    def _():
        copy_of(k - SLOTS).wait()

    fill(k % SLOTS)
    copy_of(k).start()

    @pl.when(k == count - 1)
    def _():
        for j in range(min(SLOTS, count)):
            copy_of(k - j).wait()


def forward_kernel(pieces, low, count, first, *rest):
    parts, frozen, rest = rest[:pieces], rest[pieces], rest[pieces + 1 :]
    out, held, arrived = rest[-3:]
    step, tile = held.shape[2:]

    def fetch(n, slot):
        return [
            pltpu.make_async_copy(
                tile_at(frozen.at[i, pl.ds(first, step)], low + n, tile),
                held.at[slot, i],
                arrived.at[slot, i],
            )
            for i in range(2)
        ]

    slot = ring(fetch, pl.program_id(0), count)
    x = jnp.concatenate([v[...] for v in parts], axis=0)
    for i in range(2):
        part = dot(x, held[slot, i])
        out[i] = part if len(rest) == 3 else rest[0][i] + part


def forward_chunk(pieces, frozen, start, first, tiles):
    step = pieces[0].shape[1]
    tokens = sum(v.shape[0] for v in pieces)
    hidden = frozen.shape[2]
    tile = tile_of(hidden, 256)
    low, high = tiles
    across = pl.BlockSpec((2, tokens, tile), lambda n: (0, 0, low + n))
    operands = [*pieces, frozen]
    specs = [pl.BlockSpec(v.shape, lambda n: (0, 0), pipeline_mode=ONCE) for v in pieces]
    specs.append(pl.BlockSpec(memory_space=pltpu.HBM))
    if start is not None:
        operands.append(start)
        specs.append(across)
    count = high - low
    return pl.pallas_call(
        functools.partial(forward_kernel, len(pieces), low, count, first),
        grid=(count,),
        in_specs=specs,
        out_specs=across,
        out_shape=jax.ShapeDtypeStruct((2, tokens, hidden), F32),
        scratch_shapes=[
            pltpu.VMEM((DEPTH, 2, step, tile), BF16),
            pltpu.SemaphoreType.DMA((DEPTH, 2)),
        ],
        input_output_aliases={} if start is None else {len(operands) - 1: 0},
        compiler_params=params(24),
        cost_estimate=cost(4 * tokens * step * tile * count, 4 * step * tile * count),
    )(*operands)


def low_in_kernel(segments, chunks, rows, adapters, places, which, seg, *rest):
    factors, rest = rest[:segments], rest[segments:]
    cuts, (columns, out) = rest[:-2], rest[-2:]
    pieces = len(cuts) // chunks
    for q in range(chunks):

        @pl.when(which[0] == q)
        def _():
            first = 0
            for v in cuts[q * pieces : (q + 1) * pieces]:
                columns[first : first + v.shape[0]] = v[...]
                first += v.shape[0]

    total = jnp.zeros(out.shape, F32)
    for s in range(segments):
        part = dot(columns[...], factors[s][0])
        total = total + jnp.where(seg[...] == s, part, 0.0)
    put_rows(out, total, places, rows)


def put_rows(out, total, places, rows):
    if rows % 8:
        out[...] = total
        return
    for s in range(total.shape[0] // rows):
        out[pl.ds(pl.multiple_of(places[s] * rows, rows), rows), :] = total[s * rows : (s + 1) * rows]


def of_segment(shape, s):
    return pl.BlockSpec((1,) + shape[1:], lambda *a: (a[-2][s], 0, 0))


def low_in_partial(chunks, seg, down, adapters, places, index, rows):
    segments = adapters.shape[0]
    shard, wide = down.shape[1:]
    tokens = seg.shape[0]
    if shard % 128:
        joined = [jnp.concatenate(piece, axis=1) for piece in zip(*chunks)]
        chunks = [[lax.dynamic_slice_in_dim(v, index * shard, shard, 1) for v in joined]]
        which = jnp.zeros((1,), jnp.int32)
        cuts = [pl.BlockSpec(v.shape, lambda *a: (0, 0)) for v in chunks[0]]
    else:
        inside, at, cuts, first = [], [], [], 0
        for q, pieces in enumerate(chunks):
            per = pieces[0].shape[1] // shard
            inside.append(index >= first)
            at.append(jnp.clip(index - first, 0, per - 1))
            cuts += [
                pl.BlockSpec((v.shape[0], shard), lambda i, a, p, w, q=q: (0, w[1 + q])) for v in pieces
            ]
            first += per
        which = jnp.stack([sum(v.astype(jnp.int32) for v in inside) - 1] + at).astype(jnp.int32)
    full = lambda shape: pl.BlockSpec(shape, lambda *a: (0,) * len(shape))
    factor = lambda s: pl.BlockSpec((1, shard, wide), lambda i, a, p, w: (a[s], 0, 0))
    return pl.pallas_call(
        functools.partial(low_in_kernel, segments, len(chunks), rows),
        grid_spec=pltpu.PrefetchScalarGridSpec(
            num_scalar_prefetch=3,
            grid=(1,),
            in_specs=[full(seg.shape)] + [factor(s) for s in range(segments)] + cuts,
            out_specs=[full((tokens, shard)), full((tokens, wide))],
        ),
        out_shape=[
            jax.ShapeDtypeStruct((tokens, shard), BF16),
            jax.ShapeDtypeStruct((tokens, wide), F32),
        ],
        compiler_params=params(16),
        cost_estimate=cost(2 * tokens * down[0].size * segments, 2 * down[0].size * segments),
    )(adapters, places, which, seg, *([down] * segments), *[v for pieces in chunks for v in pieces])


def middle_kernel(rows, adapters, places, base, dhidden, token_order, order, low, seg, up, *rest):
    dgate, dup, out, left, back, factors, arrived = rest
    segments, wide, tile = factors.shape[1:]
    rank = wide // 2
    tokens = order.shape[0]
    n = pl.program_id(0)
    slot = n % 2
    lane = lax.broadcasted_iota(jnp.int32, (tokens, segments * rank), 1) // rank
    mask = lane == seg[...]

    def fetch(n, slot, s):
        return pltpu.make_async_copy(
            tile_at(up.at[adapters[s]], n, tile), factors.at[slot, s], arrived.at[slot, s]
        )

    @pl.when(n == 0)
    def _():
        for s in range(segments):
            fetch(0, 0, s).start()
        mine = dot(order[...], low[...])
        for i in range(2):
            block = jnp.concatenate([mine[:, i * rank : (i + 1) * rank]] * segments, axis=1)
            left[i] = jnp.where(mask, block, 0.0).astype(BF16)
        back[...] = jnp.zeros_like(back)

    @pl.when(n + 1 < pl.num_programs(0))
    def _():
        for s in range(segments):
            fetch(n + 1, 1 - slot, s).start()

    for s in range(segments):
        fetch(n, slot, s).wait()
    up_g = jnp.concatenate([factors[slot, s, :rank] for s in range(segments)], axis=0)
    up_u = jnp.concatenate([factors[slot, s, rank:] for s in range(segments)], axis=0)
    gate = base[0] + dot(left[0], up_g)
    up_sum = base[1] + dot(left[1], up_u)
    grad = dot(token_order[...], dhidden[...])
    sigma = 1.0 / (1.0 + jnp.exp(-gate))
    g = (grad * up_sum * sigma * (1.0 + gate * (1.0 - sigma))).astype(BF16)
    u = (grad * gate * sigma).astype(BF16)
    dgate[...] = g
    dup[...] = u
    back[0] += dot(g, up_g, ((1,), (1,)))
    back[1] += dot(u, up_u, ((1,), (1,)))

    @pl.when(n == pl.num_programs(0) - 1)
    def _():
        parts = []
        for i in range(2):
            kept = jnp.where(mask, back[i], 0.0)
            parts.append(sum(kept[:, s * rank : (s + 1) * rank] for s in range(segments)))
        put_rows(out, jnp.concatenate(parts, axis=1), places, rows)


def middle(base, dhidden, token_order, order, low, seg, up, adapters, places, rows):
    segments = adapters.shape[0]
    tokens, hidden = dhidden.shape
    wide = up.shape[1]
    tile = tile_of(hidden, 256)
    full = lambda shape: pl.BlockSpec(shape, lambda *a: (0,) * len(shape))
    across = lambda lead: pl.BlockSpec(lead + (tokens, tile), lambda n, *a: (0,) * len(lead) + (0, n))
    return pl.pallas_call(
        functools.partial(middle_kernel, rows),
        grid_spec=pltpu.PrefetchScalarGridSpec(
            num_scalar_prefetch=2,
            grid=(hidden // tile,),
            in_specs=[across((2,)), across(())]
            + [full(v.shape) for v in (token_order, order, low, seg)]
            + [pl.BlockSpec(memory_space=pltpu.HBM)],
            out_specs=[across(()), across(()), full((tokens, wide))],
            scratch_shapes=[
                pltpu.VMEM((2, tokens, segments * wide // 2), BF16),
                pltpu.VMEM((2, tokens, segments * wide // 2), F32),
                pltpu.VMEM((2, segments, wide, tile), BF16),
                pltpu.SemaphoreType.DMA((2, segments)),
            ],
        ),
        out_shape=[
            jax.ShapeDtypeStruct((tokens, hidden), BF16),
            jax.ShapeDtypeStruct((tokens, hidden), BF16),
            jax.ShapeDtypeStruct((tokens, wide), F32),
        ],
        compiler_params=params(44),
        cost_estimate=cost(
            4 * tokens * hidden * segments * wide, hidden * (tokens * 14 + segments * wide * 2)
        ),
    )(adapters, places, base, dhidden, token_order, order, low, seg, up)


def grad_b_kernel(first, count, dgate, dup, order, low, adapter, *rest):
    out, left, staged, sent = rest[-4:]
    group, wide, tile = staged.shape[1:]
    groups = left.shape[1]
    rank = wide // 2
    g = pl.program_id(1)
    k = pl.program_id(0) * groups + g

    @pl.when(k == 0)
    def _():
        turned = dot(order[...], low[...]).T
        for a in range(groups * group):
            kept = jnp.where(adapter[...] == a, turned, 0.0).astype(BF16)
            at = (a // group, slice(a % group * rank, (a % group + 1) * rank))
            left[(0, *at)] = kept[:rank]
            left[(1, *at)] = kept[rank:]

    def copy_of(k):
        block = out.at[pl.ds(k % groups * group, group)]
        if out.shape[2] != tile:
            at = pl.multiple_of((first + k // groups) * tile, tile)
            block = block.at[:, :, pl.ds(at, tile)]
        return pltpu.make_async_copy(staged.at[k % SLOTS], block, sent.at[k % SLOTS])

    def fill(slot):
        for i, grad in enumerate((dgate, dup)):
            part = dot(left[i, g], grad[...])
            staged[slot, :, i * rank : (i + 1) * rank, :] = part.reshape(group, rank, tile)

    send(copy_of, k, count * groups, fill)


def grad_b_of(dgate, dup, order, low, adapter_row, adapters, start, tiles):
    tokens, hidden = dgate.shape
    wide = low.shape[1]
    tile = tile_of(hidden, 256)
    first, last = tiles
    groups = 2 if adapters % 2 == 0 else 1
    group = adapters // groups
    full = lambda shape: pl.BlockSpec(shape, lambda n, g: (0,) * len(shape))
    across = pl.BlockSpec((tokens, tile), lambda n, g: (0, first + n))
    operands = [dgate, dup, order, low, adapter_row]
    specs = [across, across, full(order.shape), full(low.shape), full(adapter_row.shape)]
    if start is not None:
        operands.append(start)
        specs.append(pl.BlockSpec(memory_space=pltpu.HBM))
    part = tile * (last - first) * adapters * wide
    return pl.pallas_call(
        functools.partial(grad_b_kernel, first, last - first),
        grid=(last - first, groups),
        in_specs=specs,
        out_specs=pl.BlockSpec(memory_space=pltpu.HBM),
        out_shape=jax.ShapeDtypeStruct((adapters, wide, hidden), F32),
        scratch_shapes=[
            pltpu.VMEM((2, groups, group * wide // 2, tokens), BF16),
            pltpu.VMEM((SLOTS, group, wide, tile), F32),
            pltpu.SemaphoreType.DMA((SLOTS,)),
        ],
        input_output_aliases={} if start is None else {5: 0},
        compiler_params=params(20),
        cost_estimate=cost(2 * tokens * part, 4 * part),
    )(*operands)


def grad_a_kernel(columns, order, low, adapter, out, turned, mine, staged, sent):
    per = staged.shape[1]
    k = pl.program_id(0)

    @pl.when(k == 0)
    def _():
        turned[...] = columns[...].astype(F32).T.astype(BF16)
        mine[...] = dot(order[...], low[...])

    def copy_of(k):
        return pltpu.make_async_copy(
            staged.at[k % SLOTS], out.at[pl.ds(k * per, per)], sent.at[k % SLOTS]
        )

    def fill(slot):
        for j in range(per):
            kept = jnp.where(adapter[...] == k * per + j, mine[...], 0.0).astype(BF16)
            staged[slot, j] = dot(turned[...], kept)

    send(copy_of, k, out.shape[0] // per, fill)


def grad_a_of(columns, order, low, adapter, adapters):
    tokens, shard = columns.shape
    wide = low.shape[1]
    per = 4 if adapters % 4 == 0 else 1
    full = lambda shape: pl.BlockSpec(shape, lambda n: (0,) * len(shape))
    return pl.pallas_call(
        grad_a_kernel,
        grid=(adapters // per,),
        in_specs=[full(columns.shape), full(order.shape), full(low.shape), full(adapter.shape)],
        out_specs=pl.BlockSpec(memory_space=pltpu.HBM),
        out_shape=jax.ShapeDtypeStruct((adapters, shard, wide), F32),
        scratch_shapes=[
            pltpu.VMEM((shard, tokens), BF16),
            pltpu.VMEM((tokens, wide), F32),
            pltpu.VMEM((SLOTS, per, shard, wide), F32),
            pltpu.SemaphoreType.DMA((SLOTS,)),
        ],
        compiler_params=params(16),
        cost_estimate=cost(2 * tokens * shard * adapters * wide, 4 * shard * adapters * wide),
    )(columns, order, low, adapter)


def side_kernel(segments, adapters, places, order, low, seg, *rest):
    near, far = rest[-2:]
    half = near.shape[0]
    mine = dot(order[...], low[...])
    total = jnp.zeros((2 * half, near.shape[1]), F32)
    for s in range(segments):
        kept = jnp.where(seg[...] == s, mine, 0.0).astype(BF16)
        total = total + dot(kept, rest[s][0], ((1,), (1,)))
    near[...] = total[:half]
    far[...] = total[half:]


def side_of(order, low, seg, down, adapters, places):
    segments = adapters.shape[0]
    tokens = order.shape[0]
    shard = down.shape[1]
    full = lambda shape: pl.BlockSpec(shape, lambda *a: (0,) * len(shape))
    return pl.pallas_call(
        functools.partial(side_kernel, segments),
        grid_spec=pltpu.PrefetchScalarGridSpec(
            num_scalar_prefetch=2,
            grid=(1,),
            in_specs=[full(order.shape), full(low.shape), full(seg.shape)]
            + [of_segment(down.shape, s) for s in range(segments)],
            out_specs=[full((tokens // 2, shard))] * 2,
        ),
        out_shape=[jax.ShapeDtypeStruct((tokens // 2, shard), F32)] * 2,
        compiler_params=params(16),
        cost_estimate=cost(2 * tokens * down[0].size * segments, 2 * down[0].size * segments),
    )(adapters, places, order, low, seg, *([down] * segments))


def backward_kernel(count, first, frozen, dgate, dup, near, far, held, arrived):
    half = near.shape[0]
    block = held.shape[2]

    def fetch(k, slot):
        rows = pl.ds(pl.multiple_of(first + k * block, block), block)
        return [
            pltpu.make_async_copy(frozen.at[i, rows, :], held.at[slot, i], arrived.at[slot, i])
            for i in range(2)
        ]

    slot = ring(fetch, pl.program_id(0), count)
    term = dot(dgate[...], held[slot, 0], ((1,), (1,))) + dot(dup[...], held[slot, 1], ((1,), (1,)))
    near[...] = term[:half].astype(BF16)
    far[...] = term[half:].astype(BF16)


def backward_chunk(frozen, dgate, dup, first, step):
    tokens, hidden = dgate.shape
    block = tile_of(step, 512)
    count = step // block
    full = lambda shape: pl.BlockSpec(shape, lambda k: (0, 0), pipeline_mode=ONCE)
    out = pl.BlockSpec((tokens // 2, block), lambda k: (0, k))
    return pl.pallas_call(
        functools.partial(backward_kernel, count, first),
        grid=(count,),
        in_specs=[pl.BlockSpec(memory_space=pltpu.HBM), full(dgate.shape), full(dup.shape)],
        out_specs=[out, out],
        out_shape=[jax.ShapeDtypeStruct((tokens // 2, step), BF16)] * 2,
        scratch_shapes=[
            pltpu.VMEM((DEPTH, 2, block, hidden), BF16),
            pltpu.SemaphoreType.DMA((DEPTH, 2)),
        ],
        compiler_params=params(20),
        cost_estimate=cost(4 * tokens * step * hidden, 4 * step * hidden),
    )(frozen, dgate, dup)


def core_sum_kernel(base, at, near, far, side, side_far, *outs):
    total = near[...].astype(F32) + far[...].astype(F32)
    rows = outs[0].shape[0]
    own = at[0] == base + pl.program_id(0)

    def store(total):
        for s, out in enumerate(outs):
            out[...] = total[s * rows : (s + 1) * rows].astype(BF16)

    @pl.when(jnp.logical_not(own))
    def _():
        store(total)

    @pl.when(jnp.logical_and(own, at[1] == 0))
    def _():
        store(total + jnp.concatenate([side[...], side_far[...]], axis=1))

    @pl.when(jnp.logical_and(own, at[1] != 0))
    def _():
        store(total + jnp.concatenate([side_far[...], side[...]], axis=1))


def core_sum(near, far, side, side_far, at, first, slots):
    half, step = near.shape
    block = 2 * side.shape[1]
    full = lambda shape: pl.BlockSpec(shape, lambda *a: (0,) * len(shape))
    across = lambda rows: pl.BlockSpec((rows, block), lambda k, at: (0, k))
    return pl.pallas_call(
        functools.partial(core_sum_kernel, first // block),
        grid_spec=pltpu.PrefetchScalarGridSpec(
            num_scalar_prefetch=1,
            grid=(step // block,),
            in_specs=[across(half), across(half), full(side.shape), full(side_far.shape)],
            out_specs=[across(half // slots)] * slots,
        ),
        out_shape=[jax.ShapeDtypeStruct((half // slots, step), BF16)] * slots,
        compiler_params=params(16),
        cost_estimate=cost(2 * half * step, 6 * half * step),
    )(at, near, far, side, side_far)


def local(
    activations,
    dhidden,
    frozen,
    adapter_down_factors,
    adapter_up_factors,
    segment_adapter_index,
    segment_row_counts,
    ranks,
):
    adapter_list, shard_width, gate_and_up = adapter_down_factors.shape
    rank = gate_and_up // 2
    width = frozen.shape[1]
    rows = activations.shape[0]
    torus = Torus(width // shard_width)
    tokens = rows * torus.size
    a, b, c = torus.dims
    index = lax.axis_index("tensor")
    slots = torus.slot_devices(index)
    token = (slots[:, None] * rows + jnp.arange(rows, dtype=jnp.int32)[None, :]).reshape(-1)

    ends = jnp.cumsum(segment_row_counts[0])
    seg_adapter = segment_adapter_index[0]
    count = ends.shape[0]

    def segment_of(place):
        return jnp.sum((place[:, None] >= ends[None, :]).astype(jnp.int32), axis=1)

    def adapter_of(segment):
        match = segment[:, None] == jnp.arange(count, dtype=jnp.int32)[None, :]
        return jnp.sum(jnp.where(match, seg_adapter[None, :], 0), axis=1)

    column = jnp.arange(gate_and_up, dtype=jnp.int32) % rank
    chips = a * b
    core = index % c
    mine = (jnp.arange(chips, dtype=jnp.int32)[:, None] * c + core) * rows
    mine = (mine + jnp.arange(rows, dtype=jnp.int32)[None, :]).reshape(-1)
    my_adapter = adapter_of(segment_of(mine))
    hit = my_adapter[:, None] == jnp.arange(adapter_list, dtype=jnp.int32)[None, :]
    my_rank = jnp.sum(jnp.where(hit, ranks[None, :], 0), axis=1)[:, None]
    factor = jnp.where(column[None, :] < my_rank, 16.0 / my_rank.astype(F32), 0.0)

    places = (slots % c - core) % c * chips + slots // c
    spot = (places[:, None] * rows + jnp.arange(rows, dtype=jnp.int32)[None, :]).reshape(-1)
    count_up = jnp.arange(tokens, dtype=jnp.int32)[None, :]
    token_order = (token[:, None] == count_up).astype(BF16)
    order = (spot[:, None] == count_up).astype(BF16)

    segment = segment_of(token)
    adapter = adapter_of(segment)

    def whole_sum(partial, beside=()):
        if rows % 8:
            at = jnp.arange(torus.size, dtype=jnp.int32)
            device = at % chips * c + (core + at // chips) % c
            partial = jnp.take(
                partial.reshape(torus.size, rows, -1),
                jnp.take(torus.slots_of(index), device),
                axis=0,
            )
        x = torus.scatter_sum(partial.reshape(c, chips * rows, gate_and_up), 2)
        x = torus.exchange_sum(x, (1, 0), beside)
        return torus.gather((x * factor).astype(BF16), 2).reshape(tokens, gate_and_up)

    hidden = frozen.shape[2]
    tiles = hidden // tile_of(hidden, 256)
    chunks = []
    for share in OUTER_SHARES:
        first = sum(v.shape[1] for v in chunks)
        chunks.append(activations[:, first : first + width * share // sum(OUTER_SHARES)])
    outer = []
    for x in chunks:
        x = torus.gather(after(x, outer[-1]) if outer else x, 0)
        outer.append(x.reshape(a * rows, -1))
    parts = []
    for x, cuts in zip(outer, INNER_CUTS):
        step = x.shape[1] // cuts
        parts += [x[:, j * step : (j + 1) * step] for j in range(cuts)]
    base = None
    gathered = []
    first = 0
    for q, x in enumerate(parts):
        near = [x] + [torus.move(x, 1, -k) for k in range(1, b)]
        near[1:] = lax.optimization_barrier((*near[1:], base if q else outer[-1]))[:-1]
        far = [torus.move(v, 2, -1) for v in near]
        gathered.append([*near, *far])
        for cut in parts_of(tiles, 4 if q == len(parts) - 1 else 1):
            base = forward_chunk(gathered[q], frozen, base, first, cut)
        first += x.shape[1]

    columns, partial_in = low_in_partial(
        gathered, segment[:, None], adapter_down_factors, seg_adapter, places, index, rows
    )
    low_in = whole_sum(partial_in)
    dgate, dup, partial_out = middle(
        base, dhidden, token_order, order, low_in, segment[:, None], adapter_up_factors,
        seg_adapter, places, rows,
    )
    thirds = parts_of(tiles, 3)
    grad_b = []

    def grad_b_part(token):
        grad_b.append(
            grad_b_of(
                dgate, dup, order, after(low_in, token), adapter[None, :], adapter_list,
                grad_b[-1] if grad_b else None, thirds[len(grad_b)],
            )
        )
        return grad_b[-1]

    cuts = []
    for share in SUM_SHARES:
        cuts.append((sum(v[1] for v in cuts), width * share // sum(SUM_SHARES)))
    terms = []

    def first_term(token):
        terms.append(backward_chunk(frozen, after(dgate, token), dup, *cuts[0]))
        return terms[0][0]

    low_out = whole_sum(partial_out, [grad_b_part] * (len(thirds) - 1) + [first_term])
    near, far = terms[0][0], after(terms[0][1], low_out)
    side, side_far = side_of(
        order, low_out, segment[:, None], adapter_down_factors, seg_adapter, places
    )
    side_far = torus.move(side_far, 2, 1)
    at = jnp.stack([index // c, core]).astype(jnp.int32)
    sums, inners, inner_moves, outer_moves, blocks = [], [], [], [], []
    for q, (first, step) in enumerate(cuts):
        if q:
            near, far = backward_chunk(frozen, after(dgate, sums[-1][0]), dup, first, step)
            ahead = inner_moves[q - 1] + (outer_moves[q - 2] if q > 1 else [])
            if q == len(cuts) - 1:
                grad_a = grad_a_of(
                    columns, order, after(low_out, near), adapter[:, None], adapter_list
                )
                ahead = ahead + [grad_a]
            far = lax.optimization_barrier((far, *ahead))[0]
        far = torus.move(far, 2, 1)
        sums.append(core_sum(near, far, side, side_far, at, first, b))
        inner_moves.append([torus.move(sums[q][k], 1, k) for k in range(1, b)])
        total = sums[q][0].astype(F32)
        for v in inner_moves[q]:
            total = total + v.astype(F32)
        inners.append(total.astype(BF16).reshape(a, rows, step))
        outer_moves.append([torus.move(inners[q][k], 0, k) for k in range(1, a)])
    grad_b = grad_b_part(sums[-1][0])
    for q, inner in enumerate(inners):
        total = inner[0].astype(F32)
        for v in outer_moves[q]:
            v = lax.optimization_barrier((v, *inner_moves[-1]))[0] if q < len(cuts) - 1 else v
            total = total + v.astype(F32)
        blocks.append(total.astype(BF16))
    dinput = jnp.concatenate(blocks, axis=1)
    return (dinput, grad_a, grad_b)


def solution(mesh):
    placed = (
        P(("groups", "tensor"), None),
        P("groups", "tensor"),
        P(None, None, "tensor"),
        P(None, "tensor", None),
        P(None, None, "tensor"),
        P("groups", None),
        P("groups", None),
        P(),
    )
    return jax.shard_map(
        local,
        mesh=mesh,
        in_specs=placed,
        out_specs=(
            P(("groups", "tensor"), None),
            P("groups", "tensor", None),
            P("groups", None, "tensor"),
        ),
        check_vma=False,
    )
```

```python
import functools

import jax
import jax.numpy as jnp
from jax import lax
from jax.experimental import pallas as pl
from jax.experimental.pallas import tpu as pltpu
from jax.sharding import PartitionSpec as P

OUTER_SHARES = (3, 5)
INNER_CUTS = (1, 2)
SUM_SHARES = (5, 3)
MIB = 1024 * 1024
BF16 = jnp.bfloat16
DEPTH = 3
SLOTS = 4
ONCE = pl.Buffered(1)
F32 = jnp.float32


def dot(left, right, dims=((1,), (0,))):
    return lax.dot_general(left, right, (dims, ((), ())), preferred_element_type=F32)


def params(mib):
    return pltpu.CompilerParams(vmem_limit_bytes=mib * MIB)


def cost(flops, moved):
    return pl.CostEstimate(flops=int(flops), bytes_accessed=int(moved), transcendentals=0)


def tile_of(size, most):
    return most if size % most == 0 else size


def parts_of(count, parts):
    parts = min(parts, count)
    ends = [count * k // parts for k in range(parts + 1)]
    return list(zip(ends[:-1], ends[1:]))


def after(x, other):
    return lax.optimization_barrier((x, other))[0]


class Torus:
    def __init__(self, size):
        core = 2 if size % 2 == 0 else 1
        chips = size // core
        inner = 1
        while inner * 2 * inner * 2 <= chips and chips % (inner * 2) == 0:
            inner *= 2
        self.size = size
        self.dims = (chips // inner, inner, core)
        self.strides = (inner * core, core, 1)

    def place(self, index):
        return [index // s % n for s, n in zip(self.strides, self.dims)]

    def shifted(self, index, dim, by):
        at = index // self.strides[dim] % self.dims[dim]
        return index + ((at + by) % self.dims[dim] - at) * self.strides[dim]

    def move(self, x, dim, by):
        pairs = [(i, self.shifted(i, dim, by)) for i in range(self.size)]
        return lax.ppermute(x, "tensor", pairs)

    def gather(self, x, dim):
        return jnp.stack([x] + [self.move(x, dim, -k) for k in range(1, self.dims[dim])])

    def scatter_sum(self, x, dim):
        total = x[0].astype(F32)
        for k in range(1, self.dims[dim]):
            total = total + self.move(x[k], dim, k).astype(F32)
        return total

    def slot_devices(self, index):
        outer, inner, core = self.place(index)
        a, b, c = self.dims
        cs = lax.broadcasted_iota(jnp.int32, (c, b, a), 0)
        bs = lax.broadcasted_iota(jnp.int32, (c, b, a), 1)
        zs = lax.broadcasted_iota(jnp.int32, (c, b, a), 2)
        return (((outer + zs) % a * b + (inner + bs) % b) * c + (core + cs) % c).reshape(-1)

    def exchange_sum(self, x, dims, beside):
        beside = list(beside)
        for dim in dims:
            k = 1
            while k < self.dims[dim]:
                stride = self.strides[dim]
                pairs = [(i, i + ((i // stride ^ k) - i // stride) * stride) for i in range(self.size)]
                done = beside.pop(0)(x) if beside else None
                x = x + lax.ppermute(x, "tensor", pairs)
                x = x if done is None else after(x, done)
                k *= 2
        return x

    def slots_of(self, index):
        outer, inner, core = self.place(index)
        a, b, c = self.dims
        zs = lax.broadcasted_iota(jnp.int32, (a, b, c), 0)
        bs = lax.broadcasted_iota(jnp.int32, (a, b, c), 1)
        cs = lax.broadcasted_iota(jnp.int32, (a, b, c), 2)
        return (((cs - core) % c * b + (bs - inner) % b) * a + (zs - outer) % a).reshape(-1)


def tile_at(ref, n, tile):
    if ref.shape[1] == tile:
        return ref
    return ref.at[:, pl.ds(pl.multiple_of(n * tile, tile), tile)]


def ring(fetch, k, count):
    @pl.when(k == 0)
    def _():
        for j in range(min(DEPTH - 1, count)):
            for copy in fetch(j, j):
                copy.start()

    @pl.when(k + DEPTH - 1 < count)
    def _():
        for copy in fetch(k + DEPTH - 1, (k + DEPTH - 1) % DEPTH):
            copy.start()

    for copy in fetch(k, k % DEPTH):
        copy.wait()
    return k % DEPTH


def send(copy_of, k, count, fill):
    @pl.when(k >= SLOTS)
    def _():
        copy_of(k - SLOTS).wait()

    fill(k % SLOTS)
    copy_of(k).start()

    @pl.when(k == count - 1)
    def _():
        for j in range(min(SLOTS, count)):
            copy_of(k - j).wait()


def forward_kernel(pieces, low, count, first, *rest):
    parts, frozen, rest = rest[:pieces], rest[pieces], rest[pieces + 1 :]
    out, held, arrived = rest[-3:]
    step, tile = held.shape[2:]

    def fetch(n, slot):
        return [
            pltpu.make_async_copy(
                tile_at(frozen.at[i, pl.ds(first, step)], low + n, tile),
                held.at[slot, i],
                arrived.at[slot, i],
            )
            for i in range(2)
        ]

    slot = ring(fetch, pl.program_id(0), count)
    x = jnp.concatenate([v[...] for v in parts], axis=0)
    for i in range(2):
        part = dot(x, held[slot, i])
        out[i] = part if len(rest) == 3 else rest[0][i] + part


def forward_chunk(pieces, frozen, start, first, tiles):
    step = pieces[0].shape[1]
    tokens = sum(v.shape[0] for v in pieces)
    hidden = frozen.shape[2]
    tile = tile_of(hidden, 256)
    low, high = tiles
    across = pl.BlockSpec((2, tokens, tile), lambda n: (0, 0, low + n))
    operands = [*pieces, frozen]
    specs = [pl.BlockSpec(v.shape, lambda n: (0, 0), pipeline_mode=ONCE) for v in pieces]
    specs.append(pl.BlockSpec(memory_space=pltpu.HBM))
    if start is not None:
        operands.append(start)
        specs.append(across)
    count = high - low
    return pl.pallas_call(
        functools.partial(forward_kernel, len(pieces), low, count, first),
        grid=(count,),
        in_specs=specs,
        out_specs=across,
        out_shape=jax.ShapeDtypeStruct((2, tokens, hidden), F32),
        scratch_shapes=[
            pltpu.VMEM((DEPTH, 2, step, tile), BF16),
            pltpu.SemaphoreType.DMA((DEPTH, 2)),
        ],
        input_output_aliases={} if start is None else {len(operands) - 1: 0},
        compiler_params=params(24),
        cost_estimate=cost(4 * tokens * step * tile * count, 4 * step * tile * count),
    )(*operands)


def low_in_kernel(segments, chunks, rows, adapters, places, which, seg, *rest):
    factors, rest = rest[:segments], rest[segments:]
    cuts, (columns, out) = rest[:-2], rest[-2:]
    pieces = len(cuts) // chunks
    for q in range(chunks):

        @pl.when(which[0] == q)
        def _():
            first = 0
            for v in cuts[q * pieces : (q + 1) * pieces]:
                columns[first : first + v.shape[0]] = v[...]
                first += v.shape[0]

    total = jnp.zeros(out.shape, F32)
    for s in range(segments):
        part = dot(columns[...], factors[s][0])
        total = total + jnp.where(seg[...] == s, part, 0.0)
    put_rows(out, total, places, rows)


def put_rows(out, total, places, rows):
    if rows % 8:
        out[...] = total
        return
    for s in range(total.shape[0] // rows):
        out[pl.ds(pl.multiple_of(places[s] * rows, rows), rows), :] = total[s * rows : (s + 1) * rows]


def of_segment(shape, s):
    return pl.BlockSpec((1,) + shape[1:], lambda *a: (a[-2][s], 0, 0))


def low_in_partial(chunks, seg, down, adapters, places, index, rows):
    segments = adapters.shape[0]
    shard, wide = down.shape[1:]
    tokens = seg.shape[0]
    if shard % 128:
        joined = [jnp.concatenate(piece, axis=1) for piece in zip(*chunks)]
        chunks = [[lax.dynamic_slice_in_dim(v, index * shard, shard, 1) for v in joined]]
        which = jnp.zeros((1,), jnp.int32)
        cuts = [pl.BlockSpec(v.shape, lambda *a: (0, 0)) for v in chunks[0]]
    else:
        inside, at, cuts, first = [], [], [], 0
        for q, pieces in enumerate(chunks):
            per = pieces[0].shape[1] // shard
            inside.append(index >= first)
            at.append(jnp.clip(index - first, 0, per - 1))
            cuts += [
                pl.BlockSpec((v.shape[0], shard), lambda i, a, p, w, q=q: (0, w[1 + q])) for v in pieces
            ]
            first += per
        which = jnp.stack([sum(v.astype(jnp.int32) for v in inside) - 1] + at).astype(jnp.int32)
    full = lambda shape: pl.BlockSpec(shape, lambda *a: (0,) * len(shape))
    factor = lambda s: pl.BlockSpec((1, shard, wide), lambda i, a, p, w: (a[s], 0, 0))
    return pl.pallas_call(
        functools.partial(low_in_kernel, segments, len(chunks), rows),
        grid_spec=pltpu.PrefetchScalarGridSpec(
            num_scalar_prefetch=3,
            grid=(1,),
            in_specs=[full(seg.shape)] + [factor(s) for s in range(segments)] + cuts,
            out_specs=[full((tokens, shard)), full((tokens, wide))],
        ),
        out_shape=[
            jax.ShapeDtypeStruct((tokens, shard), BF16),
            jax.ShapeDtypeStruct((tokens, wide), F32),
        ],
        compiler_params=params(16),
        cost_estimate=cost(2 * tokens * down[0].size * segments, 2 * down[0].size * segments),
    )(adapters, places, which, seg, *([down] * segments), *[v for pieces in chunks for v in pieces])


def middle_kernel(rows, adapters, places, base, dhidden, token_order, order, low, seg, up, *rest):
    dgate, dup, out, left, back, factors, arrived = rest
    segments, wide, tile = factors.shape[1:]
    rank = wide // 2
    tokens = order.shape[0]
    n = pl.program_id(0)
    slot = n % 2
    lane = lax.broadcasted_iota(jnp.int32, (tokens, segments * rank), 1) // rank
    mask = lane == seg[...]

    def fetch(n, slot, s):
        return pltpu.make_async_copy(
            tile_at(up.at[adapters[s]], n, tile), factors.at[slot, s], arrived.at[slot, s]
        )

    @pl.when(n == 0)
    def _():
        for s in range(segments):
            fetch(0, 0, s).start()
        mine = dot(order[...], low[...])
        for i in range(2):
            block = jnp.concatenate([mine[:, i * rank : (i + 1) * rank]] * segments, axis=1)
            left[i] = jnp.where(mask, block, 0.0).astype(BF16)
        back[...] = jnp.zeros_like(back)

    @pl.when(n + 1 < pl.num_programs(0))
    def _():
        for s in range(segments):
            fetch(n + 1, 1 - slot, s).start()

    for s in range(segments):
        fetch(n, slot, s).wait()
    up_g = jnp.concatenate([factors[slot, s, :rank] for s in range(segments)], axis=0)
    up_u = jnp.concatenate([factors[slot, s, rank:] for s in range(segments)], axis=0)
    gate = base[0] + dot(left[0], up_g)
    up_sum = base[1] + dot(left[1], up_u)
    grad = dot(token_order[...], dhidden[...])
    sigma = 1.0 / (1.0 + jnp.exp(-gate))
    g = (grad * up_sum * sigma * (1.0 + gate * (1.0 - sigma))).astype(BF16)
    u = (grad * gate * sigma).astype(BF16)
    dgate[...] = g
    dup[...] = u
    back[0] += dot(g, up_g, ((1,), (1,)))
    back[1] += dot(u, up_u, ((1,), (1,)))

    @pl.when(n == pl.num_programs(0) - 1)
    def _():
        parts = []
        for i in range(2):
            kept = jnp.where(mask, back[i], 0.0)
            parts.append(sum(kept[:, s * rank : (s + 1) * rank] for s in range(segments)))
        put_rows(out, jnp.concatenate(parts, axis=1), places, rows)


def middle(base, dhidden, token_order, order, low, seg, up, adapters, places, rows):
    segments = adapters.shape[0]
    tokens, hidden = dhidden.shape
    wide = up.shape[1]
    tile = tile_of(hidden, 256)
    full = lambda shape: pl.BlockSpec(shape, lambda *a: (0,) * len(shape))
    across = lambda lead: pl.BlockSpec(lead + (tokens, tile), lambda n, *a: (0,) * len(lead) + (0, n))
    return pl.pallas_call(
        functools.partial(middle_kernel, rows),
        grid_spec=pltpu.PrefetchScalarGridSpec(
            num_scalar_prefetch=2,
            grid=(hidden // tile,),
            in_specs=[across((2,)), across(())]
            + [full(v.shape) for v in (token_order, order, low, seg)]
            + [pl.BlockSpec(memory_space=pltpu.HBM)],
            out_specs=[across(()), across(()), full((tokens, wide))],
            scratch_shapes=[
                pltpu.VMEM((2, tokens, segments * wide // 2), BF16),
                pltpu.VMEM((2, tokens, segments * wide // 2), F32),
                pltpu.VMEM((2, segments, wide, tile), BF16),
                pltpu.SemaphoreType.DMA((2, segments)),
            ],
        ),
        out_shape=[
            jax.ShapeDtypeStruct((tokens, hidden), BF16),
            jax.ShapeDtypeStruct((tokens, hidden), BF16),
            jax.ShapeDtypeStruct((tokens, wide), F32),
        ],
        compiler_params=params(44),
        cost_estimate=cost(
            4 * tokens * hidden * segments * wide, hidden * (tokens * 14 + segments * wide * 2)
        ),
    )(adapters, places, base, dhidden, token_order, order, low, seg, up)


def grad_b_kernel(first, count, dgate, dup, order, low, adapter, *rest):
    out, left, staged, sent = rest[-4:]
    group, wide, tile = staged.shape[1:]
    groups = left.shape[1]
    rank = wide // 2
    g = pl.program_id(1)
    k = pl.program_id(0) * groups + g

    @pl.when(k == 0)
    def _():
        turned = dot(order[...], low[...]).T
        for a in range(groups * group):
            kept = jnp.where(adapter[...] == a, turned, 0.0).astype(BF16)
            at = (a // group, slice(a % group * rank, (a % group + 1) * rank))
            left[(0, *at)] = kept[:rank]
            left[(1, *at)] = kept[rank:]

    def copy_of(k):
        block = out.at[pl.ds(k % groups * group, group)]
        if out.shape[2] != tile:
            at = pl.multiple_of((first + k // groups) * tile, tile)
            block = block.at[:, :, pl.ds(at, tile)]
        return pltpu.make_async_copy(staged.at[k % SLOTS], block, sent.at[k % SLOTS])

    def fill(slot):
        for i, grad in enumerate((dgate, dup)):
            part = dot(left[i, g], grad[...])
            staged[slot, :, i * rank : (i + 1) * rank, :] = part.reshape(group, rank, tile)

    send(copy_of, k, count * groups, fill)


def grad_b_of(dgate, dup, order, low, adapter_row, adapters, start, tiles):
    tokens, hidden = dgate.shape
    wide = low.shape[1]
    tile = tile_of(hidden, 256)
    first, last = tiles
    groups = 2 if adapters % 2 == 0 else 1
    group = adapters // groups
    full = lambda shape: pl.BlockSpec(shape, lambda n, g: (0,) * len(shape))
    across = pl.BlockSpec((tokens, tile), lambda n, g: (0, first + n))
    operands = [dgate, dup, order, low, adapter_row]
    specs = [across, across, full(order.shape), full(low.shape), full(adapter_row.shape)]
    if start is not None:
        operands.append(start)
        specs.append(pl.BlockSpec(memory_space=pltpu.HBM))
    part = tile * (last - first) * adapters * wide
    return pl.pallas_call(
        functools.partial(grad_b_kernel, first, last - first),
        grid=(last - first, groups),
        in_specs=specs,
        out_specs=pl.BlockSpec(memory_space=pltpu.HBM),
        out_shape=jax.ShapeDtypeStruct((adapters, wide, hidden), F32),
        scratch_shapes=[
            pltpu.VMEM((2, groups, group * wide // 2, tokens), BF16),
            pltpu.VMEM((SLOTS, group, wide, tile), F32),
            pltpu.SemaphoreType.DMA((SLOTS,)),
        ],
        input_output_aliases={} if start is None else {5: 0},
        compiler_params=params(20),
        cost_estimate=cost(2 * tokens * part, 4 * part),
    )(*operands)


def grad_a_kernel(columns, order, low, adapter, out, turned, mine, staged, sent):
    per = staged.shape[1]
    k = pl.program_id(0)

    @pl.when(k == 0)
    def _():
        turned[...] = columns[...].astype(F32).T.astype(BF16)
        mine[...] = dot(order[...], low[...])

    def copy_of(k):
        return pltpu.make_async_copy(
            staged.at[k % SLOTS], out.at[pl.ds(k * per, per)], sent.at[k % SLOTS]
        )

    def fill(slot):
        for j in range(per):
            kept = jnp.where(adapter[...] == k * per + j, mine[...], 0.0).astype(BF16)
            staged[slot, j] = dot(turned[...], kept)

    send(copy_of, k, out.shape[0] // per, fill)


def grad_a_of(columns, order, low, adapter, adapters):
    tokens, shard = columns.shape
    wide = low.shape[1]
    per = 4 if adapters % 4 == 0 else 1
    full = lambda shape: pl.BlockSpec(shape, lambda n: (0,) * len(shape))
    return pl.pallas_call(
        grad_a_kernel,
        grid=(adapters // per,),
        in_specs=[full(columns.shape), full(order.shape), full(low.shape), full(adapter.shape)],
        out_specs=pl.BlockSpec(memory_space=pltpu.HBM),
        out_shape=jax.ShapeDtypeStruct((adapters, shard, wide), F32),
        scratch_shapes=[
            pltpu.VMEM((shard, tokens), BF16),
            pltpu.VMEM((tokens, wide), F32),
            pltpu.VMEM((SLOTS, per, shard, wide), F32),
            pltpu.SemaphoreType.DMA((SLOTS,)),
        ],
        compiler_params=params(16),
        cost_estimate=cost(tokens * shard * wide, shard * wide),
    )(columns, order, low, adapter)


def side_kernel(segments, adapters, places, order, low, seg, *rest):
    near, far = rest[-2:]
    half = near.shape[0]
    mine = dot(order[...], low[...])
    total = jnp.zeros((2 * half, near.shape[1]), F32)
    for s in range(segments):
        kept = jnp.where(seg[...] == s, mine, 0.0).astype(BF16)
        total = total + dot(kept, rest[s][0], ((1,), (1,)))
    near[...] = total[:half]
    far[...] = total[half:]


def side_of(order, low, seg, down, adapters, places):
    segments = adapters.shape[0]
    tokens = order.shape[0]
    shard = down.shape[1]
    full = lambda shape: pl.BlockSpec(shape, lambda *a: (0,) * len(shape))
    return pl.pallas_call(
        functools.partial(side_kernel, segments),
        grid_spec=pltpu.PrefetchScalarGridSpec(
            num_scalar_prefetch=2,
            grid=(1,),
            in_specs=[full(order.shape), full(low.shape), full(seg.shape)]
            + [of_segment(down.shape, s) for s in range(segments)],
            out_specs=[full((tokens // 2, shard))] * 2,
        ),
        out_shape=[jax.ShapeDtypeStruct((tokens // 2, shard), F32)] * 2,
        compiler_params=params(16),
        cost_estimate=cost(2 * tokens * down[0].size * segments, 2 * down[0].size * segments),
    )(adapters, places, order, low, seg, *([down] * segments))


def backward_kernel(count, first, frozen, dgate, dup, near, far, held, arrived):
    half = near.shape[0]
    block = held.shape[2]

    def fetch(k, slot):
        rows = pl.ds(pl.multiple_of(first + k * block, block), block)
        return [
            pltpu.make_async_copy(frozen.at[i, rows, :], held.at[slot, i], arrived.at[slot, i])
            for i in range(2)
        ]

    slot = ring(fetch, pl.program_id(0), count)
    term = dot(dgate[...], held[slot, 0], ((1,), (1,))) + dot(dup[...], held[slot, 1], ((1,), (1,)))
    near[...] = term[:half].astype(BF16)
    far[...] = term[half:].astype(BF16)


def backward_chunk(frozen, dgate, dup, first, step):
    tokens, hidden = dgate.shape
    block = tile_of(step, 512)
    count = step // block
    full = lambda shape: pl.BlockSpec(shape, lambda k: (0, 0), pipeline_mode=ONCE)
    out = pl.BlockSpec((tokens // 2, block), lambda k: (0, k))
    return pl.pallas_call(
        functools.partial(backward_kernel, count, first),
        grid=(count,),
        in_specs=[pl.BlockSpec(memory_space=pltpu.HBM), full(dgate.shape), full(dup.shape)],
        out_specs=[out, out],
        out_shape=[jax.ShapeDtypeStruct((tokens // 2, step), BF16)] * 2,
        scratch_shapes=[
            pltpu.VMEM((DEPTH, 2, block, hidden), BF16),
            pltpu.SemaphoreType.DMA((DEPTH, 2)),
        ],
        compiler_params=params(20),
        cost_estimate=cost(4 * tokens * step * hidden, 4 * step * hidden),
    )(frozen, dgate, dup)


def core_sum_kernel(base, at, near, far, side, side_far, *outs):
    total = near[...].astype(F32) + far[...].astype(F32)
    rows = outs[0].shape[0]
    own = at[0] == base + pl.program_id(0)

    def store(total):
        for s, out in enumerate(outs):
            out[...] = total[s * rows : (s + 1) * rows].astype(BF16)

    @pl.when(jnp.logical_not(own))
    def _():
        store(total)

    @pl.when(jnp.logical_and(own, at[1] == 0))
    def _():
        store(total + jnp.concatenate([side[...], side_far[...]], axis=1))

    @pl.when(jnp.logical_and(own, at[1] != 0))
    def _():
        store(total + jnp.concatenate([side_far[...], side[...]], axis=1))


def core_sum(near, far, side, side_far, at, first, slots):
    half, step = near.shape
    block = 2 * side.shape[1]
    full = lambda shape: pl.BlockSpec(shape, lambda *a: (0,) * len(shape))
    across = lambda rows: pl.BlockSpec((rows, block), lambda k, at: (0, k))
    return pl.pallas_call(
        functools.partial(core_sum_kernel, first // block),
        grid_spec=pltpu.PrefetchScalarGridSpec(
            num_scalar_prefetch=1,
            grid=(step // block,),
            in_specs=[across(half), across(half), full(side.shape), full(side_far.shape)],
            out_specs=[across(half // slots)] * slots,
        ),
        out_shape=[jax.ShapeDtypeStruct((half // slots, step), BF16)] * slots,
        compiler_params=params(16),
        cost_estimate=cost(2 * half * step, 6 * half * step),
    )(at, near, far, side, side_far)


def local(
    activations,
    dhidden,
    frozen,
    adapter_down_factors,
    adapter_up_factors,
    segment_adapter_index,
    segment_row_counts,
    ranks,
):
    adapter_list, shard_width, gate_and_up = adapter_down_factors.shape
    rank = gate_and_up // 2
    width = frozen.shape[1]
    rows = activations.shape[0]
    torus = Torus(width // shard_width)
    tokens = rows * torus.size
    a, b, c = torus.dims
    index = lax.axis_index("tensor")
    slots = torus.slot_devices(index)
    token = (slots[:, None] * rows + jnp.arange(rows, dtype=jnp.int32)[None, :]).reshape(-1)

    ends = jnp.cumsum(segment_row_counts[0])
    seg_adapter = segment_adapter_index[0]
    count = ends.shape[0]

    def segment_of(place):
        return jnp.sum((place[:, None] >= ends[None, :]).astype(jnp.int32), axis=1)

    def adapter_of(segment):
        match = segment[:, None] == jnp.arange(count, dtype=jnp.int32)[None, :]
        return jnp.sum(jnp.where(match, seg_adapter[None, :], 0), axis=1)

    column = jnp.arange(gate_and_up, dtype=jnp.int32) % rank
    chips = a * b
    core = index % c
    mine = (jnp.arange(chips, dtype=jnp.int32)[:, None] * c + core) * rows
    mine = (mine + jnp.arange(rows, dtype=jnp.int32)[None, :]).reshape(-1)
    my_adapter = adapter_of(segment_of(mine))
    hit = my_adapter[:, None] == jnp.arange(adapter_list, dtype=jnp.int32)[None, :]
    my_rank = jnp.sum(jnp.where(hit, ranks[None, :], 0), axis=1)[:, None]
    factor = jnp.where(column[None, :] < my_rank, 16.0 / my_rank.astype(F32), 0.0)

    places = (slots % c - core) % c * chips + slots // c
    spot = (places[:, None] * rows + jnp.arange(rows, dtype=jnp.int32)[None, :]).reshape(-1)
    count_up = jnp.arange(tokens, dtype=jnp.int32)[None, :]
    token_order = (token[:, None] == count_up).astype(BF16)
    order = (spot[:, None] == count_up).astype(BF16)

    segment = segment_of(token)
    adapter = adapter_of(segment)

    def whole_sum(partial, beside=()):
        if rows % 8:
            at = jnp.arange(torus.size, dtype=jnp.int32)
            device = at % chips * c + (core + at // chips) % c
            partial = jnp.take(
                partial.reshape(torus.size, rows, -1),
                jnp.take(torus.slots_of(index), device),
                axis=0,
            )
        x = torus.scatter_sum(partial.reshape(c, chips * rows, gate_and_up), 2)
        x = torus.exchange_sum(x, (1, 0), beside)
        return torus.gather((x * factor).astype(BF16), 2).reshape(tokens, gate_and_up)

    hidden = frozen.shape[2]
    tiles = hidden // tile_of(hidden, 256)
    chunks = []
    for share in OUTER_SHARES:
        first = sum(v.shape[1] for v in chunks)
        chunks.append(activations[:, first : first + width * share // sum(OUTER_SHARES)])
    outer = []
    for x in chunks:
        x = torus.gather(after(x, outer[-1]) if outer else x, 0)
        outer.append(x.reshape(a * rows, -1))
    parts = []
    for x, cuts in zip(outer, INNER_CUTS):
        step = x.shape[1] // cuts
        parts += [x[:, j * step : (j + 1) * step] for j in range(cuts)]
    base = None
    gathered = []
    first = 0
    for q, x in enumerate(parts):
        near = [x] + [torus.move(x, 1, -k) for k in range(1, b)]
        near[1:] = lax.optimization_barrier((*near[1:], base if q else outer[-1]))[:-1]
        far = [torus.move(v, 2, -1) for v in near]
        gathered.append([*near, *far])
        for cut in parts_of(tiles, 4 if q == len(parts) - 1 else 1):
            base = forward_chunk(gathered[q], frozen, base, first, cut)
        first += x.shape[1]

    columns, partial_in = low_in_partial(
        gathered, segment[:, None], adapter_down_factors, seg_adapter, places, index, rows
    )
    low_in = whole_sum(partial_in)
    dgate, dup, partial_out = middle(
        base, dhidden, token_order, order, low_in, segment[:, None], adapter_up_factors,
        seg_adapter, places, rows,
    )
    thirds = parts_of(tiles, 3)
    grad_b = []

    def grad_b_part(token):
        grad_b.append(
            grad_b_of(
                dgate, dup, order, after(low_in, token), adapter[None, :], adapter_list,
                grad_b[-1] if grad_b else None, thirds[len(grad_b)],
            )
        )
        return grad_b[-1]

    cuts = []
    for share in SUM_SHARES:
        cuts.append((sum(v[1] for v in cuts), width * share // sum(SUM_SHARES)))
    terms = []

    def first_term(token):
        terms.append(backward_chunk(frozen, after(dgate, token), dup, *cuts[0]))
        return terms[0][0]

    low_out = whole_sum(partial_out, [grad_b_part] * (len(thirds) - 1) + [first_term])
    near, far = terms[0][0], after(terms[0][1], low_out)
    side, side_far = side_of(
        order, low_out, segment[:, None], adapter_down_factors, seg_adapter, places
    )
    side_far = torus.move(side_far, 2, 1)
    at = jnp.stack([index // c, core]).astype(jnp.int32)
    sums, inners, inner_moves, outer_moves, blocks = [], [], [], [], []
    for q, (first, step) in enumerate(cuts):
        if q:
            near, far = backward_chunk(frozen, after(dgate, sums[-1][0]), dup, first, step)
            ahead = inner_moves[q - 1] + (outer_moves[q - 2] if q > 1 else [])
            if q == len(cuts) - 1:
                grad_a = grad_a_of(
                    columns, order, after(low_out, near), adapter[:, None], adapter_list
                )
                ahead = ahead + [grad_a]
            near = lax.optimization_barrier((near, *ahead))[0]
        far = torus.move(far, 2, 1)
        sums.append(core_sum(near, far, side, side_far, at, first, b))
        inner_moves.append([torus.move(sums[q][k], 1, k) for k in range(1, b)])
        total = sums[q][0].astype(F32)
        for v in inner_moves[q]:
            total = total + v.astype(F32)
        inners.append(total.astype(BF16).reshape(a, rows, step))
        outer_moves.append([torus.move(inners[q][k], 0, k) for k in range(1, a)])
    grad_b = grad_b_part(sums[-1][0])
    for q, inner in enumerate(inners):
        total = inner[0].astype(F32)
        for v in outer_moves[q]:
            v = lax.optimization_barrier((v, *inner_moves[-1]))[0] if q < len(cuts) - 1 else v
            total = total + v.astype(F32)
        blocks.append(total.astype(BF16))
    dinput = jnp.concatenate(blocks, axis=1)
    return (dinput, grad_a, grad_b)


def solution(mesh):
    placed = (
        P(("groups", "tensor"), None),
        P("groups", "tensor"),
        P(None, None, "tensor"),
        P(None, "tensor", None),
        P(None, None, "tensor"),
        P("groups", None),
        P("groups", None),
        P(),
    )
    return jax.shard_map(
        local,
        mesh=mesh,
        in_specs=placed,
        out_specs=(
            P(("groups", "tensor"), None),
            P("groups", "tensor", None),
            P("groups", None, "tensor"),
        ),
        check_vma=False,
    )
```
